32 devices in a mesh: rep: 2 (over y), dev: 4 (over z), side: 4 (over x, core).
Axes of the slice: x: 2, y: 2, z: 4, core: 2. Of those that a mesh axis runs over, the one named last changes fastest.
Arguments:
- prompts: bfloat16 [2048, 7168], P(('rep', 'dev', 'side')), parts along dimension 0, may hold values from -6 to 6
- latent_weight: bfloat16 [7168, 576], P(('dev', 'side')), may hold values from -0.0625 to 0.0625
- latent_gain: float32 [512], replicated, may hold values from 0.25 to 1.75
- row_request: int32 [2048], P('rep'), parts along dimension 0, may hold values from 0 to 15, as said below
- context_len: int32 [32], P('rep'), parts along dimension 0, may hold values from 1 to 256, as said below
- request_slot: int32 [32], P('rep'), parts along dimension 0, may hold values from 0 to 31, as said below
- latent_cache: bfloat16 [64, 256, 576], P(('rep', 'dev')), parts along dimension 0, may hold values from -6 to 6
- new_latent: bfloat16 [64, 2, 576], P(('rep', 'dev')), parts along dimension 0, may hold values from -6 to 6
- queries: bfloat16 [64, 2, 128, 192], P(('rep', 'dev'), None, 'side'), parts along dimension 0, may hold values from -80 to 80
- key_absorb: bfloat16 [128, 128, 512], P('side'), may hold values from -0.5 to 0.5
- value_absorb: bfloat16 [128, 512, 128], P('side'), may hold values from -0.25 to 0.25
- out_weight: bfloat16 [16384, 7168], P('side', 'dev'), may hold values from -0.125 to 0.125
Outputs:
- decoded: bfloat16 [128, 7168], P(('rep', 'side'), 'dev'), parts along dimension 0
The draws below stay inside these ranges and needn't reach their ends.
There are 2 independent parts, one for each index of `rep`. The reference program is written for one: setup_inputs(seed, part) draws one part's arguments, and reference() takes and returns one part's arrays. A program takes and returns all parts, laid end to end along the dimension named above; an argument that names none is the same for every part. Nothing has to cross between parts.
Inputs may be any that keep to these rules, and one draw needn't show every extreme that they name: `request_slot`: slots are distinct; each decode group (slots g*8 to g*8 + 7) holds at least one request, and one group is full. `row_request`: in each aligned block of 64 rows, at most 32 rows belong to requests of one decode group (request_slot // 8); one group receives exactly 32 rows from every block. `context_len`: some request has exactly 256 cached rows.
All inputs are finite; a program needn't handle non-finite values.
Results may differ from the reference program's by a relative error of at most 0.0081.
Values may be sent and summed in bfloat16 or wider, within the bound.
No kernel may reach another device: no remote copies, remote signals or barrier semaphores. Data moves between devices by JAX's collectives and lax.ppermute only.
A program may use at most 128 MiB of HBM per device.

```python
import jax
import jax.numpy as jnp
from jax import lax

D = 7168
H = 128
NOPE = 128
ROPE = 64
LAT = 512
TOK_DEV = 64
CTX = 256
CAP = 8
STEPS = 2
KVW = 576
NGROUP = 4
SLOTS = 32
REQS = 16
BLOCKS = 16
TOKENS = 1024
BUCKET = 32
GROUP_ROWS = 512


def group_layout(key):
    layout_key = jax.random.fold_in(key, 101)
    star_key, priority_key, order_key = jax.random.split(layout_key, 3)
    star_group = jax.random.randint(star_key, (), 0, NGROUP)
    group_ids = jnp.arange(NGROUP)[:, None]
    slot_ids = jnp.arange(CAP)[None, :]
    candidate = (group_ids != star_group) & (slot_ids >= 1)
    priority = jax.random.permutation(priority_key, NGROUP * CAP).reshape(NGROUP, CAP)
    ranked = jnp.where(candidate, priority, NGROUP * CAP + 1)
    extra_count = REQS - NGROUP - CAP + 1
    threshold = jnp.sort(ranked.reshape(-1))[extra_count - 1]
    chosen = candidate & (ranked <= threshold)
    group_load = jnp.where(jnp.arange(NGROUP) == star_group, CAP, 1 + jnp.sum(chosen.astype(jnp.int32), axis=1))
    odd_group = group_ids % 2 == 1
    low_fill = slot_ids < group_load[:, None]
    high_fill = slot_ids >= CAP - group_load[:, None]
    occupied = jnp.where(odd_group, high_fill, low_fill).reshape(-1)
    order_score = jnp.where(occupied, jax.random.permutation(order_key, SLOTS), SLOTS + 1)
    request_slots = jnp.argsort(order_score)[:REQS].astype(jnp.int32)
    return (star_group, group_load.astype(jnp.int32), request_slots)


def draw_request_slot(key, part):
    layout = group_layout(key)
    return layout[2]


def draw_row_request(key, part):
    star_group, group_load, request_slots = group_layout(key)
    key = jax.random.fold_in(key, 5)
    first_key, second_key, third_key = jax.random.split(key, 3)
    group_perms = jax.vmap(lambda subkey: jax.random.permutation(subkey, NGROUP))(jax.random.split(first_key, BLOCKS))
    group_score = jnp.where(jnp.arange(NGROUP)[None, :] == star_group, -1, group_perms)
    picked = jnp.argsort(group_score, axis=1)[:, :NGROUP // 2]
    bucket_index = jnp.broadcast_to((jnp.arange(TOK_DEV) // BUCKET)[None, :], (BLOCKS, TOK_DEV))
    row_group = jnp.take_along_axis(picked, bucket_index, axis=1)
    row_perms = jax.vmap(lambda subkey: jax.random.permutation(subkey, TOK_DEV))(jax.random.split(second_key, BLOCKS))
    row_group = jnp.take_along_axis(row_group, row_perms, axis=1)
    within = jax.random.randint(third_key, (BLOCKS, TOK_DEV), 0, group_load[row_group])
    within = jnp.where(row_group % 2 == 1, CAP - 1 - within, within)
    slot_index = row_group * CAP + within
    request_of_slot = jnp.zeros((SLOTS,), jnp.int32).at[request_slots].set(jnp.arange(REQS, dtype=jnp.int32))
    return request_of_slot[slot_index].reshape(-1).astype(jnp.int32)


def draw_context_len(key, part):
    key = jax.random.fold_in(key, 7)
    first_key, second_key = jax.random.split(key)
    lengths = jax.random.randint(first_key, (REQS,), 1, CTX + 1)
    longest = jax.random.randint(second_key, (), 0, REQS)
    return lengths.at[longest].set(CTX).astype(jnp.int32)


def draw_new_latent(key, part):
    key = jax.random.fold_in(key, 13)
    drawn = jnp.clip(jax.random.normal(key, (SLOTS, STEPS, KVW), jnp.float32), -6.0, 6.0)
    return drawn.astype(jnp.bfloat16)


def draw_queries(key, part):
    key = jax.random.fold_in(key, 17)
    first_key = jax.random.fold_in(key, 0)
    drawn = jnp.clip(jax.random.normal(first_key, (SLOTS, STEPS, H, NOPE + ROPE), jnp.float32), -6.0, 6.0)
    drawn = drawn.at[..., NOPE:].multiply(3.0)
    return drawn.astype(jnp.bfloat16)


def level_of(own_key, dims, cuts, low, top_value):
    def one(axis_at, blocks):
        draws = jax.random.uniform(jax.random.fold_in(jax.random.fold_in(own_key, 6), axis_at), (blocks,), jnp.float32, low / len(cuts), top_value / len(cuts))
        return jnp.repeat(jnp.exp(draws), dims[axis_at] // blocks).reshape((-1,) + (1,) * (len(dims) - axis_at - 1))

    factor_of = one(*cuts[0])
    for cut in cuts[1:]:
        factor_of = factor_of * one(*cut)
    return factor_of


def centred(own_key, extent, scale, most, shards=(), held_as=jnp.bfloat16):
    loudness = level_of(own_key, extent, shards, -0.22, 0.18) if shards else 1.0
    entries = jax.random.normal(own_key, extent, jnp.float32) * scale * loudness
    return jnp.minimum(jnp.maximum(entries, -most), most).astype(held_as)


def setup_inputs(seed: int = 0, part: int = 0) -> dict:
    streams_of = jax.random.split(jax.random.key(seed), 13)
    part_splits = jax.random.split(jax.random.fold_in(streams_of[12], part), 13)
    prompts = centred(part_splits[0], (TOKENS, D), 1.0, 6.0, ((0, 16),))
    latent_weight = centred(streams_of[1], (D, KVW), D ** -0.5, 0.0625, ((0, 16),))
    latent_gain = jnp.clip(1.0 + 0.15 * jax.random.normal(streams_of[2], (LAT,), jnp.float32), 0.25, 1.75)
    row_request = draw_row_request(jax.random.fold_in(jax.random.fold_in(streams_of[12], part), 71), part)
    context_len = draw_context_len(jax.random.fold_in(jax.random.fold_in(streams_of[12], part), 71), part)
    request_slot = draw_request_slot(jax.random.fold_in(jax.random.fold_in(streams_of[12], part), 71), part)
    latent_cache = centred(part_splits[6], (SLOTS, CTX, KVW), 1.0, 6.0, ((0, 4),))
    new_latent = draw_new_latent(jax.random.fold_in(jax.random.fold_in(streams_of[12], part), 71), part)
    queries = draw_queries(jax.random.fold_in(jax.random.fold_in(streams_of[12], part), 71), part)
    key_absorb = centred(streams_of[9], (H, NOPE, LAT), NOPE ** -0.5, 0.5, ((0, 4),))
    value_absorb = centred(streams_of[10], (H, LAT, NOPE), LAT ** -0.5, 0.25, ((0, 4),))
    out_weight = centred(streams_of[11], (H * NOPE, D), (H * NOPE // 8) ** -0.5, 0.125, ((0, 4), (1, 4)))
    return dict(prompts=prompts, latent_weight=latent_weight, latent_gain=latent_gain, row_request=row_request, context_len=context_len, request_slot=request_slot, latent_cache=latent_cache, new_latent=new_latent, queries=queries, key_absorb=key_absorb, value_absorb=value_absorb, out_weight=out_weight)


masked_score = -1e+30

def rotate_pairs(values, position):
    half_width = values.shape[-1] // 2
    inverse = 1.0 / 10000.0 ** (jnp.arange(half_width, dtype=jnp.float32) * (2.0 / values.shape[-1]))
    angles = position.astype(jnp.float32)[:, None] * inverse[None, :]
    cosine = jnp.cos(angles)
    sine = jnp.sin(angles)
    first_half = values[:, :half_width]
    second_half = values[:, half_width:]
    return jnp.concatenate([first_half * cosine - second_half * sine, second_half * cosine + first_half * sine], axis=1)

def norm_and_rotate(raw, gain, position, lat_width):
    latent = raw[:, :lat_width]
    spread = lax.optimization_barrier(jnp.mean(latent * latent, axis=1, keepdims=True))
    normed = latent * lax.rsqrt(spread + 1e-06) * gain[None, :]
    return jnp.concatenate([normed, rotate_pairs(raw[:, lat_width:], position)], axis=1).astype(jnp.bfloat16)

def reference(prompts, latent_weight, latent_gain, row_request, context_len, request_slot, latent_cache, new_latent, queries, key_absorb, value_absorb, out_weight):
    req_hit = (row_request[:, None] == jnp.arange(REQS, dtype=jnp.int32)[None, :]).astype(jnp.int32)
    rank_global = lax.optimization_barrier(jnp.sum((jnp.cumsum(req_hit, axis=0) - req_hit) * req_hit, axis=1))
    position = context_len[row_request] + rank_global
    block_tokens = prompts.reshape(BLOCKS, TOK_DEV, D)
    block_position = position.reshape(BLOCKS, TOK_DEV)

    def prefill_block(pair):
        raw = jnp.dot(pair[0], latent_weight, preferred_element_type=jnp.float32)
        return norm_and_rotate(raw, latent_gain, pair[1], LAT)
    prompt_latent = lax.map(prefill_block, (block_tokens, block_position)).reshape(TOKENS, KVW)
    row_slot = request_slot[row_request]
    row_group = row_slot // CAP
    sorted_index = jnp.argsort(row_group, stable=True)
    sorted_rows = jnp.concatenate([prompt_latent[sorted_index], jnp.zeros((GROUP_ROWS, KVW), jnp.bfloat16)], axis=0)
    sorted_slot = jnp.concatenate([row_slot[sorted_index], jnp.full((GROUP_ROWS,), -1, jnp.int32)], axis=0)
    group_count = lax.optimization_barrier(jnp.sum((row_group[:, None] == jnp.arange(NGROUP, dtype=jnp.int32)[None, :]).astype(jnp.int32), axis=0))
    group_first = jnp.cumsum(group_count) - group_count
    score_scale = (NOPE + ROPE) ** (-0.5)

    def one_group(group):
        first_row = group_first[group].astype(jnp.int32)
        group_rows = lax.dynamic_slice_in_dim(sorted_rows, first_row, GROUP_ROWS, 0).astype(jnp.float32)
        group_slot = lax.dynamic_slice_in_dim(sorted_slot, first_row, GROUP_ROWS, 0)
        group_slot = jnp.where(jnp.arange(GROUP_ROWS) < group_count[group], group_slot, -1)
        base_slot = (group * CAP).astype(jnp.int32)
        own_slots = base_slot + jnp.arange(CAP, dtype=jnp.int32)
        slot_hit = (own_slots[:, None] == request_slot[None, :]).astype(jnp.int32)
        occupied = (lax.optimization_barrier(jnp.sum(slot_hit, axis=1)) > 0).astype(jnp.float32)
        ctx_rows = lax.optimization_barrier(jnp.sum(slot_hit * context_len[None, :], axis=1))
        cache_rows = lax.dynamic_slice_in_dim(latent_cache, base_slot, CAP, 0).astype(jnp.float32)
        fresh_rows = lax.dynamic_slice_in_dim(new_latent, base_slot, CAP, 0).astype(jnp.float32)
        group_queries = lax.dynamic_slice_in_dim(queries, base_slot, CAP, 0)
        query_latent = jnp.einsum('sthn,hnc->sthc', group_queries[..., :NOPE].astype(jnp.float32), key_absorb.astype(jnp.float32)).astype(jnp.bfloat16)
        query_full = jnp.concatenate([query_latent, group_queries[..., NOPE:]], axis=-1).astype(jnp.float32)
        score_cache = jnp.einsum('sthc,sjc->sthj', query_full, cache_rows) * score_scale
        score_prompt = jnp.einsum('sthc,pc->sthp', query_full, group_rows) * score_scale
        score_fresh = jnp.einsum('sthc,suc->sthu', query_full, fresh_rows) * score_scale
        mask_cache = (jnp.arange(CTX)[None, :] < ctx_rows[:, None])[:, None, None, :]
        mask_prompt = (group_slot[None, :] == own_slots[:, None])[:, None, None, :]
        mask_fresh = (jnp.arange(STEPS)[None, :] <= jnp.arange(STEPS)[:, None])[None, :, None, :]
        score_cache = jnp.where(mask_cache, score_cache, masked_score)
        score_prompt = jnp.where(mask_prompt, score_prompt, masked_score)
        score_fresh = jnp.where(mask_fresh, score_fresh, masked_score)
        largest = jnp.maximum(jnp.maximum(lax.optimization_barrier(jnp.max(score_cache, axis=-1, keepdims=True)), lax.optimization_barrier(jnp.max(score_prompt, axis=-1, keepdims=True))), lax.optimization_barrier(jnp.max(score_fresh, axis=-1, keepdims=True)))
        exp_cache = jnp.where(mask_cache, jnp.exp(score_cache - largest), 0.0)
        exp_prompt = jnp.where(mask_prompt, jnp.exp(score_prompt - largest), 0.0)
        exp_fresh = jnp.where(mask_fresh, jnp.exp(score_fresh - largest), 0.0)
        denominator = lax.optimization_barrier(jnp.sum(exp_cache, axis=-1, keepdims=True)) + lax.optimization_barrier(jnp.sum(exp_prompt, axis=-1, keepdims=True)) + lax.optimization_barrier(jnp.sum(exp_fresh, axis=-1, keepdims=True))
        weight_cache = (exp_cache / denominator).astype(jnp.bfloat16).astype(jnp.float32)
        weight_prompt = (exp_prompt / denominator).astype(jnp.bfloat16).astype(jnp.float32)
        weight_fresh = (exp_fresh / denominator).astype(jnp.bfloat16).astype(jnp.float32)
        head_latent = jnp.einsum('sthj,sjc->sthc', weight_cache, cache_rows[..., :LAT])
        head_latent = head_latent + jnp.einsum('sthp,pc->sthc', weight_prompt, group_rows[:, :LAT])
        head_latent = head_latent + jnp.einsum('sthu,suc->sthc', weight_fresh, fresh_rows[..., :LAT])
        head_latent = head_latent.astype(jnp.bfloat16).astype(jnp.float32)
        head_out = jnp.einsum('sthc,hcn->sthn', head_latent, value_absorb.astype(jnp.float32)) * occupied[:, None, None, None]
        head_out = head_out.astype(jnp.bfloat16).reshape(CAP * STEPS, H * NOPE)
        return jnp.dot(head_out, out_weight, preferred_element_type=jnp.float32).astype(jnp.bfloat16)
    return lax.map(one_group, jnp.arange(NGROUP, dtype=jnp.int32)).reshape(SLOTS * STEPS, D)
```

```python
import jax
import jax.numpy as jnp
from jax import lax
from jax.sharding import PartitionSpec as P

masked_score = -1e30


def swap(value, axis, step):
    count = lax.axis_size(axis)
    return lax.ppermute(value, axis, [(i, i ^ step) for i in range(count)])


def pick(pieces, index):
    out = pieces[0]
    for k in range(1, len(pieces)):
        out = jnp.where(index == k, pieces[k], out)
    return out


def on_device(
    prompts,
    latent_weight,
    latent_gain,
    row_request,
    context_len,
    request_slot,
    latent_cache,
    new_latent,
    queries,
    key_absorb,
    value_absorb,
    out_weight,
):
    dev_count = lax.axis_size("dev")
    side_count = lax.axis_size("side")
    block_count = dev_count * side_count
    tok_rows, model_width = prompts.shape
    shard_rows, kv_width = latent_weight.shape
    lat_width = latent_gain.shape[0]
    head_count, nope_width, _ = key_absorb.shape
    rope_width = kv_width - lat_width
    req_count = request_slot.shape[0]
    cap_slots, ctx_len, _ = latent_cache.shape
    step_count = new_latent.shape[1]
    bucket_rows = 2 * tok_rows // dev_count
    slab = model_width // dev_count
    row_count = head_count * cap_slots * step_count
    my_dev = lax.axis_index("dev")
    my_side = lax.axis_index("side")
    bf16, f32 = jnp.bfloat16, jnp.float32

    columns = [prompts[:, k * slab : (k + 1) * slab] for k in range(dev_count)]
    x_pieces = [None] * dev_count
    for k in sorted(range(dev_count), reverse=True):
        mine = pick(columns, my_dev ^ k)
        x_pieces[k] = swap(mine, "dev", k) if k else mine

    held = jnp.zeros((side_count, shard_rows, kv_width), bf16)
    for k in range(0, side_count, 2):
        piece = swap(latent_weight, "side", k) if k else latent_weight
        held = lax.dynamic_update_slice(held, piece[None], (my_side ^ k, 0, 0))
    same_core = held.reshape(side_count // 2, 2, shard_rows, kv_width)
    my_core = my_side % 2
    same_core = lax.dynamic_slice_in_dim(same_core, my_core, 1, 1)
    other_core = swap(same_core, "side", 1)
    held = lax.dynamic_update_slice(
        held.reshape(side_count // 2, 2, shard_rows, kv_width), other_core, (0, 1 - my_core, 0, 0)
    )
    slab_weight = held.reshape(slab, kv_width)

    request_ids = jnp.arange(req_count, dtype=jnp.int32)
    all_requests = row_request.reshape(block_count, tok_rows)
    hit = (all_requests[:, :, None] == request_ids).astype(f32)
    below = (jnp.arange(tok_rows)[:, None] > jnp.arange(tok_rows)[None, :]).astype(f32)
    rank_local = jnp.einsum("ij,bjr->bir", below, hit, preferred_element_type=f32)
    counts = jnp.sum(hit, axis=1)
    before = (jnp.arange(block_count)[:, None] > jnp.arange(block_count)[None, :]).astype(f32)
    earlier = jnp.einsum("ab,br->ar", before, counts, precision=lax.Precision.HIGHEST)
    position = jnp.sum(
        hit * (rank_local + earlier[:, None, :] + context_len.astype(f32)), axis=2
    )
    slot_table = jnp.sum(hit * request_slot.astype(f32), axis=2).astype(jnp.int32)
    row_group = slot_table // cap_slots
    group_ids = jnp.arange(dev_count, dtype=jnp.int32)
    group_hit = (row_group[:, :, None] == group_ids).astype(f32)
    group_rank = jnp.sum(
        jnp.einsum("ij,bjg->big", below, group_hit, preferred_element_type=f32) * group_hit, axis=2
    ).astype(jnp.int32)
    placed = (
        (row_group[:, None, None, :] == group_ids[None, :, None, None])
        & (
            group_rank[:, None, None, :]
            == jnp.arange(bucket_rows, dtype=jnp.int32)[None, None, :, None]
        )
    )
    line = lax.dynamic_index_in_dim(
        placed.reshape(dev_count, side_count, dev_count, bucket_rows, tok_rows),
        my_side, 1, keepdims=False,
    )
    to_me = lax.dynamic_index_in_dim(line, my_dev, 1, keepdims=False).astype(f32)
    line_position = lax.dynamic_index_in_dim(
        position.reshape(dev_count, side_count, tok_rows), my_side, 1, keepdims=False
    )
    routed_position = jnp.sum(to_me * line_position[:, None, :], axis=2).reshape(-1)
    group_placed = lax.dynamic_index_in_dim(placed, my_dev, 1, keepdims=False)
    row_slot = jnp.max(jnp.where(group_placed, slot_table[:, None, :], -1), axis=2)
    row_slot = jnp.swapaxes(row_slot.reshape(dev_count, side_count, bucket_rows), 0, 1)

    order = my_dev ^ jnp.arange(dev_count, dtype=jnp.int32)
    by_step = jnp.take(line, order, axis=1).astype(bf16)
    same = (jnp.arange(dev_count)[:, None] == order[None, :]).astype(bf16)
    route = jnp.swapaxes(by_step, 0, 1)[:, :, :, None, :] * same[None, :, None, :, None]
    route = route.reshape(dev_count * dev_count * bucket_rows, dev_count * tok_rows)

    half = rope_width // 2
    inverse = 1.0 / 10000.0 ** (jnp.arange(half, dtype=f32) * (2.0 / rope_width))
    angles = routed_position[:, None] * inverse[None, :]
    cosine, sine = jnp.cos(angles), jnp.sin(angles)

    query_latent = jnp.einsum(
        "sthn,hnc->hstc", queries[..., :nope_width], key_absorb, preferred_element_type=f32
    ).astype(bf16)
    query_full = jnp.concatenate(
        [query_latent, jnp.transpose(queries[..., nope_width:], (2, 0, 1, 3))], axis=-1
    )
    score_scale = queries.shape[-1] ** (-0.5)
    own_slots = my_dev * cap_slots + jnp.arange(cap_slots, dtype=jnp.int32)
    slot_hit = (own_slots[:, None] == request_slot[None, :]).astype(jnp.int32)
    occupied = (jnp.sum(slot_hit, axis=1) > 0).astype(f32)
    ctx_rows = jnp.sum(slot_hit * context_len[None, :], axis=1)
    score_cache = score_scale * jnp.einsum(
        "hstc,sjc->hstj", query_full, latent_cache, preferred_element_type=f32
    )
    score_fresh = score_scale * jnp.einsum(
        "hstc,suc->hstu", query_full, new_latent, preferred_element_type=f32
    )
    mask_cache = (jnp.arange(ctx_len)[None, :] < ctx_rows[:, None])[None, :, None, :]
    mask_fresh = (jnp.arange(step_count)[None, :] <= jnp.arange(step_count)[:, None])[None, None]
    score_cache = jnp.where(mask_cache, score_cache, masked_score)
    score_fresh = jnp.where(mask_fresh, score_fresh, masked_score)
    top_held = jnp.maximum(
        jnp.max(score_cache, axis=-1, keepdims=True), jnp.max(score_fresh, axis=-1, keepdims=True)
    )
    exp_cache = jnp.exp(score_cache - top_held)
    exp_fresh = jnp.exp(score_fresh - top_held)
    sum_held = jnp.sum(exp_cache, -1, keepdims=True) + jnp.sum(exp_fresh, -1, keepdims=True)
    mix_held = jnp.einsum(
        "hstj,sjc->hstc", exp_cache.astype(bf16), latent_cache[..., :lat_width],
        preferred_element_type=f32,
    ) + jnp.einsum(
        "hstu,suc->hstc", exp_fresh.astype(bf16), new_latent[..., :lat_width],
        preferred_element_type=f32,
    )
    query_rows = query_full.reshape(row_count, kv_width)
    top_held = top_held.reshape(row_count, 1)
    sum_held = sum_held.reshape(row_count, 1)
    mix_held = mix_held.reshape(row_count, lat_width)
    query_slot = jnp.broadcast_to(
        own_slots[None, :, None], (head_count, cap_slots, step_count)
    ).reshape(row_count, 1)
    live = jnp.broadcast_to(occupied[:, None], (cap_slots, step_count)).reshape(1, -1, 1)

    x_rows = jnp.concatenate(x_pieces, axis=0)
    partial_raw = jnp.dot(x_rows, slab_weight, preferred_element_type=f32).astype(bf16)
    routed = jnp.dot(route, partial_raw, preferred_element_type=f32).astype(bf16)
    routed = routed.reshape(dev_count, dev_count * bucket_rows, kv_width)
    total = None
    for k in sorted(range(dev_count), reverse=True):
        got = (swap(routed[k], "dev", k) if k else routed[0]).astype(f32)
        total = got if total is None else total + got
    latent = total[:, :lat_width]
    spread = jnp.mean(latent * latent, axis=1, keepdims=True)
    normed = latent * lax.rsqrt(spread + 1e-06) * latent_gain[None, :]
    first = total[:, lat_width : lat_width + half]
    second = total[:, lat_width + half :]
    latent_rows = jnp.concatenate(
        [normed, first * cosine - second * sine, second * cosine + first * sine], axis=1
    ).astype(bf16)
    pieces = [latent_rows] + [swap(latent_rows, "side", k) for k in range(1, side_count)]
    group_rows = jnp.concatenate(pieces, axis=0)
    side_order = my_side ^ jnp.arange(side_count)
    row_slot = jnp.take(row_slot, side_order, axis=0).reshape(1, -1)

    score = score_scale * lax.dot_general(
        query_rows, group_rows, (((1,), (1,)), ((), ())), preferred_element_type=f32
    )
    score = jnp.where(row_slot == query_slot, score, masked_score)
    top = jnp.maximum(top_held, jnp.max(score, axis=1, keepdims=True))
    weight = jnp.exp(score - top)
    scale_held = jnp.exp(top_held - top)
    denominator = sum_held * scale_held + jnp.sum(weight, axis=1, keepdims=True)
    mix = mix_held * scale_held + jnp.dot(
        weight.astype(bf16), group_rows[:, :lat_width], preferred_element_type=f32
    )
    head_latent = (mix / denominator).astype(bf16).reshape(head_count, -1, lat_width)
    head_out = jnp.einsum(
        "hrc,hcn->hrn", head_latent, value_absorb, preferred_element_type=f32
    ) * live
    head_out = jnp.transpose(head_out.astype(bf16), (1, 0, 2)).reshape(
        cap_slots * step_count, -1
    )

    outs = [head_out] + [swap(head_out, "dev", k) for k in range(1, dev_count)]
    partial_out = jnp.dot(
        jnp.concatenate(outs, axis=0), out_weight, preferred_element_type=f32
    ).reshape(dev_count, cap_slots * step_count, -1)
    per_side = partial_out.shape[0] // side_count
    result = None
    for k in sorted(range(side_count), reverse=True):
        rows = [
            lax.dynamic_index_in_dim(
                partial_out, my_dev ^ ((my_side ^ k) * per_side + q), 0, keepdims=False
            )
            for q in range(per_side)
        ]
        rows = jnp.concatenate(rows, axis=0)
        got = swap(rows.astype(bf16), "side", k).astype(f32) if k else rows
        result = got if result is None else result + got
    return result.astype(bf16)


def solution(mesh):
    placed = (
        P(("rep", "dev", "side"), None),
        P(("dev", "side"), None),
        P(),
        P("rep"),
        P("rep"),
        P("rep"),
        P(("rep", "dev"), None, None),
        P(("rep", "dev"), None, None),
        P(("rep", "dev"), None, "side", None),
        P("side", None, None),
        P("side", None, None),
        P("side", "dev"),
    )
    return jax.shard_map(
        on_device, mesh=mesh, in_specs=placed, out_specs=P(("rep", "side"), "dev"), check_vma=False
    )
```

```python
import functools

import jax
import jax.numpy as jnp
from jax import lax
from jax.experimental import pallas as pl
from jax.experimental.pallas import tpu as pltpu
from jax.sharding import PartitionSpec as P

masked_score = -1e30
bf16, f32 = jnp.bfloat16, jnp.float32
in_vmem = pl.BlockSpec(memory_space=pltpu.VMEM)
in_smem = pl.BlockSpec(memory_space=pltpu.SMEM)
anywhere = pl.BlockSpec(memory_space=pl.ANY)
mib = 1024 * 1024


def swap(value, axis, step):
    count = lax.axis_size(axis)
    return lax.ppermute(value, axis, [(i, i ^ step) for i in range(count)])


def pick(pieces, index):
    out = pieces[0]
    for k in range(1, len(pieces)):
        out = jnp.where(index == k, pieces[k], out)
    return out


def split_kernel(slab, here_ref, prompts_ref, *refs):
    out_refs, sems = refs[:-1], refs[-1]
    copies = []
    for n, out_ref in enumerate(out_refs):
        first = pl.multiple_of((here_ref[0] ^ (n + 1)) * slab, 128)
        copies.append(
            pltpu.make_async_copy(prompts_ref.at[:, pl.ds(first, slab)], out_ref, sems.at[n])
        )
    for copy in copies:
        copy.start()
    for copy in copies:
        copy.wait()


def split_columns(prompts, here, count):
    rows, width = prompts.shape
    slab = width // count
    if slab % 128:
        columns = [prompts[:, k * slab : (k + 1) * slab] for k in range(count)]
        return [pick(columns, here[0] ^ k) for k in range(1, count)]
    return pl.pallas_call(
        functools.partial(split_kernel, slab),
        out_shape=[jax.ShapeDtypeStruct((rows, slab), prompts.dtype)] * (count - 1),
        in_specs=[in_smem, anywhere],
        out_specs=[anywhere] * (count - 1),
        scratch_shapes=[pltpu.SemaphoreType.DMA((count - 1,))],
        name="split_columns",
    )(here, prompts)


def project_kernel(dev_count, side_count, here_ref, target_ref, *refs):
    x_refs = refs[:dev_count]
    weight_refs = refs[dev_count : dev_count + side_count]
    out_refs = refs[dev_count + side_count : -2]
    slab_weight, rows = refs[-2:]
    shard = weight_refs[0].shape[0]
    tok_rows = x_refs[0].shape[0]
    if side_count > 1:
        for k in range(side_count):
            first = pl.multiple_of((here_ref[1] ^ k) * shard, 16)
            slab_weight[pl.ds(first, shard), :] = weight_refs[k][...]
    for k in range(dev_count):
        rows[k * tok_rows : (k + 1) * tok_rows, :] = jnp.dot(
            x_refs[k][...], slab_weight[...] if side_count > 1 else weight_refs[0][...],
            preferred_element_type=f32,
        ).astype(bf16)
    group_rows = out_refs[0].shape[0]
    target = target_ref[...]
    for j in range(dev_count):
        ids = lax.broadcasted_iota(jnp.int32, (group_rows, target.shape[1]), 0) + j * group_rows
        route = jnp.where(ids == target, 1.0, 0.0).astype(bf16)
        out_refs[j][...] = jnp.dot(
            route, rows[...], preferred_element_type=f32
        ).astype(out_refs[j].dtype)


def project(x_pieces, weights, here, target, group_rows):
    dev_count, width = len(x_pieces), weights[0].shape[1]
    tok_rows, slab = x_pieces[0].shape
    return pl.pallas_call(
        functools.partial(project_kernel, dev_count, len(weights)),
        out_shape=[
            jax.ShapeDtypeStruct((group_rows, width), f32 if j == 0 else bf16)
            for j in range(dev_count)
        ],
        in_specs=[in_smem] + [in_vmem] * (1 + dev_count + len(weights)),
        out_specs=[in_vmem] * dev_count,
        scratch_shapes=[
            pltpu.VMEM((slab, width), bf16),
            pltpu.VMEM((dev_count * tok_rows, width), bf16),
        ],
        compiler_params=pltpu.CompilerParams(vmem_limit_bytes=16 * mib),
        name="project",
    )(here, target, *x_pieces, *weights)


def finish_kernel(gain_ref, cos_ref, sin_ref, *refs):
    parts, out_ref = refs[:-1], refs[-1]
    lat_width = gain_ref.shape[1]
    half = cos_ref.shape[1]
    total = parts[0][...].astype(f32)
    for part in parts[1:]:
        total = total + part[...].astype(f32)
    latent = total[:, :lat_width]
    spread = jnp.mean(latent * latent, axis=1, keepdims=True)
    out_ref[:, :lat_width] = (latent * lax.rsqrt(spread + 1e-06) * gain_ref[...]).astype(bf16)
    first = total[:, lat_width : lat_width + half]
    second = total[:, lat_width + half :]
    cosine, sine = cos_ref[...], sin_ref[...]
    turned = jnp.concatenate(
        [first * cosine - second * sine, second * cosine + first * sine], axis=1
    )
    out_ref[:, lat_width:] = turned.astype(bf16)


def finish(parts, gain, cosine, sine):
    return pl.pallas_call(
        finish_kernel,
        out_shape=jax.ShapeDtypeStruct(parts[0].shape, bf16),
        in_specs=[in_vmem] * (3 + len(parts)),
        out_specs=in_vmem,
        compiler_params=pltpu.CompilerParams(vmem_limit_bytes=8 * mib),
        name="finish_rows",
    )(gain, cosine, sine, *parts)


def attend_kernel(
    scale, cap_slots, step_count, base_ref, query_ref, fresh_ref, slot_ref, top_ref, sum_ref,
    mix_ref, live_ref, value_ref, *refs
):
    pieces, out_ref = refs[:-1], refs[-1]
    lat_width = mix_ref.shape[1]
    per_head = cap_slots * step_count
    heads = value_ref.shape[0]
    chunk_heads = min(8, heads)
    chunk = chunk_heads * per_head
    piece_rows = pieces[0].shape[0]
    contract = (((1,), (1,)), ((), ()))
    row = lax.broadcasted_iota(jnp.int32, (chunk, 1), 0)
    row_slot = (row // step_count) % cap_slots
    row_step = row % step_count
    key = lax.broadcasted_iota(jnp.int32, (1, per_head), 1)
    see_fresh = (key // step_count == row_slot) & (key % step_count <= row_step)
    for c in range(heads // chunk_heads):
        here = slice(c * chunk, (c + 1) * chunk)
        query = query_ref[here, :]
        fresh = lax.dot_general(query, fresh_ref[...], contract, preferred_element_type=f32)
        fresh = jnp.where(see_fresh, fresh * scale, masked_score)
        top = jnp.maximum(top_ref[here, :], jnp.max(fresh, axis=1, keepdims=True))
        scores = []
        for n, piece in enumerate(pieces):
            score = lax.dot_general(query, piece[...], contract, preferred_element_type=f32)
            slots = slot_ref[:, n * piece_rows : (n + 1) * piece_rows] - base_ref[0] * cap_slots
            score = jnp.where(slots == row_slot, score * scale, masked_score)
            top = jnp.maximum(top, jnp.max(score, axis=1, keepdims=True))
            scores.append(score)
        held = jnp.exp(top_ref[here, :] - top)
        weight = jnp.exp(fresh - top)
        total = sum_ref[here, :] * held + jnp.sum(weight, axis=1, keepdims=True)
        mix = mix_ref[here, :] * held + jnp.dot(
            weight.astype(bf16), fresh_ref[:, :lat_width], preferred_element_type=f32
        )
        for score, piece in zip(scores, pieces):
            weight = jnp.exp(score - top)
            total = total + jnp.sum(weight, axis=1, keepdims=True)
            mix = mix + jnp.dot(
                weight.astype(bf16), piece[:, :lat_width], preferred_element_type=f32
            )
        latent = (mix / total).astype(bf16)
        for h in range(chunk_heads):
            head = c * chunk_heads + h
            value = jnp.dot(
                latent[h * per_head : (h + 1) * per_head, :], value_ref[head],
                preferred_element_type=f32,
            )
            width = value.shape[1]
            out_ref[:, head * width : (head + 1) * width] = (value * live_ref[...]).astype(bf16)


def attend(scale, here, query, fresh, row_slot, top, total, mix, live, value, pieces, cap_slots):
    heads, _, width = value.shape
    step_count = fresh.shape[0] // cap_slots
    return pl.pallas_call(
        functools.partial(attend_kernel, scale, cap_slots, step_count),
        out_shape=jax.ShapeDtypeStruct((cap_slots * step_count, heads * width), bf16),
        in_specs=[in_smem] + [in_vmem] * (8 + len(pieces)),
        out_specs=in_vmem,
        compiler_params=pltpu.CompilerParams(vmem_limit_bytes=24 * mib),
        name="attend",
    )(here, query, fresh, row_slot, top, total, mix, live, value, *pieces)


def output_kernel(dev_count, side_count, here_ref, *refs):
    head_refs = refs[:dev_count]
    weight_ref = refs[dev_count]
    out_refs = refs[dev_count + 1 : -1]
    held = refs[-1]
    rows = head_refs[0].shape[0]
    per_side = dev_count // side_count
    for j in range(dev_count):
        group = here_ref[0] ^ j
        place = ((group // per_side) ^ here_ref[1]) * per_side + group % per_side
        held[pl.ds(pl.multiple_of(place * rows, 16), rows), :] = head_refs[j][...]
    columns = weight_ref.shape[1]
    tile = 256 if columns % 256 == 0 else columns
    side_rows = rows * per_side
    for n in range(columns // tile):
        here = slice(n * tile, (n + 1) * tile)
        product = jnp.dot(held[...], weight_ref[:, here], preferred_element_type=f32)
        for k in range(side_count):
            out_refs[k][:, here] = product[k * side_rows : (k + 1) * side_rows, :].astype(
                out_refs[k].dtype
            )


def output_product(head_pieces, weight, here, side_count):
    dev_count = len(head_pieces)
    rows, depth = head_pieces[0].shape
    columns = weight.shape[1]
    side_rows = rows * dev_count // side_count
    return pl.pallas_call(
        functools.partial(output_kernel, dev_count, side_count),
        out_shape=[
            jax.ShapeDtypeStruct((side_rows, columns), f32 if k == 0 else bf16)
            for k in range(side_count)
        ],
        in_specs=[in_smem] + [in_vmem] * (dev_count + 1),
        out_specs=[in_vmem] * side_count,
        scratch_shapes=[pltpu.VMEM((dev_count * rows, depth), bf16)],
        compiler_params=pltpu.CompilerParams(vmem_limit_bytes=24 * mib),
        name="output_product",
    )(here, *head_pieces, weight)


def on_device(
    prompts,
    latent_weight,
    latent_gain,
    row_request,
    context_len,
    request_slot,
    latent_cache,
    new_latent,
    queries,
    key_absorb,
    value_absorb,
    out_weight,
):
    dev_count = lax.axis_size("dev")
    side_count = lax.axis_size("side")
    block_count = dev_count * side_count
    tok_rows, model_width = prompts.shape
    shard_rows, kv_width = latent_weight.shape
    lat_width = latent_gain.shape[0]
    head_count, nope_width, _ = key_absorb.shape
    rope_width = kv_width - lat_width
    req_count = request_slot.shape[0]
    cap_slots, ctx_len, _ = latent_cache.shape
    step_count = new_latent.shape[1]
    bucket_rows = 2 * tok_rows // dev_count
    group_rows = dev_count * bucket_rows
    slab = model_width // dev_count
    row_count = head_count * cap_slots * step_count
    my_dev = lax.axis_index("dev")
    my_side = lax.axis_index("side")
    here = jnp.stack([my_dev, my_side]).astype(jnp.int32)

    mine = split_columns(prompts, here, dev_count)
    x_pieces = [lax.dynamic_slice_in_dim(prompts, my_dev * slab, slab, 1)] + [None] * (dev_count - 1)
    for k in sorted(range(1, dev_count), reverse=True):
        x_pieces[k] = swap(mine[k - 1], "dev", k)

    weights = [None] * side_count
    for k in range(0, side_count, 2):
        weights[k] = swap(latent_weight, "side", k) if k else latent_weight
    for k in range(0, side_count, 2):
        weights[k + 1] = swap(weights[k], "side", 1)
    if shard_rows % 16:
        held = jnp.zeros((side_count, shard_rows, kv_width), bf16)
        for k in range(side_count):
            held = lax.dynamic_update_slice(held, weights[k][None], (my_side ^ k, 0, 0))
        weights = [held.reshape(slab, kv_width)]

    request_ids = jnp.arange(req_count, dtype=jnp.int32)
    all_requests = row_request.reshape(block_count, 1, tok_rows)
    hit = (all_requests == request_ids[:, None]).astype(f32)
    below = (jnp.arange(tok_rows)[:, None] < jnp.arange(tok_rows)[None, :]).astype(f32)
    rank_local = jnp.einsum("bri,ij->brj", hit, below, preferred_element_type=f32)
    counts = jnp.sum(hit, axis=2)
    before = (jnp.arange(block_count)[:, None] > jnp.arange(block_count)[None, :]).astype(f32)
    earlier = jnp.einsum("ab,br->ar", before, counts, precision=lax.Precision.HIGHEST)
    position = jnp.sum(hit * (rank_local + (earlier + context_len.astype(f32))[:, :, None]), axis=1)
    slot_table = jnp.sum(hit * request_slot.astype(f32)[:, None], axis=1).astype(jnp.int32)
    row_group = slot_table // cap_slots
    group_ids = jnp.arange(dev_count, dtype=jnp.int32)
    group_hit = (row_group[:, None, :] == group_ids[:, None]).astype(f32)
    group_rank = jnp.sum(
        jnp.einsum("bgi,ij->bgj", group_hit, below, preferred_element_type=f32) * group_hit, axis=1
    ).astype(jnp.int32)
    by_dev = jnp.arange(block_count, dtype=jnp.int32)[:, None] // side_count
    place = by_dev * bucket_rows + group_rank
    order = my_dev ^ jnp.arange(dev_count, dtype=jnp.int32)
    line_of = lambda table: lax.dynamic_index_in_dim(
        table.reshape(dev_count, side_count, tok_rows), my_side, 1, keepdims=False
    )
    line_group, line_place, line_position = (line_of(t) for t in (row_group, place, position))
    target = (line_group ^ my_dev) * group_rows + line_place
    target = jnp.take(target, order, axis=0).reshape(1, -1)
    line_mine = jnp.where(line_group == my_dev, line_place, -1).reshape(1, -1)
    routed_position = jnp.sum(
        jnp.where(
            line_mine == jnp.arange(group_rows, dtype=jnp.int32)[:, None],
            line_position.reshape(1, -1), 0.0,
        ),
        axis=1,
    )
    half = rope_width // 2
    inverse = 1.0 / 10000.0 ** (jnp.arange(half, dtype=f32) * (2.0 / rope_width))
    angles = routed_position[:, None] * inverse[None, :]
    cosine, sine = jnp.cos(angles), jnp.sin(angles)
    side_order = my_side ^ jnp.arange(side_count, dtype=jnp.int32)
    side_table = lambda table: jnp.take(
        table.reshape(dev_count, side_count, tok_rows), side_order, axis=1
    )
    side_place = jnp.where(side_table(row_group) == my_dev, side_table(place), -1)
    side_place = jnp.swapaxes(side_place, 0, 1).reshape(side_count, 1, -1)
    side_slot = jnp.swapaxes(side_table(slot_table), 0, 1).reshape(side_count, 1, -1)
    row_slot = jnp.max(
        jnp.where(
            side_place == jnp.arange(group_rows, dtype=jnp.int32)[:, None], side_slot, -1
        ),
        axis=2,
    ).reshape(1, -1)

    query_latent = jnp.einsum(
        "sthn,hnc->hstc", queries[..., :nope_width], key_absorb, preferred_element_type=f32
    ).astype(bf16)
    query_full = jnp.concatenate(
        [query_latent, jnp.transpose(queries[..., nope_width:], (2, 0, 1, 3))], axis=-1
    )
    score_scale = queries.shape[-1] ** (-0.5)
    own_slots = my_dev * cap_slots + jnp.arange(cap_slots, dtype=jnp.int32)
    slot_hit = (own_slots[:, None] == request_slot[None, :]).astype(jnp.int32)
    occupied = (jnp.sum(slot_hit, axis=1) > 0).astype(f32)
    ctx_rows = jnp.sum(slot_hit * context_len[None, :], axis=1)
    score_cache = score_scale * jnp.einsum(
        "hstc,sjc->hstj", query_full, latent_cache, preferred_element_type=f32
    )
    mask_cache = (jnp.arange(ctx_len)[None, :] < ctx_rows[:, None])[None, :, None, :]
    score_cache = jnp.where(mask_cache, score_cache, masked_score)
    top_held = jnp.max(score_cache, axis=-1, keepdims=True)
    exp_cache = jnp.exp(score_cache - top_held)
    sum_held = jnp.sum(exp_cache, -1, keepdims=True)
    mix_held = jnp.einsum(
        "hstj,sjc->hstc", exp_cache.astype(bf16), latent_cache[..., :lat_width],
        preferred_element_type=f32,
    )
    live = jnp.broadcast_to(occupied[:, None], (cap_slots, step_count)).reshape(-1, 1)

    routed = project(x_pieces, weights, here, target, group_rows)
    parts = [routed[0]] + [None] * (dev_count - 1)
    for k in sorted(range(1, dev_count), reverse=True):
        parts[k] = swap(routed[k], "dev", k)
    latent_rows = finish(parts, latent_gain.reshape(1, -1), cosine, sine)
    pieces = [latent_rows] + [swap(latent_rows, "side", k) for k in range(1, side_count)]
    head_out = attend(
        score_scale, here, query_full.reshape(row_count, kv_width),
        new_latent.reshape(-1, kv_width), row_slot, top_held.reshape(row_count, 1),
        sum_held.reshape(row_count, 1), mix_held.reshape(row_count, lat_width), live,
        value_absorb, pieces, cap_slots,
    )
    heads = [head_out] + [swap(head_out, "dev", k) for k in range(1, dev_count)]
    products = output_product(heads, out_weight, here, side_count)
    result = products[0]
    for k in sorted(range(1, side_count), reverse=True):
        result = result + swap(products[k], "side", k).astype(f32)
    return result.astype(bf16)


def solution(mesh):
    placed = (
        P(("rep", "dev", "side"), None),
        P(("dev", "side"), None),
        P(),
        P("rep"),
        P("rep"),
        P("rep"),
        P(("rep", "dev"), None, None),
        P(("rep", "dev"), None, None),
        P(("rep", "dev"), None, "side", None),
        P("side", None, None),
        P("side", None, None),
        P("side", "dev"),
    )
    return jax.shard_map(
        on_device, mesh=mesh, in_specs=placed, out_specs=P(("rep", "side"), "dev"), check_vma=False
    )
```

```python
import functools

import jax
import jax.numpy as jnp
from jax import lax
from jax.experimental import pallas as pl
from jax.experimental.pallas import tpu as pltpu
from jax.sharding import PartitionSpec as P

masked_score = -1e30
bf16, f32 = jnp.bfloat16, jnp.float32
in_vmem = pl.BlockSpec(memory_space=pltpu.VMEM)
in_smem = pl.BlockSpec(memory_space=pltpu.SMEM)
anywhere = pl.BlockSpec(memory_space=pl.ANY)
mib = 1024 * 1024
prepare_mib = 10


def swap(value, axis, step):
    count = lax.axis_size(axis)
    return lax.ppermute(value, axis, [(i, i ^ step) for i in range(count)])


def pick(pieces, index):
    out = pieces[0]
    for k in range(1, len(pieces)):
        out = jnp.where(index == k, pieces[k], out)
    return out


def lane_tiles(width):
    return [slice(n, min(n + 128, width)) for n in range(0, width, 128)]


def split_kernel(slab, prompts_ref, *refs):
    my_dev = lax.axis_index("dev")
    out_refs, sems = refs[:-1], refs[-1]
    copies = []
    for k in range(len(out_refs))[::-1]:
        first = pl.multiple_of((my_dev ^ k) * slab, 128)
        copies.append(
            pltpu.make_async_copy(prompts_ref.at[:, pl.ds(first, slab)], out_refs[k], sems.at[k])
        )
    for copy in copies:
        copy.start()
    for copy in copies:
        copy.wait()


def split_columns(prompts, count):
    rows, width = prompts.shape
    slab = width // count
    if slab % 128:
        columns = [prompts[:, k * slab : (k + 1) * slab] for k in range(count)]
        my_dev = lax.axis_index("dev")
        return [pick(columns, my_dev ^ k) for k in range(count)]
    return pl.pallas_call(
        functools.partial(split_kernel, slab),
        out_shape=[jax.ShapeDtypeStruct((rows, slab), prompts.dtype)] * count,
        in_specs=[anywhere],
        out_specs=[in_vmem] * count,
        scratch_shapes=[pltpu.SemaphoreType.DMA((count,))],
        compiler_params=pltpu.CompilerParams(vmem_limit_bytes=8 * mib),
        name="split_columns",
    )(prompts)


def fill_tables(
    dev_count, side_count, bucket, cap_slots, length_ref, slot_ref, request_ref, inverse_ref,
    target_ref, cos_ref, sin_ref, spot_ref, to_ref, place_ref, local_ref, position_ref,
):
    my_dev, my_side = lax.axis_index("dev"), lax.axis_index("side")
    requests = request_ref[...]
    lane_rows, lanes = requests.shape
    tok_rows = bucket * dev_count // 2
    per_row = lanes // tok_rows
    group_rows = dev_count * bucket
    before = lax.broadcasted_iota(jnp.int32, (lanes, lanes), 0)
    after = lax.broadcasted_iota(jnp.int32, (lanes, lanes), 1)
    below = jnp.where(before < after, 1.0, 0.0)
    near = jnp.where((before < after) & (before // tok_rows == after // tok_rows), 1.0, 0.0)
    scan = jnp.concatenate([below, jnp.ones_like(below)], axis=1).astype(bf16)
    lower = lax.broadcasted_iota(jnp.int32, (lane_rows, lane_rows), 0)
    upper = lax.broadcasted_iota(jnp.int32, (lane_rows, lane_rows), 1)
    rows_before = jnp.where(upper < lower, 1.0, 0.0)
    position = jnp.zeros(requests.shape, f32)
    slot = jnp.zeros(requests.shape, jnp.int32)
    for q in range(slot_ref.shape[0]):
        hit = requests == q
        ranks = jnp.dot(
            jnp.where(hit, 1.0, 0.0).astype(bf16), scan, preferred_element_type=f32
        )
        earlier = jnp.dot(rows_before, ranks[:, lanes:], preferred_element_type=f32)
        start = length_ref[q].astype(f32)
        position = jnp.where(hit, ranks[:, :lanes] + earlier + start, position)
        slot = jnp.where(hit, slot_ref[q], slot)
    group = lax.div(slot, cap_slots)
    rank = jnp.zeros(requests.shape, f32)
    for g in range(dev_count):
        hit = group == g
        ranks = jnp.dot(
            jnp.where(hit, 1.0, 0.0).astype(bf16), near.astype(bf16), preferred_element_type=f32
        )
        rank = jnp.where(hit, ranks, rank)
    block = lax.broadcasted_iota(jnp.int32, requests.shape, 0) * per_row + lax.div(
        lax.broadcasted_iota(jnp.int32, requests.shape, 1), tok_rows
    )
    place = lax.div(block, side_count) * bucket + rank.astype(jnp.int32)
    to_ref[...] = (group ^ my_dev) * group_rows + place
    place_ref[...] = jnp.where(group == my_dev, place, -1)
    local_ref[...] = (slot - my_dev * cap_slots + 1).astype(f32)
    position_ref[...] = position
    lane_block = lax.div(lax.broadcasted_iota(jnp.int32, (1, lanes), 1), tok_rows)
    ids = lax.broadcasted_iota(jnp.int32, (group_rows, 1), 0)

    def find(dev, side):
        held = dev * side_count + side
        return pl.ds(lax.div(held, per_row), 1), lane_block == lax.rem(held, per_row)

    for k in range(dev_count):
        row, inside = find(my_dev ^ k, my_side)
        target_ref[:, k * lanes : (k + 1) * lanes] = jnp.where(inside, to_ref[row, :], -1)
    found = jnp.zeros((group_rows, lanes), f32)
    for d in range(dev_count):
        row, inside = find(d, my_side)
        found = jnp.where((place_ref[row, :] == ids) & inside, position_ref[row, :], found)
    angles = jnp.sum(found, axis=1, keepdims=True) * inverse_ref[...]
    cos_ref[...] = jnp.cos(angles)
    sin_ref[...] = jnp.sin(angles)
    for k in range(side_count):
        total = jnp.zeros((8, group_rows), f32)
        for d in range(dev_count):
            row, inside = find(d, my_side ^ k)
            chosen = jnp.where((place_ref[row, :] == ids) & inside, 1.0, 0.0).astype(bf16)
            values = jnp.broadcast_to(local_ref[row, :], (8, lanes)).astype(bf16)
            total = total + lax.dot_general(
                values, chosen, (((1,), (1,)), ((), ())), preferred_element_type=f32
            )
        spot_ref[:, k * group_rows : (k + 1) * group_rows] = total[:1].astype(jnp.int32)


def prepare_kernel(
    scale, steps, layout, length_ref, slot_ref, request_ref, inverse_ref, query_ref, absorb_ref,
    cache_ref, value_hbm, out_hbm, full_ref, top_ref, sum_ref, mix_ref, live_ref, target_ref,
    cos_ref, sin_ref, spot_ref, value_ref, out_ref, plain, full, to_ref, place_ref, local_ref,
    position_ref, sems,
):
    copies = [pltpu.make_async_copy(value_hbm, value_ref, sems.at[0])]
    parts = sems.shape[0] - 1
    rows = out_hbm.shape[0] // parts
    for n in range(parts):
        part = pl.ds(n * rows, rows)
        copies.append(pltpu.make_async_copy(out_hbm.at[part], out_ref.at[part], sems.at[n + 1]))
    for copy in copies:
        copy.start()
    slots, _, context = cache_ref.shape
    heads, nope, lat_width = absorb_ref.shape
    per_head = slots * steps
    fill_tables(
        *layout, slots, length_ref, slot_ref, request_ref, inverse_ref, target_ref, cos_ref,
        sin_ref, spot_ref, to_ref, place_ref, local_ref, position_ref,
    )
    first_slot = lax.axis_index("dev") * slots
    lengths = []
    for s in range(slots):
        length = jnp.int32(0)
        for q in range(slot_ref.shape[0]):
            length = jnp.where(slot_ref[q] == first_slot + s, length_ref[q], length)
        lengths.append(length)
    slot_of = lax.div(lax.broadcasted_iota(jnp.int32, live_ref.shape, 0), steps)
    live = jnp.zeros(live_ref.shape, f32)
    for s in range(slots):
        live = jnp.where((slot_of == s) & (lengths[s] > 0), 1.0, live)
    live_ref[...] = live
    for n, here in enumerate(lane_tiles(query_ref.shape[1])):
        plain[n, :, : here.stop - here.start] = query_ref[:, here].astype(f32)
    wide = lane_tiles(full_ref.shape[1])
    for h in range(heads):
        there = pl.ds(h, per_head, stride=heads)
        query = plain[0, there, :].astype(bf16)
        latent = jnp.dot(query, absorb_ref[h], preferred_element_type=f32).astype(bf16).astype(f32)
        here = slice(h * per_head, (h + 1) * per_head)
        for n, lanes in enumerate(lane_tiles(lat_width)):
            full[n, here, :] = latent[:, lanes]
        full[len(wide) - 1, here, :] = plain[1, there, :]
    for n, lanes in enumerate(wide):
        full_ref[:, lanes] = full[n, :, : lanes.stop - lanes.start].astype(bf16)
    key = lax.broadcasted_iota(jnp.int32, (1, context), 1)
    for s in range(slots):
        theres = [pl.ds(s * steps + t, heads, stride=per_head) for t in range(steps)]
        query = jnp.concatenate(
            [
                jnp.concatenate([full[n, there, :] for there in theres], axis=0)[
                    :, : lanes.stop - lanes.start
                ].astype(bf16)
                for n, lanes in enumerate(wide)
            ],
            axis=1,
        )
        rows = cache_ref[s]
        score = jnp.dot(query, rows, preferred_element_type=f32)
        score = jnp.where(key < lengths[s], score * scale, masked_score)
        top = jnp.max(score, axis=1, keepdims=True)
        weight = jnp.exp(score - top)
        total = jnp.sum(weight, axis=1, keepdims=True)
        mix = lax.dot_general(
            weight.astype(bf16), rows[:lat_width, :], (((1,), (1,)), ((), ())),
            preferred_element_type=f32,
        )
        lanes = top_ref.shape[1]
        for t in range(steps):
            there = theres[t]
            here = slice(t * heads, (t + 1) * heads)
            top_ref[there, :] = jnp.broadcast_to(top[here], (heads, lanes))
            sum_ref[there, :] = jnp.broadcast_to(total[here], (heads, lanes))
            for n, part in enumerate(lane_tiles(lat_width)):
                mix_ref[n, there, :] = mix[here, part]
    for copy in copies:
        copy.wait()


def prepare(
    scale, dev_count, side_count, bucket, lengths, request_slot, requests, inverse, queries,
    absorb, cache, value, out_weight,
):
    slots, steps, heads, width = queries.shape
    kv_width = cache.shape[1]
    lat_width = absorb.shape[2]
    rows = slots * steps * heads
    group_rows = dev_count * bucket
    parts = 8
    lanes = requests.shape[1]
    half = inverse.shape[1]
    shapes = [
        ((rows, kv_width), bf16), ((rows, 128), f32), ((rows, 128), f32),
        ((lat_width // 128, rows, 128), f32), ((slots * steps, 128), f32),
        ((1, dev_count * lanes), jnp.int32), ((group_rows, half), f32), ((group_rows, half), f32),
        ((1, side_count * group_rows), jnp.int32), (value.shape, bf16), (out_weight.shape, bf16),
    ]
    return pl.pallas_call(
        functools.partial(prepare_kernel, scale, steps, (dev_count, side_count, bucket)),
        out_shape=[jax.ShapeDtypeStruct(*shape) for shape in shapes],
        in_specs=[in_smem] * 2 + [in_vmem] * 5 + [anywhere] * 2,
        out_specs=[in_vmem] * len(shapes),
        scratch_shapes=[
            pltpu.VMEM((len(lane_tiles(width)), rows, 128), f32),
            pltpu.VMEM((len(lane_tiles(kv_width)), rows, 128), f32),
            pltpu.VMEM(requests.shape, jnp.int32),
            pltpu.VMEM(requests.shape, jnp.int32),
            pltpu.VMEM(requests.shape, f32),
            pltpu.VMEM(requests.shape, f32),
            pltpu.SemaphoreType.DMA((parts + 1,)),
        ],
        compiler_params=pltpu.CompilerParams(vmem_limit_bytes=prepare_mib * mib),
        cost_estimate=pl.CostEstimate(
            flops=4 * 10**9, bytes_accessed=28 * 10**6, transcendentals=10**5
        ),
        name="prepare",
    )(lengths, request_slot, requests, inverse, queries.reshape(rows, width), absorb, cache, value,
      out_weight)


def project_kernel(dev_count, side_count, target_ref, *refs):
    my_side = lax.axis_index("side")
    x_refs = refs[:dev_count]
    weight_refs = refs[dev_count : dev_count + side_count]
    out_refs = refs[dev_count + side_count : -2]
    slab_weight, rows = refs[-2:]
    shard = weight_refs[0].shape[0]
    tok_rows = x_refs[0].shape[0]
    if side_count > 1:
        for k in range(side_count):
            first = pl.multiple_of((my_side ^ k) * shard, 16)
            slab_weight[pl.ds(first, shard), :] = weight_refs[k][...]
    copies = target_ref.shape[1] // (dev_count * tok_rows)
    for k in range(dev_count):
        part = jnp.dot(
            x_refs[k][...], slab_weight[...] if side_count > 1 else weight_refs[0][...],
            preferred_element_type=f32,
        ).astype(bf16)
        for n in range(k * copies, (k + 1) * copies):
            rows[n * tok_rows : (n + 1) * tok_rows, :] = part
    group_rows = out_refs[0].shape[0]
    target = target_ref[...]
    for j in range(dev_count):
        ids = lax.broadcasted_iota(jnp.int32, (group_rows, target.shape[1]), 0) + j * group_rows
        route = jnp.where(ids == target, 1.0, 0.0).astype(bf16)
        out_refs[j][...] = jnp.dot(
            route, rows[...], preferred_element_type=f32
        ).astype(out_refs[j].dtype)


def project(x_pieces, weights, target, group_rows):
    dev_count, width = len(x_pieces), weights[0].shape[1]
    tok_rows, slab = x_pieces[0].shape
    return pl.pallas_call(
        functools.partial(project_kernel, dev_count, len(weights)),
        out_shape=[
            jax.ShapeDtypeStruct((group_rows, width), f32 if j == 0 else bf16)
            for j in range(dev_count)
        ],
        in_specs=[in_vmem] * (1 + dev_count + len(weights)),
        out_specs=[in_vmem] * dev_count,
        scratch_shapes=[
            pltpu.VMEM((slab, width), bf16),
            pltpu.VMEM((target.shape[1], width), bf16),
        ],
        compiler_params=pltpu.CompilerParams(vmem_limit_bytes=10 * mib),
        name="project",
    )(target, *x_pieces, *weights)


def finish_kernel(gain_ref, cos_ref, sin_ref, *refs):
    parts, out_ref = refs[:-1], refs[-1]
    lat_width = gain_ref.shape[1]
    half = cos_ref.shape[1]
    total = parts[0][...].astype(f32)
    for part in parts[1:]:
        total = total + part[...].astype(f32)
    latent = total[:, :lat_width]
    spread = jnp.mean(latent * latent, axis=1, keepdims=True)
    out_ref[:, :lat_width] = (latent * lax.rsqrt(spread + 1e-06) * gain_ref[...]).astype(bf16)
    first = total[:, lat_width : lat_width + half]
    second = total[:, lat_width + half :]
    cosine, sine = cos_ref[...], sin_ref[...]
    turned = jnp.concatenate(
        [first * cosine - second * sine, second * cosine + first * sine], axis=1
    )
    out_ref[:, lat_width:] = turned.astype(bf16)


def finish(parts, gain, cosine, sine):
    return pl.pallas_call(
        finish_kernel,
        out_shape=jax.ShapeDtypeStruct(parts[0].shape, bf16),
        in_specs=[in_vmem] * (3 + len(parts)),
        out_specs=in_vmem,
        compiler_params=pltpu.CompilerParams(vmem_limit_bytes=8 * mib),
        name="finish_rows",
    )(gain, cosine, sine, *parts)


def attend_kernel(
    scale, cap_slots, steps, part, parts, query_ref, fresh_ref, slot_ref, top_ref,
    sum_ref, mix_ref, live_ref, value_ref, *refs
):
    pieces, out_ref, keys = refs[:-2], refs[-2], refs[-1]
    lat_width = mix_ref.shape[0] * mix_ref.shape[2]
    per_head = cap_slots * steps
    rows = query_ref.shape[0] // parts
    heads = rows // per_head
    mine = slice(part * rows, (part + 1) * rows)
    piece_rows = pieces[0].shape[0]
    for n, piece in enumerate(pieces):
        keys[n * piece_rows : (n + 1) * piece_rows, :] = piece[...]
    contract = (((1,), (1,)), ((), ()))
    row = lax.broadcasted_iota(jnp.int32, (rows, 1), 0)
    row_slot = (row // steps) % cap_slots
    key = lax.broadcasted_iota(jnp.int32, (1, per_head), 1)
    see_fresh = (key // steps == row_slot) & (key % steps <= row % steps)
    query = query_ref[mine, :]
    fresh = lax.dot_general(query, fresh_ref[...], contract, preferred_element_type=f32)
    fresh = jnp.where(see_fresh, fresh * scale, masked_score)
    score = lax.dot_general(query, keys[...], contract, preferred_element_type=f32)
    score = jnp.where(
        slot_ref[...] == row_slot + 1, score * scale, masked_score
    )
    top_held = top_ref[mine, :1]
    top = jnp.maximum(
        jnp.maximum(top_held, jnp.max(fresh, axis=1, keepdims=True)),
        jnp.max(score, axis=1, keepdims=True),
    )
    held = jnp.exp(top_held - top)
    weight_fresh = jnp.exp(fresh - top)
    weight = jnp.exp(score - top)
    total = (
        sum_ref[mine, :1] * held
        + jnp.sum(weight_fresh, axis=1, keepdims=True)
        + jnp.sum(weight, axis=1, keepdims=True)
    )
    mix = jnp.dot(
        weight_fresh.astype(bf16), fresh_ref[:, :lat_width], preferred_element_type=f32
    ) + jnp.dot(weight.astype(bf16), keys[:, :lat_width], preferred_element_type=f32)
    mix_held = jnp.concatenate([mix_ref[n, mine, :] for n in range(mix_ref.shape[0])], axis=1)
    latent = ((mix_held * held + mix) / total).astype(bf16)
    live = live_ref[:, :1]
    width = value_ref.shape[2]
    for h in range(0, heads, 2):
        head = part * heads + h
        pair = jnp.concatenate([value_ref[head], value_ref[head + 1]], axis=1)
        both = jnp.dot(
            latent[h * per_head : (h + 2) * per_head, :], pair, preferred_element_type=f32
        )
        out_ref[:, h * width : (h + 1) * width] = (both[:per_head, :width] * live).astype(bf16)
        out_ref[:, (h + 1) * width : (h + 2) * width] = (both[per_head:, width:] * live).astype(bf16)


def attend(scale, query, fresh, row_slot, top, total, mix, live, value, pieces, cap_slots,
           part, parts):
    heads, _, width = value.shape
    steps = fresh.shape[0] // cap_slots
    part_heads = heads // parts
    return pl.pallas_call(
        functools.partial(attend_kernel, scale, cap_slots, steps, part, parts),
        out_shape=jax.ShapeDtypeStruct((cap_slots * steps, part_heads * width), bf16),
        in_specs=[in_vmem] * (8 + len(pieces)),
        out_specs=in_vmem,
        scratch_shapes=[pltpu.VMEM((len(pieces) * pieces[0].shape[0], query.shape[1]), bf16)],
        compiler_params=pltpu.CompilerParams(vmem_limit_bytes=10 * mib),
        name="attend",
    )(query, fresh, row_slot, top, total, mix, live, value, *pieces)


def output_kernel(dev_count, side_count, part, parts, *refs):
    my_dev, my_side = lax.axis_index("dev"), lax.axis_index("side")
    head_refs = refs[:dev_count]
    weight_ref = refs[dev_count]
    earlier_ref = refs[dev_count + 1] if part else None
    out_refs = refs[dev_count + 1 + (part > 0) : -1]
    held = refs[-1]
    rows, depth = head_refs[0].shape
    per_side = dev_count // side_count
    for j in range(dev_count):
        group = my_dev ^ j
        place = (lax.div(group, per_side) ^ my_side) * per_side + lax.rem(group, per_side)
        held[pl.ds(pl.multiple_of(place * rows, 16), rows), :] = head_refs[j][...]
    columns = weight_ref.shape[1]
    tile = 256 if columns % 256 == 0 else columns
    side_rows = rows * per_side
    for n in range(columns // tile):
        here = slice(n * tile, (n + 1) * tile)
        product = jnp.dot(
            held[...], weight_ref[part * depth : (part + 1) * depth, here],
            preferred_element_type=f32,
        )
        if part:
            product = product + earlier_ref[:, here]
        if part + 1 < parts:
            out_refs[0][:, here] = product
        else:
            for k in range(side_count):
                out_refs[k][:, here] = product[k * side_rows : (k + 1) * side_rows, :].astype(
                    out_refs[k].dtype
                )


def output_product(head_pieces, weight, side_count, earlier, part, parts):
    dev_count = len(head_pieces)
    rows, depth = head_pieces[0].shape
    columns = weight.shape[1]
    side_rows = rows * dev_count // side_count
    if part + 1 < parts:
        shapes = [((rows * dev_count, columns), f32)]
    else:
        shapes = [((side_rows, columns), f32 if k == 0 else bf16) for k in range(side_count)]
    earlier = [] if earlier is None else [earlier]
    return pl.pallas_call(
        functools.partial(output_kernel, dev_count, side_count, part, parts),
        out_shape=[jax.ShapeDtypeStruct(*shape) for shape in shapes],
        in_specs=[in_vmem] * (dev_count + 1 + len(earlier)),
        out_specs=[in_vmem] * len(shapes),
        scratch_shapes=[pltpu.VMEM((dev_count * rows, depth), bf16)],
        compiler_params=pltpu.CompilerParams(vmem_limit_bytes=10 * mib),
        name="output_product",
    )(*head_pieces, weight, *earlier)


def on_device(
    prompts,
    latent_weight,
    latent_gain,
    row_request,
    context_len,
    request_slot,
    latent_cache,
    new_latent,
    queries,
    key_absorb,
    value_absorb,
    out_weight,
):
    dev_count = lax.axis_size("dev")
    side_count = lax.axis_size("side")
    tok_rows, model_width = prompts.shape
    shard_rows, kv_width = latent_weight.shape
    lat_width = latent_gain.shape[0]
    head_count, nope_width, _ = key_absorb.shape
    rope_width = kv_width - lat_width
    cap_slots, ctx_len, _ = latent_cache.shape
    step_count = new_latent.shape[1]
    bucket_rows = 2 * tok_rows // dev_count
    group_rows = dev_count * bucket_rows
    slab = model_width // dev_count

    x_pieces = list(split_columns(prompts, dev_count))
    for k in sorted(range(1, dev_count), reverse=True):
        x_pieces[k] = swap(x_pieces[k], "dev", k)

    weights = [None] * side_count
    for k in range(0, side_count, 2):
        weights[k] = swap(latent_weight, "side", k) if k else latent_weight
    for k in range(0, side_count, 2):
        weights[k + 1] = swap(weights[k], "side", 1)
    if shard_rows % 16:
        my_side = lax.axis_index("side")
        held = jnp.zeros((side_count, shard_rows, kv_width), bf16)
        for k in range(side_count):
            held = lax.dynamic_update_slice(held, weights[k][None], (my_side ^ k, 0, 0))
        weights = [held.reshape(slab, kv_width)]

    score_scale = queries.shape[-1] ** (-0.5)
    half = rope_width // 2
    inverse = 1.0 / 10000.0 ** (jnp.arange(half, dtype=f32) * (2.0 / rope_width))
    fresh, lengths = lax.optimization_barrier((new_latent.reshape(-1, kv_width), context_len))
    (
        query_full, top_held, sum_held, mix_held, live, target, cosine, sine, row_slot,
        value_here, out_here,
    ) = prepare(
        score_scale, dev_count, side_count, bucket_rows, lengths, request_slot,
        row_request.reshape(-1, 128), inverse.reshape(1, -1), queries, key_absorb,
        jnp.swapaxes(latent_cache, 1, 2), value_absorb, out_weight,
    )

    routed = project(x_pieces, weights, target, group_rows)
    parts = [routed[0]] + [None] * (dev_count - 1)
    for k in sorted(range(1, dev_count), reverse=True):
        parts[k] = swap(routed[k], "dev", k)
    latent_rows = finish(parts, latent_gain.reshape(1, -1), cosine, sine)
    pieces = [latent_rows] + [swap(latent_rows, "side", k) for k in range(1, side_count)]
    product, parts = None, 2
    for part in range(parts):
        head_out = attend(
            score_scale, query_full, fresh, row_slot, top_held,
            sum_held, mix_held, live, value_here, pieces, cap_slots, part, parts,
        )
        heads = [head_out] + [None] * (dev_count - 1)
        for k in sorted(range(1, dev_count), reverse=True):
            heads[k] = swap(head_out, "dev", k)
        products = output_product(heads, out_here, side_count, product, part, parts)
        product = products[0]
    result = products[0]
    for k in sorted(range(1, side_count), reverse=True):
        result = result + swap(products[k], "side", k).astype(f32)
    return result.astype(bf16)


def solution(mesh):
    placed = (
        P(("rep", "dev", "side"), None),
        P(("dev", "side"), None),
        P(),
        P("rep"),
        P("rep"),
        P("rep"),
        P(("rep", "dev"), None, None),
        P(("rep", "dev"), None, None),
        P(("rep", "dev"), None, "side", None),
        P("side", None, None),
        P("side", None, None),
        P("side", "dev"),
    )
    return jax.shard_map(
        on_device, mesh=mesh, in_specs=placed, out_specs=P(("rep", "side"), "dev"), check_vma=False
    )
```

```python
import functools

import jax
import jax.numpy as jnp
from jax import lax
from jax.experimental import pallas as pl
from jax.experimental.pallas import tpu as pltpu
from jax.sharding import PartitionSpec as P

masked_score = -1e30
bf16, f32 = jnp.bfloat16, jnp.float32
in_vmem = pl.BlockSpec(memory_space=pltpu.VMEM)
in_smem = pl.BlockSpec(memory_space=pltpu.SMEM)
in_hbm = pl.BlockSpec(memory_space=pltpu.HBM)
mib = 1024 * 1024
prepare_mib = 16


def swap(value, axis, step):
    count = lax.axis_size(axis)
    return lax.ppermute(value, axis, [(i, i ^ step) for i in range(count)])


def pick(pieces, index):
    out = pieces[0]
    for k in range(1, len(pieces)):
        out = jnp.where(index == k, pieces[k], out)
    return out


def lane_tiles(width):
    return [slice(n, min(n + 128, width)) for n in range(0, width, 128)]


def split_kernel(slab, prompts_ref, *refs):
    my_dev = lax.axis_index("dev")
    out_refs, sems = refs[:-1], refs[-1]
    copies = []
    for k in range(len(out_refs))[::-1]:
        first = pl.multiple_of((my_dev ^ k) * slab, 128)
        copies.append(
            pltpu.make_async_copy(prompts_ref.at[:, pl.ds(first, slab)], out_refs[k], sems.at[k])
        )
    for copy in copies:
        copy.start()
    for copy in copies:
        copy.wait()


def split_columns(prompts, count):
    rows, width = prompts.shape
    slab = width // count
    if slab % 128:
        columns = [prompts[:, k * slab : (k + 1) * slab] for k in range(count)]
        my_dev = lax.axis_index("dev")
        return [pick(columns, my_dev ^ k) for k in range(count)]
    return pl.pallas_call(
        functools.partial(split_kernel, slab),
        out_shape=[jax.ShapeDtypeStruct((rows, slab), prompts.dtype)] * count,
        in_specs=[in_hbm],
        out_specs=[in_vmem] * count,
        scratch_shapes=[pltpu.SemaphoreType.DMA((count,))],
        compiler_params=pltpu.CompilerParams(vmem_limit_bytes=8 * mib),
        name="split_columns",
    )(prompts)


def fill_tables(
    dev_count, side_count, bucket, cap_slots, length_ref, slot_ref, request_ref, inverse_ref,
    target_ref, cos_ref, sin_ref, spot_ref, to_ref, place_ref, local_ref, position_ref,
):
    my_dev, my_side = lax.axis_index("dev"), lax.axis_index("side")
    requests = request_ref[...]
    lane_rows, lanes = requests.shape
    tok_rows = bucket * dev_count // 2
    per_row = lanes // tok_rows
    group_rows = dev_count * bucket
    before = lax.broadcasted_iota(jnp.int32, (lanes, lanes), 0)
    after = lax.broadcasted_iota(jnp.int32, (lanes, lanes), 1)
    below = jnp.where(before < after, 1.0, 0.0)
    near = jnp.where((before < after) & (before // tok_rows == after // tok_rows), 1.0, 0.0)
    scan = jnp.concatenate([below, jnp.ones_like(below)], axis=1).astype(bf16)
    lower = lax.broadcasted_iota(jnp.int32, (lane_rows, lane_rows), 0)
    upper = lax.broadcasted_iota(jnp.int32, (lane_rows, lane_rows), 1)
    rows_before = jnp.where(upper < lower, 1.0, 0.0)
    position = jnp.zeros(requests.shape, f32)
    slot = jnp.zeros(requests.shape, jnp.int32)
    for q in range(slot_ref.shape[0]):
        hit = requests == q
        ranks = jnp.dot(
            jnp.where(hit, 1.0, 0.0).astype(bf16), scan, preferred_element_type=f32
        )
        earlier = jnp.dot(rows_before, ranks[:, lanes:], preferred_element_type=f32)
        start = length_ref[q].astype(f32)
        position = jnp.where(hit, ranks[:, :lanes] + earlier + start, position)
        slot = jnp.where(hit, slot_ref[q], slot)
    group = lax.div(slot, cap_slots)
    rank = jnp.zeros(requests.shape, f32)
    for g in range(dev_count):
        hit = group == g
        ranks = jnp.dot(
            jnp.where(hit, 1.0, 0.0).astype(bf16), near.astype(bf16), preferred_element_type=f32
        )
        rank = jnp.where(hit, ranks, rank)
    block = lax.broadcasted_iota(jnp.int32, requests.shape, 0) * per_row + lax.div(
        lax.broadcasted_iota(jnp.int32, requests.shape, 1), tok_rows
    )
    place = lax.div(block, side_count) * bucket + rank.astype(jnp.int32)
    to_ref[...] = (group ^ my_dev) * group_rows + place
    place_ref[...] = jnp.where(group == my_dev, place, -1)
    local_ref[...] = (slot - my_dev * cap_slots + 1).astype(f32)
    position_ref[...] = position
    lane_block = lax.div(lax.broadcasted_iota(jnp.int32, (1, lanes), 1), tok_rows)
    ids = lax.broadcasted_iota(jnp.int32, (group_rows, 1), 0)

    def find(dev, side):
        held = dev * side_count + side
        return pl.ds(lax.div(held, per_row), 1), lane_block == lax.rem(held, per_row)

    for k in range(dev_count):
        row, inside = find(my_dev ^ k, my_side)
        target_ref[:, k * lanes : (k + 1) * lanes] = jnp.where(inside, to_ref[row, :], -1)
    found = jnp.zeros((group_rows, lanes), f32)
    for d in range(dev_count):
        row, inside = find(d, my_side)
        found = jnp.where((place_ref[row, :] == ids) & inside, position_ref[row, :], found)
    angles = jnp.sum(found, axis=1, keepdims=True) * inverse_ref[...]
    cos_ref[...] = jnp.cos(angles)
    sin_ref[...] = jnp.sin(angles)
    for k in range(side_count):
        total = jnp.zeros((8, group_rows), f32)
        for d in range(dev_count):
            row, inside = find(d, my_side ^ k)
            chosen = jnp.where((place_ref[row, :] == ids) & inside, 1.0, 0.0).astype(bf16)
            values = jnp.broadcast_to(local_ref[row, :], (8, lanes)).astype(bf16)
            total = total + lax.dot_general(
                values, chosen, (((1,), (1,)), ((), ())), preferred_element_type=f32
            )
        spot_ref[:, k * group_rows : (k + 1) * group_rows] = total[:1].astype(jnp.int32)


def prepare_kernel(
    scale, steps, layout, inverse_ref, length_hbm, slot_hbm, request_hbm, query_hbm, absorb_hbm,
    cache_hbm, value_hbm, out_hbm, full_ref, top_ref, sum_ref, mix_ref, live_ref, target_ref,
    cos_ref, sin_ref, spot_ref, value_ref, out_ref, length_ref, slot_ref, request_ref, query_ref,
    absorb_ref, cache_ref, plain, full, to_ref, place_ref, local_ref, position_ref, sems,
):
    pairs = [
        (length_hbm, length_ref), (slot_hbm, slot_ref), (request_hbm, request_ref),
        (query_hbm, query_ref), (absorb_hbm, absorb_ref), (cache_hbm, cache_ref),
        (value_hbm, value_ref),
    ]
    parts = sems.shape[0] - len(pairs)
    rows = out_hbm.shape[0] // parts
    for n in range(parts):
        part = pl.ds(n * rows, rows)
        pairs.append((out_hbm.at[part], out_ref.at[part]))
    copies = [pltpu.make_async_copy(*pair, sems.at[n]) for n, pair in enumerate(pairs)]
    for copy in copies:
        copy.start()
    for copy in copies[:3]:
        copy.wait()
    slots, _, context = cache_ref.shape
    heads, nope, lat_width = absorb_ref.shape
    per_head = slots * steps
    fill_tables(
        *layout, slots, length_ref, slot_ref, request_ref, inverse_ref, target_ref, cos_ref,
        sin_ref, spot_ref, to_ref, place_ref, local_ref, position_ref,
    )
    first_slot = lax.axis_index("dev") * slots
    lengths = []
    for s in range(slots):
        length = jnp.int32(0)
        for q in range(slot_ref.shape[0]):
            length = jnp.where(slot_ref[q] == first_slot + s, length_ref[q], length)
        lengths.append(length)
    slot_of = lax.div(lax.broadcasted_iota(jnp.int32, live_ref.shape, 0), steps)
    live = jnp.zeros(live_ref.shape, f32)
    for s in range(slots):
        live = jnp.where((slot_of == s) & (lengths[s] > 0), 1.0, live)
    live_ref[...] = live
    copies[3].wait()
    copies[4].wait()
    for n, here in enumerate(lane_tiles(query_ref.shape[1])):
        plain[n, :, : here.stop - here.start] = query_ref[:, here].astype(f32)
    wide = lane_tiles(full_ref.shape[1])
    for h in range(heads):
        there = pl.ds(h, per_head, stride=heads)
        query = plain[0, there, :].astype(bf16)
        latent = jnp.dot(query, absorb_ref[h], preferred_element_type=f32).astype(bf16).astype(f32)
        here = slice(h * per_head, (h + 1) * per_head)
        for n, lanes in enumerate(lane_tiles(lat_width)):
            full[n, here, :] = latent[:, lanes]
        full[len(wide) - 1, here, :] = plain[1, there, :]
    for n, lanes in enumerate(wide):
        full_ref[:, lanes] = full[n, :, : lanes.stop - lanes.start].astype(bf16)
    key = lax.broadcasted_iota(jnp.int32, (1, context), 1)
    copies[5].wait()
    for s in range(slots):
        theres = [pl.ds(s * steps + t, heads, stride=per_head) for t in range(steps)]
        query = jnp.concatenate(
            [
                jnp.concatenate([full[n, there, :] for there in theres], axis=0)[
                    :, : lanes.stop - lanes.start
                ].astype(bf16)
                for n, lanes in enumerate(wide)
            ],
            axis=1,
        )
        rows = cache_ref[s]
        score = jnp.dot(query, rows, preferred_element_type=f32)
        score = jnp.where(key < lengths[s], score * scale, masked_score)
        top = jnp.max(score, axis=1, keepdims=True)
        weight = jnp.exp(score - top)
        total = jnp.sum(weight, axis=1, keepdims=True)
        mix = lax.dot_general(
            weight.astype(bf16), rows[:lat_width, :], (((1,), (1,)), ((), ())),
            preferred_element_type=f32,
        )
        lanes = top_ref.shape[1]
        for t in range(steps):
            there = theres[t]
            here = slice(t * heads, (t + 1) * heads)
            top_ref[there, :] = jnp.broadcast_to(top[here], (heads, lanes))
            sum_ref[there, :] = jnp.broadcast_to(total[here], (heads, lanes))
            for n, part in enumerate(lane_tiles(lat_width)):
                mix_ref[n, there, :] = mix[here, part]
    for copy in copies[6:]:
        copy.wait()


def prepare(
    scale, dev_count, side_count, bucket, lengths, request_slot, requests, inverse, queries,
    absorb, cache, value, out_weight,
):
    slots, steps, heads, width = queries.shape
    kv_width = cache.shape[1]
    lat_width = absorb.shape[2]
    rows = slots * steps * heads
    group_rows = dev_count * bucket
    parts = 8
    lanes = requests.shape[1]
    half = inverse.shape[1]
    shapes = [
        ((rows, kv_width), bf16), ((rows, 128), f32), ((rows, 128), f32),
        ((lat_width // 128, rows, 128), f32), ((slots * steps, 128), f32),
        ((1, dev_count * lanes), jnp.int32), ((group_rows, half), f32), ((group_rows, half), f32),
        ((1, side_count * group_rows), jnp.int32), (value.shape, bf16), (out_weight.shape, bf16),
    ]
    return pl.pallas_call(
        functools.partial(prepare_kernel, scale, steps, (dev_count, side_count, bucket)),
        out_shape=[jax.ShapeDtypeStruct(*shape) for shape in shapes],
        in_specs=[in_vmem] + [in_hbm] * 8,
        out_specs=[in_vmem] * len(shapes),
        scratch_shapes=[
            pltpu.SMEM(lengths.shape, lengths.dtype),
            pltpu.SMEM(request_slot.shape, request_slot.dtype),
            pltpu.VMEM(requests.shape, requests.dtype),
            pltpu.VMEM((rows, width), queries.dtype),
            pltpu.VMEM(absorb.shape, absorb.dtype),
            pltpu.VMEM(cache.shape, cache.dtype),
            pltpu.VMEM((len(lane_tiles(width)), rows, 128), f32),
            pltpu.VMEM((len(lane_tiles(kv_width)), rows, 128), f32),
            pltpu.VMEM(requests.shape, jnp.int32),
            pltpu.VMEM(requests.shape, jnp.int32),
            pltpu.VMEM(requests.shape, f32),
            pltpu.VMEM(requests.shape, f32),
            pltpu.SemaphoreType.DMA((parts + 7,)),
        ],
        compiler_params=pltpu.CompilerParams(vmem_limit_bytes=prepare_mib * mib),
        cost_estimate=pl.CostEstimate(
            flops=4 * 10**9, bytes_accessed=28 * 10**6, transcendentals=10**5
        ),
        name="prepare",
    )(inverse, lengths, request_slot, requests, queries.reshape(rows, width), absorb, cache, value,
      out_weight)


def project_kernel(dev_count, side_count, target_ref, *refs):
    my_side = lax.axis_index("side")
    x_refs = refs[:dev_count]
    weight_refs = refs[dev_count : dev_count + side_count]
    out_refs = refs[dev_count + side_count : -3]
    x_rows, slab_weight, rows = refs[-3:]
    shard = weight_refs[0].shape[0]
    tok_rows = x_refs[0].shape[0]
    if side_count > 1:
        for k in range(side_count):
            first = pl.multiple_of((my_side ^ k) * shard, 16)
            slab_weight[pl.ds(first, shard), :] = weight_refs[k][...]
    for k in range(dev_count):
        x_rows[k * tok_rows : (k + 1) * tok_rows, :] = x_refs[k][...]
    slab = slab_weight[...] if side_count > 1 else weight_refs[0][...]
    raw = jnp.dot(x_rows[...], slab, preferred_element_type=f32).astype(bf16)
    copies = target_ref.shape[1] // (dev_count * tok_rows)
    for k in range(dev_count):
        for n in range(k * copies, (k + 1) * copies):
            rows[n * tok_rows : (n + 1) * tok_rows, :] = raw[k * tok_rows : (k + 1) * tok_rows, :]
    group_rows = out_refs[0].shape[0]
    target = target_ref[...]
    for j in range(dev_count):
        ids = lax.broadcasted_iota(jnp.int32, (group_rows, target.shape[1]), 0) + j * group_rows
        route = jnp.where(ids == target, 1.0, 0.0).astype(bf16)
        out_refs[j][...] = jnp.dot(
            route, rows[...], preferred_element_type=f32
        ).astype(out_refs[j].dtype)


def project(x_pieces, weights, target, group_rows):
    dev_count, width = len(x_pieces), weights[0].shape[1]
    tok_rows, slab = x_pieces[0].shape
    return pl.pallas_call(
        functools.partial(project_kernel, dev_count, len(weights)),
        out_shape=[
            jax.ShapeDtypeStruct((group_rows, width), f32 if j == 0 else bf16)
            for j in range(dev_count)
        ],
        in_specs=[in_vmem] * (1 + dev_count + len(weights)),
        out_specs=[in_vmem] * dev_count,
        scratch_shapes=[
            pltpu.VMEM((dev_count * tok_rows, slab), bf16),
            pltpu.VMEM((slab, width), bf16),
            pltpu.VMEM((target.shape[1], width), bf16),
        ],
        compiler_params=pltpu.CompilerParams(vmem_limit_bytes=10 * mib),
        name="project",
    )(target, *x_pieces, *weights)


def finish_kernel(gain_ref, cos_ref, sin_ref, *refs):
    parts, out_ref = refs[:-1], refs[-1]
    lat_width = gain_ref.shape[1]
    half = cos_ref.shape[1]
    total = parts[0][...].astype(f32)
    for part in parts[1:]:
        total = total + part[...].astype(f32)
    latent = total[:, :lat_width]
    spread = jnp.mean(latent * latent, axis=1, keepdims=True)
    out_ref[:, :lat_width] = (latent * lax.rsqrt(spread + 1e-06) * gain_ref[...]).astype(bf16)
    first = total[:, lat_width : lat_width + half]
    second = total[:, lat_width + half :]
    cosine, sine = cos_ref[...], sin_ref[...]
    turned = jnp.concatenate(
        [first * cosine - second * sine, second * cosine + first * sine], axis=1
    )
    out_ref[:, lat_width:] = turned.astype(bf16)


def finish(parts, gain, cosine, sine):
    return pl.pallas_call(
        finish_kernel,
        out_shape=jax.ShapeDtypeStruct(parts[0].shape, bf16),
        in_specs=[in_vmem] * (3 + len(parts)),
        out_specs=in_vmem,
        compiler_params=pltpu.CompilerParams(vmem_limit_bytes=8 * mib),
        name="finish_rows",
    )(gain, cosine, sine, *parts)


def attend_kernel(
    scale, cap_slots, steps, part, parts, query_ref, fresh_ref, slot_ref, top_ref,
    sum_ref, mix_ref, live_ref, value_ref, *refs
):
    pieces, out_ref, keys = refs[:-2], refs[-2], refs[-1]
    lat_width = mix_ref.shape[0] * mix_ref.shape[2]
    per_head = cap_slots * steps
    rows = query_ref.shape[0] // parts
    heads = rows // per_head
    mine = slice(part * rows, (part + 1) * rows)
    piece_rows = pieces[0].shape[0]
    for n, piece in enumerate(pieces):
        keys[n * piece_rows : (n + 1) * piece_rows, :] = piece[...]
    contract = (((1,), (1,)), ((), ()))
    row = lax.broadcasted_iota(jnp.int32, (rows, 1), 0)
    row_slot = (row // steps) % cap_slots
    key = lax.broadcasted_iota(jnp.int32, (1, per_head), 1)
    see_fresh = (key // steps == row_slot) & (key % steps <= row % steps)
    query = query_ref[mine, :]
    fresh = lax.dot_general(query, fresh_ref[...], contract, preferred_element_type=f32)
    fresh = jnp.where(see_fresh, fresh * scale, masked_score)
    score = lax.dot_general(query, keys[...], contract, preferred_element_type=f32)
    score = jnp.where(
        slot_ref[...] == row_slot + 1, score * scale, masked_score
    )
    top_held = top_ref[mine, :1]
    top = jnp.maximum(
        jnp.maximum(top_held, jnp.max(fresh, axis=1, keepdims=True)),
        jnp.max(score, axis=1, keepdims=True),
    )
    held = jnp.exp(top_held - top)
    weight_fresh = jnp.exp(fresh - top)
    weight = jnp.exp(score - top)
    total = (
        sum_ref[mine, :1] * held
        + jnp.sum(weight_fresh, axis=1, keepdims=True)
        + jnp.sum(weight, axis=1, keepdims=True)
    )
    mix = jnp.dot(
        weight_fresh.astype(bf16), fresh_ref[:, :lat_width], preferred_element_type=f32
    ) + jnp.dot(weight.astype(bf16), keys[:, :lat_width], preferred_element_type=f32)
    mix_held = jnp.concatenate([mix_ref[n, mine, :] for n in range(mix_ref.shape[0])], axis=1)
    latent = ((mix_held * held + mix) / total).astype(bf16)
    live = live_ref[:, :1]
    width = value_ref.shape[2]
    for h in range(0, heads, 2):
        head = part * heads + h
        pair = jnp.concatenate([value_ref[head], value_ref[head + 1]], axis=1)
        both = jnp.dot(
            latent[h * per_head : (h + 2) * per_head, :], pair, preferred_element_type=f32
        )
        out_ref[:, h * width : (h + 1) * width] = (both[:per_head, :width] * live).astype(bf16)
        out_ref[:, (h + 1) * width : (h + 2) * width] = (both[per_head:, width:] * live).astype(bf16)


def attend(scale, query, fresh, row_slot, top, total, mix, live, value, pieces, cap_slots,
           part, parts):
    heads, _, width = value.shape
    steps = fresh.shape[0] // cap_slots
    part_heads = heads // parts
    return pl.pallas_call(
        functools.partial(attend_kernel, scale, cap_slots, steps, part, parts),
        out_shape=jax.ShapeDtypeStruct((cap_slots * steps, part_heads * width), bf16),
        in_specs=[in_vmem] * (8 + len(pieces)),
        out_specs=in_vmem,
        scratch_shapes=[pltpu.VMEM((len(pieces) * pieces[0].shape[0], query.shape[1]), bf16)],
        compiler_params=pltpu.CompilerParams(vmem_limit_bytes=10 * mib),
        name="attend",
    )(query, fresh, row_slot, top, total, mix, live, value, *pieces)


def output_kernel(dev_count, side_count, part, parts, *refs):
    my_dev, my_side = lax.axis_index("dev"), lax.axis_index("side")
    head_refs = refs[:dev_count]
    weight_ref = refs[dev_count]
    earlier_ref = refs[dev_count + 1] if part else None
    out_refs = refs[dev_count + 1 + (part > 0) : -1]
    held = refs[-1]
    rows, depth = head_refs[0].shape
    per_side = dev_count // side_count
    for j in range(dev_count):
        group = my_dev ^ j
        place = (lax.div(group, per_side) ^ my_side) * per_side + lax.rem(group, per_side)
        held[pl.ds(pl.multiple_of(place * rows, 16), rows), :] = head_refs[j][...]
    columns = weight_ref.shape[1]
    tile = 256 if columns % 256 == 0 else columns
    side_rows = rows * per_side
    for n in range(columns // tile):
        here = slice(n * tile, (n + 1) * tile)
        product = jnp.dot(
            held[...], weight_ref[part * depth : (part + 1) * depth, here],
            preferred_element_type=f32,
        )
        if part:
            product = product + earlier_ref[:, here]
        if part + 1 < parts:
            out_refs[0][:, here] = product
        else:
            for k in range(side_count):
                out_refs[k][:, here] = product[k * side_rows : (k + 1) * side_rows, :].astype(
                    out_refs[k].dtype
                )


def output_product(head_pieces, weight, side_count, earlier, part, parts):
    dev_count = len(head_pieces)
    rows, depth = head_pieces[0].shape
    columns = weight.shape[1]
    side_rows = rows * dev_count // side_count
    if part + 1 < parts:
        shapes = [((rows * dev_count, columns), f32)]
    else:
        shapes = [((side_rows, columns), f32 if k == 0 else bf16) for k in range(side_count)]
    earlier = [] if earlier is None else [earlier]
    return pl.pallas_call(
        functools.partial(output_kernel, dev_count, side_count, part, parts),
        out_shape=[jax.ShapeDtypeStruct(*shape) for shape in shapes],
        in_specs=[in_vmem] * (dev_count + 1 + len(earlier)),
        out_specs=[in_vmem] * len(shapes),
        scratch_shapes=[pltpu.VMEM((dev_count * rows, depth), bf16)],
        compiler_params=pltpu.CompilerParams(vmem_limit_bytes=10 * mib),
        name="output_product",
    )(*head_pieces, weight, *earlier)


def on_device(
    prompts,
    latent_weight,
    latent_gain,
    row_request,
    context_len,
    request_slot,
    latent_cache,
    new_latent,
    queries,
    key_absorb,
    value_absorb,
    out_weight,
):
    dev_count = lax.axis_size("dev")
    side_count = lax.axis_size("side")
    tok_rows, model_width = prompts.shape
    shard_rows, kv_width = latent_weight.shape
    lat_width = latent_gain.shape[0]
    head_count, nope_width, _ = key_absorb.shape
    rope_width = kv_width - lat_width
    cap_slots, ctx_len, _ = latent_cache.shape
    step_count = new_latent.shape[1]
    bucket_rows = 2 * tok_rows // dev_count
    group_rows = dev_count * bucket_rows
    slab = model_width // dev_count

    x_pieces = list(split_columns(prompts, dev_count))
    weights = [latent_weight] + [None] * (side_count - 1)
    for k in sorted(range(2, dev_count), reverse=True):
        x_pieces[k] = swap(x_pieces[k], "dev", k)
    for k in range(1, side_count):
        weights[k] = swap(latent_weight, "side", k)
    x_pieces[1], weights[1] = lax.optimization_barrier((x_pieces[1], weights[1]))
    x_pieces[1] = swap(x_pieces[1], "dev", 1)

    score_scale = queries.shape[-1] ** (-0.5)
    half = rope_width // 2
    inverse = 1.0 / 10000.0 ** (jnp.arange(half, dtype=f32) * (2.0 / rope_width))
    fresh, lengths, x_pieces[0] = lax.optimization_barrier(
        (new_latent.reshape(-1, kv_width), context_len, x_pieces[0])
    )
    (
        query_full, top_held, sum_held, mix_held, live, target, cosine, sine, row_slot,
        value_here, out_here,
    ) = prepare(
        score_scale, dev_count, side_count, bucket_rows, lengths, request_slot,
        row_request.reshape(-1, 128), inverse.reshape(1, -1), queries, key_absorb,
        jnp.swapaxes(latent_cache, 1, 2), value_absorb, out_weight,
    )

    if shard_rows % 16:
        my_side = lax.axis_index("side")
        held = jnp.zeros((side_count, shard_rows, kv_width), bf16)
        for k in range(side_count):
            held = lax.dynamic_update_slice(held, weights[k][None], (my_side ^ k, 0, 0))
        weights = [held.reshape(slab, kv_width)]

    routed = project(x_pieces, weights, target, group_rows)
    parts = [routed[0]] + [None] * (dev_count - 1)
    for k in sorted(range(1, dev_count), reverse=True):
        parts[k] = swap(routed[k], "dev", k)
    latent_rows = finish(parts, latent_gain.reshape(1, -1), cosine, sine)
    pieces = [latent_rows] + [swap(latent_rows, "side", k) for k in range(1, side_count)]
    product, parts = None, 2
    for part in range(parts):
        head_out = attend(
            score_scale, query_full, fresh, row_slot, top_held,
            sum_held, mix_held, live, value_here, pieces, cap_slots, part, parts,
        )
        heads = [head_out] + [None] * (dev_count - 1)
        for k in sorted(range(1, dev_count), reverse=True):
            heads[k] = swap(head_out, "dev", k)
        products = output_product(heads, out_here, side_count, product, part, parts)
        product = products[0]
    result = products[0]
    for k in sorted(range(1, side_count), reverse=True):
        result = result + swap(products[k], "side", k).astype(f32)
    return result.astype(bf16)


def solution(mesh):
    placed = (
        P(("rep", "dev", "side"), None),
        P(("dev", "side"), None),
        P(),
        P("rep"),
        P("rep"),
        P("rep"),
        P(("rep", "dev"), None, None),
        P(("rep", "dev"), None, None),
        P(("rep", "dev"), None, "side", None),
        P("side", None, None),
        P("side", None, None),
        P("side", "dev"),
    )
    return jax.shard_map(
        on_device, mesh=mesh, in_specs=placed, out_specs=P(("rep", "side"), "dev"), check_vma=False
    )
```

```python
import functools

import jax
import jax.numpy as jnp
from jax import lax
from jax.experimental import pallas as pl
from jax.experimental.pallas import tpu as pltpu
from jax.sharding import PartitionSpec as P

masked_score = -1e30
bf16, f32 = jnp.bfloat16, jnp.float32
in_vmem = pl.BlockSpec(memory_space=pltpu.VMEM)
in_smem = pl.BlockSpec(memory_space=pltpu.SMEM)
in_hbm = pl.BlockSpec(memory_space=pltpu.HBM)
mib = 1024 * 1024
prepare_mib = 16


def swap(value, axis, step):
    count = lax.axis_size(axis)
    return lax.ppermute(value, axis, [(i, i ^ step) for i in range(count)])


def pick(pieces, index):
    out = pieces[0]
    for k in range(1, len(pieces)):
        out = jnp.where(index == k, pieces[k], out)
    return out


def lane_tiles(width):
    return [slice(n, min(n + 128, width)) for n in range(0, width, 128)]


def packed_rows(rows, width):
    return rows * (width // 128) + rows // 2


def pack(value):
    rows, width = value.shape
    full = width // 128
    rest = value[:, full * 128 :]
    parts = [value[:, n * 128 : (n + 1) * 128] for n in range(full)]
    return parts + [jnp.concatenate([rest[: rows // 2], rest[rows // 2 :]], axis=1)]


def store_packed(ref, value):
    first = 0
    for part in pack(value):
        ref[first : first + part.shape[0], :] = part.astype(ref.dtype)
        first += part.shape[0]


def load_packed(ref, rows):
    full = ref.shape[0] // rows
    tiles = [ref[n * rows : (n + 1) * rows, :] for n in range(full)]
    rest = ref[full * rows :, :]
    return tiles, jnp.concatenate([rest[:, :64], rest[:, 64:]], axis=0)


def pack_kernel(value_ref, out_ref):
    store_packed(out_ref, value_ref[...])


def pack_weight(weight):
    rows, width = weight.shape
    return pl.pallas_call(
        pack_kernel,
        out_shape=jax.ShapeDtypeStruct((packed_rows(rows, width), 128), weight.dtype),
        in_specs=[in_vmem],
        out_specs=in_vmem,
        compiler_params=pltpu.CompilerParams(vmem_limit_bytes=8 * mib),
        cost_estimate=pl.CostEstimate(flops=10**10, bytes_accessed=10**6, transcendentals=0),
        name="pack_weight",
    )(weight)


def split_kernel(slab, prompts_ref, *refs):
    my_dev = lax.axis_index("dev")
    out_refs, sems = refs[:-1], refs[-1]
    copies = []
    for k in range(len(out_refs))[::-1]:
        first = pl.multiple_of((my_dev ^ k) * slab, 128)
        copies.append(
            pltpu.make_async_copy(prompts_ref.at[:, pl.ds(first, slab)], out_refs[k], sems.at[k])
        )
    for copy in copies:
        copy.start()
    for copy in copies:
        copy.wait()


def split_columns(prompts, count):
    rows, width = prompts.shape
    slab = width // count
    if slab % 128:
        columns = [prompts[:, k * slab : (k + 1) * slab] for k in range(count)]
        my_dev = lax.axis_index("dev")
        return [pick(columns, my_dev ^ k) for k in range(count)]
    return pl.pallas_call(
        functools.partial(split_kernel, slab),
        out_shape=[jax.ShapeDtypeStruct((rows, slab), prompts.dtype)] * count,
        in_specs=[in_hbm],
        out_specs=[in_vmem] * count,
        scratch_shapes=[pltpu.SemaphoreType.DMA((count,))],
        compiler_params=pltpu.CompilerParams(vmem_limit_bytes=8 * mib),
        cost_estimate=pl.CostEstimate(
            flops=10**10, bytes_accessed=4 * 10**7, transcendentals=0
        ),
        name="split_columns",
    )(prompts)


def fill_tables(
    dev_count, side_count, bucket, cap_slots, length_ref, slot_ref, request_ref, inverse_ref,
    target_ref, cos_ref, sin_ref, spot_ref, to_ref, place_ref, local_ref, position_ref,
):
    my_dev, my_side = lax.axis_index("dev"), lax.axis_index("side")
    requests = request_ref[...]
    lane_rows, lanes = requests.shape
    tok_rows = bucket * dev_count // 2
    per_row = lanes // tok_rows
    group_rows = dev_count * bucket
    before = lax.broadcasted_iota(jnp.int32, (lanes, lanes), 0)
    after = lax.broadcasted_iota(jnp.int32, (lanes, lanes), 1)
    below = jnp.where(before < after, 1.0, 0.0)
    near = jnp.where((before < after) & (before // tok_rows == after // tok_rows), 1.0, 0.0)
    scan = jnp.concatenate([below, jnp.ones_like(below)], axis=1).astype(bf16)
    lower = lax.broadcasted_iota(jnp.int32, (lane_rows, lane_rows), 0)
    upper = lax.broadcasted_iota(jnp.int32, (lane_rows, lane_rows), 1)
    rows_before = jnp.where(upper < lower, 1.0, 0.0)
    position = jnp.zeros(requests.shape, f32)
    slot = jnp.zeros(requests.shape, jnp.int32)
    for q in range(slot_ref.shape[0]):
        hit = requests == q
        ranks = jnp.dot(
            jnp.where(hit, 1.0, 0.0).astype(bf16), scan, preferred_element_type=f32
        )
        earlier = jnp.dot(rows_before, ranks[:, lanes:], preferred_element_type=f32)
        start = length_ref[q].astype(f32)
        position = jnp.where(hit, ranks[:, :lanes] + earlier + start, position)
        slot = jnp.where(hit, slot_ref[q], slot)
    group = lax.div(slot, cap_slots)
    rank = jnp.zeros(requests.shape, f32)
    for g in range(dev_count):
        hit = group == g
        ranks = jnp.dot(
            jnp.where(hit, 1.0, 0.0).astype(bf16), near.astype(bf16), preferred_element_type=f32
        )
        rank = jnp.where(hit, ranks, rank)
    block = lax.broadcasted_iota(jnp.int32, requests.shape, 0) * per_row + lax.div(
        lax.broadcasted_iota(jnp.int32, requests.shape, 1), tok_rows
    )
    place = lax.div(block, side_count) * bucket + rank.astype(jnp.int32)
    to_ref[...] = (group ^ my_dev) * group_rows + place
    place_ref[...] = jnp.where(group == my_dev, place, -1)
    local_ref[...] = (slot - my_dev * cap_slots + 1).astype(f32)
    position_ref[...] = position
    lane_block = lax.div(lax.broadcasted_iota(jnp.int32, (1, lanes), 1), tok_rows)
    ids = lax.broadcasted_iota(jnp.int32, (group_rows, 1), 0)

    def find(dev, side):
        held = dev * side_count + side
        return pl.ds(lax.div(held, per_row), 1), lane_block == lax.rem(held, per_row)

    for k in range(dev_count):
        row, inside = find(my_dev ^ k, my_side)
        target_ref[:, k * lanes : (k + 1) * lanes] = jnp.where(inside, to_ref[row, :], -1)
    found = jnp.zeros((group_rows, lanes), f32)
    for d in range(dev_count):
        row, inside = find(d, my_side)
        found = jnp.where((place_ref[row, :] == ids) & inside, position_ref[row, :], found)
    angles = jnp.sum(found, axis=1, keepdims=True) * inverse_ref[...]
    cos_ref[...] = jnp.cos(angles)
    sin_ref[...] = jnp.sin(angles)
    for k in range(side_count):
        total = jnp.zeros((8, group_rows), f32)
        for d in range(dev_count):
            row, inside = find(d, my_side ^ k)
            chosen = jnp.where((place_ref[row, :] == ids) & inside, 1.0, 0.0).astype(bf16)
            values = jnp.broadcast_to(local_ref[row, :], (8, lanes)).astype(bf16)
            total = total + lax.dot_general(
                values, chosen, (((1,), (1,)), ((), ())), preferred_element_type=f32
            )
        spot_ref[:, k * group_rows : (k + 1) * group_rows] = total[:1].astype(jnp.int32)


def prepare_kernel(
    scale, steps, layout, inverse_ref, length_hbm, slot_hbm, request_hbm, query_hbm, absorb_hbm,
    cache_hbm, value_hbm, out_hbm, full_ref, top_ref, sum_ref, mix_ref, live_ref, target_ref,
    cos_ref, sin_ref, spot_ref, value_ref, out_ref, length_ref, slot_ref, request_ref, query_ref,
    absorb_ref, cache_ref, plain, full, to_ref, place_ref, local_ref, position_ref, sems,
):
    pairs = [
        (length_hbm, length_ref), (slot_hbm, slot_ref), (request_hbm, request_ref),
        (query_hbm, query_ref), (absorb_hbm, absorb_ref), (cache_hbm, cache_ref),
        (value_hbm, value_ref),
    ]
    parts = sems.shape[0] - len(pairs)
    rows = out_hbm.shape[0] // parts
    for n in range(parts):
        part = pl.ds(n * rows, rows)
        pairs.append((out_hbm.at[part], out_ref.at[part]))
    copies = [pltpu.make_async_copy(*pair, sems.at[n]) for n, pair in enumerate(pairs)]
    for copy in copies:
        copy.start()
    for copy in copies[:3]:
        copy.wait()
    slots, _, context = cache_ref.shape
    heads, nope, lat_width = absorb_ref.shape
    per_head = slots * steps
    fill_tables(
        *layout, slots, length_ref, slot_ref, request_ref, inverse_ref, target_ref, cos_ref,
        sin_ref, spot_ref, to_ref, place_ref, local_ref, position_ref,
    )
    first_slot = lax.axis_index("dev") * slots
    lengths = []
    for s in range(slots):
        length = jnp.int32(0)
        for q in range(slot_ref.shape[0]):
            length = jnp.where(slot_ref[q] == first_slot + s, length_ref[q], length)
        lengths.append(length)
    slot_of = lax.div(lax.broadcasted_iota(jnp.int32, live_ref.shape, 0), steps)
    live = jnp.zeros(live_ref.shape, f32)
    for s in range(slots):
        live = jnp.where((slot_of == s) & (lengths[s] > 0), 1.0, live)
    live_ref[...] = live
    copies[3].wait()
    copies[4].wait()
    for n, here in enumerate(lane_tiles(query_ref.shape[1])):
        plain[n, :, : here.stop - here.start] = query_ref[:, here].astype(f32)
    wide = lane_tiles(full_ref.shape[1])
    for h in range(heads):
        there = pl.ds(h, per_head, stride=heads)
        query = plain[0, there, :].astype(bf16)
        latent = jnp.dot(query, absorb_ref[h], preferred_element_type=f32).astype(bf16).astype(f32)
        here = slice(h * per_head, (h + 1) * per_head)
        for n, lanes in enumerate(lane_tiles(lat_width)):
            full[n, here, :] = latent[:, lanes]
        full[len(wide) - 1, here, :] = plain[1, there, :]
    for n, lanes in enumerate(wide):
        full_ref[:, lanes] = full[n, :, : lanes.stop - lanes.start].astype(bf16)
    key = lax.broadcasted_iota(jnp.int32, (1, context), 1)
    copies[5].wait()
    for s in range(slots):
        theres = [pl.ds(s * steps + t, heads, stride=per_head) for t in range(steps)]
        query = jnp.concatenate(
            [
                jnp.concatenate([full[n, there, :] for there in theres], axis=0)[
                    :, : lanes.stop - lanes.start
                ].astype(bf16)
                for n, lanes in enumerate(wide)
            ],
            axis=1,
        )
        rows = cache_ref[s]
        score = jnp.dot(query, rows, preferred_element_type=f32)
        score = jnp.where(key < lengths[s], score * scale, masked_score)
        top = jnp.max(score, axis=1, keepdims=True)
        weight = jnp.exp(score - top)
        total = jnp.sum(weight, axis=1, keepdims=True)
        mix = lax.dot_general(
            weight.astype(bf16), rows[:lat_width, :], (((1,), (1,)), ((), ())),
            preferred_element_type=f32,
        )
        lanes = top_ref.shape[1]
        for t in range(steps):
            there = theres[t]
            here = slice(t * heads, (t + 1) * heads)
            top_ref[there, :] = jnp.broadcast_to(top[here], (heads, lanes))
            sum_ref[there, :] = jnp.broadcast_to(total[here], (heads, lanes))
            for n, part in enumerate(lane_tiles(lat_width)):
                mix_ref[n, there, :] = mix[here, part]
    for copy in copies[6:]:
        copy.wait()


def prepare(
    scale, dev_count, side_count, bucket, lengths, request_slot, requests, inverse, queries,
    absorb, cache, value, out_weight,
):
    slots, steps, heads, width = queries.shape
    kv_width = cache.shape[1]
    lat_width = absorb.shape[2]
    rows = slots * steps * heads
    group_rows = dev_count * bucket
    parts = 8
    lanes = requests.shape[1]
    half = inverse.shape[1]
    shapes = [
        ((rows, kv_width), bf16), ((rows, 128), f32), ((rows, 128), f32),
        ((lat_width // 128, rows, 128), f32), ((slots * steps, 128), f32),
        ((1, dev_count * lanes), jnp.int32), ((group_rows, half), f32), ((group_rows, half), f32),
        ((1, side_count * group_rows), jnp.int32), (value.shape, bf16), (out_weight.shape, bf16),
    ]
    return pl.pallas_call(
        functools.partial(prepare_kernel, scale, steps, (dev_count, side_count, bucket)),
        out_shape=[jax.ShapeDtypeStruct(*shape) for shape in shapes],
        in_specs=[in_vmem] + [in_hbm] * 8,
        out_specs=[in_vmem] * len(shapes),
        scratch_shapes=[
            pltpu.SMEM(lengths.shape, lengths.dtype),
            pltpu.SMEM(request_slot.shape, request_slot.dtype),
            pltpu.VMEM(requests.shape, requests.dtype),
            pltpu.VMEM((rows, width), queries.dtype),
            pltpu.VMEM(absorb.shape, absorb.dtype),
            pltpu.VMEM(cache.shape, cache.dtype),
            pltpu.VMEM((len(lane_tiles(width)), rows, 128), f32),
            pltpu.VMEM((len(lane_tiles(kv_width)), rows, 128), f32),
            pltpu.VMEM(requests.shape, jnp.int32),
            pltpu.VMEM(requests.shape, jnp.int32),
            pltpu.VMEM(requests.shape, f32),
            pltpu.VMEM(requests.shape, f32),
            pltpu.SemaphoreType.DMA((parts + 7,)),
        ],
        compiler_params=pltpu.CompilerParams(vmem_limit_bytes=prepare_mib * mib),
        cost_estimate=pl.CostEstimate(
            flops=4 * 10**9, bytes_accessed=28 * 10**6, transcendentals=10**5
        ),
        name="prepare",
    )(inverse, lengths, request_slot, requests, queries.reshape(rows, width), absorb, cache, value,
      out_weight)


def project_kernel(dev_count, side_count, target_ref, *refs):
    my_side = lax.axis_index("side")
    x_refs = refs[:dev_count]
    weight_refs = refs[dev_count : dev_count + side_count]
    out_refs = refs[dev_count + side_count : -3]
    x_rows, slab_weight, rows = refs[-3:]
    tok_rows = x_refs[0].shape[0]
    full = slab_weight.shape[1] // 128
    if side_count > 1:
        shard = slab_weight.shape[0] // side_count
        for k in range(side_count):
            first = pl.multiple_of((my_side ^ k) * shard, 16)
            tiles, rest = load_packed(weight_refs[k], shard)
            for n, tile in enumerate(tiles):
                slab_weight[pl.ds(first, shard), n * 128 : (n + 1) * 128] = tile
            slab_weight[pl.ds(first, shard), full * 128 :] = rest
    for k in range(dev_count):
        x_rows[k * tok_rows : (k + 1) * tok_rows, :] = x_refs[k][...]
    slab = slab_weight[...] if side_count > 1 else weight_refs[0][...]
    raw = jnp.dot(x_rows[...], slab, preferred_element_type=f32).astype(bf16)
    copies = target_ref.shape[1] // (dev_count * tok_rows)
    for k in range(dev_count):
        for n in range(k * copies, (k + 1) * copies):
            rows[n * tok_rows : (n + 1) * tok_rows, :] = raw[k * tok_rows : (k + 1) * tok_rows, :]
    target = target_ref[...]
    group_rows = 2 * tok_rows
    step = max(1, min(dev_count, 512 // group_rows))
    for j in range(0, dev_count, step):
        ids = lax.broadcasted_iota(jnp.int32, (step * group_rows, target.shape[1]), 0)
        route = jnp.where(ids + j * group_rows == target, 1.0, 0.0).astype(bf16)
        placed = jnp.dot(route, rows[...], preferred_element_type=f32)
        for n in range(step):
            store_packed(out_refs[j + n], placed[n * group_rows : (n + 1) * group_rows])


def project(x_pieces, weights, target, width):
    dev_count = len(x_pieces)
    tok_rows, slab = x_pieces[0].shape
    return pl.pallas_call(
        functools.partial(project_kernel, dev_count, len(weights)),
        out_shape=[
            jax.ShapeDtypeStruct((packed_rows(2 * tok_rows, width), 128), f32 if j == 0 else bf16)
            for j in range(dev_count)
        ],
        in_specs=[in_vmem] * (1 + dev_count + len(weights)),
        out_specs=[in_vmem] * dev_count,
        scratch_shapes=[
            pltpu.VMEM((dev_count * tok_rows, slab), bf16),
            pltpu.VMEM((slab, width), bf16),
            pltpu.VMEM((target.shape[1], width), bf16),
        ],
        compiler_params=pltpu.CompilerParams(vmem_limit_bytes=20 * mib),
        name="project",
    )(target, *x_pieces, *weights)


def finish_kernel(gain_ref, cos_ref, sin_ref, *refs):
    parts, out_ref = refs[:-1], refs[-1]
    rows, half = cos_ref.shape
    total = parts[0][...].astype(f32)
    for part in parts[1:]:
        total = total + part[...].astype(f32)
    tiles, rest = load_packed(total, rows)
    latent = jnp.concatenate(tiles, axis=1)
    spread = jnp.mean(latent * latent, axis=1, keepdims=True)
    latent = latent * lax.rsqrt(spread + 1e-06) * gain_ref[...]
    first, second = rest[:, :half], rest[:, half:]
    cosine, sine = cos_ref[...], sin_ref[...]
    store_packed(
        out_ref,
        jnp.concatenate(
            [latent, first * cosine - second * sine, second * cosine + first * sine], axis=1
        ),
    )


def finish(parts, gain, cosine, sine):
    return pl.pallas_call(
        finish_kernel,
        out_shape=jax.ShapeDtypeStruct(parts[0].shape, bf16),
        in_specs=[in_vmem] * (3 + len(parts)),
        out_specs=in_vmem,
        compiler_params=pltpu.CompilerParams(vmem_limit_bytes=8 * mib),
        name="finish_rows",
    )(gain, cosine, sine, *parts)


def attend_kernel(
    scale, cap_slots, steps, part, parts, query_ref, fresh_ref, slot_ref, top_ref,
    sum_ref, mix_ref, live_ref, value_ref, *refs
):
    pieces, out_ref, keys = refs[:-2], refs[-2], refs[-1]
    lat_width = mix_ref.shape[0] * mix_ref.shape[2]
    per_head = cap_slots * steps
    rows = query_ref.shape[0] // parts
    heads = rows // per_head
    mine = slice(part * rows, (part + 1) * rows)
    piece_rows = keys.shape[0] // len(pieces)
    for n, piece in enumerate(pieces):
        tiles, rest = load_packed(piece, piece_rows)
        there = slice(n * piece_rows, (n + 1) * piece_rows)
        for j, tile in enumerate(tiles):
            keys[there, j * 128 : (j + 1) * 128] = tile
        keys[there, lat_width:] = rest
    contract = (((1,), (1,)), ((), ()))
    row = lax.broadcasted_iota(jnp.int32, (rows, 1), 0)
    row_slot = (row // steps) % cap_slots
    key = lax.broadcasted_iota(jnp.int32, (1, per_head), 1)
    see_fresh = (key // steps == row_slot) & (key % steps <= row % steps)
    query = query_ref[mine, :]
    fresh = lax.dot_general(query, fresh_ref[...], contract, preferred_element_type=f32)
    fresh = jnp.where(see_fresh, fresh * scale, masked_score)
    score = lax.dot_general(query, keys[...], contract, preferred_element_type=f32)
    score = jnp.where(
        slot_ref[...] == row_slot + 1, score * scale, masked_score
    )
    top_held = top_ref[mine, :1]
    top = jnp.maximum(
        jnp.maximum(top_held, jnp.max(fresh, axis=1, keepdims=True)),
        jnp.max(score, axis=1, keepdims=True),
    )
    held = jnp.exp(top_held - top)
    weight_fresh = jnp.exp(fresh - top)
    weight = jnp.exp(score - top)
    total = (
        sum_ref[mine, :1] * held
        + jnp.sum(weight_fresh, axis=1, keepdims=True)
        + jnp.sum(weight, axis=1, keepdims=True)
    )
    mix = jnp.dot(
        weight_fresh.astype(bf16), fresh_ref[:, :lat_width], preferred_element_type=f32
    ) + jnp.dot(weight.astype(bf16), keys[:, :lat_width], preferred_element_type=f32)
    mix_held = jnp.concatenate([mix_ref[n, mine, :] for n in range(mix_ref.shape[0])], axis=1)
    latent = ((mix_held * held + mix) / total).astype(bf16)
    live = live_ref[:, :1]
    width = value_ref.shape[2]
    for h in range(0, heads, 2):
        head = part * heads + h
        pair = jnp.concatenate([value_ref[head], value_ref[head + 1]], axis=1)
        both = jnp.dot(
            latent[h * per_head : (h + 2) * per_head, :], pair, preferred_element_type=f32
        )
        out_ref[:, h * width : (h + 1) * width] = (both[:per_head, :width] * live).astype(bf16)
        out_ref[:, (h + 1) * width : (h + 2) * width] = (both[per_head:, width:] * live).astype(bf16)


def attend(scale, query, fresh, row_slot, top, total, mix, live, value, pieces, cap_slots,
           part, parts):
    heads, _, width = value.shape
    steps = fresh.shape[0] // cap_slots
    part_heads = heads // parts
    return pl.pallas_call(
        functools.partial(attend_kernel, scale, cap_slots, steps, part, parts),
        out_shape=jax.ShapeDtypeStruct((cap_slots * steps, part_heads * width), bf16),
        in_specs=[in_vmem] * (8 + len(pieces)),
        out_specs=in_vmem,
        scratch_shapes=[pltpu.VMEM((row_slot.shape[1], query.shape[1]), bf16)],
        compiler_params=pltpu.CompilerParams(vmem_limit_bytes=10 * mib),
        name="attend",
    )(query, fresh, row_slot, top, total, mix, live, value, *pieces)


def output_kernel(dev_count, side_count, part, parts, *refs):
    my_dev, my_side = lax.axis_index("dev"), lax.axis_index("side")
    head_refs = refs[:dev_count]
    weight_ref = refs[dev_count]
    earlier_ref = refs[dev_count + 1] if part else None
    out_refs = refs[dev_count + 1 + (part > 0) : -1]
    held = refs[-1]
    rows, depth = head_refs[0].shape
    per_side = dev_count // side_count
    for j in range(dev_count):
        group = my_dev ^ j
        place = (lax.div(group, per_side) ^ my_side) * per_side + lax.rem(group, per_side)
        held[pl.ds(pl.multiple_of(place * rows, 16), rows), :] = head_refs[j][...]
    columns = weight_ref.shape[1]
    tile = 256 if columns % 256 == 0 else columns
    side_rows = rows * per_side
    for n in range(columns // tile):
        here = slice(n * tile, (n + 1) * tile)
        product = jnp.dot(
            held[...], weight_ref[part * depth : (part + 1) * depth, here],
            preferred_element_type=f32,
        )
        if part:
            product = product + earlier_ref[:, here]
        if part + 1 < parts:
            out_refs[0][:, here] = product
        else:
            for k in range(side_count):
                out_refs[k][:, here] = product[k * side_rows : (k + 1) * side_rows, :].astype(
                    out_refs[k].dtype
                )


def output_product(head_pieces, weight, side_count, earlier, part, parts):
    dev_count = len(head_pieces)
    rows, depth = head_pieces[0].shape
    columns = weight.shape[1]
    side_rows = rows * dev_count // side_count
    if part + 1 < parts:
        shapes = [((rows * dev_count, columns), f32)]
    else:
        shapes = [((side_rows, columns), f32 if k == 0 else bf16) for k in range(side_count)]
    earlier = [] if earlier is None else [earlier]
    return pl.pallas_call(
        functools.partial(output_kernel, dev_count, side_count, part, parts),
        out_shape=[jax.ShapeDtypeStruct(*shape) for shape in shapes],
        in_specs=[in_vmem] * (dev_count + 1 + len(earlier)),
        out_specs=[in_vmem] * len(shapes),
        scratch_shapes=[pltpu.VMEM((dev_count * rows, depth), bf16)],
        compiler_params=pltpu.CompilerParams(vmem_limit_bytes=10 * mib),
        name="output_product",
    )(*head_pieces, weight, *earlier)


def on_device(
    prompts,
    latent_weight,
    latent_gain,
    row_request,
    context_len,
    request_slot,
    latent_cache,
    new_latent,
    queries,
    key_absorb,
    value_absorb,
    out_weight,
):
    dev_count = lax.axis_size("dev")
    side_count = lax.axis_size("side")
    tok_rows, model_width = prompts.shape
    shard_rows, kv_width = latent_weight.shape
    lat_width = latent_gain.shape[0]
    head_count, nope_width, _ = key_absorb.shape
    rope_width = kv_width - lat_width
    cap_slots, ctx_len, _ = latent_cache.shape
    step_count = new_latent.shape[1]
    bucket_rows = 2 * tok_rows // dev_count
    group_rows = dev_count * bucket_rows
    slab = model_width // dev_count

    x_pieces = list(split_columns(prompts, dev_count))
    packs = shard_rows % 32 == 0
    weights = [pack_weight(latent_weight) if packs else latent_weight] + [None] * (side_count - 1)
    for k in sorted(range(2, dev_count), reverse=True):
        x_pieces[k] = swap(x_pieces[k], "dev", k)
    for k in range(1, side_count):
        weights[k] = swap(weights[0], "side", k)
    x_pieces[1], weights[1] = lax.optimization_barrier((x_pieces[1], weights[1]))
    x_pieces[1] = swap(x_pieces[1], "dev", 1)

    score_scale = queries.shape[-1] ** (-0.5)
    half = rope_width // 2
    inverse = 1.0 / 10000.0 ** (jnp.arange(half, dtype=f32) * (2.0 / rope_width))
    fresh, lengths, x_pieces[0] = lax.optimization_barrier(
        (new_latent.reshape(-1, kv_width), context_len, x_pieces[0])
    )
    (
        query_full, top_held, sum_held, mix_held, live, target, cosine, sine, row_slot,
        value_here, out_here,
    ) = prepare(
        score_scale, dev_count, side_count, bucket_rows, lengths, request_slot,
        row_request.reshape(-1, 128), inverse.reshape(1, -1), queries, key_absorb,
        jnp.swapaxes(latent_cache, 1, 2), value_absorb, out_weight,
    )

    if not packs:
        my_side = lax.axis_index("side")
        held = jnp.zeros((side_count, shard_rows, kv_width), bf16)
        for k in range(side_count):
            held = lax.dynamic_update_slice(held, weights[k][None], (my_side ^ k, 0, 0))
        weights = [held.reshape(slab, kv_width)]

    routed = project(x_pieces, weights, target, kv_width)
    parts = [routed[0]] + [None] * (dev_count - 1)
    for k in sorted(range(1, dev_count), reverse=True):
        parts[k] = swap(routed[k], "dev", k)
    latent_rows = finish(parts, latent_gain.reshape(1, -1), cosine, sine)
    pieces = [latent_rows] + [swap(latent_rows, "side", k) for k in range(1, side_count)]
    product, parts = None, 2
    for part in range(parts):
        head_out = attend(
            score_scale, query_full, fresh, row_slot, top_held,
            sum_held, mix_held, live, value_here, pieces, cap_slots, part, parts,
        )
        heads = [head_out] + [None] * (dev_count - 1)
        for k in sorted(range(1, dev_count), reverse=True):
            heads[k] = swap(head_out, "dev", k)
        products = output_product(heads, out_here, side_count, product, part, parts)
        product = products[0]
    result = products[0]
    for k in sorted(range(1, side_count), reverse=True):
        result = result + swap(products[k], "side", k).astype(f32)
    return result.astype(bf16)


def solution(mesh):
    placed = (
        P(("rep", "dev", "side"), None),
        P(("dev", "side"), None),
        P(),
        P("rep"),
        P("rep"),
        P("rep"),
        P(("rep", "dev"), None, None),
        P(("rep", "dev"), None, None),
        P(("rep", "dev"), None, "side", None),
        P("side", None, None),
        P("side", None, None),
        P("side", "dev"),
    )
    return jax.shard_map(
        on_device, mesh=mesh, in_specs=placed, out_specs=P(("rep", "side"), "dev"), check_vma=False
    )
```

```python
import functools

import jax
import jax.numpy as jnp
from jax import lax
from jax.experimental import pallas as pl
from jax.experimental.pallas import tpu as pltpu
from jax.sharding import PartitionSpec as P

masked_score = -1e30
bf16, f32 = jnp.bfloat16, jnp.float32
in_vmem = pl.BlockSpec(memory_space=pltpu.VMEM)
in_smem = pl.BlockSpec(memory_space=pltpu.SMEM)
in_hbm = pl.BlockSpec(memory_space=pltpu.HBM)
mib = 1024 * 1024
prepare_mib = 16


def swap(value, axis, step):
    count = lax.axis_size(axis)
    return lax.ppermute(value, axis, [(i, i ^ step) for i in range(count)])


def pick(pieces, index):
    out = pieces[0]
    for k in range(1, len(pieces)):
        out = jnp.where(index == k, pieces[k], out)
    return out


def lane_tiles(width):
    return [slice(n, min(n + 128, width)) for n in range(0, width, 128)]


def packed_rows(rows, width):
    return rows * (width // 128) + rows // 2


def pack(value):
    rows, width = value.shape
    full = width // 128
    rest = value[:, full * 128 :]
    parts = [value[:, n * 128 : (n + 1) * 128] for n in range(full)]
    return parts + [jnp.concatenate([rest[: rows // 2], rest[rows // 2 :]], axis=1)]


def store_packed(ref, value):
    first = 0
    for part in pack(value):
        ref[first : first + part.shape[0], :] = part.astype(ref.dtype)
        first += part.shape[0]


def load_packed(ref, rows):
    full = ref.shape[0] // rows
    tiles = [ref[n * rows : (n + 1) * rows, :] for n in range(full)]
    rest = ref[full * rows :, :]
    return tiles, jnp.concatenate([rest[:, :64], rest[:, 64:]], axis=0)


def pack_kernel(value_ref, out_ref):
    store_packed(out_ref, value_ref[...])


def pack_weight(weight):
    rows, width = weight.shape
    return pl.pallas_call(
        pack_kernel,
        out_shape=jax.ShapeDtypeStruct((packed_rows(rows, width), 128), weight.dtype),
        in_specs=[in_vmem],
        out_specs=in_vmem,
        compiler_params=pltpu.CompilerParams(vmem_limit_bytes=8 * mib),
        cost_estimate=pl.CostEstimate(flops=10**10, bytes_accessed=10**6, transcendentals=0),
        name="pack_weight",
    )(weight)


def split_kernel(slab, prompts_ref, *refs):
    my_dev = lax.axis_index("dev")
    out_refs, sems = refs[:-1], refs[-1]
    copies = []
    for k in range(len(out_refs))[::-1]:
        first = pl.multiple_of((my_dev ^ k) * slab, 128)
        copies.append(
            pltpu.make_async_copy(prompts_ref.at[:, pl.ds(first, slab)], out_refs[k], sems.at[k])
        )
    for copy in copies:
        copy.start()
    for copy in copies:
        copy.wait()


def split_columns(prompts, count):
    rows, width = prompts.shape
    slab = width // count
    if slab % 128:
        columns = [prompts[:, k * slab : (k + 1) * slab] for k in range(count)]
        my_dev = lax.axis_index("dev")
        return [pick(columns, my_dev ^ k) for k in range(count)]
    return pl.pallas_call(
        functools.partial(split_kernel, slab),
        out_shape=[jax.ShapeDtypeStruct((rows, slab), prompts.dtype)] * count,
        in_specs=[in_hbm],
        out_specs=[in_vmem] * count,
        scratch_shapes=[pltpu.SemaphoreType.DMA((count,))],
        compiler_params=pltpu.CompilerParams(vmem_limit_bytes=8 * mib),
        cost_estimate=pl.CostEstimate(
            flops=10**10, bytes_accessed=4 * 10**7, transcendentals=0
        ),
        name="split_columns",
    )(prompts)


def fill_tables(
    dev_count, side_count, bucket, cap_slots, length_ref, slot_ref, request_ref, inverse_ref,
    target_ref, cos_ref, sin_ref, spot_ref, to_ref, place_ref, local_ref, position_ref,
):
    my_dev, my_side = lax.axis_index("dev"), lax.axis_index("side")
    requests = request_ref[...]
    lane_rows, lanes = requests.shape
    tok_rows = bucket * dev_count // 2
    per_row = lanes // tok_rows
    half_bucket = bucket // 2
    half_rows = dev_count * half_bucket
    group_rows = 2 * half_rows
    before = lax.broadcasted_iota(jnp.int32, (lanes, lanes), 0)
    after = lax.broadcasted_iota(jnp.int32, (lanes, lanes), 1)
    below = jnp.where(before < after, 1.0, 0.0)
    near = jnp.where((before < after) & (before // tok_rows == after // tok_rows), 1.0, 0.0)
    scan = jnp.concatenate([below, jnp.ones_like(below)], axis=1).astype(bf16)
    lower = lax.broadcasted_iota(jnp.int32, (lane_rows, lane_rows), 0)
    upper = lax.broadcasted_iota(jnp.int32, (lane_rows, lane_rows), 1)
    rows_before = jnp.where(upper < lower, 1.0, 0.0)
    position = jnp.zeros(requests.shape, f32)
    slot = jnp.zeros(requests.shape, jnp.int32)
    for q in range(slot_ref.shape[0]):
        hit = requests == q
        ranks = jnp.dot(
            jnp.where(hit, 1.0, 0.0).astype(bf16), scan, preferred_element_type=f32
        )
        earlier = jnp.dot(rows_before, ranks[:, lanes:], preferred_element_type=f32)
        start = length_ref[q].astype(f32)
        position = jnp.where(hit, ranks[:, :lanes] + earlier + start, position)
        slot = jnp.where(hit, slot_ref[q], slot)
    group = lax.div(slot, cap_slots)
    rank = jnp.zeros(requests.shape, f32)
    for g in range(dev_count):
        hit = group == g
        ranks = jnp.dot(
            jnp.where(hit, 1.0, 0.0).astype(bf16), near.astype(bf16), preferred_element_type=f32
        )
        rank = jnp.where(hit, ranks, rank)
    block = lax.broadcasted_iota(jnp.int32, requests.shape, 0) * per_row + lax.div(
        lax.broadcasted_iota(jnp.int32, requests.shape, 1), tok_rows
    )
    rank = rank.astype(jnp.int32)
    which = lax.div(rank, half_bucket)
    place = lax.div(block, side_count) * half_bucket + lax.rem(rank, half_bucket)
    to_ref[...] = (which * dev_count + (group ^ my_dev)) * half_rows + place
    place = which * half_rows + place
    place_ref[...] = jnp.where(group == my_dev, place, -1)
    local_ref[...] = (slot - my_dev * cap_slots + 1).astype(f32)
    position_ref[...] = position
    lane_block = lax.div(lax.broadcasted_iota(jnp.int32, (1, lanes), 1), tok_rows)
    ids = lax.broadcasted_iota(jnp.int32, (group_rows, 1), 0)

    def find(dev, side):
        held = dev * side_count + side
        return pl.ds(lax.div(held, per_row), 1), lane_block == lax.rem(held, per_row)

    targets = []
    for k in range(dev_count):
        held = (my_dev ^ k) * side_count + my_side
        row = jnp.broadcast_to(to_ref[pl.ds(lax.div(held, per_row), 1), :], (8, lanes))
        start = lax.rem(lanes - tok_rows * lax.rem(held, per_row), lanes)
        targets.append(pltpu.roll(row, start, 1)[:1, :tok_rows])
    for k in range(0, dev_count, per_row):
        target_ref[:, k * tok_rows : k * tok_rows + lanes] = jnp.concatenate(
            targets[k : k + per_row], axis=1
        )
    found = jnp.zeros((group_rows, lanes), f32)
    for d in range(dev_count):
        row, inside = find(d, my_side)
        found = jnp.where((place_ref[row, :] == ids) & inside, position_ref[row, :], found)
    angles = jnp.sum(found, axis=1, keepdims=True) * inverse_ref[...]
    cos_ref[...] = jnp.cos(angles)
    sin_ref[...] = jnp.sin(angles)
    for k in range(side_count):
        total = jnp.zeros((8, group_rows), f32)
        for d in range(dev_count):
            row, inside = find(d, my_side ^ k)
            chosen = jnp.where((place_ref[row, :] == ids) & inside, 1.0, 0.0).astype(bf16)
            values = jnp.broadcast_to(local_ref[row, :], (8, lanes)).astype(bf16)
            total = total + lax.dot_general(
                values, chosen, (((1,), (1,)), ((), ())), preferred_element_type=f32
            )
        spot_ref[:, k * group_rows : (k + 1) * group_rows] = total[:1].astype(jnp.int32)


def prepare_kernel(
    scale, steps, layout, inverse_ref, length_hbm, slot_hbm, request_hbm, query_hbm, absorb_hbm,
    cache_hbm, fresh_hbm, value_hbm, out_hbm, full_ref, top_ref, sum_ref, mix_ref, live_ref, target_ref,
    cos_ref, sin_ref, spot_ref, value_ref, out_ref, length_ref, slot_ref, request_ref, query_ref,
    absorb_ref, cache_ref, fresh_ref, plain, full, to_ref, place_ref, local_ref, position_ref, sems,
):
    pairs = [
        (length_hbm, length_ref), (slot_hbm, slot_ref), (request_hbm, request_ref),
        (query_hbm, query_ref), (absorb_hbm, absorb_ref), (cache_hbm, cache_ref),
        (fresh_hbm, fresh_ref), (value_hbm, value_ref),
    ]
    parts = sems.shape[0] - len(pairs)
    rows = out_hbm.shape[0] // parts
    for n in range(parts):
        part = pl.ds(n * rows, rows)
        pairs.append((out_hbm.at[part], out_ref.at[part]))
    copies = [pltpu.make_async_copy(*pair, sems.at[n]) for n, pair in enumerate(pairs)]
    for copy in copies:
        copy.start()
    for copy in copies[:3]:
        copy.wait()
    slots, _, context = cache_ref.shape
    heads, nope, lat_width = absorb_ref.shape
    per_head = slots * steps
    fill_tables(
        *layout, slots, length_ref, slot_ref, request_ref, inverse_ref, target_ref, cos_ref,
        sin_ref, spot_ref, to_ref, place_ref, local_ref, position_ref,
    )
    first_slot = lax.axis_index("dev") * slots
    lengths = []
    for s in range(slots):
        length = jnp.int32(0)
        for q in range(slot_ref.shape[0]):
            length = jnp.where(slot_ref[q] == first_slot + s, length_ref[q], length)
        lengths.append(length)
    slot_of = lax.div(lax.broadcasted_iota(jnp.int32, live_ref.shape, 0), steps)
    live = jnp.zeros(live_ref.shape, f32)
    for s in range(slots):
        live = jnp.where((slot_of == s) & (lengths[s] > 0), 1.0, live)
    live_ref[...] = live
    copies[3].wait()
    copies[4].wait()
    for n, here in enumerate(lane_tiles(query_ref.shape[1])):
        plain[n, :, : here.stop - here.start] = query_ref[:, here].astype(f32)
    wide = lane_tiles(full_ref.shape[1])
    for h in range(heads):
        there = pl.ds(h, per_head, stride=heads)
        query = plain[0, there, :].astype(bf16)
        latent = jnp.dot(query, absorb_ref[h], preferred_element_type=f32).astype(bf16).astype(f32)
        here = slice(h * per_head, (h + 1) * per_head)
        for n, lanes in enumerate(lane_tiles(lat_width)):
            full[n, here, :] = latent[:, lanes]
        full[len(wide) - 1, here, :] = plain[1, there, :]
    for n, lanes in enumerate(wide):
        full_ref[:, lanes] = full[n, :, : lanes.stop - lanes.start].astype(bf16)
    key = lax.broadcasted_iota(jnp.int32, (1, context), 1)
    copies[5].wait()
    copies[6].wait()
    late = lax.broadcasted_iota(jnp.int32, (steps * heads, steps), 1)
    late = late > lax.div(lax.broadcasted_iota(jnp.int32, (steps * heads, steps), 0), heads)
    for s in range(slots):
        theres = [pl.ds(s * steps + t, heads, stride=per_head) for t in range(steps)]
        query = jnp.concatenate(
            [
                jnp.concatenate([full[n, there, :] for there in theres], axis=0)[
                    :, : lanes.stop - lanes.start
                ].astype(bf16)
                for n, lanes in enumerate(wide)
            ],
            axis=1,
        )
        rows = cache_ref[s]
        score = jnp.dot(query, rows, preferred_element_type=f32)
        score = jnp.where(key < lengths[s], score * scale, masked_score)
        fresh = fresh_ref[s]
        new = lax.dot_general(
            query, fresh, (((1,), (1,)), ((), ())), preferred_element_type=f32
        )
        new = jnp.where(late, masked_score, new * scale)
        top = jnp.maximum(
            jnp.max(score, axis=1, keepdims=True), jnp.max(new, axis=1, keepdims=True)
        )
        weight = jnp.exp(score - top)
        new = jnp.exp(new - top)
        total = jnp.sum(weight, axis=1, keepdims=True) + jnp.sum(new, axis=1, keepdims=True)
        mix = lax.dot_general(
            weight.astype(bf16), rows[:lat_width, :], (((1,), (1,)), ((), ())),
            preferred_element_type=f32,
        )
        for u in range(steps):
            mix = mix + new[:, u : u + 1].astype(bf16).astype(f32) * fresh[
                u : u + 1, :lat_width
            ].astype(f32)
        lanes = top_ref.shape[1]
        for t in range(steps):
            there = theres[t]
            here = slice(t * heads, (t + 1) * heads)
            top_ref[there, :] = jnp.broadcast_to(top[here], (heads, lanes))
            sum_ref[there, :] = jnp.broadcast_to(total[here], (heads, lanes))
            for n, part in enumerate(lane_tiles(lat_width)):
                mix_ref[n, there, :] = mix[here, part]
    for copy in copies[7:]:
        copy.wait()


def prepare(
    scale, dev_count, side_count, bucket, lengths, request_slot, requests, inverse, queries,
    absorb, cache, fresh, value, out_weight,
):
    slots, steps, heads, width = queries.shape
    kv_width = cache.shape[1]
    lat_width = absorb.shape[2]
    rows = slots * steps * heads
    group_rows = dev_count * bucket
    parts = 8
    lanes = requests.shape[1]
    half = inverse.shape[1]
    shapes = [
        ((rows, kv_width), bf16), ((rows, 128), f32), ((rows, 128), f32),
        ((lat_width // 128, rows, 128), f32), ((slots * steps, 128), f32),
        ((1, group_rows // 2 * dev_count), jnp.int32), ((group_rows, half), f32), ((group_rows, half), f32),
        ((1, side_count * group_rows), jnp.int32), (value.shape, bf16), (out_weight.shape, bf16),
    ]
    return pl.pallas_call(
        functools.partial(prepare_kernel, scale, steps, (dev_count, side_count, bucket)),
        out_shape=[jax.ShapeDtypeStruct(*shape) for shape in shapes],
        in_specs=[in_vmem] + [in_hbm] * 9,
        out_specs=[in_vmem] * len(shapes),
        scratch_shapes=[
            pltpu.SMEM(lengths.shape, lengths.dtype),
            pltpu.SMEM(request_slot.shape, request_slot.dtype),
            pltpu.VMEM(requests.shape, requests.dtype),
            pltpu.VMEM((rows, width), queries.dtype),
            pltpu.VMEM(absorb.shape, absorb.dtype),
            pltpu.VMEM(cache.shape, cache.dtype),
            pltpu.VMEM(fresh.shape, fresh.dtype),
            pltpu.VMEM((len(lane_tiles(width)), rows, 128), f32),
            pltpu.VMEM((len(lane_tiles(kv_width)), rows, 128), f32),
            pltpu.VMEM(requests.shape, jnp.int32),
            pltpu.VMEM(requests.shape, jnp.int32),
            pltpu.VMEM(requests.shape, f32),
            pltpu.VMEM(requests.shape, f32),
            pltpu.SemaphoreType.DMA((parts + 8,)),
        ],
        compiler_params=pltpu.CompilerParams(vmem_limit_bytes=prepare_mib * mib),
        cost_estimate=pl.CostEstimate(
            flops=4 * 10**9, bytes_accessed=28 * 10**6, transcendentals=10**5
        ),
        name="prepare",
    )(inverse, lengths, request_slot, requests, queries.reshape(rows, width), absorb, cache, fresh,
      value, out_weight)


def project_kernel(dev_count, side_count, target_ref, *refs):
    my_side = lax.axis_index("side")
    x_refs = refs[:dev_count]
    weight_refs = refs[dev_count : dev_count + side_count]
    out_refs = refs[dev_count + side_count : -3]
    x_rows, slab_weight, rows = refs[-3:]
    tok_rows = x_refs[0].shape[0]
    full = slab_weight.shape[1] // 128
    if side_count > 1:
        shard = slab_weight.shape[0] // side_count
        for k in range(side_count):
            first = pl.multiple_of((my_side ^ k) * shard, 16)
            tiles, rest = load_packed(weight_refs[k], shard)
            for n, tile in enumerate(tiles):
                slab_weight[pl.ds(first, shard), n * 128 : (n + 1) * 128] = tile
            slab_weight[pl.ds(first, shard), full * 128 :] = rest
    for k in range(dev_count):
        x_rows[k * tok_rows : (k + 1) * tok_rows, :] = x_refs[k][...]
    slab = slab_weight[...] if side_count > 1 else weight_refs[0][...]
    raw = jnp.dot(x_rows[...], slab, preferred_element_type=f32).astype(bf16)
    rows[...] = raw
    target = target_ref[...]
    half_rows = tok_rows
    for j in range(2 * dev_count):
        ids = lax.broadcasted_iota(jnp.int32, (half_rows, target.shape[1]), 0)
        route = jnp.where(ids + j * half_rows == target, 1.0, 0.0).astype(bf16)
        store_packed(out_refs[j], jnp.dot(route, rows[...], preferred_element_type=f32))


def project(x_pieces, weights, target, width):
    dev_count = len(x_pieces)
    tok_rows, slab = x_pieces[0].shape
    return pl.pallas_call(
        functools.partial(project_kernel, dev_count, len(weights)),
        out_shape=[
            jax.ShapeDtypeStruct(
                (packed_rows(tok_rows, width), 128), f32 if j % dev_count == 0 else bf16
            )
            for j in range(2 * dev_count)
        ],
        in_specs=[in_vmem] * (1 + dev_count + len(weights)),
        out_specs=[in_vmem] * (2 * dev_count),
        scratch_shapes=[
            pltpu.VMEM((dev_count * tok_rows, slab), bf16),
            pltpu.VMEM((slab, width), bf16),
            pltpu.VMEM((target.shape[1], width), bf16),
        ],
        compiler_params=pltpu.CompilerParams(vmem_limit_bytes=20 * mib),
        name="project",
    )(target, *x_pieces, *weights)


def finish_kernel(which, gain_ref, cos_ref, sin_ref, *refs):
    parts, out_ref = refs[:-1], refs[-1]
    rows, half = cos_ref.shape[0] // 2, cos_ref.shape[1]
    mine = slice(which * rows, (which + 1) * rows)
    total = parts[0][...].astype(f32)
    for part in parts[1:]:
        total = total + part[...].astype(f32)
    tiles, rest = load_packed(total, rows)
    latent = jnp.concatenate(tiles, axis=1)
    spread = jnp.mean(latent * latent, axis=1, keepdims=True)
    latent = latent * lax.rsqrt(spread + 1e-06) * gain_ref[...]
    first, second = rest[:, :half], rest[:, half:]
    cosine, sine = cos_ref[mine, :], sin_ref[mine, :]
    store_packed(
        out_ref,
        jnp.concatenate(
            [latent, first * cosine - second * sine, second * cosine + first * sine], axis=1
        ),
    )


def finish(parts, gain, cosine, sine, which):
    return pl.pallas_call(
        functools.partial(finish_kernel, which),
        out_shape=jax.ShapeDtypeStruct(parts[0].shape, bf16),
        in_specs=[in_vmem] * (3 + len(parts)),
        out_specs=in_vmem,
        compiler_params=pltpu.CompilerParams(vmem_limit_bytes=8 * mib),
        name="finish_rows",
    )(gain, cosine, sine, *parts)


def attend_kernel(
    scale, cap_slots, steps, part, parts, query_ref, slot_ref, top_ref,
    sum_ref, mix_ref, live_ref, value_ref, *refs
):
    pieces, out_ref, keys = refs[:-2], refs[-2], refs[-1]
    lat_width = mix_ref.shape[0] * mix_ref.shape[2]
    per_head = cap_slots * steps
    rows = query_ref.shape[0] // parts
    heads = rows // per_head
    mine = slice(part * rows, (part + 1) * rows)
    sides = len(pieces) // 2
    piece_rows = keys.shape[0] // len(pieces)
    for n, piece in enumerate(pieces):
        tiles, rest = load_packed(piece, piece_rows)
        place = (n % sides) * 2 + n // sides
        there = slice(place * piece_rows, (place + 1) * piece_rows)
        for j, tile in enumerate(tiles):
            keys[there, j * 128 : (j + 1) * 128] = tile
        keys[there, lat_width:] = rest
    contract = (((1,), (1,)), ((), ()))
    row = lax.broadcasted_iota(jnp.int32, (rows, 1), 0)
    row_slot = (row // steps) % cap_slots
    query = query_ref[mine, :]
    score = lax.dot_general(query, keys[...], contract, preferred_element_type=f32)
    score = jnp.where(
        slot_ref[...] == row_slot + 1, score * scale, masked_score
    )
    top_held = top_ref[mine, :1]
    top = jnp.maximum(top_held, jnp.max(score, axis=1, keepdims=True))
    held = jnp.exp(top_held - top)
    weight = jnp.exp(score - top)
    total = sum_ref[mine, :1] * held + jnp.sum(weight, axis=1, keepdims=True)
    mix = jnp.dot(weight.astype(bf16), keys[:, :lat_width], preferred_element_type=f32)
    mix_held = jnp.concatenate([mix_ref[n, mine, :] for n in range(mix_ref.shape[0])], axis=1)
    latent = ((mix_held * held + mix) / total).astype(bf16)
    live = live_ref[:, :1]
    width = value_ref.shape[2]
    for h in range(0, heads, 2):
        head = part * heads + h
        pair = jnp.concatenate([value_ref[head], value_ref[head + 1]], axis=1)
        both = jnp.dot(
            latent[h * per_head : (h + 2) * per_head, :], pair, preferred_element_type=f32
        )
        out_ref[:, h * width : (h + 1) * width] = (both[:per_head, :width] * live).astype(bf16)
        out_ref[:, (h + 1) * width : (h + 2) * width] = (both[per_head:, width:] * live).astype(bf16)


def attend(scale, query, row_slot, top, total, mix, live, value, pieces, cap_slots, steps, part,
           parts):
    heads, _, width = value.shape
    part_heads = heads // parts
    return pl.pallas_call(
        functools.partial(attend_kernel, scale, cap_slots, steps, part, parts),
        out_shape=jax.ShapeDtypeStruct((cap_slots * steps, part_heads * width), bf16),
        in_specs=[in_vmem] * (7 + len(pieces)),
        out_specs=in_vmem,
        scratch_shapes=[pltpu.VMEM((row_slot.shape[1], query.shape[1]), bf16)],
        compiler_params=pltpu.CompilerParams(vmem_limit_bytes=10 * mib),
        name="attend",
    )(query, row_slot, top, total, mix, live, value, *pieces)


def output_kernel(dev_count, side_count, part, parts, *refs):
    my_dev, my_side = lax.axis_index("dev"), lax.axis_index("side")
    head_refs = refs[:dev_count]
    weight_ref = refs[dev_count]
    earlier_ref = refs[dev_count + 1] if part else None
    out_refs = refs[dev_count + 1 + (part > 0) : -1]
    held = refs[-1]
    rows, depth = head_refs[0].shape
    per_side = dev_count // side_count
    for j in range(dev_count):
        group = my_dev ^ j
        place = (lax.div(group, per_side) ^ my_side) * per_side + lax.rem(group, per_side)
        held[pl.ds(pl.multiple_of(place * rows, 16), rows), :] = head_refs[j][...]
    columns = weight_ref.shape[1]
    tile = 256 if columns % 256 == 0 else columns
    side_rows = rows * per_side
    for n in range(columns // tile):
        here = slice(n * tile, (n + 1) * tile)
        product = jnp.dot(
            held[...], weight_ref[part * depth : (part + 1) * depth, here],
            preferred_element_type=f32,
        )
        if part:
            product = product + earlier_ref[:, here]
        if part + 1 < parts:
            out_refs[0][:, here] = product
        else:
            for k in range(side_count):
                out_refs[k][:, here] = product[k * side_rows : (k + 1) * side_rows, :].astype(
                    out_refs[k].dtype
                )


def output_product(head_pieces, weight, side_count, earlier, part, parts):
    dev_count = len(head_pieces)
    rows, depth = head_pieces[0].shape
    columns = weight.shape[1]
    side_rows = rows * dev_count // side_count
    if part + 1 < parts:
        shapes = [((rows * dev_count, columns), f32)]
    else:
        shapes = [((side_rows, columns), f32 if k == 0 else bf16) for k in range(side_count)]
    earlier = [] if earlier is None else [earlier]
    return pl.pallas_call(
        functools.partial(output_kernel, dev_count, side_count, part, parts),
        out_shape=[jax.ShapeDtypeStruct(*shape) for shape in shapes],
        in_specs=[in_vmem] * (dev_count + 1 + len(earlier)),
        out_specs=[in_vmem] * len(shapes),
        scratch_shapes=[pltpu.VMEM((dev_count * rows, depth), bf16)],
        compiler_params=pltpu.CompilerParams(vmem_limit_bytes=10 * mib),
        name="output_product",
    )(*head_pieces, weight, *earlier)


def on_device(
    prompts,
    latent_weight,
    latent_gain,
    row_request,
    context_len,
    request_slot,
    latent_cache,
    new_latent,
    queries,
    key_absorb,
    value_absorb,
    out_weight,
):
    dev_count = lax.axis_size("dev")
    side_count = lax.axis_size("side")
    tok_rows, model_width = prompts.shape
    shard_rows, kv_width = latent_weight.shape
    lat_width = latent_gain.shape[0]
    head_count, nope_width, _ = key_absorb.shape
    rope_width = kv_width - lat_width
    cap_slots, ctx_len, _ = latent_cache.shape
    step_count = new_latent.shape[1]
    bucket_rows = 2 * tok_rows // dev_count
    group_rows = dev_count * bucket_rows
    slab = model_width // dev_count

    x_pieces = list(split_columns(prompts, dev_count))
    packs = shard_rows % 32 == 0
    weights = [pack_weight(latent_weight) if packs else latent_weight] + [None] * (side_count - 1)
    for k in sorted(range(2, dev_count), reverse=True):
        x_pieces[k] = swap(x_pieces[k], "dev", k)
    for k in range(1, side_count):
        weights[k] = swap(weights[0], "side", k)
    x_pieces[1], weights[1] = lax.optimization_barrier((x_pieces[1], weights[1]))
    x_pieces[1] = swap(x_pieces[1], "dev", 1)

    score_scale = queries.shape[-1] ** (-0.5)
    half = rope_width // 2
    inverse = 1.0 / 10000.0 ** (jnp.arange(half, dtype=f32) * (2.0 / rope_width))
    lengths, x_pieces[0] = lax.optimization_barrier((context_len, x_pieces[0]))
    (
        query_full, top_held, sum_held, mix_held, live, target, cosine, sine, row_slot,
        value_here, out_here,
    ) = prepare(
        score_scale, dev_count, side_count, bucket_rows, lengths, request_slot,
        row_request.reshape(-1, 128), inverse.reshape(1, -1), queries, key_absorb,
        jnp.swapaxes(latent_cache, 1, 2), new_latent, value_absorb, out_weight,
    )

    if not packs:
        my_side = lax.axis_index("side")
        held = jnp.zeros((side_count, shard_rows, kv_width), bf16)
        for k in range(side_count):
            held = lax.dynamic_update_slice(held, weights[k][None], (my_side ^ k, 0, 0))
        weights = [held.reshape(slab, kv_width)]

    routed = project(x_pieces, weights, target, kv_width)
    pieces = []
    for which in range(2):
        half = list(routed[which * dev_count : (which + 1) * dev_count])
        for k in sorted(range(1, dev_count), reverse=True):
            half[k] = swap(half[k], "dev", k)
        latent_rows = finish(half, latent_gain.reshape(1, -1), cosine, sine, which)
        pieces += [latent_rows] + [swap(latent_rows, "side", k) for k in range(1, side_count)]
    product, parts = None, 2
    for part in range(parts):
        head_out = attend(
            score_scale, query_full, row_slot, top_held, sum_held, mix_held, live, value_here,
            pieces, cap_slots, step_count, part, parts,
        )
        heads = [head_out] + [None] * (dev_count - 1)
        for k in sorted(range(1, dev_count), reverse=True):
            heads[k] = swap(head_out, "dev", k)
        products = output_product(heads, out_here, side_count, product, part, parts)
        product = products[0]
    result = products[0]
    for k in sorted(range(1, side_count), reverse=True):
        result = result + swap(products[k], "side", k).astype(f32)
    return result.astype(bf16)


def solution(mesh):
    placed = (
        P(("rep", "dev", "side"), None),
        P(("dev", "side"), None),
        P(),
        P("rep"),
        P("rep"),
        P("rep"),
        P(("rep", "dev"), None, None),
        P(("rep", "dev"), None, None),
        P(("rep", "dev"), None, "side", None),
        P("side", None, None),
        P("side", None, None),
        P("side", "dev"),
    )
    return jax.shard_map(
        on_device, mesh=mesh, in_specs=placed, out_specs=P(("rep", "side"), "dev"), check_vma=False
    )
```

```python
import functools

import jax
import jax.numpy as jnp
from jax import lax
from jax.experimental import pallas as pl
from jax.experimental.pallas import tpu as pltpu
from jax.sharding import PartitionSpec as P

masked_score = -1e30
bf16, f32 = jnp.bfloat16, jnp.float32
in_vmem = pl.BlockSpec(memory_space=pltpu.VMEM)
in_smem = pl.BlockSpec(memory_space=pltpu.SMEM)
in_hbm = pl.BlockSpec(memory_space=pltpu.HBM)
mib = 1024 * 1024
prepare_mib = 16


def swap(value, axis, step):
    count = lax.axis_size(axis)
    return lax.ppermute(value, axis, [(i, i ^ step) for i in range(count)])


def pick(pieces, index):
    out = pieces[0]
    for k in range(1, len(pieces)):
        out = jnp.where(index == k, pieces[k], out)
    return out


def lane_tiles(width):
    return [slice(n, min(n + 128, width)) for n in range(0, width, 128)]


def packed_rows(rows, width):
    return rows * (width // 128) + rows // 2


def pack(value):
    rows, width = value.shape
    full = width // 128
    rest = value[:, full * 128 :]
    parts = [value[:, n * 128 : (n + 1) * 128] for n in range(full)]
    return parts + [jnp.concatenate([rest[: rows // 2], rest[rows // 2 :]], axis=1)]


def store_packed(ref, value):
    first = 0
    for part in pack(value):
        ref[first : first + part.shape[0], :] = part.astype(ref.dtype)
        first += part.shape[0]


def load_packed(ref, rows):
    full = ref.shape[0] // rows
    tiles = [ref[n * rows : (n + 1) * rows, :] for n in range(full)]
    rest = ref[full * rows :, :]
    return tiles, jnp.concatenate([rest[:, :64], rest[:, 64:]], axis=0)


def pack_kernel(value_ref, out_ref):
    store_packed(out_ref, value_ref[...])


def pack_weight(weight):
    rows, width = weight.shape
    return pl.pallas_call(
        pack_kernel,
        out_shape=jax.ShapeDtypeStruct((packed_rows(rows, width), 128), weight.dtype),
        in_specs=[in_vmem],
        out_specs=in_vmem,
        compiler_params=pltpu.CompilerParams(vmem_limit_bytes=8 * mib),
        cost_estimate=pl.CostEstimate(flops=10**10, bytes_accessed=10**6, transcendentals=0),
        name="pack_weight",
    )(weight)


def split_kernel(slab, prompts_ref, *refs):
    my_dev = lax.axis_index("dev")
    out_refs, sems = refs[:-1], refs[-1]
    copies = []
    for k in range(len(out_refs))[::-1]:
        first = pl.multiple_of((my_dev ^ k) * slab, 128)
        copies.append(
            pltpu.make_async_copy(prompts_ref.at[:, pl.ds(first, slab)], out_refs[k], sems.at[k])
        )
    for copy in copies:
        copy.start()
    for copy in copies:
        copy.wait()


def split_columns(prompts, count):
    rows, width = prompts.shape
    slab = width // count
    if slab % 128:
        columns = [prompts[:, k * slab : (k + 1) * slab] for k in range(count)]
        my_dev = lax.axis_index("dev")
        return [pick(columns, my_dev ^ k) for k in range(count)]
    return pl.pallas_call(
        functools.partial(split_kernel, slab),
        out_shape=[jax.ShapeDtypeStruct((rows, slab), prompts.dtype)] * count,
        in_specs=[in_hbm],
        out_specs=[in_vmem] * count,
        scratch_shapes=[pltpu.SemaphoreType.DMA((count,))],
        compiler_params=pltpu.CompilerParams(vmem_limit_bytes=8 * mib),
        cost_estimate=pl.CostEstimate(
            flops=10**10, bytes_accessed=4 * 10**7, transcendentals=0
        ),
        name="split_columns",
    )(prompts)


def fill_tables(
    dev_count, side_count, bucket, cap_slots, length_ref, slot_ref, request_ref, inverse_ref,
    target_ref, cos_ref, sin_ref, spot_ref, to_ref, place_ref, local_ref, position_ref,
):
    my_dev, my_side = lax.axis_index("dev"), lax.axis_index("side")
    requests = request_ref[...]
    lane_rows, lanes = requests.shape
    tok_rows = bucket * dev_count // 2
    per_row = lanes // tok_rows
    half_bucket = bucket // 2
    half_rows = dev_count * half_bucket
    group_rows = 2 * half_rows
    before = lax.broadcasted_iota(jnp.int32, (lanes, lanes), 0)
    after = lax.broadcasted_iota(jnp.int32, (lanes, lanes), 1)
    below = jnp.where(before < after, 1.0, 0.0)
    near = jnp.where((before < after) & (before // tok_rows == after // tok_rows), 1.0, 0.0)
    scan = jnp.concatenate([below, jnp.ones_like(below)], axis=1).astype(bf16)
    lower = lax.broadcasted_iota(jnp.int32, (lane_rows, lane_rows), 0)
    upper = lax.broadcasted_iota(jnp.int32, (lane_rows, lane_rows), 1)
    rows_before = jnp.where(upper < lower, 1.0, 0.0)
    position = jnp.zeros(requests.shape, f32)
    slot = jnp.zeros(requests.shape, jnp.int32)
    for q in range(slot_ref.shape[0]):
        hit = requests == q
        ranks = jnp.dot(
            jnp.where(hit, 1.0, 0.0).astype(bf16), scan, preferred_element_type=f32
        )
        earlier = jnp.dot(rows_before, ranks[:, lanes:], preferred_element_type=f32)
        start = length_ref[q].astype(f32)
        position = jnp.where(hit, ranks[:, :lanes] + earlier + start, position)
        slot = jnp.where(hit, slot_ref[q], slot)
    group = lax.div(slot, cap_slots)
    rank = jnp.zeros(requests.shape, f32)
    for g in range(dev_count):
        hit = group == g
        ranks = jnp.dot(
            jnp.where(hit, 1.0, 0.0).astype(bf16), near.astype(bf16), preferred_element_type=f32
        )
        rank = jnp.where(hit, ranks, rank)
    block = lax.broadcasted_iota(jnp.int32, requests.shape, 0) * per_row + lax.div(
        lax.broadcasted_iota(jnp.int32, requests.shape, 1), tok_rows
    )
    rank = rank.astype(jnp.int32)
    which = lax.div(rank, half_bucket)
    place = lax.div(block, side_count) * half_bucket + lax.rem(rank, half_bucket)
    to_ref[...] = (which * dev_count + (group ^ my_dev)) * half_rows + place
    place = which * half_rows + place
    place_ref[...] = jnp.where(group == my_dev, place, -1)
    local_ref[...] = (slot - my_dev * cap_slots + 1).astype(f32)
    position_ref[...] = position
    lane_block = lax.div(lax.broadcasted_iota(jnp.int32, (1, lanes), 1), tok_rows)
    ids = lax.broadcasted_iota(jnp.int32, (group_rows, 1), 0)

    def find(dev, side):
        held = dev * side_count + side
        return pl.ds(lax.div(held, per_row), 1), lane_block == lax.rem(held, per_row)

    targets = []
    for k in range(dev_count):
        held = (my_dev ^ k) * side_count + my_side
        row = jnp.broadcast_to(to_ref[pl.ds(lax.div(held, per_row), 1), :], (8, lanes))
        start = lax.rem(lanes - tok_rows * lax.rem(held, per_row), lanes)
        targets.append(pltpu.roll(row, start, 1)[:1, :tok_rows])
    for k in range(0, dev_count, per_row):
        target_ref[:, k * tok_rows : k * tok_rows + lanes] = jnp.concatenate(
            targets[k : k + per_row], axis=1
        )
    found = jnp.zeros((group_rows, lanes), f32)
    for d in range(dev_count):
        row, inside = find(d, my_side)
        found = jnp.where((place_ref[row, :] == ids) & inside, position_ref[row, :], found)
    angles = jnp.sum(found, axis=1, keepdims=True) * inverse_ref[...]
    cos_ref[...] = jnp.cos(angles)
    sin_ref[...] = jnp.sin(angles)
    for k in range(side_count):
        total = jnp.zeros((8, group_rows), f32)
        for d in range(dev_count):
            row, inside = find(d, my_side ^ k)
            chosen = jnp.where((place_ref[row, :] == ids) & inside, 1.0, 0.0).astype(bf16)
            values = jnp.broadcast_to(local_ref[row, :], (8, lanes)).astype(bf16)
            total = total + lax.dot_general(
                values, chosen, (((1,), (1,)), ((), ())), preferred_element_type=f32
            )
        spot_ref[:, k * group_rows : (k + 1) * group_rows] = total[:1].astype(jnp.int32)


def prepare_kernel(
    scale, steps, layout, inverse_ref, length_hbm, slot_hbm, request_hbm, query_hbm, absorb_hbm,
    cache_hbm, fresh_hbm, value_hbm, out_hbm, full_ref, top_ref, sum_ref, mix_ref, live_ref, target_ref,
    cos_ref, sin_ref, spot_ref, value_ref, out_ref, length_ref, slot_ref, request_ref, query_ref,
    absorb_ref, cache_ref, fresh_ref, plain, full, to_ref, place_ref, local_ref, position_ref, sems,
):
    pairs = [
        (length_hbm, length_ref), (slot_hbm, slot_ref), (request_hbm, request_ref),
        (query_hbm, query_ref), (absorb_hbm, absorb_ref), (cache_hbm, cache_ref),
        (fresh_hbm, fresh_ref), (value_hbm, value_ref),
    ]
    parts = sems.shape[0] - len(pairs)
    rows = out_hbm.shape[0] // parts
    for n in range(parts):
        part = pl.ds(n * rows, rows)
        pairs.append((out_hbm.at[part], out_ref.at[part]))
    copies = [pltpu.make_async_copy(*pair, sems.at[n]) for n, pair in enumerate(pairs)]
    for copy in copies:
        copy.start()
    for copy in copies[:3]:
        copy.wait()
    slots, _, context = cache_ref.shape
    heads, nope, lat_width = absorb_ref.shape
    per_head = slots * steps
    fill_tables(
        *layout, slots, length_ref, slot_ref, request_ref, inverse_ref, target_ref, cos_ref,
        sin_ref, spot_ref, to_ref, place_ref, local_ref, position_ref,
    )
    first_slot = lax.axis_index("dev") * slots
    lengths = []
    for s in range(slots):
        length = jnp.int32(0)
        for q in range(slot_ref.shape[0]):
            length = jnp.where(slot_ref[q] == first_slot + s, length_ref[q], length)
        lengths.append(length)
    slot_of = lax.div(lax.broadcasted_iota(jnp.int32, live_ref.shape, 0), steps)
    live = jnp.zeros(live_ref.shape, f32)
    for s in range(slots):
        live = jnp.where((slot_of == s) & (lengths[s] > 0), 1.0, live)
    live_ref[...] = live
    copies[3].wait()
    copies[4].wait()
    for n, here in enumerate(lane_tiles(query_ref.shape[1])):
        plain[n, :, : here.stop - here.start] = query_ref[:, here].astype(f32)
    wide = lane_tiles(full_ref.shape[1])
    for h in range(heads):
        there = pl.ds(h, per_head, stride=heads)
        query = plain[0, there, :].astype(bf16)
        latent = jnp.dot(query, absorb_ref[h], preferred_element_type=f32).astype(bf16).astype(f32)
        here = slice(h * per_head, (h + 1) * per_head)
        for n, lanes in enumerate(lane_tiles(lat_width)):
            full[n, here, :] = latent[:, lanes]
        full[len(wide) - 1, here, :] = plain[1, there, :]
    for n, lanes in enumerate(wide):
        full_ref[:, lanes] = full[n, :, : lanes.stop - lanes.start].astype(bf16)
    key = lax.broadcasted_iota(jnp.int32, (1, context), 1)
    copies[5].wait()
    copies[6].wait()
    late = lax.broadcasted_iota(jnp.int32, (steps * heads, steps), 1)
    late = late > lax.div(lax.broadcasted_iota(jnp.int32, (steps * heads, steps), 0), heads)
    for s in range(slots):
        theres = [pl.ds(s * steps + t, heads, stride=per_head) for t in range(steps)]
        query = jnp.concatenate(
            [
                jnp.concatenate([full[n, there, :] for there in theres], axis=0)[
                    :, : lanes.stop - lanes.start
                ].astype(bf16)
                for n, lanes in enumerate(wide)
            ],
            axis=1,
        )
        rows = cache_ref[s]
        score = jnp.dot(query, rows, preferred_element_type=f32)
        score = jnp.where(key < lengths[s], score * scale, masked_score)
        fresh = fresh_ref[s]
        new = lax.dot_general(
            query, fresh, (((1,), (1,)), ((), ())), preferred_element_type=f32
        )
        new = jnp.where(late, masked_score, new * scale)
        top = jnp.maximum(
            jnp.max(score, axis=1, keepdims=True), jnp.max(new, axis=1, keepdims=True)
        )
        weight = jnp.exp(score - top)
        new = jnp.exp(new - top)
        total = jnp.sum(weight, axis=1, keepdims=True) + jnp.sum(new, axis=1, keepdims=True)
        mix = lax.dot_general(
            weight.astype(bf16), rows[:lat_width, :], (((1,), (1,)), ((), ())),
            preferred_element_type=f32,
        )
        for u in range(steps):
            mix = mix + new[:, u : u + 1].astype(bf16).astype(f32) * fresh[
                u : u + 1, :lat_width
            ].astype(f32)
        lanes = top_ref.shape[1]
        for t in range(steps):
            there = theres[t]
            here = slice(t * heads, (t + 1) * heads)
            top_ref[there, :] = jnp.broadcast_to(top[here], (heads, lanes))
            sum_ref[there, :] = jnp.broadcast_to(total[here], (heads, lanes))
            for n, part in enumerate(lane_tiles(lat_width)):
                mix_ref[n, there, :] = mix[here, part]
    for copy in copies[7:]:
        copy.wait()


def prepare(
    scale, dev_count, side_count, bucket, lengths, request_slot, requests, inverse, queries,
    absorb, cache, fresh, value, out_weight,
):
    slots, steps, heads, width = queries.shape
    kv_width = cache.shape[1]
    lat_width = absorb.shape[2]
    rows = slots * steps * heads
    group_rows = dev_count * bucket
    parts = 8
    lanes = requests.shape[1]
    half = inverse.shape[1]
    shapes = [
        ((rows, kv_width), bf16), ((rows, 128), f32), ((rows, 128), f32),
        ((lat_width // 128, rows, 128), f32), ((slots * steps, 128), f32),
        ((1, group_rows // 2 * dev_count), jnp.int32), ((group_rows, half), f32), ((group_rows, half), f32),
        ((1, side_count * group_rows), jnp.int32), (value.shape, bf16), (out_weight.shape, bf16),
    ]
    return pl.pallas_call(
        functools.partial(prepare_kernel, scale, steps, (dev_count, side_count, bucket)),
        out_shape=[jax.ShapeDtypeStruct(*shape) for shape in shapes],
        in_specs=[in_vmem] + [in_hbm] * 9,
        out_specs=[in_vmem] * len(shapes),
        scratch_shapes=[
            pltpu.SMEM(lengths.shape, lengths.dtype),
            pltpu.SMEM(request_slot.shape, request_slot.dtype),
            pltpu.VMEM(requests.shape, requests.dtype),
            pltpu.VMEM((rows, width), queries.dtype),
            pltpu.VMEM(absorb.shape, absorb.dtype),
            pltpu.VMEM(cache.shape, cache.dtype),
            pltpu.VMEM(fresh.shape, fresh.dtype),
            pltpu.VMEM((len(lane_tiles(width)), rows, 128), f32),
            pltpu.VMEM((len(lane_tiles(kv_width)), rows, 128), f32),
            pltpu.VMEM(requests.shape, jnp.int32),
            pltpu.VMEM(requests.shape, jnp.int32),
            pltpu.VMEM(requests.shape, f32),
            pltpu.VMEM(requests.shape, f32),
            pltpu.SemaphoreType.DMA((parts + 8,)),
        ],
        compiler_params=pltpu.CompilerParams(vmem_limit_bytes=prepare_mib * mib),
        cost_estimate=pl.CostEstimate(
            flops=4 * 10**9, bytes_accessed=28 * 10**6, transcendentals=10**5
        ),
        name="prepare",
    )(inverse, lengths, request_slot, requests, queries.reshape(rows, width), absorb, cache, fresh,
      value, out_weight)


def project_kernel(dev_count, side_count, target_ref, *refs):
    my_side = lax.axis_index("side")
    x_refs = refs[:dev_count]
    weight_refs = refs[dev_count : dev_count + side_count]
    out_refs = refs[dev_count + side_count : -3]
    x_rows, slab_weight, rows = refs[-3:]
    tok_rows = x_refs[0].shape[0]
    full = slab_weight.shape[1] // 128
    if side_count > 1:
        shard = slab_weight.shape[0] // side_count
        for k in range(side_count):
            first = pl.multiple_of((my_side ^ k) * shard, 16)
            tiles, rest = load_packed(weight_refs[k], shard)
            for n, tile in enumerate(tiles):
                slab_weight[pl.ds(first, shard), n * 128 : (n + 1) * 128] = tile
            slab_weight[pl.ds(first, shard), full * 128 :] = rest
    for k in range(dev_count):
        x_rows[k * tok_rows : (k + 1) * tok_rows, :] = x_refs[k][...]
    slab = slab_weight[...] if side_count > 1 else weight_refs[0][...]
    raw = jnp.dot(x_rows[...], slab, preferred_element_type=f32).astype(bf16)
    rows[...] = raw
    target = target_ref[...]
    half_rows = tok_rows
    step = min(4, 2 * dev_count)
    for j in range(0, 2 * dev_count, step):
        ids = lax.broadcasted_iota(jnp.int32, (step * half_rows, target.shape[1]), 0)
        route = jnp.where(ids + j * half_rows == target, 1.0, 0.0).astype(bf16)
        placed = jnp.dot(route, rows[...], preferred_element_type=f32)
        for n in range(step):
            store_packed(out_refs[j + n], placed[n * half_rows : (n + 1) * half_rows])


def project(x_pieces, weights, target, width):
    dev_count = len(x_pieces)
    tok_rows, slab = x_pieces[0].shape
    return pl.pallas_call(
        functools.partial(project_kernel, dev_count, len(weights)),
        out_shape=[
            jax.ShapeDtypeStruct(
                (packed_rows(tok_rows, width), 128), f32 if j % dev_count == 0 else bf16
            )
            for j in range(2 * dev_count)
        ],
        in_specs=[in_vmem] * (1 + dev_count + len(weights)),
        out_specs=[in_vmem] * (2 * dev_count),
        scratch_shapes=[
            pltpu.VMEM((dev_count * tok_rows, slab), bf16),
            pltpu.VMEM((slab, width), bf16),
            pltpu.VMEM((target.shape[1], width), bf16),
        ],
        compiler_params=pltpu.CompilerParams(vmem_limit_bytes=20 * mib),
        name="project",
    )(target, *x_pieces, *weights)


def finish_kernel(which, gain_ref, cos_ref, sin_ref, *refs):
    parts, out_ref = refs[:-1], refs[-1]
    rows, half = cos_ref.shape[0] // 2, cos_ref.shape[1]
    mine = slice(which * rows, (which + 1) * rows)
    total = parts[0][...].astype(f32)
    for part in parts[1:]:
        total = total + part[...].astype(f32)
    tiles, rest = load_packed(total, rows)
    latent = jnp.concatenate(tiles, axis=1)
    spread = jnp.mean(latent * latent, axis=1, keepdims=True)
    latent = latent * lax.rsqrt(spread + 1e-06) * gain_ref[...]
    first, second = rest[:, :half], rest[:, half:]
    cosine, sine = cos_ref[mine, :], sin_ref[mine, :]
    store_packed(
        out_ref,
        jnp.concatenate(
            [latent, first * cosine - second * sine, second * cosine + first * sine], axis=1
        ),
    )


def finish(parts, gain, cosine, sine, which):
    return pl.pallas_call(
        functools.partial(finish_kernel, which),
        out_shape=jax.ShapeDtypeStruct(parts[0].shape, bf16),
        in_specs=[in_vmem] * (3 + len(parts)),
        out_specs=in_vmem,
        compiler_params=pltpu.CompilerParams(vmem_limit_bytes=8 * mib),
        name="finish_rows",
    )(gain, cosine, sine, *parts)


def attend_kernel(
    scale, cap_slots, steps, first_head, heads, query_ref, slot_ref, top_ref,
    sum_ref, mix_ref, live_ref, value_ref, *refs
):
    pieces, out_ref, keys = refs[:-2], refs[-2], refs[-1]
    lat_width = mix_ref.shape[0] * mix_ref.shape[2]
    per_head = cap_slots * steps
    rows = heads * per_head
    mine = slice(first_head * per_head, first_head * per_head + rows)
    sides = len(pieces) // 2
    piece_rows = keys.shape[0] // len(pieces)
    for n, piece in enumerate(pieces):
        tiles, rest = load_packed(piece, piece_rows)
        place = (n % sides) * 2 + n // sides
        there = slice(place * piece_rows, (place + 1) * piece_rows)
        for j, tile in enumerate(tiles):
            keys[there, j * 128 : (j + 1) * 128] = tile
        keys[there, lat_width:] = rest
    contract = (((1,), (1,)), ((), ()))
    row = lax.broadcasted_iota(jnp.int32, (rows, 1), 0)
    row_slot = (row // steps) % cap_slots
    query = query_ref[mine, :]
    score = lax.dot_general(query, keys[...], contract, preferred_element_type=f32)
    score = jnp.where(
        slot_ref[...] == row_slot + 1, score * scale, masked_score
    )
    top_held = top_ref[mine, :1]
    top = jnp.maximum(top_held, jnp.max(score, axis=1, keepdims=True))
    held = jnp.exp(top_held - top)
    weight = jnp.exp(score - top)
    total = sum_ref[mine, :1] * held + jnp.sum(weight, axis=1, keepdims=True)
    mix = jnp.dot(weight.astype(bf16), keys[:, :lat_width], preferred_element_type=f32)
    mix_held = jnp.concatenate([mix_ref[n, mine, :] for n in range(mix_ref.shape[0])], axis=1)
    latent = ((mix_held * held + mix) / total).astype(bf16)
    live = live_ref[:, :1]
    width = value_ref.shape[2]
    for h in range(0, heads, 2):
        head = first_head + h
        pair = jnp.concatenate([value_ref[head], value_ref[head + 1]], axis=1)
        both = jnp.dot(
            latent[h * per_head : (h + 2) * per_head, :], pair, preferred_element_type=f32
        )
        out_ref[:, h * width : (h + 1) * width] = (both[:per_head, :width] * live).astype(bf16)
        out_ref[:, (h + 1) * width : (h + 2) * width] = (both[per_head:, width:] * live).astype(bf16)


def attend(scale, query, row_slot, top, total, mix, live, value, pieces, cap_slots, steps,
           first_head, heads):
    width = value.shape[2]
    return pl.pallas_call(
        functools.partial(attend_kernel, scale, cap_slots, steps, first_head, heads),
        out_shape=jax.ShapeDtypeStruct((cap_slots * steps, heads * width), bf16),
        in_specs=[in_vmem] * (7 + len(pieces)),
        out_specs=in_vmem,
        scratch_shapes=[pltpu.VMEM((row_slot.shape[1], query.shape[1]), bf16)],
        compiler_params=pltpu.CompilerParams(vmem_limit_bytes=10 * mib),
        name="attend",
    )(query, row_slot, top, total, mix, live, value, *pieces)


def output_kernel(dev_count, side_count, start, last, *refs):
    my_dev, my_side = lax.axis_index("dev"), lax.axis_index("side")
    head_refs = refs[:dev_count]
    weight_ref = refs[dev_count]
    earlier_ref = refs[dev_count + 1] if start else None
    out_refs = refs[dev_count + 1 + (start > 0) : -1]
    held = refs[-1]
    rows, depth = head_refs[0].shape
    per_side = dev_count // side_count
    for j in range(dev_count):
        group = my_dev ^ j
        place = (lax.div(group, per_side) ^ my_side) * per_side + lax.rem(group, per_side)
        held[pl.ds(pl.multiple_of(place * rows, 16), rows), :] = head_refs[j][...]
    columns = weight_ref.shape[1]
    tile = 256 if columns % 256 == 0 else columns
    side_rows = rows * per_side
    for n in range(columns // tile):
        here = slice(n * tile, (n + 1) * tile)
        product = jnp.dot(
            held[...], weight_ref[start : start + depth, here],
            preferred_element_type=f32,
        )
        if start:
            product = product + earlier_ref[:, here]
        if not last:
            out_refs[0][:, here] = product
        else:
            for k in range(side_count):
                out_refs[k][:, here] = product[k * side_rows : (k + 1) * side_rows, :].astype(
                    out_refs[k].dtype
                )


def output_product(head_pieces, weight, side_count, earlier, start, last):
    dev_count = len(head_pieces)
    rows, depth = head_pieces[0].shape
    columns = weight.shape[1]
    side_rows = rows * dev_count // side_count
    if not last:
        shapes = [((rows * dev_count, columns), f32)]
    else:
        shapes = [((side_rows, columns), f32 if k == 0 else bf16) for k in range(side_count)]
    earlier = [] if earlier is None else [earlier]
    return pl.pallas_call(
        functools.partial(output_kernel, dev_count, side_count, start, last),
        out_shape=[jax.ShapeDtypeStruct(*shape) for shape in shapes],
        in_specs=[in_vmem] * (dev_count + 1 + len(earlier)),
        out_specs=[in_vmem] * len(shapes),
        scratch_shapes=[pltpu.VMEM((dev_count * rows, depth), bf16)],
        compiler_params=pltpu.CompilerParams(vmem_limit_bytes=10 * mib),
        name="output_product",
    )(*head_pieces, weight, *earlier)


def on_device(
    prompts,
    latent_weight,
    latent_gain,
    row_request,
    context_len,
    request_slot,
    latent_cache,
    new_latent,
    queries,
    key_absorb,
    value_absorb,
    out_weight,
):
    dev_count = lax.axis_size("dev")
    side_count = lax.axis_size("side")
    tok_rows, model_width = prompts.shape
    shard_rows, kv_width = latent_weight.shape
    lat_width = latent_gain.shape[0]
    nope_width = value_absorb.shape[2]
    rope_width = kv_width - lat_width
    cap_slots, ctx_len, _ = latent_cache.shape
    step_count = new_latent.shape[1]
    bucket_rows = 2 * tok_rows // dev_count
    group_rows = dev_count * bucket_rows
    slab = model_width // dev_count

    x_pieces = list(split_columns(prompts, dev_count))
    packs = shard_rows % 32 == 0
    weights = [pack_weight(latent_weight) if packs else latent_weight] + [None] * (side_count - 1)
    for k in sorted(range(2, dev_count), reverse=True):
        x_pieces[k] = swap(x_pieces[k], "dev", k)
    for k in range(1, side_count):
        weights[k] = swap(weights[0], "side", k)
    x_pieces[1], weights[1] = lax.optimization_barrier((x_pieces[1], weights[1]))
    x_pieces[1] = swap(x_pieces[1], "dev", 1)

    score_scale = queries.shape[-1] ** (-0.5)
    half = rope_width // 2
    inverse = 1.0 / 10000.0 ** (jnp.arange(half, dtype=f32) * (2.0 / rope_width))
    lengths, x_pieces[0] = lax.optimization_barrier((context_len, x_pieces[0]))
    (
        query_full, top_held, sum_held, mix_held, live, target, cosine, sine, row_slot,
        value_here, out_here,
    ) = prepare(
        score_scale, dev_count, side_count, bucket_rows, lengths, request_slot,
        row_request.reshape(-1, 128), inverse.reshape(1, -1), queries, key_absorb,
        jnp.swapaxes(latent_cache, 1, 2), new_latent, value_absorb, out_weight,
    )

    if not packs:
        my_side = lax.axis_index("side")
        held = jnp.zeros((side_count, shard_rows, kv_width), bf16)
        for k in range(side_count):
            held = lax.dynamic_update_slice(held, weights[k][None], (my_side ^ k, 0, 0))
        weights = [held.reshape(slab, kv_width)]

    routed = project(x_pieces, weights, target, kv_width)
    pieces = []
    for which in range(2):
        half = list(routed[which * dev_count : (which + 1) * dev_count])
        for k in sorted(range(1, dev_count), reverse=True):
            half[k] = swap(half[k], "dev", k)
        latent_rows = finish(half[:1] + half[:0:-1], latent_gain.reshape(1, -1), cosine, sine, which)
        pieces += [latent_rows] + [swap(latent_rows, "side", k) for k in range(1, side_count)]
    product, first_head, head_count = None, 0, value_absorb.shape[0]
    for part_heads in (head_count * 3 // 4, head_count // 4):
        head_out = attend(
            score_scale, query_full, row_slot, top_held, sum_held, mix_held, live, value_here,
            pieces, cap_slots, step_count, first_head, part_heads,
        )
        heads = [head_out] + [None] * (dev_count - 1)
        for k in sorted(range(1, dev_count), reverse=True):
            heads[k] = swap(head_out, "dev", k)
        start, first_head = first_head * nope_width, first_head + part_heads
        products = output_product(
            heads, out_here, side_count, product, start, first_head == head_count
        )
        product = products[0]
    result = products[0]
    for k in sorted(range(1, side_count), reverse=True):
        result = result + swap(products[k], "side", k).astype(f32)
    return result.astype(bf16)


def solution(mesh):
    placed = (
        P(("rep", "dev", "side"), None),
        P(("dev", "side"), None),
        P(),
        P("rep"),
        P("rep"),
        P("rep"),
        P(("rep", "dev"), None, None),
        P(("rep", "dev"), None, None),
        P(("rep", "dev"), None, "side", None),
        P("side", None, None),
        P("side", None, None),
        P("side", "dev"),
    )
    return jax.shard_map(
        on_device, mesh=mesh, in_specs=placed, out_specs=P(("rep", "side"), "dev"), check_vma=False
    )
```

```python
import functools

import jax
import jax.numpy as jnp
from jax import lax
from jax.experimental import pallas as pl
from jax.experimental.pallas import tpu as pltpu
from jax.sharding import PartitionSpec as P

masked_score = -1e30
bf16, f32 = jnp.bfloat16, jnp.float32
in_vmem = pl.BlockSpec(memory_space=pltpu.VMEM)
in_smem = pl.BlockSpec(memory_space=pltpu.SMEM)
in_hbm = pl.BlockSpec(memory_space=pltpu.HBM)
mib = 1024 * 1024
prepare_mib = 16


def swap(value, axis, step):
    count = lax.axis_size(axis)
    return lax.ppermute(value, axis, [(i, i ^ step) for i in range(count)])


def pick(pieces, index):
    out = pieces[0]
    for k in range(1, len(pieces)):
        out = jnp.where(index == k, pieces[k], out)
    return out


def lane_tiles(width):
    return [slice(n, min(n + 128, width)) for n in range(0, width, 128)]


def packed_rows(rows, width):
    return rows * (width // 128) + rows // 2


def pack(value):
    rows, width = value.shape
    full = width // 128
    rest = value[:, full * 128 :]
    parts = [value[:, n * 128 : (n + 1) * 128] for n in range(full)]
    return parts + [jnp.concatenate([rest[: rows // 2], rest[rows // 2 :]], axis=1)]


def store_packed(ref, value):
    first = 0
    for part in pack(value):
        ref[first : first + part.shape[0], :] = part.astype(ref.dtype)
        first += part.shape[0]


def load_packed(ref, rows):
    full = ref.shape[0] // rows
    tiles = [ref[n * rows : (n + 1) * rows, :] for n in range(full)]
    rest = ref[full * rows :, :]
    return tiles, jnp.concatenate([rest[:, :64], rest[:, 64:]], axis=0)


def pack_kernel(value_ref, out_ref):
    store_packed(out_ref, value_ref[...])


def pack_weight(weight):
    rows, width = weight.shape
    return pl.pallas_call(
        pack_kernel,
        out_shape=jax.ShapeDtypeStruct((packed_rows(rows, width), 128), weight.dtype),
        in_specs=[in_vmem],
        out_specs=in_vmem,
        compiler_params=pltpu.CompilerParams(vmem_limit_bytes=8 * mib),
        cost_estimate=pl.CostEstimate(flops=10**10, bytes_accessed=10**6, transcendentals=0),
        name="pack_weight",
    )(weight)


def split_kernel(slab, prompts_ref, *refs):
    my_dev = lax.axis_index("dev")
    out_refs, sems = refs[:-1], refs[-1]
    copies = []
    for k in range(len(out_refs))[::-1]:
        first = pl.multiple_of((my_dev ^ k) * slab, 128)
        copies.append(
            pltpu.make_async_copy(prompts_ref.at[:, pl.ds(first, slab)], out_refs[k], sems.at[k])
        )
    for copy in copies:
        copy.start()
    for copy in copies:
        copy.wait()


def split_columns(prompts, count):
    rows, width = prompts.shape
    slab = width // count
    if slab % 128:
        columns = [prompts[:, k * slab : (k + 1) * slab] for k in range(count)]
        my_dev = lax.axis_index("dev")
        return [pick(columns, my_dev ^ k) for k in range(count)]
    return pl.pallas_call(
        functools.partial(split_kernel, slab),
        out_shape=[jax.ShapeDtypeStruct((rows, slab), prompts.dtype)] * count,
        in_specs=[in_hbm],
        out_specs=[in_vmem] * count,
        scratch_shapes=[pltpu.SemaphoreType.DMA((count,))],
        compiler_params=pltpu.CompilerParams(vmem_limit_bytes=8 * mib),
        cost_estimate=pl.CostEstimate(
            flops=10**10, bytes_accessed=4 * 10**7, transcendentals=0
        ),
        name="split_columns",
    )(prompts)


def fill_tables(
    dev_count, side_count, bucket, cap_slots, length_ref, slot_ref, request_ref, inverse_ref,
    target_ref, cos_ref, sin_ref, spot_ref, to_ref, place_ref, local_ref, position_ref,
):
    my_dev, my_side = lax.axis_index("dev"), lax.axis_index("side")
    requests = request_ref[...]
    lane_rows, lanes = requests.shape
    tok_rows = bucket * dev_count // 2
    per_row = lanes // tok_rows
    half_bucket = bucket // 2
    half_rows = dev_count * half_bucket
    group_rows = 2 * half_rows
    before = lax.broadcasted_iota(jnp.int32, (lanes, lanes), 0)
    after = lax.broadcasted_iota(jnp.int32, (lanes, lanes), 1)
    below = jnp.where(before < after, 1.0, 0.0)
    near = jnp.where((before < after) & (before // tok_rows == after // tok_rows), 1.0, 0.0)
    scan = jnp.concatenate([below, jnp.ones_like(below)], axis=1).astype(bf16)
    lower = lax.broadcasted_iota(jnp.int32, (lane_rows, lane_rows), 0)
    upper = lax.broadcasted_iota(jnp.int32, (lane_rows, lane_rows), 1)
    rows_before = jnp.where(upper < lower, 1.0, 0.0)
    position = jnp.zeros(requests.shape, f32)
    slot = jnp.zeros(requests.shape, jnp.int32)
    for q in range(slot_ref.shape[0]):
        hit = requests == q
        ranks = jnp.dot(
            jnp.where(hit, 1.0, 0.0).astype(bf16), scan, preferred_element_type=f32
        )
        earlier = jnp.dot(rows_before, ranks[:, lanes:], preferred_element_type=f32)
        start = length_ref[q].astype(f32)
        position = jnp.where(hit, ranks[:, :lanes] + earlier + start, position)
        slot = jnp.where(hit, slot_ref[q], slot)
    group = lax.div(slot, cap_slots)
    rank = jnp.zeros(requests.shape, f32)
    for g in range(dev_count):
        hit = group == g
        ranks = jnp.dot(
            jnp.where(hit, 1.0, 0.0).astype(bf16), near.astype(bf16), preferred_element_type=f32
        )
        rank = jnp.where(hit, ranks, rank)
    block = lax.broadcasted_iota(jnp.int32, requests.shape, 0) * per_row + lax.div(
        lax.broadcasted_iota(jnp.int32, requests.shape, 1), tok_rows
    )
    rank = rank.astype(jnp.int32)
    which = lax.div(rank, half_bucket)
    place = lax.div(block, side_count) * half_bucket + lax.rem(rank, half_bucket)
    to_ref[...] = (which * dev_count + (group ^ my_dev)) * half_rows + place
    place = which * half_rows + place
    place_ref[...] = jnp.where(group == my_dev, place, -1)
    local_ref[...] = (slot - my_dev * cap_slots + 1).astype(f32)
    position_ref[...] = position
    lane_block = lax.div(lax.broadcasted_iota(jnp.int32, (1, lanes), 1), tok_rows)
    ids = lax.broadcasted_iota(jnp.int32, (group_rows, 1), 0)

    def find(dev, side):
        held = dev * side_count + side
        return pl.ds(lax.div(held, per_row), 1), lane_block == lax.rem(held, per_row)

    targets = []
    for k in range(dev_count):
        held = (my_dev ^ k) * side_count + my_side
        row = jnp.broadcast_to(to_ref[pl.ds(lax.div(held, per_row), 1), :], (8, lanes))
        start = lax.rem(lanes - tok_rows * lax.rem(held, per_row), lanes)
        targets.append(pltpu.roll(row, start, 1)[:1, :tok_rows])
    for k in range(0, dev_count, per_row):
        target_ref[:, k * tok_rows : k * tok_rows + lanes] = jnp.concatenate(
            targets[k : k + per_row], axis=1
        )
    found = jnp.zeros((group_rows, lanes), f32)
    for d in range(dev_count):
        row, inside = find(d, my_side)
        found = jnp.where((place_ref[row, :] == ids) & inside, position_ref[row, :], found)
    angles = jnp.sum(found, axis=1, keepdims=True) * inverse_ref[...]
    cos_ref[...] = jnp.cos(angles)
    sin_ref[...] = jnp.sin(angles)
    for k in range(side_count):
        total = jnp.zeros((8, group_rows), f32)
        for d in range(dev_count):
            row, inside = find(d, my_side ^ k)
            chosen = jnp.where((place_ref[row, :] == ids) & inside, 1.0, 0.0).astype(bf16)
            values = jnp.broadcast_to(local_ref[row, :], (8, lanes)).astype(bf16)
            total = total + lax.dot_general(
                values, chosen, (((1,), (1,)), ((), ())), preferred_element_type=f32
            )
        spot_ref[:, k * group_rows : (k + 1) * group_rows] = total[:1].astype(jnp.int32)


def prepare_kernel(
    scale, steps, layout, inverse_ref, length_hbm, slot_hbm, request_hbm, query_hbm, absorb_hbm,
    cache_hbm, fresh_hbm, value_hbm, out_hbm, full_ref, top_ref, sum_ref, mix_ref, live_ref, target_ref,
    cos_ref, sin_ref, spot_ref, value_ref, out_ref, length_ref, slot_ref, request_ref, query_ref,
    absorb_ref, cache_ref, fresh_ref, plain, full, to_ref, place_ref, local_ref, position_ref, sems,
):
    pairs = [
        (length_hbm, length_ref), (slot_hbm, slot_ref), (request_hbm, request_ref),
        (query_hbm, query_ref), (absorb_hbm, absorb_ref), (cache_hbm, cache_ref),
        (fresh_hbm, fresh_ref), (value_hbm, value_ref),
    ]
    parts = sems.shape[0] - len(pairs)
    rows = out_hbm.shape[0] // parts
    for n in range(parts):
        part = pl.ds(n * rows, rows)
        pairs.append((out_hbm.at[part], out_ref.at[part]))
    copies = [pltpu.make_async_copy(*pair, sems.at[n]) for n, pair in enumerate(pairs)]
    for copy in copies:
        copy.start()
    for copy in copies[:3]:
        copy.wait()
    slots, _, context = cache_ref.shape
    heads, nope, lat_width = absorb_ref.shape
    per_head = slots * steps
    fill_tables(
        *layout, slots, length_ref, slot_ref, request_ref, inverse_ref, target_ref, cos_ref,
        sin_ref, spot_ref, to_ref, place_ref, local_ref, position_ref,
    )
    first_slot = lax.axis_index("dev") * slots
    lengths = []
    for s in range(slots):
        length = jnp.int32(0)
        for q in range(slot_ref.shape[0]):
            length = jnp.where(slot_ref[q] == first_slot + s, length_ref[q], length)
        lengths.append(length)
    slot_of = lax.div(lax.broadcasted_iota(jnp.int32, live_ref.shape, 0), steps)
    live = jnp.zeros(live_ref.shape, f32)
    for s in range(slots):
        live = jnp.where((slot_of == s) & (lengths[s] > 0), 1.0, live)
    live_ref[...] = live
    copies[3].wait()
    copies[4].wait()
    for n, here in enumerate(lane_tiles(query_ref.shape[1])):
        plain[n, :, : here.stop - here.start] = query_ref[:, here].astype(f32)
    wide = lane_tiles(full_ref.shape[1])
    for h in range(heads):
        there = pl.ds(h, per_head, stride=heads)
        query = plain[0, there, :].astype(bf16)
        latent = jnp.dot(query, absorb_ref[h], preferred_element_type=f32).astype(bf16).astype(f32)
        here = slice(h * per_head, (h + 1) * per_head)
        for n, lanes in enumerate(lane_tiles(lat_width)):
            full[n, here, :] = latent[:, lanes]
        full[len(wide) - 1, here, :] = plain[1, there, :]
    for n, lanes in enumerate(wide):
        full_ref[:, lanes] = full[n, :, : lanes.stop - lanes.start].astype(bf16)
    key = lax.broadcasted_iota(jnp.int32, (1, context), 1)
    copies[5].wait()
    copies[6].wait()
    late = lax.broadcasted_iota(jnp.int32, (steps * heads, steps), 1)
    late = late > lax.div(lax.broadcasted_iota(jnp.int32, (steps * heads, steps), 0), heads)
    for s in range(slots):
        theres = [pl.ds(s * steps + t, heads, stride=per_head) for t in range(steps)]
        query = jnp.concatenate(
            [
                jnp.concatenate([full[n, there, :] for there in theres], axis=0)[
                    :, : lanes.stop - lanes.start
                ].astype(bf16)
                for n, lanes in enumerate(wide)
            ],
            axis=1,
        )
        rows = cache_ref[s]
        score = jnp.dot(query, rows, preferred_element_type=f32)
        score = jnp.where(key < lengths[s], score * scale, masked_score)
        fresh = fresh_ref[s]
        new = lax.dot_general(
            query, fresh, (((1,), (1,)), ((), ())), preferred_element_type=f32
        )
        new = jnp.where(late, masked_score, new * scale)
        top = jnp.maximum(
            jnp.max(score, axis=1, keepdims=True), jnp.max(new, axis=1, keepdims=True)
        )
        weight = jnp.exp(score - top)
        new = jnp.exp(new - top)
        total = jnp.sum(weight, axis=1, keepdims=True) + jnp.sum(new, axis=1, keepdims=True)
        mix = lax.dot_general(
            weight.astype(bf16), rows[:lat_width, :], (((1,), (1,)), ((), ())),
            preferred_element_type=f32,
        )
        for u in range(steps):
            mix = mix + new[:, u : u + 1].astype(bf16).astype(f32) * fresh[
                u : u + 1, :lat_width
            ].astype(f32)
        lanes = top_ref.shape[1]
        for t in range(steps):
            there = theres[t]
            here = slice(t * heads, (t + 1) * heads)
            top_ref[there, :] = jnp.broadcast_to(top[here], (heads, lanes))
            sum_ref[there, :] = jnp.broadcast_to(total[here], (heads, lanes))
            for n, part in enumerate(lane_tiles(lat_width)):
                mix_ref[n, there, :] = mix[here, part]
    for copy in copies[7:]:
        copy.wait()


def prepare(
    scale, dev_count, side_count, bucket, lengths, request_slot, requests, inverse, queries,
    absorb, cache, fresh, value, out_weight,
):
    slots, steps, heads, width = queries.shape
    kv_width = cache.shape[1]
    lat_width = absorb.shape[2]
    rows = slots * steps * heads
    group_rows = dev_count * bucket
    parts = 8
    lanes = requests.shape[1]
    half = inverse.shape[1]
    shapes = [
        ((rows, kv_width), bf16), ((rows, 128), f32), ((rows, 128), f32),
        ((lat_width // 128, rows, 128), f32), ((slots * steps, 128), f32),
        ((1, group_rows // 2 * dev_count), jnp.int32), ((group_rows, half), f32), ((group_rows, half), f32),
        ((1, side_count * group_rows), jnp.int32), (value.shape, bf16), (out_weight.shape, bf16),
    ]
    return pl.pallas_call(
        functools.partial(prepare_kernel, scale, steps, (dev_count, side_count, bucket)),
        out_shape=[jax.ShapeDtypeStruct(*shape) for shape in shapes],
        in_specs=[in_vmem] + [in_hbm] * 9,
        out_specs=[in_vmem] * len(shapes),
        scratch_shapes=[
            pltpu.SMEM(lengths.shape, lengths.dtype),
            pltpu.SMEM(request_slot.shape, request_slot.dtype),
            pltpu.VMEM(requests.shape, requests.dtype),
            pltpu.VMEM((rows, width), queries.dtype),
            pltpu.VMEM(absorb.shape, absorb.dtype),
            pltpu.VMEM(cache.shape, cache.dtype),
            pltpu.VMEM(fresh.shape, fresh.dtype),
            pltpu.VMEM((len(lane_tiles(width)), rows, 128), f32),
            pltpu.VMEM((len(lane_tiles(kv_width)), rows, 128), f32),
            pltpu.VMEM(requests.shape, jnp.int32),
            pltpu.VMEM(requests.shape, jnp.int32),
            pltpu.VMEM(requests.shape, f32),
            pltpu.VMEM(requests.shape, f32),
            pltpu.SemaphoreType.DMA((parts + 8,)),
        ],
        compiler_params=pltpu.CompilerParams(vmem_limit_bytes=prepare_mib * mib),
        cost_estimate=pl.CostEstimate(
            flops=4 * 10**9, bytes_accessed=28 * 10**6, transcendentals=10**5
        ),
        name="prepare",
    )(inverse, lengths, request_slot, requests, queries.reshape(rows, width), absorb, cache, fresh,
      value, out_weight)


def stack_kernel(*refs):
    out_ref = refs[-1]
    rows = refs[0].shape[0]
    for n, ref in enumerate(refs[:-1]):
        k = (len(refs) - 1 - n) % (len(refs) - 1)
        out_ref[k * rows : (k + 1) * rows, :] = ref[...]


def stack_rows(pieces):
    rows, width = pieces[0].shape
    return pl.pallas_call(
        stack_kernel,
        out_shape=jax.ShapeDtypeStruct((len(pieces) * rows, width), bf16),
        in_specs=[in_vmem] * len(pieces),
        out_specs=in_vmem,
        compiler_params=pltpu.CompilerParams(vmem_limit_bytes=8 * mib),
        cost_estimate=pl.CostEstimate(flops=2 * 10**10, bytes_accessed=10**6, transcendentals=0),
        name="stack_rows",
    )(pieces[0], *pieces[:0:-1])


def project_kernel(dev_count, side_count, target_ref, x_ref, *refs):
    my_side = lax.axis_index("side")
    weight_refs = refs[:side_count]
    out_refs = refs[side_count:-2]
    slab_weight, rows = refs[-2:]
    tok_rows = x_ref.shape[0] // dev_count
    full = slab_weight.shape[1] // 128
    if side_count > 1:
        shard = slab_weight.shape[0] // side_count
        for k in range(side_count):
            first = pl.multiple_of((my_side ^ k) * shard, 16)
            tiles, rest = load_packed(weight_refs[k], shard)
            for n, tile in enumerate(tiles):
                slab_weight[pl.ds(first, shard), n * 128 : (n + 1) * 128] = tile
            slab_weight[pl.ds(first, shard), full * 128 :] = rest
    slab = slab_weight[...] if side_count > 1 else weight_refs[0][...]
    raw = jnp.dot(x_ref[...], slab, preferred_element_type=f32).astype(bf16)
    rows[...] = raw
    target = target_ref[...]
    half_rows = tok_rows
    step = min(4, 2 * dev_count)
    for j in range(0, 2 * dev_count, step):
        ids = lax.broadcasted_iota(jnp.int32, (step * half_rows, target.shape[1]), 0)
        route = jnp.where(ids + j * half_rows == target, 1.0, 0.0).astype(bf16)
        placed = jnp.dot(route, rows[...], preferred_element_type=f32)
        for n in range(step):
            store_packed(out_refs[j + n], placed[n * half_rows : (n + 1) * half_rows])


def project(x_rows, weights, target, width, dev_count):
    tok_rows, slab = x_rows.shape[0] // dev_count, x_rows.shape[1]
    return pl.pallas_call(
        functools.partial(project_kernel, dev_count, len(weights)),
        out_shape=[
            jax.ShapeDtypeStruct(
                (packed_rows(tok_rows, width), 128), f32 if j % dev_count == 0 else bf16
            )
            for j in range(2 * dev_count)
        ],
        in_specs=[in_vmem] * (2 + len(weights)),
        out_specs=[in_vmem] * (2 * dev_count),
        scratch_shapes=[
            pltpu.VMEM((slab, width), bf16),
            pltpu.VMEM((target.shape[1], width), bf16),
        ],
        compiler_params=pltpu.CompilerParams(vmem_limit_bytes=20 * mib),
        name="project",
    )(target, x_rows, *weights)


def finish_kernel(which, gain_ref, cos_ref, sin_ref, *refs):
    parts, out_ref = refs[:-1], refs[-1]
    rows, half = cos_ref.shape[0] // 2, cos_ref.shape[1]
    mine = slice(which * rows, (which + 1) * rows)
    total = parts[0][...].astype(f32)
    for part in parts[1:]:
        total = total + part[...].astype(f32)
    tiles, rest = load_packed(total, rows)
    latent = jnp.concatenate(tiles, axis=1)
    spread = jnp.mean(latent * latent, axis=1, keepdims=True)
    latent = latent * lax.rsqrt(spread + 1e-06) * gain_ref[...]
    first, second = rest[:, :half], rest[:, half:]
    cosine, sine = cos_ref[mine, :], sin_ref[mine, :]
    store_packed(
        out_ref,
        jnp.concatenate(
            [latent, first * cosine - second * sine, second * cosine + first * sine], axis=1
        ),
    )


def finish(parts, gain, cosine, sine, which):
    return pl.pallas_call(
        functools.partial(finish_kernel, which),
        out_shape=jax.ShapeDtypeStruct(parts[0].shape, bf16),
        in_specs=[in_vmem] * (3 + len(parts)),
        out_specs=in_vmem,
        compiler_params=pltpu.CompilerParams(vmem_limit_bytes=8 * mib),
        name="finish_rows",
    )(gain, cosine, sine, *parts)


def attend_kernel(
    scale, cap_slots, steps, first_head, heads, query_ref, slot_ref, top_ref,
    sum_ref, mix_ref, live_ref, value_ref, *refs
):
    pieces, out_ref, keys = refs[:-2], refs[-2], refs[-1]
    lat_width = mix_ref.shape[0] * mix_ref.shape[2]
    per_head = cap_slots * steps
    rows = heads * per_head
    mine = slice(first_head * per_head, first_head * per_head + rows)
    sides = len(pieces) // 2
    piece_rows = keys.shape[0] // len(pieces)
    for n, piece in enumerate(pieces):
        tiles, rest = load_packed(piece, piece_rows)
        place = (n % sides) * 2 + n // sides
        there = slice(place * piece_rows, (place + 1) * piece_rows)
        for j, tile in enumerate(tiles):
            keys[there, j * 128 : (j + 1) * 128] = tile
        keys[there, lat_width:] = rest
    contract = (((1,), (1,)), ((), ()))
    row = lax.broadcasted_iota(jnp.int32, (rows, 1), 0)
    row_slot = (row // steps) % cap_slots
    query = query_ref[mine, :]
    score = lax.dot_general(query, keys[...], contract, preferred_element_type=f32)
    score = jnp.where(
        slot_ref[...] == row_slot + 1, score * scale, masked_score
    )
    top_held = top_ref[mine, :1]
    top = jnp.maximum(top_held, jnp.max(score, axis=1, keepdims=True))
    held = jnp.exp(top_held - top)
    weight = jnp.exp(score - top)
    total = sum_ref[mine, :1] * held + jnp.sum(weight, axis=1, keepdims=True)
    mix = jnp.dot(weight.astype(bf16), keys[:, :lat_width], preferred_element_type=f32)
    mix_held = jnp.concatenate([mix_ref[n, mine, :] for n in range(mix_ref.shape[0])], axis=1)
    latent = ((mix_held * held + mix) / total).astype(bf16)
    live = live_ref[:, :1]
    width = value_ref.shape[2]
    for h in range(0, heads, 2):
        head = first_head + h
        pair = jnp.concatenate([value_ref[head], value_ref[head + 1]], axis=1)
        both = jnp.dot(
            latent[h * per_head : (h + 2) * per_head, :], pair, preferred_element_type=f32
        )
        out_ref[:, h * width : (h + 1) * width] = (both[:per_head, :width] * live).astype(bf16)
        out_ref[:, (h + 1) * width : (h + 2) * width] = (both[per_head:, width:] * live).astype(bf16)


def attend(scale, query, row_slot, top, total, mix, live, value, pieces, cap_slots, steps,
           first_head, heads):
    width = value.shape[2]
    return pl.pallas_call(
        functools.partial(attend_kernel, scale, cap_slots, steps, first_head, heads),
        out_shape=jax.ShapeDtypeStruct((cap_slots * steps, heads * width), bf16),
        in_specs=[in_vmem] * (7 + len(pieces)),
        out_specs=in_vmem,
        scratch_shapes=[pltpu.VMEM((row_slot.shape[1], query.shape[1]), bf16)],
        compiler_params=pltpu.CompilerParams(vmem_limit_bytes=10 * mib),
        name="attend",
    )(query, row_slot, top, total, mix, live, value, *pieces)


def output_kernel(dev_count, side_count, start, last, *refs):
    my_dev, my_side = lax.axis_index("dev"), lax.axis_index("side")
    head_refs = refs[:dev_count]
    weight_ref = refs[dev_count]
    earlier_ref = refs[dev_count + 1] if start else None
    out_refs = refs[dev_count + 1 + (start > 0) : -1]
    held = refs[-1]
    rows, depth = head_refs[0].shape
    per_side = dev_count // side_count
    for j in range(dev_count):
        group = my_dev ^ j
        place = (lax.div(group, per_side) ^ my_side) * per_side + lax.rem(group, per_side)
        held[pl.ds(pl.multiple_of(place * rows, 16), rows), :] = head_refs[j][...]
    columns = weight_ref.shape[1]
    tile = 256 if columns % 256 == 0 else columns
    side_rows = rows * per_side
    for n in range(columns // tile):
        here = slice(n * tile, (n + 1) * tile)
        product = jnp.dot(
            held[...], weight_ref[start : start + depth, here],
            preferred_element_type=f32,
        )
        if start:
            product = product + earlier_ref[:, here]
        if not last:
            out_refs[0][:, here] = product
        else:
            for k in range(side_count):
                out_refs[k][:, here] = product[k * side_rows : (k + 1) * side_rows, :].astype(
                    out_refs[k].dtype
                )


def output_product(head_pieces, weight, side_count, earlier, start, last):
    dev_count = len(head_pieces)
    rows, depth = head_pieces[0].shape
    columns = weight.shape[1]
    side_rows = rows * dev_count // side_count
    if not last:
        shapes = [((rows * dev_count, columns), f32)]
    else:
        shapes = [((side_rows, columns), f32 if k == 0 else bf16) for k in range(side_count)]
    earlier = [] if earlier is None else [earlier]
    return pl.pallas_call(
        functools.partial(output_kernel, dev_count, side_count, start, last),
        out_shape=[jax.ShapeDtypeStruct(*shape) for shape in shapes],
        in_specs=[in_vmem] * (dev_count + 1 + len(earlier)),
        out_specs=[in_vmem] * len(shapes),
        scratch_shapes=[pltpu.VMEM((dev_count * rows, depth), bf16)],
        compiler_params=pltpu.CompilerParams(vmem_limit_bytes=10 * mib),
        name="output_product",
    )(*head_pieces, weight, *earlier)


def on_device(
    prompts,
    latent_weight,
    latent_gain,
    row_request,
    context_len,
    request_slot,
    latent_cache,
    new_latent,
    queries,
    key_absorb,
    value_absorb,
    out_weight,
):
    dev_count = lax.axis_size("dev")
    side_count = lax.axis_size("side")
    tok_rows, model_width = prompts.shape
    shard_rows, kv_width = latent_weight.shape
    lat_width = latent_gain.shape[0]
    nope_width = value_absorb.shape[2]
    rope_width = kv_width - lat_width
    cap_slots, ctx_len, _ = latent_cache.shape
    step_count = new_latent.shape[1]
    bucket_rows = 2 * tok_rows // dev_count
    group_rows = dev_count * bucket_rows
    slab = model_width // dev_count

    x_pieces = list(split_columns(prompts, dev_count))
    packs = shard_rows % 32 == 0
    weights = [pack_weight(latent_weight) if packs else latent_weight] + [None] * (side_count - 1)
    for k in range(2, side_count, 2):
        weights[k] = swap(weights[0], "side", k)
    for k in sorted(range(1, dev_count), reverse=True):
        x_pieces[k] = swap(x_pieces[k], "dev", k)

    score_scale = queries.shape[-1] ** (-0.5)
    half = rope_width // 2
    inverse = 1.0 / 10000.0 ** (jnp.arange(half, dtype=f32) * (2.0 / rope_width))
    lengths, x_pieces[0] = lax.optimization_barrier((context_len, x_pieces[0]))
    (
        query_full, top_held, sum_held, mix_held, live, target, cosine, sine, row_slot,
        value_here, out_here,
    ) = prepare(
        score_scale, dev_count, side_count, bucket_rows, lengths, request_slot,
        row_request.reshape(-1, 128), inverse.reshape(1, -1), queries, key_absorb,
        jnp.swapaxes(latent_cache, 1, 2), new_latent, value_absorb, out_weight,
    )

    weights[0::2], top_held = lax.optimization_barrier((weights[0::2], top_held))
    for k in range(0, side_count, 2):
        weights[k + 1] = swap(weights[k], "side", 1)
    if not packs:
        my_side = lax.axis_index("side")
        held = jnp.zeros((side_count, shard_rows, kv_width), bf16)
        for k in range(side_count):
            held = lax.dynamic_update_slice(held, weights[k][None], (my_side ^ k, 0, 0))
        weights = [held.reshape(slab, kv_width)]

    routed = project(stack_rows(x_pieces), weights, target, kv_width, dev_count)
    pieces = []
    for which in range(2):
        half = list(routed[which * dev_count : (which + 1) * dev_count])
        for k in sorted(range(1, dev_count), reverse=True):
            half[k] = swap(half[k], "dev", k)
        latent_rows = finish(half[:1] + half[:0:-1], latent_gain.reshape(1, -1), cosine, sine, which)
        pieces += [latent_rows] + [swap(latent_rows, "side", k) for k in range(1, side_count)]
    product, first_head, head_count = None, 0, value_absorb.shape[0]
    for part_heads in (head_count * 3 // 4, head_count // 4):
        head_out = attend(
            score_scale, query_full, row_slot, top_held, sum_held, mix_held, live, value_here,
            pieces, cap_slots, step_count, first_head, part_heads,
        )
        heads = [head_out] + [None] * (dev_count - 1)
        for k in sorted(range(1, dev_count), reverse=True):
            heads[k] = swap(head_out, "dev", k)
        start, first_head = first_head * nope_width, first_head + part_heads
        products = output_product(
            heads, out_here, side_count, product, start, first_head == head_count
        )
        product = products[0]
    result = products[0]
    for k in sorted(range(1, side_count), reverse=True):
        result = result + swap(products[k], "side", k).astype(f32)
    return result.astype(bf16)


def solution(mesh):
    placed = (
        P(("rep", "dev", "side"), None),
        P(("dev", "side"), None),
        P(),
        P("rep"),
        P("rep"),
        P("rep"),
        P(("rep", "dev"), None, None),
        P(("rep", "dev"), None, None),
        P(("rep", "dev"), None, "side", None),
        P("side", None, None),
        P("side", None, None),
        P("side", "dev"),
    )
    return jax.shard_map(
        on_device, mesh=mesh, in_specs=placed, out_specs=P(("rep", "side"), "dev"), check_vma=False
    )
```

```python
import functools

import jax
import jax.numpy as jnp
from jax import lax
from jax.experimental import pallas as pl
from jax.experimental.pallas import tpu as pltpu
from jax.sharding import PartitionSpec as P

masked_score = -1e30
bf16, f32 = jnp.bfloat16, jnp.float32
in_vmem = pl.BlockSpec(memory_space=pltpu.VMEM)
in_smem = pl.BlockSpec(memory_space=pltpu.SMEM)
in_hbm = pl.BlockSpec(memory_space=pltpu.HBM)
mib = 1024 * 1024
prepare_mib = 16


def swap(value, axis, step):
    count = lax.axis_size(axis)
    return lax.ppermute(value, axis, [(i, i ^ step) for i in range(count)])


def pick(pieces, index):
    out = pieces[0]
    for k in range(1, len(pieces)):
        out = jnp.where(index == k, pieces[k], out)
    return out


def lane_tiles(width):
    return [slice(n, min(n + 128, width)) for n in range(0, width, 128)]


def packed_rows(rows, width):
    return rows * (width // 128) + rows // 2


def pack(value):
    rows, width = value.shape
    full = width // 128
    rest = value[:, full * 128 :]
    parts = [value[:, n * 128 : (n + 1) * 128] for n in range(full)]
    return parts + [jnp.concatenate([rest[: rows // 2], rest[rows // 2 :]], axis=1)]


def store_packed(ref, value):
    first = 0
    for part in pack(value):
        ref[first : first + part.shape[0], :] = part.astype(ref.dtype)
        first += part.shape[0]


def load_packed(ref, rows):
    full = ref.shape[0] // rows
    tiles = [ref[n * rows : (n + 1) * rows, :] for n in range(full)]
    rest = ref[full * rows :, :]
    return tiles, jnp.concatenate([rest[:, :64], rest[:, 64:]], axis=0)


def pack_kernel(value_ref, out_ref):
    store_packed(out_ref, value_ref[...])


def pack_weight(weight):
    rows, width = weight.shape
    return pl.pallas_call(
        pack_kernel,
        out_shape=jax.ShapeDtypeStruct((packed_rows(rows, width), 128), weight.dtype),
        in_specs=[in_vmem],
        out_specs=in_vmem,
        compiler_params=pltpu.CompilerParams(vmem_limit_bytes=8 * mib),
        cost_estimate=pl.CostEstimate(flops=10**10, bytes_accessed=10**6, transcendentals=0),
        name="pack_weight",
    )(weight)


def split_kernel(slab, prompts_ref, *refs):
    my_dev = lax.axis_index("dev")
    out_refs, sems = refs[:-1], refs[-1]
    copies = []
    for k in range(len(out_refs))[::-1]:
        first = pl.multiple_of((my_dev ^ k) * slab, 128)
        copies.append(
            pltpu.make_async_copy(prompts_ref.at[:, pl.ds(first, slab)], out_refs[k], sems.at[k])
        )
    for copy in copies:
        copy.start()
    for copy in copies:
        copy.wait()


def split_columns(prompts, count):
    rows, width = prompts.shape
    slab = width // count
    if slab % 128:
        columns = [prompts[:, k * slab : (k + 1) * slab] for k in range(count)]
        my_dev = lax.axis_index("dev")
        return [pick(columns, my_dev ^ k) for k in range(count)]
    return pl.pallas_call(
        functools.partial(split_kernel, slab),
        out_shape=[jax.ShapeDtypeStruct((rows, slab), prompts.dtype)] * count,
        in_specs=[in_hbm],
        out_specs=[in_vmem] * count,
        scratch_shapes=[pltpu.SemaphoreType.DMA((count,))],
        compiler_params=pltpu.CompilerParams(vmem_limit_bytes=8 * mib),
        cost_estimate=pl.CostEstimate(
            flops=10**10, bytes_accessed=4 * 10**7, transcendentals=0
        ),
        name="split_columns",
    )(prompts)


def fill_tables(
    dev_count, side_count, bucket, cap_slots, length_ref, slot_ref, request_ref, inverse_ref,
    target_ref, cos_ref, sin_ref, spot_ref, to_ref, place_ref, local_ref, position_ref,
):
    my_dev, my_side = lax.axis_index("dev"), lax.axis_index("side")
    requests = request_ref[...]
    lane_rows, lanes = requests.shape
    tok_rows = bucket * dev_count // 2
    per_row = lanes // tok_rows
    half_bucket = bucket // 2
    half_rows = dev_count * half_bucket
    group_rows = 2 * half_rows
    before = lax.broadcasted_iota(jnp.int32, (lanes, lanes), 0)
    after = lax.broadcasted_iota(jnp.int32, (lanes, lanes), 1)
    below = jnp.where(before < after, 1.0, 0.0)
    near = jnp.where((before < after) & (before // tok_rows == after // tok_rows), 1.0, 0.0)
    scan = jnp.concatenate([below, jnp.ones_like(below)], axis=1).astype(bf16)
    lower = lax.broadcasted_iota(jnp.int32, (lane_rows, lane_rows), 0)
    upper = lax.broadcasted_iota(jnp.int32, (lane_rows, lane_rows), 1)
    rows_before = jnp.where(upper < lower, 1.0, 0.0)
    position = jnp.zeros(requests.shape, f32)
    slot = jnp.zeros(requests.shape, jnp.int32)
    for q in range(slot_ref.shape[0]):
        hit = requests == q
        ranks = jnp.dot(
            jnp.where(hit, 1.0, 0.0).astype(bf16), scan, preferred_element_type=f32
        )
        earlier = jnp.dot(rows_before, ranks[:, lanes:], preferred_element_type=f32)
        start = length_ref[q].astype(f32)
        position = jnp.where(hit, ranks[:, :lanes] + earlier + start, position)
        slot = jnp.where(hit, slot_ref[q], slot)
    group = lax.div(slot, cap_slots)
    rank = jnp.zeros(requests.shape, f32)
    for g in range(dev_count):
        hit = group == g
        ranks = jnp.dot(
            jnp.where(hit, 1.0, 0.0).astype(bf16), near.astype(bf16), preferred_element_type=f32
        )
        rank = jnp.where(hit, ranks, rank)
    block = lax.broadcasted_iota(jnp.int32, requests.shape, 0) * per_row + lax.div(
        lax.broadcasted_iota(jnp.int32, requests.shape, 1), tok_rows
    )
    rank = rank.astype(jnp.int32)
    which = lax.div(rank, half_bucket)
    place = lax.div(block, side_count) * half_bucket + lax.rem(rank, half_bucket)
    to_ref[...] = (which * dev_count + (group ^ my_dev)) * half_rows + place
    place = which * half_rows + place
    place_ref[...] = jnp.where(group == my_dev, place, -1)
    local_ref[...] = (slot - my_dev * cap_slots + 1).astype(f32)
    position_ref[...] = position
    lane_block = lax.div(lax.broadcasted_iota(jnp.int32, (1, lanes), 1), tok_rows)
    ids = lax.broadcasted_iota(jnp.int32, (group_rows, 1), 0)

    def find(dev, side):
        held = dev * side_count + side
        return pl.ds(lax.div(held, per_row), 1), lane_block == lax.rem(held, per_row)

    targets = []
    for k in range(dev_count):
        held = (my_dev ^ k) * side_count + my_side
        row = jnp.broadcast_to(to_ref[pl.ds(lax.div(held, per_row), 1), :], (8, lanes))
        start = lax.rem(lanes - tok_rows * lax.rem(held, per_row), lanes)
        targets.append(pltpu.roll(row, start, 1)[:1, :tok_rows])
    for k in range(0, dev_count, per_row):
        target_ref[:, k * tok_rows : k * tok_rows + lanes] = jnp.concatenate(
            targets[k : k + per_row], axis=1
        )
    found = jnp.zeros((group_rows, lanes), f32)
    for d in range(dev_count):
        row, inside = find(d, my_side)
        found = jnp.where((place_ref[row, :] == ids) & inside, position_ref[row, :], found)
    angles = jnp.sum(found, axis=1, keepdims=True) * inverse_ref[...]
    cos_ref[...] = jnp.cos(angles)
    sin_ref[...] = jnp.sin(angles)
    for k in range(side_count):
        total = jnp.zeros((8, group_rows), f32)
        for d in range(dev_count):
            row, inside = find(d, my_side ^ k)
            chosen = jnp.where((place_ref[row, :] == ids) & inside, 1.0, 0.0).astype(bf16)
            values = jnp.broadcast_to(local_ref[row, :], (8, lanes)).astype(bf16)
            total = total + lax.dot_general(
                values, chosen, (((1,), (1,)), ((), ())), preferred_element_type=f32
            )
        spot_ref[:, k * group_rows : (k + 1) * group_rows] = total[:1].astype(jnp.int32)


def prepare_kernel(
    scale, steps, layout, inverse_ref, length_hbm, slot_hbm, request_hbm, query_hbm, absorb_hbm,
    cache_hbm, fresh_hbm, value_hbm, out_hbm, full_ref, top_ref, sum_ref, mix_ref, live_ref, target_ref,
    cos_ref, sin_ref, spot_ref, value_ref, out_ref, length_ref, slot_ref, request_ref, query_ref,
    absorb_ref, cache_ref, fresh_ref, plain, full, to_ref, place_ref, local_ref, position_ref, sems,
):
    pairs = [
        (length_hbm, length_ref), (slot_hbm, slot_ref), (request_hbm, request_ref),
        (query_hbm, query_ref), (absorb_hbm, absorb_ref), (cache_hbm, cache_ref),
        (fresh_hbm, fresh_ref), (value_hbm, value_ref),
    ]
    parts = sems.shape[0] - len(pairs)
    rows = out_hbm.shape[0] // parts
    for n in range(parts):
        part = pl.ds(n * rows, rows)
        pairs.append((out_hbm.at[part], out_ref.at[part]))
    copies = [pltpu.make_async_copy(*pair, sems.at[n]) for n, pair in enumerate(pairs)]
    for copy in copies:
        copy.start()
    for copy in copies[:3]:
        copy.wait()
    slots, _, context = cache_ref.shape
    heads, nope, lat_width = absorb_ref.shape
    per_head = slots * steps
    fill_tables(
        *layout, slots, length_ref, slot_ref, request_ref, inverse_ref, target_ref, cos_ref,
        sin_ref, spot_ref, to_ref, place_ref, local_ref, position_ref,
    )
    first_slot = lax.axis_index("dev") * slots
    lengths = []
    for s in range(slots):
        length = jnp.int32(0)
        for q in range(slot_ref.shape[0]):
            length = jnp.where(slot_ref[q] == first_slot + s, length_ref[q], length)
        lengths.append(length)
    slot_of = lax.div(lax.broadcasted_iota(jnp.int32, live_ref.shape, 0), steps)
    live = jnp.zeros(live_ref.shape, f32)
    for s in range(slots):
        live = jnp.where((slot_of == s) & (lengths[s] > 0), 1.0, live)
    live_ref[...] = live
    copies[3].wait()
    copies[4].wait()
    for n, here in enumerate(lane_tiles(query_ref.shape[1])):
        plain[n, :, : here.stop - here.start] = query_ref[:, here].astype(f32)
    wide = lane_tiles(full_ref.shape[1])
    for h in range(heads):
        there = pl.ds(h, per_head, stride=heads)
        query = plain[0, there, :].astype(bf16)
        latent = jnp.dot(query, absorb_ref[h], preferred_element_type=f32).astype(bf16).astype(f32)
        here = slice(h * per_head, (h + 1) * per_head)
        for n, lanes in enumerate(lane_tiles(lat_width)):
            full[n, here, :] = latent[:, lanes]
        full[len(wide) - 1, here, :] = plain[1, there, :]
    for n, lanes in enumerate(wide):
        full_ref[:, lanes] = full[n, :, : lanes.stop - lanes.start].astype(bf16)
    key = lax.broadcasted_iota(jnp.int32, (1, context), 1)
    copies[5].wait()
    copies[6].wait()
    late = lax.broadcasted_iota(jnp.int32, (steps * heads, steps), 1)
    late = late > lax.div(lax.broadcasted_iota(jnp.int32, (steps * heads, steps), 0), heads)
    for s in range(slots):
        theres = [pl.ds(s * steps + t, heads, stride=per_head) for t in range(steps)]
        query = jnp.concatenate(
            [
                jnp.concatenate([full[n, there, :] for there in theres], axis=0)[
                    :, : lanes.stop - lanes.start
                ].astype(bf16)
                for n, lanes in enumerate(wide)
            ],
            axis=1,
        )
        rows = cache_ref[s]
        score = jnp.dot(query, rows, preferred_element_type=f32)
        score = jnp.where(key < lengths[s], score * scale, masked_score)
        fresh = fresh_ref[s]
        new = lax.dot_general(
            query, fresh, (((1,), (1,)), ((), ())), preferred_element_type=f32
        )
        new = jnp.where(late, masked_score, new * scale)
        top = jnp.maximum(
            jnp.max(score, axis=1, keepdims=True), jnp.max(new, axis=1, keepdims=True)
        )
        weight = jnp.exp(score - top)
        new = jnp.exp(new - top)
        total = jnp.sum(weight, axis=1, keepdims=True) + jnp.sum(new, axis=1, keepdims=True)
        mix = lax.dot_general(
            weight.astype(bf16), rows[:lat_width, :], (((1,), (1,)), ((), ())),
            preferred_element_type=f32,
        )
        for u in range(steps):
            mix = mix + new[:, u : u + 1].astype(bf16).astype(f32) * fresh[
                u : u + 1, :lat_width
            ].astype(f32)
        lanes = top_ref.shape[1]
        for t in range(steps):
            there = theres[t]
            here = slice(t * heads, (t + 1) * heads)
            top_ref[there, :] = jnp.broadcast_to(top[here], (heads, lanes))
            sum_ref[there, :] = jnp.broadcast_to(total[here], (heads, lanes))
            for n, part in enumerate(lane_tiles(lat_width)):
                mix_ref[n, there, :] = mix[here, part]
    for copy in copies[7:]:
        copy.wait()


def prepare(
    scale, dev_count, side_count, bucket, lengths, request_slot, requests, inverse, queries,
    absorb, cache, fresh, value, out_weight,
):
    slots, steps, heads, width = queries.shape
    kv_width = cache.shape[1]
    lat_width = absorb.shape[2]
    rows = slots * steps * heads
    group_rows = dev_count * bucket
    parts = 8
    lanes = requests.shape[1]
    half = inverse.shape[1]
    shapes = [
        ((rows, kv_width), bf16), ((rows, 128), f32), ((rows, 128), f32),
        ((lat_width // 128, rows, 128), f32), ((slots * steps, 128), f32),
        ((1, group_rows // 2 * dev_count), jnp.int32), ((group_rows, half), f32), ((group_rows, half), f32),
        ((1, side_count * group_rows), jnp.int32), (value.shape, bf16), (out_weight.shape, bf16),
    ]
    return pl.pallas_call(
        functools.partial(prepare_kernel, scale, steps, (dev_count, side_count, bucket)),
        out_shape=[jax.ShapeDtypeStruct(*shape) for shape in shapes],
        in_specs=[in_vmem] + [in_hbm] * 9,
        out_specs=[in_vmem] * len(shapes),
        scratch_shapes=[
            pltpu.SMEM(lengths.shape, lengths.dtype),
            pltpu.SMEM(request_slot.shape, request_slot.dtype),
            pltpu.VMEM(requests.shape, requests.dtype),
            pltpu.VMEM((rows, width), queries.dtype),
            pltpu.VMEM(absorb.shape, absorb.dtype),
            pltpu.VMEM(cache.shape, cache.dtype),
            pltpu.VMEM(fresh.shape, fresh.dtype),
            pltpu.VMEM((len(lane_tiles(width)), rows, 128), f32),
            pltpu.VMEM((len(lane_tiles(kv_width)), rows, 128), f32),
            pltpu.VMEM(requests.shape, jnp.int32),
            pltpu.VMEM(requests.shape, jnp.int32),
            pltpu.VMEM(requests.shape, f32),
            pltpu.VMEM(requests.shape, f32),
            pltpu.SemaphoreType.DMA((parts + 8,)),
        ],
        compiler_params=pltpu.CompilerParams(vmem_limit_bytes=prepare_mib * mib),
        cost_estimate=pl.CostEstimate(
            flops=4 * 10**10, bytes_accessed=28 * 10**6, transcendentals=10**5
        ),
        name="prepare",
    )(inverse, lengths, request_slot, requests, queries.reshape(rows, width), absorb, cache, fresh,
      value, out_weight)


def stack_kernel(*refs):
    out_ref = refs[-1]
    rows = refs[0].shape[0]
    for n, ref in enumerate(refs[:-1]):
        k = (len(refs) - 1 - n) % (len(refs) - 1)
        out_ref[k * rows : (k + 1) * rows, :] = ref[...]


def stack_rows(pieces):
    rows, width = pieces[0].shape
    return pl.pallas_call(
        stack_kernel,
        out_shape=jax.ShapeDtypeStruct((len(pieces) * rows, width), bf16),
        in_specs=[in_vmem] * len(pieces),
        out_specs=in_vmem,
        compiler_params=pltpu.CompilerParams(vmem_limit_bytes=8 * mib),
        cost_estimate=pl.CostEstimate(flops=2 * 10**10, bytes_accessed=10**6, transcendentals=0),
        name="stack_rows",
    )(pieces[0], *pieces[:0:-1])


def project_kernel(dev_count, side_count, target_ref, x_ref, *refs):
    my_side = lax.axis_index("side")
    weight_refs = refs[:side_count]
    out_refs = refs[side_count:-2]
    slab_weight, rows = refs[-2:]
    tok_rows = x_ref.shape[0] // dev_count
    full = slab_weight.shape[1] // 128
    if side_count > 1:
        shard = slab_weight.shape[0] // side_count
        for k in range(side_count):
            first = pl.multiple_of((my_side ^ k) * shard, 16)
            tiles, rest = load_packed(weight_refs[k], shard)
            for n, tile in enumerate(tiles):
                slab_weight[pl.ds(first, shard), n * 128 : (n + 1) * 128] = tile
            slab_weight[pl.ds(first, shard), full * 128 :] = rest
    slab = slab_weight[...] if side_count > 1 else weight_refs[0][...]
    raw = jnp.dot(x_ref[...], slab, preferred_element_type=f32).astype(bf16)
    rows[...] = raw
    target = target_ref[...]
    half_rows = tok_rows
    step = min(4, 2 * dev_count)
    for j in range(0, 2 * dev_count, step):
        ids = lax.broadcasted_iota(jnp.int32, (step * half_rows, target.shape[1]), 0)
        route = jnp.where(ids + j * half_rows == target, 1.0, 0.0).astype(bf16)
        placed = jnp.dot(route, rows[...], preferred_element_type=f32)
        for n in range(step):
            store_packed(out_refs[j + n], placed[n * half_rows : (n + 1) * half_rows])


def project(x_rows, weights, target, width, dev_count):
    tok_rows, slab = x_rows.shape[0] // dev_count, x_rows.shape[1]
    return pl.pallas_call(
        functools.partial(project_kernel, dev_count, len(weights)),
        out_shape=[
            jax.ShapeDtypeStruct(
                (packed_rows(tok_rows, width), 128), f32 if j % dev_count == 0 else bf16
            )
            for j in range(2 * dev_count)
        ],
        in_specs=[in_vmem] * (2 + len(weights)),
        out_specs=[in_vmem] * (2 * dev_count),
        scratch_shapes=[
            pltpu.VMEM((slab, width), bf16),
            pltpu.VMEM((target.shape[1], width), bf16),
        ],
        compiler_params=pltpu.CompilerParams(vmem_limit_bytes=20 * mib),
        name="project",
    )(target, x_rows, *weights)


def finish_kernel(which, gain_ref, cos_ref, sin_ref, *refs):
    parts, out_ref = refs[:-1], refs[-1]
    rows, half = cos_ref.shape[0] // 2, cos_ref.shape[1]
    mine = slice(which * rows, (which + 1) * rows)
    total = parts[0][...].astype(f32)
    for part in parts[1:]:
        total = total + part[...].astype(f32)
    tiles, rest = load_packed(total, rows)
    latent = jnp.concatenate(tiles, axis=1)
    spread = jnp.mean(latent * latent, axis=1, keepdims=True)
    latent = latent * lax.rsqrt(spread + 1e-06) * gain_ref[...]
    first, second = rest[:, :half], rest[:, half:]
    cosine, sine = cos_ref[mine, :], sin_ref[mine, :]
    store_packed(
        out_ref,
        jnp.concatenate(
            [latent, first * cosine - second * sine, second * cosine + first * sine], axis=1
        ),
    )


def finish(parts, gain, cosine, sine, which):
    return pl.pallas_call(
        functools.partial(finish_kernel, which),
        out_shape=jax.ShapeDtypeStruct(parts[0].shape, bf16),
        in_specs=[in_vmem] * (3 + len(parts)),
        out_specs=in_vmem,
        compiler_params=pltpu.CompilerParams(vmem_limit_bytes=8 * mib),
        name="finish_rows",
    )(gain, cosine, sine, *parts)


def take_keys(keys, pieces, lat_width):
    rows = keys.shape[0] // len(pieces)
    for n, piece in enumerate(pieces):
        tiles, rest = load_packed(piece, rows)
        there = slice(n * rows, (n + 1) * rows)
        for j, tile in enumerate(tiles):
            keys[there, j * 128 : (j + 1) * 128] = tile
        keys[there, lat_width:] = rest


def merge(layout, which, mine, query_ref, slot_ref, top_ref, sum_ref, mix_ref, keys):
    scale, cap_slots, steps, half_rows = layout
    lat_width = mix_ref.shape[0] * mix_ref.shape[2]
    row = lax.broadcasted_iota(jnp.int32, (mine.stop - mine.start, 1), 0)
    row_slot = (row // steps) % cap_slots
    query = query_ref[mine, :]
    score = lax.dot_general(
        query, keys[...], (((1,), (1,)), ((), ())), preferred_element_type=f32
    )
    count = slot_ref.shape[1]
    part = half_rows
    slots = jnp.concatenate(
        [slot_ref[:, n + which * part : n + (which + 1) * part] for n in range(0, count, 2 * part)],
        axis=1,
    )
    score = jnp.where(slots == row_slot + 1, score * scale, masked_score)
    top_held = top_ref[mine, :1]
    top = jnp.maximum(top_held, jnp.max(score, axis=1, keepdims=True))
    held = jnp.exp(top_held - top)
    weight = jnp.exp(score - top)
    total = sum_ref[mine, :1] * held + jnp.sum(weight, axis=1, keepdims=True)
    mix = jnp.dot(weight.astype(bf16), keys[:, :lat_width], preferred_element_type=f32)
    mix_held = jnp.concatenate([mix_ref[n, mine, :] for n in range(mix_ref.shape[0])], axis=1)
    return top, total, mix_held * held + mix


def absorb_kernel(layout, which, query_ref, slot_ref, top_ref, sum_ref, mix_ref, *refs):
    pieces, (new_top, new_sum, new_mix, keys) = refs[:-4], refs[-4:]
    take_keys(keys, pieces, mix_ref.shape[0] * mix_ref.shape[2])
    rows, lanes = top_ref.shape
    step = rows // 2
    for first in range(0, rows, step):
        mine = slice(first, first + step)
        top, total, mix = merge(
            layout, which, mine, query_ref, slot_ref, top_ref, sum_ref, mix_ref, keys
        )
        new_top[mine, :] = jnp.broadcast_to(top, (step, lanes))
        new_sum[mine, :] = jnp.broadcast_to(total, (step, lanes))
        for n, part in enumerate(lane_tiles(mix.shape[1])):
            new_mix[n, mine, :] = mix[:, part]


def absorb(layout, which, query, row_slot, top, total, mix, pieces):
    return pl.pallas_call(
        functools.partial(absorb_kernel, layout, which),
        out_shape=[jax.ShapeDtypeStruct(x.shape, f32) for x in (top, total, mix)],
        in_specs=[in_vmem] * (5 + len(pieces)),
        out_specs=[in_vmem] * 3,
        scratch_shapes=[pltpu.VMEM((row_slot.shape[1] // 2, query.shape[1]), bf16)],
        compiler_params=pltpu.CompilerParams(vmem_limit_bytes=10 * mib),
        cost_estimate=pl.CostEstimate(flops=2 * 10**9, bytes_accessed=10**6, transcendentals=0),
        name="absorb",
    )(query, row_slot, top, total, mix, *pieces)


def attend_kernel(
    layout, which, first_head, heads, query_ref, slot_ref, top_ref, sum_ref, mix_ref, live_ref,
    value_ref, *refs
):
    pieces, out_ref, keys = refs[:-2], refs[-2], refs[-1]
    per_head = layout[1] * layout[2]
    take_keys(keys, pieces, mix_ref.shape[0] * mix_ref.shape[2])
    mine = slice(first_head * per_head, (first_head + heads) * per_head)
    _, total, mix = merge(
        layout, which, mine, query_ref, slot_ref, top_ref, sum_ref, mix_ref, keys
    )
    latent = (mix / total).astype(bf16)
    live = live_ref[:, :1]
    width = value_ref.shape[2]
    for h in range(0, heads, 2):
        head = first_head + h
        pair = jnp.concatenate([value_ref[head], value_ref[head + 1]], axis=1)
        both = jnp.dot(
            latent[h * per_head : (h + 2) * per_head, :], pair, preferred_element_type=f32
        )
        out_ref[:, h * width : (h + 1) * width] = (both[:per_head, :width] * live).astype(bf16)
        out_ref[:, (h + 1) * width : (h + 2) * width] = (both[per_head:, width:] * live).astype(bf16)


def attend(layout, which, query, row_slot, top, total, mix, live, value, pieces, first_head, heads):
    return pl.pallas_call(
        functools.partial(attend_kernel, layout, which, first_head, heads),
        out_shape=jax.ShapeDtypeStruct((live.shape[0], heads * value.shape[2]), bf16),
        in_specs=[in_vmem] * (7 + len(pieces)),
        out_specs=in_vmem,
        scratch_shapes=[pltpu.VMEM((row_slot.shape[1] // 2, query.shape[1]), bf16)],
        compiler_params=pltpu.CompilerParams(vmem_limit_bytes=10 * mib),
        name="attend",
    )(query, row_slot, top, total, mix, live, value, *pieces)


def output_kernel(dev_count, side_count, start, last, *refs):
    my_dev, my_side = lax.axis_index("dev"), lax.axis_index("side")
    head_refs = refs[:dev_count]
    weight_ref = refs[dev_count]
    earlier_ref = refs[dev_count + 1] if start else None
    out_refs = refs[dev_count + 1 + (start > 0) : -1]
    held = refs[-1]
    rows, depth = head_refs[0].shape
    per_side = dev_count // side_count
    for j in range(dev_count):
        group = my_dev ^ j
        place = (lax.div(group, per_side) ^ my_side) * per_side + lax.rem(group, per_side)
        held[pl.ds(pl.multiple_of(place * rows, 16), rows), :] = head_refs[j][...]
    columns = weight_ref.shape[1]
    tile = 256 if columns % 256 == 0 else columns
    side_rows = rows * per_side
    for n in range(columns // tile):
        here = slice(n * tile, (n + 1) * tile)
        product = jnp.dot(
            held[...], weight_ref[start : start + depth, here],
            preferred_element_type=f32,
        )
        if start:
            product = product + earlier_ref[:, here]
        if not last:
            out_refs[0][:, here] = product
        else:
            for k in range(side_count):
                out_refs[k][:, here] = product[k * side_rows : (k + 1) * side_rows, :].astype(
                    out_refs[k].dtype
                )


def output_product(head_pieces, weight, side_count, earlier, start, last):
    dev_count = len(head_pieces)
    rows, depth = head_pieces[0].shape
    columns = weight.shape[1]
    side_rows = rows * dev_count // side_count
    if not last:
        shapes = [((rows * dev_count, columns), f32)]
    else:
        shapes = [((side_rows, columns), f32 if k == 0 else bf16) for k in range(side_count)]
    earlier = [] if earlier is None else [earlier]
    return pl.pallas_call(
        functools.partial(output_kernel, dev_count, side_count, start, last),
        out_shape=[jax.ShapeDtypeStruct(*shape) for shape in shapes],
        in_specs=[in_vmem] * (dev_count + 1 + len(earlier)),
        out_specs=[in_vmem] * len(shapes),
        scratch_shapes=[pltpu.VMEM((dev_count * rows, depth), bf16)],
        compiler_params=pltpu.CompilerParams(vmem_limit_bytes=10 * mib),
        name="output_product",
    )(*head_pieces, weight, *earlier)


def on_device(
    prompts,
    latent_weight,
    latent_gain,
    row_request,
    context_len,
    request_slot,
    latent_cache,
    new_latent,
    queries,
    key_absorb,
    value_absorb,
    out_weight,
):
    dev_count = lax.axis_size("dev")
    side_count = lax.axis_size("side")
    tok_rows, model_width = prompts.shape
    shard_rows, kv_width = latent_weight.shape
    lat_width = latent_gain.shape[0]
    nope_width = value_absorb.shape[2]
    rope_width = kv_width - lat_width
    cap_slots, ctx_len, _ = latent_cache.shape
    step_count = new_latent.shape[1]
    bucket_rows = 2 * tok_rows // dev_count
    group_rows = dev_count * bucket_rows
    slab = model_width // dev_count

    x_pieces = list(split_columns(prompts, dev_count))
    packs = shard_rows % 32 == 0
    x_pieces[0], own_weight = lax.optimization_barrier((x_pieces[0], latent_weight))
    weights = [pack_weight(own_weight) if packs else own_weight] + [None] * (side_count - 1)
    for k in range(2, side_count, 2):
        weights[k] = swap(weights[0], "side", k)
    for k in sorted(range(1, dev_count), reverse=True):
        x_pieces[k] = swap(x_pieces[k], "dev", k)

    score_scale = queries.shape[-1] ** (-0.5)
    half = rope_width // 2
    inverse = 1.0 / 10000.0 ** (jnp.arange(half, dtype=f32) * (2.0 / rope_width))
    lengths, x_pieces[0] = lax.optimization_barrier((context_len, x_pieces[0]))
    (
        query_full, top_held, sum_held, mix_held, live, target, cosine, sine, row_slot,
        value_here, out_here,
    ) = prepare(
        score_scale, dev_count, side_count, bucket_rows, lengths, request_slot,
        row_request.reshape(-1, 128), inverse.reshape(1, -1), queries, key_absorb,
        jnp.swapaxes(latent_cache, 1, 2), new_latent, value_absorb, out_weight,
    )

    weights[0::2], top_held = lax.optimization_barrier((weights[0::2], top_held))
    for k in range(0, side_count, 2):
        weights[k + 1] = swap(weights[k], "side", 1)
    if not packs:
        my_side = lax.axis_index("side")
        held = jnp.zeros((side_count, shard_rows, kv_width), bf16)
        for k in range(side_count):
            held = lax.dynamic_update_slice(held, weights[k][None], (my_side ^ k, 0, 0))
        weights = [held.reshape(slab, kv_width)]

    routed = project(stack_rows(x_pieces), weights, target, kv_width, dev_count)
    layout = (score_scale, cap_slots, step_count, group_rows // 2)
    state = top_held, sum_held, mix_held
    for which in range(2):
        half = list(routed[which * dev_count : (which + 1) * dev_count])
        for k in sorted(range(1, dev_count), reverse=True):
            half[k] = swap(half[k], "dev", k)
        latent_rows = finish(half[:1] + half[:0:-1], latent_gain.reshape(1, -1), cosine, sine, which)
        pieces = [latent_rows] + [swap(latent_rows, "side", k) for k in range(1, side_count)]
        if which == 0:
            state = absorb(layout, which, query_full, row_slot, *state, pieces)
    product, first_head, head_count = None, 0, value_absorb.shape[0]
    for part_heads in (head_count * 3 // 4, head_count // 4):
        head_out = attend(
            layout, 1, query_full, row_slot, *state, live, value_here, pieces, first_head,
            part_heads,
        )
        heads = [head_out] + [None] * (dev_count - 1)
        for k in sorted(range(1, dev_count), reverse=True):
            heads[k] = swap(head_out, "dev", k)
        start, first_head = first_head * nope_width, first_head + part_heads
        products = output_product(
            heads, out_here, side_count, product, start, first_head == head_count
        )
        product = products[0]
    result = products[0]
    for k in sorted(range(1, side_count), reverse=True):
        result = result + swap(products[k], "side", k).astype(f32)
    return result.astype(bf16)


def solution(mesh):
    placed = (
        P(("rep", "dev", "side"), None),
        P(("dev", "side"), None),
        P(),
        P("rep"),
        P("rep"),
        P("rep"),
        P(("rep", "dev"), None, None),
        P(("rep", "dev"), None, None),
        P(("rep", "dev"), None, "side", None),
        P("side", None, None),
        P("side", None, None),
        P("side", "dev"),
    )
    return jax.shard_map(
        on_device, mesh=mesh, in_specs=placed, out_specs=P(("rep", "side"), "dev"), check_vma=False
    )
```

```python
import functools

import jax
import jax.numpy as jnp
from jax import lax
from jax.experimental import pallas as pl
from jax.experimental.pallas import tpu as pltpu
from jax.sharding import PartitionSpec as P

masked_score = -1e30
bf16, f32 = jnp.bfloat16, jnp.float32
in_vmem = pl.BlockSpec(memory_space=pltpu.VMEM)
in_smem = pl.BlockSpec(memory_space=pltpu.SMEM)
in_hbm = pl.BlockSpec(memory_space=pltpu.HBM)
mib = 1024 * 1024
prepare_mib = 16


def swap(value, axis, step):
    count = lax.axis_size(axis)
    return lax.ppermute(value, axis, [(i, i ^ step) for i in range(count)])


def pick(pieces, index):
    out = pieces[0]
    for k in range(1, len(pieces)):
        out = jnp.where(index == k, pieces[k], out)
    return out


def lane_tiles(width):
    return [slice(n, min(n + 128, width)) for n in range(0, width, 128)]


def packed_rows(rows, width):
    return rows * (width // 128) + rows // 2


def pack(value):
    rows, width = value.shape
    full = width // 128
    rest = value[:, full * 128 :]
    parts = [value[:, n * 128 : (n + 1) * 128] for n in range(full)]
    return parts + [jnp.concatenate([rest[: rows // 2], rest[rows // 2 :]], axis=1)]


def store_packed(ref, value):
    first = 0
    for part in pack(value):
        ref[first : first + part.shape[0], :] = part.astype(ref.dtype)
        first += part.shape[0]


def load_packed(ref, rows):
    full = ref.shape[0] // rows
    tiles = [ref[n * rows : (n + 1) * rows, :] for n in range(full)]
    rest = ref[full * rows :, :]
    return tiles, jnp.concatenate([rest[:, :64], rest[:, 64:]], axis=0)


def pack_kernel(value_ref, out_ref):
    store_packed(out_ref, value_ref[...])


def pack_weight(weight):
    rows, width = weight.shape
    return pl.pallas_call(
        pack_kernel,
        out_shape=jax.ShapeDtypeStruct((packed_rows(rows, width), 128), weight.dtype),
        in_specs=[in_vmem],
        out_specs=in_vmem,
        compiler_params=pltpu.CompilerParams(vmem_limit_bytes=8 * mib),
        cost_estimate=pl.CostEstimate(flops=10**10, bytes_accessed=10**6, transcendentals=0),
        name="pack_weight",
    )(weight)


def split_kernel(slab, prompts_ref, *refs):
    my_dev = lax.axis_index("dev")
    out_refs, sems = refs[:-1], refs[-1]
    copies = []
    for k in range(len(out_refs))[::-1]:
        first = pl.multiple_of((my_dev ^ k) * slab, 128)
        copies.append(
            pltpu.make_async_copy(prompts_ref.at[:, pl.ds(first, slab)], out_refs[k], sems.at[k])
        )
    for copy in copies:
        copy.start()
    for copy in copies:
        copy.wait()


def split_columns(prompts, count):
    rows, width = prompts.shape
    slab = width // count
    if slab % 128:
        columns = [prompts[:, k * slab : (k + 1) * slab] for k in range(count)]
        my_dev = lax.axis_index("dev")
        return [pick(columns, my_dev ^ k) for k in range(count)]
    return pl.pallas_call(
        functools.partial(split_kernel, slab),
        out_shape=[jax.ShapeDtypeStruct((rows, slab), prompts.dtype)] * count,
        in_specs=[in_hbm],
        out_specs=[in_vmem] * count,
        scratch_shapes=[pltpu.SemaphoreType.DMA((count,))],
        compiler_params=pltpu.CompilerParams(vmem_limit_bytes=8 * mib),
        cost_estimate=pl.CostEstimate(
            flops=10**10, bytes_accessed=4 * 10**7, transcendentals=0
        ),
        name="split_columns",
    )(pltpu.with_memory_space_constraint(prompts, pltpu.HBM))


def fill_tables(
    dev_count, side_count, bucket, cap_slots, length_ref, slot_ref, request_ref, inverse_ref,
    target_ref, cos_ref, sin_ref, spot_ref, to_ref, place_ref, local_ref, position_ref,
):
    my_dev, my_side = lax.axis_index("dev"), lax.axis_index("side")
    requests = request_ref[...]
    lane_rows, lanes = requests.shape
    tok_rows = bucket * dev_count // 2
    per_row = lanes // tok_rows
    half_bucket = bucket // 2
    half_rows = dev_count * half_bucket
    group_rows = 2 * half_rows
    before = lax.broadcasted_iota(jnp.int32, (lanes, lanes), 0)
    after = lax.broadcasted_iota(jnp.int32, (lanes, lanes), 1)
    below = jnp.where(before < after, 1.0, 0.0)
    near = jnp.where((before < after) & (before // tok_rows == after // tok_rows), 1.0, 0.0)
    scan = jnp.concatenate([below, jnp.ones_like(below)], axis=1).astype(bf16)
    lower = lax.broadcasted_iota(jnp.int32, (lane_rows, lane_rows), 0)
    upper = lax.broadcasted_iota(jnp.int32, (lane_rows, lane_rows), 1)
    rows_before = jnp.where(upper < lower, 1.0, 0.0)
    position = jnp.zeros(requests.shape, f32)
    slot = jnp.zeros(requests.shape, jnp.int32)
    for q in range(slot_ref.shape[0]):
        hit = requests == q
        ranks = jnp.dot(
            jnp.where(hit, 1.0, 0.0).astype(bf16), scan, preferred_element_type=f32
        )
        earlier = jnp.dot(rows_before, ranks[:, lanes:], preferred_element_type=f32)
        start = length_ref[q].astype(f32)
        position = jnp.where(hit, ranks[:, :lanes] + earlier + start, position)
        slot = jnp.where(hit, slot_ref[q], slot)
    group = lax.div(slot, cap_slots)
    rank = jnp.zeros(requests.shape, f32)
    for g in range(dev_count):
        hit = group == g
        ranks = jnp.dot(
            jnp.where(hit, 1.0, 0.0).astype(bf16), near.astype(bf16), preferred_element_type=f32
        )
        rank = jnp.where(hit, ranks, rank)
    block = lax.broadcasted_iota(jnp.int32, requests.shape, 0) * per_row + lax.div(
        lax.broadcasted_iota(jnp.int32, requests.shape, 1), tok_rows
    )
    rank = rank.astype(jnp.int32)
    which = lax.div(rank, half_bucket)
    place = lax.div(block, side_count) * half_bucket + lax.rem(rank, half_bucket)
    to_ref[...] = (which * dev_count + (group ^ my_dev)) * half_rows + place
    place = which * half_rows + place
    place_ref[...] = jnp.where(group == my_dev, place, -1)
    local_ref[...] = (slot - my_dev * cap_slots + 1).astype(f32)
    position_ref[...] = position
    lane_block = lax.div(lax.broadcasted_iota(jnp.int32, (1, lanes), 1), tok_rows)
    ids = lax.broadcasted_iota(jnp.int32, (group_rows, 1), 0)

    def find(dev, side):
        held = dev * side_count + side
        return pl.ds(lax.div(held, per_row), 1), lane_block == lax.rem(held, per_row)

    targets = []
    for k in range(dev_count):
        held = (my_dev ^ k) * side_count + my_side
        row = jnp.broadcast_to(to_ref[pl.ds(lax.div(held, per_row), 1), :], (8, lanes))
        start = lax.rem(lanes - tok_rows * lax.rem(held, per_row), lanes)
        targets.append(pltpu.roll(row, start, 1)[:1, :tok_rows])
    for k in range(0, dev_count, per_row):
        target_ref[:, k * tok_rows : k * tok_rows + lanes] = jnp.concatenate(
            targets[k : k + per_row], axis=1
        )
    found = jnp.zeros((group_rows, lanes), f32)
    for d in range(dev_count):
        row, inside = find(d, my_side)
        found = jnp.where((place_ref[row, :] == ids) & inside, position_ref[row, :], found)
    angles = jnp.sum(found, axis=1, keepdims=True) * inverse_ref[...]
    cos_ref[...] = jnp.cos(angles)
    sin_ref[...] = jnp.sin(angles)
    for k in range(side_count):
        total = jnp.zeros((8, group_rows), f32)
        for d in range(dev_count):
            row, inside = find(d, my_side ^ k)
            chosen = jnp.where((place_ref[row, :] == ids) & inside, 1.0, 0.0).astype(bf16)
            values = jnp.broadcast_to(local_ref[row, :], (8, lanes)).astype(bf16)
            total = total + lax.dot_general(
                values, chosen, (((1,), (1,)), ((), ())), preferred_element_type=f32
            )
        spot_ref[:, k * group_rows : (k + 1) * group_rows] = total[:1].astype(jnp.int32)


def prepare_kernel(
    scale, steps, layout, inverse_ref, length_hbm, slot_hbm, request_hbm, query_hbm, absorb_hbm,
    cache_hbm, fresh_hbm, value_hbm, out_hbm, full_ref, top_ref, sum_ref, mix_ref, live_ref, target_ref,
    cos_ref, sin_ref, spot_ref, value_ref, out_ref, length_ref, slot_ref, request_ref, query_ref,
    absorb_ref, cache_ref, fresh_ref, plain, full, to_ref, place_ref, local_ref, position_ref, sems,
):
    pairs = [
        (length_hbm, length_ref), (slot_hbm, slot_ref), (request_hbm, request_ref),
        (query_hbm, query_ref), (absorb_hbm, absorb_ref), (cache_hbm, cache_ref),
        (fresh_hbm, fresh_ref), (value_hbm, value_ref),
    ]
    parts = sems.shape[0] - len(pairs)
    rows = out_hbm.shape[0] // parts
    for n in range(parts):
        part = pl.ds(n * rows, rows)
        pairs.append((out_hbm.at[part], out_ref.at[part]))
    copies = [pltpu.make_async_copy(*pair, sems.at[n]) for n, pair in enumerate(pairs)]
    for copy in copies:
        copy.start()
    for copy in copies[:3]:
        copy.wait()
    slots, _, context = cache_ref.shape
    heads, nope, lat_width = absorb_ref.shape
    per_head = slots * steps
    fill_tables(
        *layout, slots, length_ref, slot_ref, request_ref, inverse_ref, target_ref, cos_ref,
        sin_ref, spot_ref, to_ref, place_ref, local_ref, position_ref,
    )
    first_slot = lax.axis_index("dev") * slots
    lengths = []
    for s in range(slots):
        length = jnp.int32(0)
        for q in range(slot_ref.shape[0]):
            length = jnp.where(slot_ref[q] == first_slot + s, length_ref[q], length)
        lengths.append(length)
    slot_of = lax.div(lax.broadcasted_iota(jnp.int32, live_ref.shape, 0), steps)
    live = jnp.zeros(live_ref.shape, f32)
    for s in range(slots):
        live = jnp.where((slot_of == s) & (lengths[s] > 0), 1.0, live)
    live_ref[...] = live
    copies[3].wait()
    copies[4].wait()
    for n, here in enumerate(lane_tiles(query_ref.shape[1])):
        plain[n, :, : here.stop - here.start] = query_ref[:, here].astype(f32)
    wide = lane_tiles(full_ref.shape[1])
    for h in range(heads):
        there = pl.ds(h, per_head, stride=heads)
        query = plain[0, there, :].astype(bf16)
        latent = jnp.dot(query, absorb_ref[h], preferred_element_type=f32).astype(bf16).astype(f32)
        here = slice(h * per_head, (h + 1) * per_head)
        for n, lanes in enumerate(lane_tiles(lat_width)):
            full[n, here, :] = latent[:, lanes]
        full[len(wide) - 1, here, :] = plain[1, there, :]
    for n, lanes in enumerate(wide):
        full_ref[:, lanes] = full[n, :, : lanes.stop - lanes.start].astype(bf16)
    key = lax.broadcasted_iota(jnp.int32, (1, context), 1)
    copies[5].wait()
    copies[6].wait()
    late = lax.broadcasted_iota(jnp.int32, (steps * heads, steps), 1)
    late = late > lax.div(lax.broadcasted_iota(jnp.int32, (steps * heads, steps), 0), heads)
    for s in range(slots):
        theres = [pl.ds(s * steps + t, heads, stride=per_head) for t in range(steps)]
        query = jnp.concatenate(
            [
                jnp.concatenate([full[n, there, :] for there in theres], axis=0)[
                    :, : lanes.stop - lanes.start
                ].astype(bf16)
                for n, lanes in enumerate(wide)
            ],
            axis=1,
        )
        rows = cache_ref[s]
        score = jnp.dot(query, rows, preferred_element_type=f32)
        score = jnp.where(key < lengths[s], score * scale, masked_score)
        fresh = fresh_ref[s]
        new = lax.dot_general(
            query, fresh, (((1,), (1,)), ((), ())), preferred_element_type=f32
        )
        new = jnp.where(late, masked_score, new * scale)
        top = jnp.maximum(
            jnp.max(score, axis=1, keepdims=True), jnp.max(new, axis=1, keepdims=True)
        )
        weight = jnp.exp(score - top)
        new = jnp.exp(new - top)
        total = jnp.sum(weight, axis=1, keepdims=True) + jnp.sum(new, axis=1, keepdims=True)
        mix = lax.dot_general(
            weight.astype(bf16), rows[:lat_width, :], (((1,), (1,)), ((), ())),
            preferred_element_type=f32,
        )
        for u in range(steps):
            mix = mix + new[:, u : u + 1].astype(bf16).astype(f32) * fresh[
                u : u + 1, :lat_width
            ].astype(f32)
        lanes = top_ref.shape[1]
        for t in range(steps):
            there = theres[t]
            here = slice(t * heads, (t + 1) * heads)
            top_ref[there, :] = jnp.broadcast_to(top[here], (heads, lanes))
            sum_ref[there, :] = jnp.broadcast_to(total[here], (heads, lanes))
            for n, part in enumerate(lane_tiles(lat_width)):
                mix_ref[n, there, :] = mix[here, part]
    for copy in copies[7:]:
        copy.wait()


def prepare(
    scale, dev_count, side_count, bucket, lengths, request_slot, requests, inverse, queries,
    absorb, cache, fresh, value, out_weight,
):
    slots, steps, heads, width = queries.shape
    kv_width = cache.shape[1]
    lat_width = absorb.shape[2]
    rows = slots * steps * heads
    group_rows = dev_count * bucket
    parts = 8
    lanes = requests.shape[1]
    half = inverse.shape[1]
    shapes = [
        ((rows, kv_width), bf16), ((rows, 128), f32), ((rows, 128), f32),
        ((lat_width // 128, rows, 128), f32), ((slots * steps, 128), f32),
        ((1, group_rows // 2 * dev_count), jnp.int32), ((group_rows, half), f32), ((group_rows, half), f32),
        ((1, side_count * group_rows), jnp.int32), (value.shape, bf16), (out_weight.shape, bf16),
    ]
    return pl.pallas_call(
        functools.partial(prepare_kernel, scale, steps, (dev_count, side_count, bucket)),
        out_shape=[jax.ShapeDtypeStruct(*shape) for shape in shapes],
        in_specs=[in_vmem] + [in_hbm] * 9,
        out_specs=[in_vmem] * len(shapes),
        scratch_shapes=[
            pltpu.SMEM(lengths.shape, lengths.dtype),
            pltpu.SMEM(request_slot.shape, request_slot.dtype),
            pltpu.VMEM(requests.shape, requests.dtype),
            pltpu.VMEM((rows, width), queries.dtype),
            pltpu.VMEM(absorb.shape, absorb.dtype),
            pltpu.VMEM(cache.shape, cache.dtype),
            pltpu.VMEM(fresh.shape, fresh.dtype),
            pltpu.VMEM((len(lane_tiles(width)), rows, 128), f32),
            pltpu.VMEM((len(lane_tiles(kv_width)), rows, 128), f32),
            pltpu.VMEM(requests.shape, jnp.int32),
            pltpu.VMEM(requests.shape, jnp.int32),
            pltpu.VMEM(requests.shape, f32),
            pltpu.VMEM(requests.shape, f32),
            pltpu.SemaphoreType.DMA((parts + 8,)),
        ],
        compiler_params=pltpu.CompilerParams(vmem_limit_bytes=prepare_mib * mib),
        cost_estimate=pl.CostEstimate(
            flops=4 * 10**10, bytes_accessed=28 * 10**6, transcendentals=10**5
        ),
        name="prepare",
    )(inverse, lengths, request_slot, requests, queries.reshape(rows, width), absorb, cache, fresh,
      value, out_weight)


def stack_kernel(*refs):
    out_ref = refs[-1]
    rows = refs[0].shape[0]
    for n, ref in enumerate(refs[:-1]):
        k = (len(refs) - 1 - n) % (len(refs) - 1)
        out_ref[k * rows : (k + 1) * rows, :] = ref[...]


def stack_rows(pieces):
    rows, width = pieces[0].shape
    return pl.pallas_call(
        stack_kernel,
        out_shape=jax.ShapeDtypeStruct((len(pieces) * rows, width), bf16),
        in_specs=[in_vmem] * len(pieces),
        out_specs=in_vmem,
        compiler_params=pltpu.CompilerParams(vmem_limit_bytes=8 * mib),
        cost_estimate=pl.CostEstimate(flops=2 * 10**10, bytes_accessed=10**6, transcendentals=0),
        name="stack_rows",
    )(pieces[0], *pieces[:0:-1])


def project_kernel(dev_count, side_count, target_ref, x_ref, *refs):
    my_side = lax.axis_index("side")
    weight_refs = refs[:side_count]
    out_refs = refs[side_count:-2]
    slab_weight, rows = refs[-2:]
    tok_rows = x_ref.shape[0] // dev_count
    full = slab_weight.shape[1] // 128
    if side_count > 1:
        shard = slab_weight.shape[0] // side_count
        for k in range(side_count):
            first = pl.multiple_of((my_side ^ k) * shard, 16)
            tiles, rest = load_packed(weight_refs[k], shard)
            for n, tile in enumerate(tiles):
                slab_weight[pl.ds(first, shard), n * 128 : (n + 1) * 128] = tile
            slab_weight[pl.ds(first, shard), full * 128 :] = rest
    slab = slab_weight[...] if side_count > 1 else weight_refs[0][...]
    raw = jnp.dot(x_ref[...], slab, preferred_element_type=f32).astype(bf16)
    rows[...] = raw
    target = target_ref[...]
    half_rows = tok_rows
    step = min(4, 2 * dev_count)
    for j in range(0, 2 * dev_count, step):
        ids = lax.broadcasted_iota(jnp.int32, (step * half_rows, target.shape[1]), 0)
        route = jnp.where(ids + j * half_rows == target, 1.0, 0.0).astype(bf16)
        placed = jnp.dot(route, rows[...], preferred_element_type=f32)
        for n in range(step):
            store_packed(out_refs[j + n], placed[n * half_rows : (n + 1) * half_rows])


def project(x_rows, weights, target, width, dev_count):
    tok_rows, slab = x_rows.shape[0] // dev_count, x_rows.shape[1]
    return pl.pallas_call(
        functools.partial(project_kernel, dev_count, len(weights)),
        out_shape=[
            jax.ShapeDtypeStruct(
                (packed_rows(tok_rows, width), 128), f32 if j % dev_count == 0 else bf16
            )
            for j in range(2 * dev_count)
        ],
        in_specs=[in_vmem] * (2 + len(weights)),
        out_specs=[in_vmem] * (2 * dev_count),
        scratch_shapes=[
            pltpu.VMEM((slab, width), bf16),
            pltpu.VMEM((target.shape[1], width), bf16),
        ],
        compiler_params=pltpu.CompilerParams(vmem_limit_bytes=20 * mib),
        name="project",
    )(target, x_rows, *weights)


def finish_kernel(which, gain_ref, cos_ref, sin_ref, *refs):
    parts, out_ref = refs[:-1], refs[-1]
    rows, half = cos_ref.shape[0] // 2, cos_ref.shape[1]
    mine = slice(which * rows, (which + 1) * rows)
    total = parts[0][...].astype(f32)
    for part in parts[1:]:
        total = total + part[...].astype(f32)
    tiles, rest = load_packed(total, rows)
    latent = jnp.concatenate(tiles, axis=1)
    spread = jnp.mean(latent * latent, axis=1, keepdims=True)
    latent = latent * lax.rsqrt(spread + 1e-06) * gain_ref[...]
    first, second = rest[:, :half], rest[:, half:]
    cosine, sine = cos_ref[mine, :], sin_ref[mine, :]
    store_packed(
        out_ref,
        jnp.concatenate(
            [latent, first * cosine - second * sine, second * cosine + first * sine], axis=1
        ),
    )


def finish(parts, gain, cosine, sine, which):
    return pl.pallas_call(
        functools.partial(finish_kernel, which),
        out_shape=jax.ShapeDtypeStruct(parts[0].shape, bf16),
        in_specs=[in_vmem] * (3 + len(parts)),
        out_specs=in_vmem,
        compiler_params=pltpu.CompilerParams(vmem_limit_bytes=8 * mib),
        name="finish_rows",
    )(gain, cosine, sine, *parts)


def take_keys(keys, pieces, lat_width):
    rows = keys.shape[0] // len(pieces)
    for n, piece in enumerate(pieces):
        tiles, rest = load_packed(piece, rows)
        there = slice(n * rows, (n + 1) * rows)
        for j, tile in enumerate(tiles):
            keys[there, j * 128 : (j + 1) * 128] = tile
        keys[there, lat_width:] = rest


def merge(layout, which, mine, query_ref, slot_ref, top_ref, sum_ref, mix_ref, keys):
    scale, cap_slots, steps, half_rows = layout
    lat_width = mix_ref.shape[0] * mix_ref.shape[2]
    row = lax.broadcasted_iota(jnp.int32, (mine.stop - mine.start, 1), 0)
    row_slot = (row // steps) % cap_slots
    query = query_ref[mine, :]
    score = lax.dot_general(
        query, keys[...], (((1,), (1,)), ((), ())), preferred_element_type=f32
    )
    count = slot_ref.shape[1]
    part = half_rows
    slots = jnp.concatenate(
        [slot_ref[:, n + which * part : n + (which + 1) * part] for n in range(0, count, 2 * part)],
        axis=1,
    )
    score = jnp.where(slots == row_slot + 1, score * scale, masked_score)
    top_held = top_ref[mine, :1]
    top = jnp.maximum(top_held, jnp.max(score, axis=1, keepdims=True))
    held = jnp.exp(top_held - top)
    weight = jnp.exp(score - top)
    total = sum_ref[mine, :1] * held + jnp.sum(weight, axis=1, keepdims=True)
    mix = jnp.dot(weight.astype(bf16), keys[:, :lat_width], preferred_element_type=f32)
    mix_held = jnp.concatenate([mix_ref[n, mine, :] for n in range(mix_ref.shape[0])], axis=1)
    return top, total, mix_held * held + mix


def absorb_kernel(layout, which, query_ref, slot_ref, top_ref, sum_ref, mix_ref, *refs):
    pieces, (new_top, new_sum, new_mix, keys) = refs[:-4], refs[-4:]
    take_keys(keys, pieces, mix_ref.shape[0] * mix_ref.shape[2])
    rows, lanes = top_ref.shape
    step = rows // 2
    for first in range(0, rows, step):
        mine = slice(first, first + step)
        top, total, mix = merge(
            layout, which, mine, query_ref, slot_ref, top_ref, sum_ref, mix_ref, keys
        )
        new_top[mine, :] = jnp.broadcast_to(top, (step, lanes))
        new_sum[mine, :] = jnp.broadcast_to(total, (step, lanes))
        for n, part in enumerate(lane_tiles(mix.shape[1])):
            new_mix[n, mine, :] = mix[:, part]


def absorb(layout, which, query, row_slot, top, total, mix, pieces):
    return pl.pallas_call(
        functools.partial(absorb_kernel, layout, which),
        out_shape=[jax.ShapeDtypeStruct(x.shape, f32) for x in (top, total, mix)],
        in_specs=[in_vmem] * (5 + len(pieces)),
        out_specs=[in_vmem] * 3,
        scratch_shapes=[pltpu.VMEM((row_slot.shape[1] // 2, query.shape[1]), bf16)],
        compiler_params=pltpu.CompilerParams(vmem_limit_bytes=10 * mib),
        cost_estimate=pl.CostEstimate(flops=2 * 10**9, bytes_accessed=10**6, transcendentals=0),
        name="absorb",
    )(query, row_slot, top, total, mix, *pieces)


def attend_kernel(
    layout, which, first_head, heads, query_ref, slot_ref, top_ref, sum_ref, mix_ref, live_ref,
    value_ref, *refs
):
    pieces, out_ref, keys = refs[:-2], refs[-2], refs[-1]
    per_head = layout[1] * layout[2]
    take_keys(keys, pieces, mix_ref.shape[0] * mix_ref.shape[2])
    mine = slice(first_head * per_head, (first_head + heads) * per_head)
    _, total, mix = merge(
        layout, which, mine, query_ref, slot_ref, top_ref, sum_ref, mix_ref, keys
    )
    latent = (mix / total).astype(bf16)
    live = live_ref[:, :1]
    width = value_ref.shape[2]
    for h in range(heads):
        mixed = latent[h * per_head : (h + 1) * per_head, :]
        value = jnp.dot(mixed, value_ref[first_head + h], preferred_element_type=f32) * live
        out_ref[:, h * width : (h + 1) * width] = value.astype(bf16)


def attend(layout, which, query, row_slot, top, total, mix, live, value, pieces, first_head, heads):
    return pl.pallas_call(
        functools.partial(attend_kernel, layout, which, first_head, heads),
        out_shape=jax.ShapeDtypeStruct((live.shape[0], heads * value.shape[2]), bf16),
        in_specs=[in_vmem] * (7 + len(pieces)),
        out_specs=in_vmem,
        scratch_shapes=[pltpu.VMEM((row_slot.shape[1] // 2, query.shape[1]), bf16)],
        compiler_params=pltpu.CompilerParams(vmem_limit_bytes=10 * mib),
        name="attend",
    )(query, row_slot, top, total, mix, live, value, *pieces)


def output_kernel(dev_count, side_count, start, last, *refs):
    my_dev, my_side = lax.axis_index("dev"), lax.axis_index("side")
    head_refs = refs[:dev_count]
    weight_ref = refs[dev_count]
    earlier_ref = refs[dev_count + 1] if start else None
    out_refs = refs[dev_count + 1 + (start > 0) : -1]
    held = refs[-1]
    rows, depth = head_refs[0].shape
    per_side = dev_count // side_count
    for j in range(dev_count):
        group = my_dev ^ j
        place = (lax.div(group, per_side) ^ my_side) * per_side + lax.rem(group, per_side)
        held[pl.ds(pl.multiple_of(place * rows, 16), rows), :] = head_refs[j][...]
    columns = weight_ref.shape[1]
    tile = 256 if columns % 256 == 0 else columns
    side_rows = rows * per_side
    for n in range(columns // tile):
        here = slice(n * tile, (n + 1) * tile)
        product = jnp.dot(
            held[...], weight_ref[start : start + depth, here],
            preferred_element_type=f32,
        )
        if start:
            product = product + earlier_ref[:, here]
        if not last:
            out_refs[0][:, here] = product
        else:
            for k in range(side_count):
                out_refs[k][:, here] = product[k * side_rows : (k + 1) * side_rows, :].astype(
                    out_refs[k].dtype
                )


def output_product(head_pieces, weight, side_count, earlier, start, last):
    dev_count = len(head_pieces)
    rows, depth = head_pieces[0].shape
    columns = weight.shape[1]
    side_rows = rows * dev_count // side_count
    if not last:
        shapes = [((rows * dev_count, columns), f32)]
    else:
        shapes = [((side_rows, columns), f32 if k == 0 else bf16) for k in range(side_count)]
    earlier = [] if earlier is None else [earlier]
    return pl.pallas_call(
        functools.partial(output_kernel, dev_count, side_count, start, last),
        out_shape=[jax.ShapeDtypeStruct(*shape) for shape in shapes],
        in_specs=[in_vmem] * (dev_count + 1 + len(earlier)),
        out_specs=[in_vmem] * len(shapes),
        scratch_shapes=[pltpu.VMEM((dev_count * rows, depth), bf16)],
        compiler_params=pltpu.CompilerParams(vmem_limit_bytes=10 * mib),
        name="output_product",
    )(*head_pieces, weight, *earlier)


def on_device(
    prompts,
    latent_weight,
    latent_gain,
    row_request,
    context_len,
    request_slot,
    latent_cache,
    new_latent,
    queries,
    key_absorb,
    value_absorb,
    out_weight,
):
    dev_count = lax.axis_size("dev")
    side_count = lax.axis_size("side")
    tok_rows, model_width = prompts.shape
    shard_rows, kv_width = latent_weight.shape
    lat_width = latent_gain.shape[0]
    nope_width = value_absorb.shape[2]
    rope_width = kv_width - lat_width
    cap_slots, ctx_len, _ = latent_cache.shape
    step_count = new_latent.shape[1]
    bucket_rows = 2 * tok_rows // dev_count
    group_rows = dev_count * bucket_rows
    slab = model_width // dev_count

    x_pieces = list(split_columns(prompts, dev_count))
    packs = shard_rows % 32 == 0
    x_pieces[0], own_weight = lax.optimization_barrier((x_pieces[0], latent_weight))
    weights = [pack_weight(own_weight) if packs else own_weight] + [None] * (side_count - 1)
    for k in range(2, side_count, 2):
        weights[k] = swap(weights[0], "side", k)
    for k in sorted(range(1, dev_count), reverse=True):
        x_pieces[k] = swap(x_pieces[k], "dev", k)

    score_scale = queries.shape[-1] ** (-0.5)
    half = rope_width // 2
    inverse = 1.0 / 10000.0 ** (jnp.arange(half, dtype=f32) * (2.0 / rope_width))
    lengths, x_pieces[0] = lax.optimization_barrier((context_len, x_pieces[0]))
    (
        query_full, top_held, sum_held, mix_held, live, target, cosine, sine, row_slot,
        value_here, out_here,
    ) = prepare(
        score_scale, dev_count, side_count, bucket_rows, lengths, request_slot,
        row_request.reshape(-1, 128), inverse.reshape(1, -1), queries, key_absorb,
        jnp.swapaxes(latent_cache, 1, 2), new_latent, value_absorb, out_weight,
    )

    weights[0::2], top_held = lax.optimization_barrier((weights[0::2], top_held))
    for k in range(0, side_count, 2):
        weights[k + 1] = swap(weights[k], "side", 1)
    if not packs:
        my_side = lax.axis_index("side")
        held = jnp.zeros((side_count, shard_rows, kv_width), bf16)
        for k in range(side_count):
            held = lax.dynamic_update_slice(held, weights[k][None], (my_side ^ k, 0, 0))
        weights = [held.reshape(slab, kv_width)]

    routed = project(stack_rows(x_pieces), weights, target, kv_width, dev_count)
    layout = (score_scale, cap_slots, step_count, group_rows // 2)
    state = top_held, sum_held, mix_held
    for which in range(2):
        half = list(routed[which * dev_count : (which + 1) * dev_count])
        for k in sorted(range(1, dev_count), reverse=True):
            half[k] = swap(half[k], "dev", k)
        latent_rows = finish(half[:1] + half[:0:-1], latent_gain.reshape(1, -1), cosine, sine, which)
        pieces = [latent_rows] + [swap(latent_rows, "side", k) for k in range(1, side_count)]
        if which == 0:
            state = absorb(layout, which, query_full, row_slot, *state, pieces)
    product, first_head, head_count = None, 0, value_absorb.shape[0]
    for part_heads in (head_count * 5 // 8, head_count * 3 // 8):
        head_out = attend(
            layout, 1, query_full, row_slot, *state, live, value_here, pieces, first_head,
            part_heads,
        )
        heads = [head_out] + [None] * (dev_count - 1)
        for k in sorted(range(1, dev_count), reverse=True):
            if k == 1 or k % 2 == 0:
                heads[k] = swap(head_out, "dev", k)
        for k in range(3, dev_count, 2):
            heads[k] = swap(heads[k - 1], "dev", 1)
        start, first_head = first_head * nope_width, first_head + part_heads
        products = output_product(
            heads, out_here, side_count, product, start, first_head == head_count
        )
        product = products[0]
    result = products[0]
    for k in sorted(range(1, side_count), reverse=True):
        result = result + swap(products[k], "side", k).astype(f32)
    return result.astype(bf16)


def solution(mesh):
    placed = (
        P(("rep", "dev", "side"), None),
        P(("dev", "side"), None),
        P(),
        P("rep"),
        P("rep"),
        P("rep"),
        P(("rep", "dev"), None, None),
        P(("rep", "dev"), None, None),
        P(("rep", "dev"), None, "side", None),
        P("side", None, None),
        P("side", None, None),
        P("side", "dev"),
    )
    return jax.shard_map(
        on_device, mesh=mesh, in_specs=placed, out_specs=P(("rep", "side"), "dev"), check_vma=False
    )
```

```python
import functools

import jax
import jax.numpy as jnp
from jax import lax
from jax.experimental import pallas as pl
from jax.experimental.pallas import tpu as pltpu
from jax.sharding import PartitionSpec as P

masked_score = -1e30
bf16, f32 = jnp.bfloat16, jnp.float32
in_vmem = pl.BlockSpec(memory_space=pltpu.VMEM)
in_smem = pl.BlockSpec(memory_space=pltpu.SMEM)
in_hbm = pl.BlockSpec(memory_space=pltpu.HBM)
mib = 1024 * 1024
prepare_mib = 16


def swap(value, axis, step):
    count = lax.axis_size(axis)
    return lax.ppermute(value, axis, [(i, i ^ step) for i in range(count)])


def pick(pieces, index):
    out = pieces[0]
    for k in range(1, len(pieces)):
        out = jnp.where(index == k, pieces[k], out)
    return out


def lane_tiles(width):
    return [slice(n, min(n + 128, width)) for n in range(0, width, 128)]


def packed_rows(rows, width):
    return rows * (width // 128) + rows // 2


def pack(value):
    rows, width = value.shape
    full = width // 128
    rest = value[:, full * 128 :]
    parts = [value[:, n * 128 : (n + 1) * 128] for n in range(full)]
    return parts + [jnp.concatenate([rest[: rows // 2], rest[rows // 2 :]], axis=1)]


def store_packed(ref, value):
    first = 0
    for part in pack(value):
        ref[first : first + part.shape[0], :] = part.astype(ref.dtype)
        first += part.shape[0]


def load_packed(ref, rows):
    full = ref.shape[0] // rows
    tiles = [ref[n * rows : (n + 1) * rows, :] for n in range(full)]
    rest = ref[full * rows :, :]
    return tiles, jnp.concatenate([rest[:, :64], rest[:, 64:]], axis=0)


def pack_kernel(value_ref, out_ref):
    store_packed(out_ref, value_ref[...])


def pack_weight(weight):
    rows, width = weight.shape
    return pl.pallas_call(
        pack_kernel,
        out_shape=jax.ShapeDtypeStruct((packed_rows(rows, width), 128), weight.dtype),
        in_specs=[in_vmem],
        out_specs=in_vmem,
        compiler_params=pltpu.CompilerParams(vmem_limit_bytes=8 * mib),
        cost_estimate=pl.CostEstimate(flops=10**10, bytes_accessed=10**6, transcendentals=0),
        name="pack_weight",
    )(weight)


def split_kernel(slab, prompts_ref, *refs):
    my_dev = lax.axis_index("dev")
    out_refs, sems = refs[:-1], refs[-1]
    copies = []
    for k in range(len(out_refs))[::-1]:
        first = pl.multiple_of((my_dev ^ k) * slab, 128)
        copies.append(
            pltpu.make_async_copy(prompts_ref.at[:, pl.ds(first, slab)], out_refs[k], sems.at[k])
        )
    for copy in copies:
        copy.start()
    for copy in copies:
        copy.wait()


def split_columns(prompts, count):
    rows, width = prompts.shape
    slab = width // count
    if slab % 128:
        columns = [prompts[:, k * slab : (k + 1) * slab] for k in range(count)]
        my_dev = lax.axis_index("dev")
        return [pick(columns, my_dev ^ k) for k in range(count)]
    return pl.pallas_call(
        functools.partial(split_kernel, slab),
        out_shape=[jax.ShapeDtypeStruct((rows, slab), prompts.dtype)] * count,
        in_specs=[in_hbm],
        out_specs=[in_vmem] * count,
        scratch_shapes=[pltpu.SemaphoreType.DMA((count,))],
        compiler_params=pltpu.CompilerParams(vmem_limit_bytes=8 * mib),
        cost_estimate=pl.CostEstimate(
            flops=10**10, bytes_accessed=4 * 10**7, transcendentals=0
        ),
        name="split_columns",
    )(pltpu.with_memory_space_constraint(prompts, pltpu.HBM))


def fill_tables(
    dev_count, side_count, bucket, cap_slots, length_ref, slot_ref, request_ref, inverse_ref,
    target_ref, cos_ref, sin_ref, spot_ref, to_ref, place_ref, local_ref, position_ref,
):
    my_dev, my_side = lax.axis_index("dev"), lax.axis_index("side")
    requests = request_ref[...]
    lane_rows, lanes = requests.shape
    tok_rows = bucket * dev_count // 2
    per_row = lanes // tok_rows
    half_bucket = bucket // 2
    half_rows = dev_count * half_bucket
    group_rows = 2 * half_rows
    before = lax.broadcasted_iota(jnp.int32, (lanes, lanes), 0)
    after = lax.broadcasted_iota(jnp.int32, (lanes, lanes), 1)
    below = jnp.where(before < after, 1.0, 0.0)
    near = jnp.where((before < after) & (before // tok_rows == after // tok_rows), 1.0, 0.0)
    scan = jnp.concatenate([below, jnp.ones_like(below)], axis=1).astype(bf16)
    lower = lax.broadcasted_iota(jnp.int32, (lane_rows, lane_rows), 0)
    upper = lax.broadcasted_iota(jnp.int32, (lane_rows, lane_rows), 1)
    rows_before = jnp.where(upper < lower, 1.0, 0.0)
    position = jnp.zeros(requests.shape, f32)
    slot = jnp.zeros(requests.shape, jnp.int32)
    for q in range(slot_ref.shape[0]):
        hit = requests == q
        ranks = jnp.dot(
            jnp.where(hit, 1.0, 0.0).astype(bf16), scan, preferred_element_type=f32
        )
        earlier = jnp.dot(rows_before, ranks[:, lanes:], preferred_element_type=f32)
        start = length_ref[q].astype(f32)
        position = jnp.where(hit, ranks[:, :lanes] + earlier + start, position)
        slot = jnp.where(hit, slot_ref[q], slot)
    group = lax.div(slot, cap_slots)
    rank = jnp.zeros(requests.shape, f32)
    for g in range(dev_count):
        hit = group == g
        ranks = jnp.dot(
            jnp.where(hit, 1.0, 0.0).astype(bf16), near.astype(bf16), preferred_element_type=f32
        )
        rank = jnp.where(hit, ranks, rank)
    block = lax.broadcasted_iota(jnp.int32, requests.shape, 0) * per_row + lax.div(
        lax.broadcasted_iota(jnp.int32, requests.shape, 1), tok_rows
    )
    rank = rank.astype(jnp.int32)
    which = lax.div(rank, half_bucket)
    place = lax.div(block, side_count) * half_bucket + lax.rem(rank, half_bucket)
    to_ref[...] = (which * dev_count + (group ^ my_dev)) * half_rows + place
    place = which * half_rows + place
    place_ref[...] = jnp.where(group == my_dev, place, -1)
    local_ref[...] = (slot - my_dev * cap_slots + 1).astype(f32)
    position_ref[...] = position
    lane_block = lax.div(lax.broadcasted_iota(jnp.int32, (1, lanes), 1), tok_rows)
    ids = lax.broadcasted_iota(jnp.int32, (group_rows, 1), 0)

    def find(dev, side):
        held = dev * side_count + side
        return pl.ds(lax.div(held, per_row), 1), lane_block == lax.rem(held, per_row)

    targets = []
    for k in range(dev_count):
        held = (my_dev ^ k) * side_count + my_side
        row = jnp.broadcast_to(to_ref[pl.ds(lax.div(held, per_row), 1), :], (8, lanes))
        start = lax.rem(lanes - tok_rows * lax.rem(held, per_row), lanes)
        targets.append(pltpu.roll(row, start, 1)[:1, :tok_rows])
    for k in range(0, dev_count, per_row):
        target_ref[:, k * tok_rows : k * tok_rows + lanes] = jnp.concatenate(
            targets[k : k + per_row], axis=1
        )
    found = jnp.zeros((group_rows, lanes), f32)
    for d in range(dev_count):
        row, inside = find(d, my_side)
        found = jnp.where((place_ref[row, :] == ids) & inside, position_ref[row, :], found)
    angles = jnp.sum(found, axis=1, keepdims=True) * inverse_ref[...]
    cos_ref[...] = jnp.cos(angles)
    sin_ref[...] = jnp.sin(angles)
    for k in range(side_count):
        total = jnp.zeros((8, group_rows), f32)
        for d in range(dev_count):
            row, inside = find(d, my_side ^ k)
            chosen = jnp.where((place_ref[row, :] == ids) & inside, 1.0, 0.0).astype(bf16)
            values = jnp.broadcast_to(local_ref[row, :], (8, lanes)).astype(bf16)
            total = total + lax.dot_general(
                values, chosen, (((1,), (1,)), ((), ())), preferred_element_type=f32
            )
        spot_ref[:, k * group_rows : (k + 1) * group_rows] = total[:1].astype(jnp.int32)


def prepare_kernel(
    scale, steps, layout, inverse_ref, length_hbm, slot_hbm, request_hbm, query_hbm, absorb_hbm,
    cache_hbm, fresh_hbm, value_hbm, out_hbm, full_ref, top_ref, sum_ref, mix_ref, live_ref, target_ref,
    cos_ref, sin_ref, spot_ref, value_ref, out_ref, length_ref, slot_ref, request_ref, query_ref,
    absorb_ref, cache_ref, fresh_ref, plain, full, to_ref, place_ref, local_ref, position_ref, sems,
):
    pairs = [
        (length_hbm, length_ref), (slot_hbm, slot_ref), (request_hbm, request_ref),
        (query_hbm, query_ref), (absorb_hbm, absorb_ref), (cache_hbm, cache_ref),
        (fresh_hbm, fresh_ref), (value_hbm, value_ref),
    ]
    parts = sems.shape[0] - len(pairs)
    rows = out_hbm.shape[0] // parts
    for n in range(parts):
        part = pl.ds(n * rows, rows)
        pairs.append((out_hbm.at[part], out_ref.at[part]))
    copies = [pltpu.make_async_copy(*pair, sems.at[n]) for n, pair in enumerate(pairs)]
    for copy in copies:
        copy.start()
    for copy in copies[:3]:
        copy.wait()
    slots, _, context = cache_ref.shape
    heads, nope, lat_width = absorb_ref.shape
    per_head = slots * steps
    fill_tables(
        *layout, slots, length_ref, slot_ref, request_ref, inverse_ref, target_ref, cos_ref,
        sin_ref, spot_ref, to_ref, place_ref, local_ref, position_ref,
    )
    first_slot = lax.axis_index("dev") * slots
    lengths = []
    for s in range(slots):
        length = jnp.int32(0)
        for q in range(slot_ref.shape[0]):
            length = jnp.where(slot_ref[q] == first_slot + s, length_ref[q], length)
        lengths.append(length)
    slot_of = lax.div(lax.broadcasted_iota(jnp.int32, live_ref.shape, 0), steps)
    live = jnp.zeros(live_ref.shape, f32)
    for s in range(slots):
        live = jnp.where((slot_of == s) & (lengths[s] > 0), 1.0, live)
    live_ref[...] = live
    copies[3].wait()
    copies[4].wait()
    for n, here in enumerate(lane_tiles(query_ref.shape[1])):
        plain[n, :, : here.stop - here.start] = query_ref[:, here].astype(f32)
    wide = lane_tiles(full_ref.shape[1])
    for h in range(heads):
        there = pl.ds(h, per_head, stride=heads)
        query = plain[0, there, :].astype(bf16)
        latent = jnp.dot(query, absorb_ref[h], preferred_element_type=f32).astype(bf16).astype(f32)
        here = slice(h * per_head, (h + 1) * per_head)
        for n, lanes in enumerate(lane_tiles(lat_width)):
            full[n, here, :] = latent[:, lanes]
        full[len(wide) - 1, here, :] = plain[1, there, :]
    for n, lanes in enumerate(wide):
        full_ref[:, lanes] = full[n, :, : lanes.stop - lanes.start].astype(bf16)
    key = lax.broadcasted_iota(jnp.int32, (1, context), 1)
    copies[5].wait()
    copies[6].wait()
    late = lax.broadcasted_iota(jnp.int32, (steps * heads, steps), 1)
    late = late > lax.div(lax.broadcasted_iota(jnp.int32, (steps * heads, steps), 0), heads)
    for s in range(slots):
        theres = [pl.ds(s * steps + t, heads, stride=per_head) for t in range(steps)]
        query = jnp.concatenate(
            [
                jnp.concatenate([full[n, there, :] for there in theres], axis=0)[
                    :, : lanes.stop - lanes.start
                ].astype(bf16)
                for n, lanes in enumerate(wide)
            ],
            axis=1,
        )
        rows = cache_ref[s]
        score = jnp.dot(query, rows, preferred_element_type=f32)
        score = jnp.where(key < lengths[s], score * scale, masked_score)
        fresh = fresh_ref[s]
        new = lax.dot_general(
            query, fresh, (((1,), (1,)), ((), ())), preferred_element_type=f32
        )
        new = jnp.where(late, masked_score, new * scale)
        top = jnp.maximum(
            jnp.max(score, axis=1, keepdims=True), jnp.max(new, axis=1, keepdims=True)
        )
        weight = jnp.exp(score - top)
        new = jnp.exp(new - top)
        total = jnp.sum(weight, axis=1, keepdims=True) + jnp.sum(new, axis=1, keepdims=True)
        mix = lax.dot_general(
            weight.astype(bf16), rows[:lat_width, :], (((1,), (1,)), ((), ())),
            preferred_element_type=f32,
        )
        for u in range(steps):
            mix = mix + new[:, u : u + 1].astype(bf16).astype(f32) * fresh[
                u : u + 1, :lat_width
            ].astype(f32)
        lanes = top_ref.shape[1]
        for t in range(steps):
            there = theres[t]
            here = slice(t * heads, (t + 1) * heads)
            top_ref[there, :] = jnp.broadcast_to(top[here], (heads, lanes))
            sum_ref[there, :] = jnp.broadcast_to(total[here], (heads, lanes))
            for n, part in enumerate(lane_tiles(lat_width)):
                mix_ref[n, there, :] = mix[here, part]
    for copy in copies[7:]:
        copy.wait()


def prepare(
    scale, dev_count, side_count, bucket, lengths, request_slot, requests, inverse, queries,
    absorb, cache, fresh, value, out_weight,
):
    slots, steps, heads, width = queries.shape
    kv_width = cache.shape[1]
    lat_width = absorb.shape[2]
    rows = slots * steps * heads
    group_rows = dev_count * bucket
    parts = 8
    lanes = requests.shape[1]
    half = inverse.shape[1]
    shapes = [
        ((rows, kv_width), bf16), ((rows, 128), f32), ((rows, 128), f32),
        ((lat_width // 128, rows, 128), f32), ((slots * steps, 128), f32),
        ((1, group_rows // 2 * dev_count), jnp.int32), ((group_rows, half), f32), ((group_rows, half), f32),
        ((1, side_count * group_rows), jnp.int32), (value.shape, bf16), (out_weight.shape, bf16),
    ]
    return pl.pallas_call(
        functools.partial(prepare_kernel, scale, steps, (dev_count, side_count, bucket)),
        out_shape=[jax.ShapeDtypeStruct(*shape) for shape in shapes],
        in_specs=[in_vmem] + [in_hbm] * 9,
        out_specs=[in_vmem] * len(shapes),
        scratch_shapes=[
            pltpu.SMEM(lengths.shape, lengths.dtype),
            pltpu.SMEM(request_slot.shape, request_slot.dtype),
            pltpu.VMEM(requests.shape, requests.dtype),
            pltpu.VMEM((rows, width), queries.dtype),
            pltpu.VMEM(absorb.shape, absorb.dtype),
            pltpu.VMEM(cache.shape, cache.dtype),
            pltpu.VMEM(fresh.shape, fresh.dtype),
            pltpu.VMEM((len(lane_tiles(width)), rows, 128), f32),
            pltpu.VMEM((len(lane_tiles(kv_width)), rows, 128), f32),
            pltpu.VMEM(requests.shape, jnp.int32),
            pltpu.VMEM(requests.shape, jnp.int32),
            pltpu.VMEM(requests.shape, f32),
            pltpu.VMEM(requests.shape, f32),
            pltpu.SemaphoreType.DMA((parts + 8,)),
        ],
        compiler_params=pltpu.CompilerParams(vmem_limit_bytes=prepare_mib * mib),
        cost_estimate=pl.CostEstimate(
            flops=4 * 10**10, bytes_accessed=28 * 10**6, transcendentals=10**5
        ),
        name="prepare",
    )(inverse, lengths, request_slot, requests, queries.reshape(rows, width), absorb, cache, fresh,
      value, out_weight)


def stack_kernel(*refs):
    out_ref = refs[-1]
    rows = refs[0].shape[0]
    for n, ref in enumerate(refs[:-1]):
        k = (len(refs) - 1 - n) % (len(refs) - 1)
        out_ref[k * rows : (k + 1) * rows, :] = ref[...]


def stack_rows(pieces):
    rows, width = pieces[0].shape
    return pl.pallas_call(
        stack_kernel,
        out_shape=jax.ShapeDtypeStruct((len(pieces) * rows, width), bf16),
        in_specs=[in_vmem] * len(pieces),
        out_specs=in_vmem,
        compiler_params=pltpu.CompilerParams(vmem_limit_bytes=8 * mib),
        cost_estimate=pl.CostEstimate(flops=2 * 10**10, bytes_accessed=10**6, transcendentals=0),
        name="stack_rows",
    )(pieces[0], *pieces[:0:-1])


def project_kernel(dev_count, side_count, target_ref, x_ref, *refs):
    my_side = lax.axis_index("side")
    weight_refs = refs[:side_count]
    out_refs = refs[side_count:-2]
    slab_weight, rows = refs[-2:]
    tok_rows = x_ref.shape[0] // dev_count
    full = slab_weight.shape[1] // 128
    if side_count > 1:
        shard = slab_weight.shape[0] // side_count
        for k in range(side_count):
            first = pl.multiple_of((my_side ^ k) * shard, 16)
            tiles, rest = load_packed(weight_refs[k], shard)
            for n, tile in enumerate(tiles):
                slab_weight[pl.ds(first, shard), n * 128 : (n + 1) * 128] = tile
            slab_weight[pl.ds(first, shard), full * 128 :] = rest
    slab = slab_weight[...] if side_count > 1 else weight_refs[0][...]
    raw = jnp.dot(x_ref[...], slab, preferred_element_type=f32).astype(bf16)
    rows[...] = raw
    target = target_ref[...]
    half_rows = tok_rows
    step = min(4, 2 * dev_count)
    for j in range(0, 2 * dev_count, step):
        ids = lax.broadcasted_iota(jnp.int32, (step * half_rows, target.shape[1]), 0)
        route = jnp.where(ids + j * half_rows == target, 1.0, 0.0).astype(bf16)
        placed = jnp.dot(route, rows[...], preferred_element_type=f32)
        for n in range(step):
            store_packed(out_refs[j + n], placed[n * half_rows : (n + 1) * half_rows])


def project(x_rows, weights, target, width, dev_count):
    tok_rows, slab = x_rows.shape[0] // dev_count, x_rows.shape[1]
    return pl.pallas_call(
        functools.partial(project_kernel, dev_count, len(weights)),
        out_shape=[
            jax.ShapeDtypeStruct(
                (packed_rows(tok_rows, width), 128), f32 if j % dev_count == 0 else bf16
            )
            for j in range(2 * dev_count)
        ],
        in_specs=[in_vmem] * (2 + len(weights)),
        out_specs=[in_vmem] * (2 * dev_count),
        scratch_shapes=[
            pltpu.VMEM((slab, width), bf16),
            pltpu.VMEM((target.shape[1], width), bf16),
        ],
        compiler_params=pltpu.CompilerParams(vmem_limit_bytes=20 * mib),
        name="project",
    )(target, x_rows, *weights)


def finish_kernel(which, gain_ref, cos_ref, sin_ref, *refs):
    parts, out_ref = refs[:-1], refs[-1]
    rows, half = cos_ref.shape[0] // 2, cos_ref.shape[1]
    mine = slice(which * rows, (which + 1) * rows)
    total = parts[0][...].astype(f32)
    for part in parts[1:]:
        total = total + part[...].astype(f32)
    tiles, rest = load_packed(total, rows)
    latent = jnp.concatenate(tiles, axis=1)
    spread = jnp.mean(latent * latent, axis=1, keepdims=True)
    latent = latent * lax.rsqrt(spread + 1e-06) * gain_ref[...]
    first, second = rest[:, :half], rest[:, half:]
    cosine, sine = cos_ref[mine, :], sin_ref[mine, :]
    store_packed(
        out_ref,
        jnp.concatenate(
            [latent, first * cosine - second * sine, second * cosine + first * sine], axis=1
        ),
    )


def finish(parts, gain, cosine, sine, which):
    return pl.pallas_call(
        functools.partial(finish_kernel, which),
        out_shape=jax.ShapeDtypeStruct(parts[0].shape, bf16),
        in_specs=[in_vmem] * (3 + len(parts)),
        out_specs=in_vmem,
        compiler_params=pltpu.CompilerParams(vmem_limit_bytes=8 * mib),
        name="finish_rows",
    )(gain, cosine, sine, *parts)


def take_keys(keys, pieces, lat_width):
    rows = keys.shape[0] // len(pieces)
    for n, piece in enumerate(pieces):
        tiles, rest = load_packed(piece, rows)
        there = slice(n * rows, (n + 1) * rows)
        for j, tile in enumerate(tiles):
            keys[there, j * 128 : (j + 1) * 128] = tile
        keys[there, lat_width:] = rest


def merge(layout, which, mine, query_ref, slot_ref, top_ref, sum_ref, mix_ref, keys):
    scale, cap_slots, steps, half_rows = layout
    lat_width = mix_ref.shape[0] * mix_ref.shape[2]
    row = lax.broadcasted_iota(jnp.int32, (mine.stop - mine.start, 1), 0)
    row_slot = (row // steps) % cap_slots
    query = query_ref[mine, :]
    score = lax.dot_general(
        query, keys[...], (((1,), (1,)), ((), ())), preferred_element_type=f32
    )
    count = slot_ref.shape[1]
    part = half_rows
    slots = jnp.concatenate(
        [slot_ref[:, n + which * part : n + (which + 1) * part] for n in range(0, count, 2 * part)],
        axis=1,
    )
    score = jnp.where(slots == row_slot + 1, score * scale, masked_score)
    top_held = top_ref[mine, :1]
    top = jnp.maximum(top_held, jnp.max(score, axis=1, keepdims=True))
    held = jnp.exp(top_held - top)
    weight = jnp.exp(score - top)
    total = sum_ref[mine, :1] * held + jnp.sum(weight, axis=1, keepdims=True)
    mix = jnp.dot(weight.astype(bf16), keys[:, :lat_width], preferred_element_type=f32)
    mix_held = jnp.concatenate([mix_ref[n, mine, :] for n in range(mix_ref.shape[0])], axis=1)
    return top, total, mix_held * held + mix


def absorb_kernel(layout, which, query_ref, slot_ref, top_ref, sum_ref, mix_ref, *refs):
    pieces, (new_top, new_sum, new_mix, keys) = refs[:-4], refs[-4:]
    take_keys(keys, pieces, mix_ref.shape[0] * mix_ref.shape[2])
    rows, lanes = top_ref.shape
    step = rows // 2
    for first in range(0, rows, step):
        mine = slice(first, first + step)
        top, total, mix = merge(
            layout, which, mine, query_ref, slot_ref, top_ref, sum_ref, mix_ref, keys
        )
        new_top[mine, :] = jnp.broadcast_to(top, (step, lanes))
        new_sum[mine, :] = jnp.broadcast_to(total, (step, lanes))
        for n, part in enumerate(lane_tiles(mix.shape[1])):
            new_mix[n, mine, :] = mix[:, part]


def absorb(layout, which, query, row_slot, top, total, mix, pieces):
    return pl.pallas_call(
        functools.partial(absorb_kernel, layout, which),
        out_shape=[jax.ShapeDtypeStruct(x.shape, f32) for x in (top, total, mix)],
        in_specs=[in_vmem] * (5 + len(pieces)),
        out_specs=[in_vmem] * 3,
        scratch_shapes=[pltpu.VMEM((row_slot.shape[1] // 2, query.shape[1]), bf16)],
        compiler_params=pltpu.CompilerParams(vmem_limit_bytes=10 * mib),
        cost_estimate=pl.CostEstimate(flops=2 * 10**9, bytes_accessed=10**6, transcendentals=0),
        name="absorb",
    )(query, row_slot, top, total, mix, *pieces)


def attend_kernel(
    layout, which, first_head, heads, query_ref, slot_ref, top_ref, sum_ref, mix_ref, live_ref,
    value_ref, *refs
):
    pieces, out_ref, keys = refs[:-2], refs[-2], refs[-1]
    per_head = layout[1] * layout[2]
    take_keys(keys, pieces, mix_ref.shape[0] * mix_ref.shape[2])
    mine = slice(first_head * per_head, (first_head + heads) * per_head)
    _, total, mix = merge(
        layout, which, mine, query_ref, slot_ref, top_ref, sum_ref, mix_ref, keys
    )
    latent = (mix / total).astype(bf16)
    live = live_ref[:, :1]
    width = value_ref.shape[2]
    for h in range(heads):
        mixed = latent[h * per_head : (h + 1) * per_head, :]
        value = jnp.dot(mixed, value_ref[first_head + h], preferred_element_type=f32) * live
        out_ref[:, h * width : (h + 1) * width] = value.astype(bf16)


def attend(layout, which, query, row_slot, top, total, mix, live, value, pieces, first_head, heads):
    return pl.pallas_call(
        functools.partial(attend_kernel, layout, which, first_head, heads),
        out_shape=jax.ShapeDtypeStruct((live.shape[0], heads * value.shape[2]), bf16),
        in_specs=[in_vmem] * (7 + len(pieces)),
        out_specs=in_vmem,
        scratch_shapes=[pltpu.VMEM((row_slot.shape[1] // 2, query.shape[1]), bf16)],
        compiler_params=pltpu.CompilerParams(vmem_limit_bytes=10 * mib),
        name="attend",
    )(query, row_slot, top, total, mix, live, value, *pieces)


def output_kernel(dev_count, side_count, start, last, *refs):
    my_dev, my_side = lax.axis_index("dev"), lax.axis_index("side")
    head_refs = refs[:dev_count]
    weight_ref = refs[dev_count]
    earlier_ref = refs[dev_count + 1] if start else None
    out_refs = refs[dev_count + 1 + (start > 0) : -1]
    held = refs[-1]
    rows, depth = head_refs[0].shape
    per_side = dev_count // side_count
    for j in range(dev_count):
        group = my_dev ^ j
        place = (lax.div(group, per_side) ^ my_side) * per_side + lax.rem(group, per_side)
        held[pl.ds(pl.multiple_of(place * rows, 16), rows), :] = head_refs[j][...]
    columns = weight_ref.shape[1]
    tile = 256 if columns % 256 == 0 else columns
    side_rows = rows * per_side
    for n in range(columns // tile):
        here = slice(n * tile, (n + 1) * tile)
        product = jnp.dot(
            held[...], weight_ref[start : start + depth, here],
            preferred_element_type=f32,
        )
        if start:
            product = product + earlier_ref[:, here]
        if not last:
            out_refs[0][:, here] = product
        else:
            for k in range(side_count):
                out_refs[k][:, here] = product[k * side_rows : (k + 1) * side_rows, :].astype(
                    out_refs[k].dtype
                )


def output_product(head_pieces, weight, side_count, earlier, start, last):
    dev_count = len(head_pieces)
    rows, depth = head_pieces[0].shape
    columns = weight.shape[1]
    side_rows = rows * dev_count // side_count
    if not last:
        shapes = [((rows * dev_count, columns), f32)]
    else:
        shapes = [((side_rows, columns), f32 if k == 0 else bf16) for k in range(side_count)]
    earlier = [] if earlier is None else [earlier]
    return pl.pallas_call(
        functools.partial(output_kernel, dev_count, side_count, start, last),
        out_shape=[jax.ShapeDtypeStruct(*shape) for shape in shapes],
        in_specs=[in_vmem] * (dev_count + 1 + len(earlier)),
        out_specs=[in_vmem] * len(shapes),
        scratch_shapes=[pltpu.VMEM((dev_count * rows, depth), bf16)],
        compiler_params=pltpu.CompilerParams(vmem_limit_bytes=10 * mib),
        name="output_product",
    )(*head_pieces, weight, *earlier)


def on_device(
    prompts,
    latent_weight,
    latent_gain,
    row_request,
    context_len,
    request_slot,
    latent_cache,
    new_latent,
    queries,
    key_absorb,
    value_absorb,
    out_weight,
):
    dev_count = lax.axis_size("dev")
    side_count = lax.axis_size("side")
    tok_rows, model_width = prompts.shape
    shard_rows, kv_width = latent_weight.shape
    lat_width = latent_gain.shape[0]
    nope_width = value_absorb.shape[2]
    rope_width = kv_width - lat_width
    cap_slots, ctx_len, _ = latent_cache.shape
    step_count = new_latent.shape[1]
    bucket_rows = 2 * tok_rows // dev_count
    group_rows = dev_count * bucket_rows
    slab = model_width // dev_count

    x_pieces = list(split_columns(prompts, dev_count))
    packs = shard_rows % 32 == 0
    x_pieces[0], own_weight = lax.optimization_barrier((x_pieces[0], latent_weight))
    weights = [pack_weight(own_weight) if packs else own_weight] + [None] * (side_count - 1)
    for k in range(2, side_count, 2):
        weights[k] = swap(weights[0], "side", k)
    for k in sorted(range(1, dev_count), reverse=True):
        x_pieces[k] = swap(x_pieces[k], "dev", k)

    score_scale = queries.shape[-1] ** (-0.5)
    half = rope_width // 2
    inverse = 1.0 / 10000.0 ** (jnp.arange(half, dtype=f32) * (2.0 / rope_width))
    lengths, x_pieces[0] = lax.optimization_barrier((context_len, x_pieces[0]))
    (
        query_full, top_held, sum_held, mix_held, live, target, cosine, sine, row_slot,
        value_here, out_here,
    ) = prepare(
        score_scale, dev_count, side_count, bucket_rows, lengths, request_slot,
        row_request.reshape(-1, 128), inverse.reshape(1, -1), queries, key_absorb,
        jnp.swapaxes(latent_cache, 1, 2), new_latent, value_absorb, out_weight,
    )

    weights[0::2], top_held = lax.optimization_barrier((weights[0::2], top_held))
    for k in range(0, side_count, 2):
        weights[k + 1] = swap(weights[k], "side", 1)
    if not packs:
        my_side = lax.axis_index("side")
        held = jnp.zeros((side_count, shard_rows, kv_width), bf16)
        for k in range(side_count):
            held = lax.dynamic_update_slice(held, weights[k][None], (my_side ^ k, 0, 0))
        weights = [held.reshape(slab, kv_width)]

    routed = project(stack_rows(x_pieces), weights, target, kv_width, dev_count)
    layout = (score_scale, cap_slots, step_count, group_rows // 2)
    state = top_held, sum_held, mix_held
    for which in range(2):
        half = list(routed[which * dev_count : (which + 1) * dev_count])
        for k in sorted(range(1, dev_count), reverse=True):
            half[k] = swap(half[k], "dev", k)
        latent_rows = finish(half[:1] + half[:0:-1], latent_gain.reshape(1, -1), cosine, sine, which)
        pieces = [latent_rows] + [swap(latent_rows, "side", k) for k in range(1, side_count)]
        if which == 0:
            state = absorb(layout, which, query_full, row_slot, *state, pieces)
    head_count = value_absorb.shape[0]
    near = head_count * 7 // 16
    bounds = ((0, near), (near, head_count - near))
    gathered = []
    for first_head, part_heads in bounds:
        head_out = attend(
            layout, 1, query_full, row_slot, *state, live, value_here, pieces, first_head,
            part_heads,
        )
        by_way = [] if first_head else list(range(3, dev_count, 2))
        heads = [head_out] + [None] * (dev_count - 1)
        for k in sorted(range(1, dev_count), reverse=True):
            if k not in by_way:
                heads[k] = swap(head_out, "dev", k)
        gathered.append(heads)
    gathered[1][0], gathered[0][2::2] = lax.optimization_barrier(
        (gathered[1][0], gathered[0][2::2])
    )
    for k in range(3, dev_count, 2):
        gathered[0][k] = swap(gathered[0][k - 1], "dev", 1)
    product = None
    for heads, (first_head, part_heads) in zip(gathered, bounds):
        products = output_product(
            heads, out_here, side_count, product, first_head * nope_width,
            first_head + part_heads == head_count,
        )
        product = products[0]
    result = products[0]
    for k in sorted(range(1, side_count), reverse=True):
        result = result + swap(products[k], "side", k).astype(f32)
    return result.astype(bf16)


def solution(mesh):
    placed = (
        P(("rep", "dev", "side"), None),
        P(("dev", "side"), None),
        P(),
        P("rep"),
        P("rep"),
        P("rep"),
        P(("rep", "dev"), None, None),
        P(("rep", "dev"), None, None),
        P(("rep", "dev"), None, "side", None),
        P("side", None, None),
        P("side", None, None),
        P("side", "dev"),
    )
    return jax.shard_map(
        on_device, mesh=mesh, in_specs=placed, out_specs=P(("rep", "side"), "dev"), check_vma=False
    )
```

```python
import functools

import jax
import jax.numpy as jnp
from jax import lax
from jax.experimental import pallas as pl
from jax.experimental.pallas import tpu as pltpu
from jax.sharding import PartitionSpec as P

masked_score = -1e30
bf16, f32 = jnp.bfloat16, jnp.float32
in_vmem = pl.BlockSpec(memory_space=pltpu.VMEM)
in_smem = pl.BlockSpec(memory_space=pltpu.SMEM)
in_hbm = pl.BlockSpec(memory_space=pltpu.HBM)
mib = 1024 * 1024
prepare_mib = 16


def swap(value, axis, step):
    count = lax.axis_size(axis)
    return lax.ppermute(value, axis, [(i, i ^ step) for i in range(count)])


def pick(pieces, index):
    out = pieces[0]
    for k in range(1, len(pieces)):
        out = jnp.where(index == k, pieces[k], out)
    return out


def lane_tiles(width):
    return [slice(n, min(n + 128, width)) for n in range(0, width, 128)]


def packed_rows(rows, width):
    return rows * (width // 128) + rows // 2


def pack(value):
    rows, width = value.shape
    full = width // 128
    rest = value[:, full * 128 :]
    parts = [value[:, n * 128 : (n + 1) * 128] for n in range(full)]
    return parts + [jnp.concatenate([rest[: rows // 2], rest[rows // 2 :]], axis=1)]


def store_packed(ref, value):
    first = 0
    for part in pack(value):
        ref[first : first + part.shape[0], :] = part.astype(ref.dtype)
        first += part.shape[0]


def load_packed(ref, rows):
    full = ref.shape[0] // rows
    tiles = [ref[n * rows : (n + 1) * rows, :] for n in range(full)]
    rest = ref[full * rows :, :]
    return tiles, jnp.concatenate([rest[:, :64], rest[:, 64:]], axis=0)


def pack_kernel(value_ref, out_ref):
    store_packed(out_ref, value_ref[...])


def pack_weight(weight):
    rows, width = weight.shape
    return pl.pallas_call(
        pack_kernel,
        out_shape=jax.ShapeDtypeStruct((packed_rows(rows, width), 128), weight.dtype),
        in_specs=[in_vmem],
        out_specs=in_vmem,
        compiler_params=pltpu.CompilerParams(vmem_limit_bytes=8 * mib),
        cost_estimate=pl.CostEstimate(flops=10**10, bytes_accessed=10**6, transcendentals=0),
        name="pack_weight",
    )(weight)


def split_kernel(slab, prompts_ref, *refs):
    my_dev = lax.axis_index("dev")
    out_refs, sems = refs[:-1], refs[-1]
    copies = []
    for k in range(len(out_refs))[::-1]:
        first = pl.multiple_of((my_dev ^ k) * slab, 128)
        copies.append(
            pltpu.make_async_copy(prompts_ref.at[:, pl.ds(first, slab)], out_refs[k], sems.at[k])
        )
    for copy in copies:
        copy.start()
    for copy in copies:
        copy.wait()


def split_columns(prompts, count):
    rows, width = prompts.shape
    slab = width // count
    if slab % 128:
        columns = [prompts[:, k * slab : (k + 1) * slab] for k in range(count)]
        my_dev = lax.axis_index("dev")
        return [pick(columns, my_dev ^ k) for k in range(count)]
    return pl.pallas_call(
        functools.partial(split_kernel, slab),
        out_shape=[jax.ShapeDtypeStruct((rows, slab), prompts.dtype)] * count,
        in_specs=[in_hbm],
        out_specs=[in_vmem] * count,
        scratch_shapes=[pltpu.SemaphoreType.DMA((count,))],
        compiler_params=pltpu.CompilerParams(vmem_limit_bytes=8 * mib),
        cost_estimate=pl.CostEstimate(
            flops=10**10, bytes_accessed=4 * 10**7, transcendentals=0
        ),
        name="split_columns",
    )(pltpu.with_memory_space_constraint(prompts, pltpu.HBM))


def fill_tables(
    dev_count, side_count, bucket, cap_slots, length_ref, slot_ref, request_ref, inverse_ref,
    target_ref, cos_ref, sin_ref, spot_ref, to_ref, place_ref, local_ref, position_ref,
):
    my_dev, my_side = lax.axis_index("dev"), lax.axis_index("side")
    requests = request_ref[...]
    lane_rows, lanes = requests.shape
    tok_rows = bucket * dev_count // 2
    per_row = lanes // tok_rows
    half_bucket = bucket // 2
    half_rows = dev_count * half_bucket
    group_rows = 2 * half_rows
    before = lax.broadcasted_iota(jnp.int32, (lanes, lanes), 0)
    after = lax.broadcasted_iota(jnp.int32, (lanes, lanes), 1)
    below = jnp.where(before < after, 1.0, 0.0)
    near = jnp.where((before < after) & (before // tok_rows == after // tok_rows), 1.0, 0.0)
    scan = jnp.concatenate([below, jnp.ones_like(below)], axis=1).astype(bf16)
    lower = lax.broadcasted_iota(jnp.int32, (lane_rows, lane_rows), 0)
    upper = lax.broadcasted_iota(jnp.int32, (lane_rows, lane_rows), 1)
    rows_before = jnp.where(upper < lower, 1.0, 0.0)
    position = jnp.zeros(requests.shape, f32)
    slot = jnp.zeros(requests.shape, jnp.int32)
    for q in range(slot_ref.shape[0]):
        hit = requests == q
        ranks = jnp.dot(
            jnp.where(hit, 1.0, 0.0).astype(bf16), scan, preferred_element_type=f32
        )
        earlier = jnp.dot(rows_before, ranks[:, lanes:], preferred_element_type=f32)
        start = length_ref[q].astype(f32)
        position = jnp.where(hit, ranks[:, :lanes] + earlier + start, position)
        slot = jnp.where(hit, slot_ref[q], slot)
    group = lax.div(slot, cap_slots)
    rank = jnp.zeros(requests.shape, f32)
    for g in range(dev_count):
        hit = group == g
        ranks = jnp.dot(
            jnp.where(hit, 1.0, 0.0).astype(bf16), near.astype(bf16), preferred_element_type=f32
        )
        rank = jnp.where(hit, ranks, rank)
    block = lax.broadcasted_iota(jnp.int32, requests.shape, 0) * per_row + lax.div(
        lax.broadcasted_iota(jnp.int32, requests.shape, 1), tok_rows
    )
    rank = rank.astype(jnp.int32)
    which = lax.div(rank, half_bucket)
    place = lax.div(block, side_count) * half_bucket + lax.rem(rank, half_bucket)
    to_ref[...] = (which * dev_count + (group ^ my_dev)) * half_rows + place
    place = which * half_rows + place
    place_ref[...] = jnp.where(group == my_dev, place, -1)
    local_ref[...] = (slot - my_dev * cap_slots + 1).astype(f32)
    position_ref[...] = position
    lane_block = lax.div(lax.broadcasted_iota(jnp.int32, (1, lanes), 1), tok_rows)
    ids = lax.broadcasted_iota(jnp.int32, (group_rows, 1), 0)

    def find(dev, side):
        held = dev * side_count + side
        return pl.ds(lax.div(held, per_row), 1), lane_block == lax.rem(held, per_row)

    targets = []
    for k in range(dev_count):
        held = (my_dev ^ k) * side_count + my_side
        row = jnp.broadcast_to(to_ref[pl.ds(lax.div(held, per_row), 1), :], (8, lanes))
        start = lax.rem(lanes - tok_rows * lax.rem(held, per_row), lanes)
        targets.append(pltpu.roll(row, start, 1)[:1, :tok_rows])
    for k in range(0, dev_count, per_row):
        target_ref[:, k * tok_rows : k * tok_rows + lanes] = jnp.concatenate(
            targets[k : k + per_row], axis=1
        )
    found = jnp.zeros((group_rows, lanes), f32)
    for d in range(dev_count):
        row, inside = find(d, my_side)
        found = jnp.where((place_ref[row, :] == ids) & inside, position_ref[row, :], found)
    angles = jnp.sum(found, axis=1, keepdims=True) * inverse_ref[...]
    cos_ref[...] = jnp.cos(angles)
    sin_ref[...] = jnp.sin(angles)
    for k in range(side_count):
        total = jnp.zeros((8, group_rows), f32)
        for d in range(dev_count):
            row, inside = find(d, my_side ^ k)
            chosen = jnp.where((place_ref[row, :] == ids) & inside, 1.0, 0.0).astype(bf16)
            values = jnp.broadcast_to(local_ref[row, :], (8, lanes)).astype(bf16)
            total = total + lax.dot_general(
                values, chosen, (((1,), (1,)), ((), ())), preferred_element_type=f32
            )
        spot_ref[:, k * group_rows : (k + 1) * group_rows] = total[:1].astype(jnp.int32)


def prepare_kernel(
    scale, steps, layout, inverse_ref, length_hbm, slot_hbm, request_hbm, query_hbm, absorb_hbm,
    cache_hbm, fresh_hbm, value_hbm, out_hbm, full_ref, top_ref, sum_ref, mix_ref, live_ref, target_ref,
    cos_ref, sin_ref, spot_ref, value_ref, out_ref, length_ref, slot_ref, request_ref, query_ref,
    absorb_ref, cache_ref, fresh_ref, plain, full, to_ref, place_ref, local_ref, position_ref, sems,
):
    pairs = [
        (length_hbm, length_ref), (slot_hbm, slot_ref), (request_hbm, request_ref),
        (query_hbm, query_ref), (absorb_hbm, absorb_ref), (cache_hbm, cache_ref),
        (fresh_hbm, fresh_ref), (value_hbm, value_ref),
    ]
    parts = sems.shape[0] - len(pairs)
    rows = out_hbm.shape[0] // parts
    for n in range(parts):
        part = pl.ds(n * rows, rows)
        pairs.append((out_hbm.at[part], out_ref.at[part]))
    copies = [pltpu.make_async_copy(*pair, sems.at[n]) for n, pair in enumerate(pairs)]
    for copy in copies:
        copy.start()
    for copy in copies[:3]:
        copy.wait()
    slots, _, context = cache_ref.shape
    heads, nope, lat_width = absorb_ref.shape
    per_head = slots * steps
    fill_tables(
        *layout, slots, length_ref, slot_ref, request_ref, inverse_ref, target_ref, cos_ref,
        sin_ref, spot_ref, to_ref, place_ref, local_ref, position_ref,
    )
    first_slot = lax.axis_index("dev") * slots
    lengths = []
    for s in range(slots):
        length = jnp.int32(0)
        for q in range(slot_ref.shape[0]):
            length = jnp.where(slot_ref[q] == first_slot + s, length_ref[q], length)
        lengths.append(length)
    slot_of = lax.div(lax.broadcasted_iota(jnp.int32, live_ref.shape, 0), steps)
    live = jnp.zeros(live_ref.shape, f32)
    for s in range(slots):
        live = jnp.where((slot_of == s) & (lengths[s] > 0), 1.0, live)
    live_ref[...] = live
    copies[3].wait()
    copies[4].wait()
    for n, here in enumerate(lane_tiles(query_ref.shape[1])):
        plain[n, :, : here.stop - here.start] = query_ref[:, here].astype(f32)
    wide = lane_tiles(full_ref.shape[1])
    for h in range(heads):
        there = pl.ds(h, per_head, stride=heads)
        query = plain[0, there, :].astype(bf16)
        latent = jnp.dot(query, absorb_ref[h], preferred_element_type=f32).astype(bf16).astype(f32)
        here = slice(h * per_head, (h + 1) * per_head)
        for n, lanes in enumerate(lane_tiles(lat_width)):
            full[n, here, :] = latent[:, lanes]
        full[len(wide) - 1, here, :] = plain[1, there, :]
    for n, lanes in enumerate(wide):
        full_ref[:, lanes] = full[n, :, : lanes.stop - lanes.start].astype(bf16)
    key = lax.broadcasted_iota(jnp.int32, (1, context), 1)
    copies[5].wait()
    copies[6].wait()
    late = lax.broadcasted_iota(jnp.int32, (steps * heads, steps), 1)
    late = late > lax.div(lax.broadcasted_iota(jnp.int32, (steps * heads, steps), 0), heads)
    for s in range(slots):
        theres = [pl.ds(s * steps + t, heads, stride=per_head) for t in range(steps)]
        query = jnp.concatenate(
            [
                jnp.concatenate([full[n, there, :] for there in theres], axis=0)[
                    :, : lanes.stop - lanes.start
                ].astype(bf16)
                for n, lanes in enumerate(wide)
            ],
            axis=1,
        )
        rows = cache_ref[s]
        score = jnp.dot(query, rows, preferred_element_type=f32)
        score = jnp.where(key < lengths[s], score * scale, masked_score)
        fresh = fresh_ref[s]
        new = lax.dot_general(
            query, fresh, (((1,), (1,)), ((), ())), preferred_element_type=f32
        )
        new = jnp.where(late, masked_score, new * scale)
        top = jnp.maximum(
            jnp.max(score, axis=1, keepdims=True), jnp.max(new, axis=1, keepdims=True)
        )
        weight = jnp.exp(score - top)
        new = jnp.exp(new - top)
        total = jnp.sum(weight, axis=1, keepdims=True) + jnp.sum(new, axis=1, keepdims=True)
        mix = lax.dot_general(
            weight.astype(bf16), rows[:lat_width, :], (((1,), (1,)), ((), ())),
            preferred_element_type=f32,
        )
        for u in range(steps):
            mix = mix + new[:, u : u + 1].astype(bf16).astype(f32) * fresh[
                u : u + 1, :lat_width
            ].astype(f32)
        lanes = top_ref.shape[1]
        for t in range(steps):
            there = theres[t]
            here = slice(t * heads, (t + 1) * heads)
            top_ref[there, :] = jnp.broadcast_to(top[here], (heads, lanes))
            sum_ref[there, :] = jnp.broadcast_to(total[here], (heads, lanes))
            for n, part in enumerate(lane_tiles(lat_width)):
                mix_ref[n, there, :] = mix[here, part]
    for copy in copies[7:]:
        copy.wait()


def prepare(
    scale, dev_count, side_count, bucket, lengths, request_slot, requests, inverse, queries,
    absorb, cache, fresh, value, out_weight,
):
    slots, steps, heads, width = queries.shape
    kv_width = cache.shape[1]
    lat_width = absorb.shape[2]
    rows = slots * steps * heads
    group_rows = dev_count * bucket
    parts = 8
    lanes = requests.shape[1]
    half = inverse.shape[1]
    shapes = [
        ((rows, kv_width), bf16), ((rows, 128), f32), ((rows, 128), f32),
        ((lat_width // 128, rows, 128), f32), ((slots * steps, 128), f32),
        ((1, group_rows // 2 * dev_count), jnp.int32), ((group_rows, half), f32), ((group_rows, half), f32),
        ((1, side_count * group_rows), jnp.int32), (value.shape, bf16), (out_weight.shape, bf16),
    ]
    return pl.pallas_call(
        functools.partial(prepare_kernel, scale, steps, (dev_count, side_count, bucket)),
        out_shape=[jax.ShapeDtypeStruct(*shape) for shape in shapes],
        in_specs=[in_vmem] + [in_hbm] * 9,
        out_specs=[in_vmem] * len(shapes),
        scratch_shapes=[
            pltpu.SMEM(lengths.shape, lengths.dtype),
            pltpu.SMEM(request_slot.shape, request_slot.dtype),
            pltpu.VMEM(requests.shape, requests.dtype),
            pltpu.VMEM((rows, width), queries.dtype),
            pltpu.VMEM(absorb.shape, absorb.dtype),
            pltpu.VMEM(cache.shape, cache.dtype),
            pltpu.VMEM(fresh.shape, fresh.dtype),
            pltpu.VMEM((len(lane_tiles(width)), rows, 128), f32),
            pltpu.VMEM((len(lane_tiles(kv_width)), rows, 128), f32),
            pltpu.VMEM(requests.shape, jnp.int32),
            pltpu.VMEM(requests.shape, jnp.int32),
            pltpu.VMEM(requests.shape, f32),
            pltpu.VMEM(requests.shape, f32),
            pltpu.SemaphoreType.DMA((parts + 8,)),
        ],
        compiler_params=pltpu.CompilerParams(vmem_limit_bytes=prepare_mib * mib),
        cost_estimate=pl.CostEstimate(
            flops=4 * 10**10, bytes_accessed=28 * 10**6, transcendentals=10**5
        ),
        name="prepare",
    )(inverse, lengths, request_slot, requests, queries.reshape(rows, width), absorb, cache, fresh,
      value, out_weight)


def stack_kernel(*refs):
    out_ref = refs[-1]
    rows = refs[0].shape[0]
    for n, ref in enumerate(refs[:-1]):
        k = (len(refs) - 1 - n) % (len(refs) - 1)
        out_ref[k * rows : (k + 1) * rows, :] = ref[...]


def stack_rows(pieces):
    rows, width = pieces[0].shape
    return pl.pallas_call(
        stack_kernel,
        out_shape=jax.ShapeDtypeStruct((len(pieces) * rows, width), bf16),
        in_specs=[in_vmem] * len(pieces),
        out_specs=in_vmem,
        compiler_params=pltpu.CompilerParams(vmem_limit_bytes=8 * mib),
        cost_estimate=pl.CostEstimate(flops=2 * 10**10, bytes_accessed=10**6, transcendentals=0),
        name="stack_rows",
    )(pieces[0], *pieces[:0:-1])


def project_kernel(dev_count, side_count, target_ref, x_ref, *refs):
    my_side = lax.axis_index("side")
    weight_refs = refs[:side_count]
    out_refs = refs[side_count:-2]
    slab_weight, rows = refs[-2:]
    tok_rows = x_ref.shape[0] // dev_count
    full = slab_weight.shape[1] // 128
    if side_count > 1:
        shard = slab_weight.shape[0] // side_count
        for k in range(side_count):
            first = pl.multiple_of((my_side ^ k) * shard, 16)
            tiles, rest = load_packed(weight_refs[k], shard)
            for n, tile in enumerate(tiles):
                slab_weight[pl.ds(first, shard), n * 128 : (n + 1) * 128] = tile
            slab_weight[pl.ds(first, shard), full * 128 :] = rest
    slab = slab_weight[...] if side_count > 1 else weight_refs[0][...]
    raw = jnp.dot(x_ref[...], slab, preferred_element_type=f32).astype(bf16)
    rows[...] = raw
    target = target_ref[...]
    half_rows = tok_rows
    step = min(4, 2 * dev_count)
    for j in range(0, 2 * dev_count, step):
        ids = lax.broadcasted_iota(jnp.int32, (step * half_rows, target.shape[1]), 0)
        route = jnp.where(ids + j * half_rows == target, 1.0, 0.0).astype(bf16)
        placed = jnp.dot(route, rows[...], preferred_element_type=f32)
        for n in range(step):
            store_packed(out_refs[j + n], placed[n * half_rows : (n + 1) * half_rows])


def project(x_rows, weights, target, width, dev_count):
    tok_rows, slab = x_rows.shape[0] // dev_count, x_rows.shape[1]
    return pl.pallas_call(
        functools.partial(project_kernel, dev_count, len(weights)),
        out_shape=[
            jax.ShapeDtypeStruct(
                (packed_rows(tok_rows, width), 128), f32 if j % dev_count == 0 else bf16
            )
            for j in range(2 * dev_count)
        ],
        in_specs=[in_vmem] * (2 + len(weights)),
        out_specs=[in_vmem] * (2 * dev_count),
        scratch_shapes=[
            pltpu.VMEM((slab, width), bf16),
            pltpu.VMEM((target.shape[1], width), bf16),
        ],
        compiler_params=pltpu.CompilerParams(vmem_limit_bytes=20 * mib),
        name="project",
    )(target, x_rows, *weights)


def finish_kernel(which, gain_ref, cos_ref, sin_ref, *refs):
    parts, out_ref = refs[:-1], refs[-1]
    rows, half = cos_ref.shape[0] // 2, cos_ref.shape[1]
    mine = slice(which * rows, (which + 1) * rows)
    total = parts[0][...].astype(f32)
    for part in parts[1:]:
        total = total + part[...].astype(f32)
    tiles, rest = load_packed(total, rows)
    latent = jnp.concatenate(tiles, axis=1)
    spread = jnp.mean(latent * latent, axis=1, keepdims=True)
    latent = latent * lax.rsqrt(spread + 1e-06) * gain_ref[...]
    first, second = rest[:, :half], rest[:, half:]
    cosine, sine = cos_ref[mine, :], sin_ref[mine, :]
    store_packed(
        out_ref,
        jnp.concatenate(
            [latent, first * cosine - second * sine, second * cosine + first * sine], axis=1
        ),
    )


def finish(parts, gain, cosine, sine, which):
    return pl.pallas_call(
        functools.partial(finish_kernel, which),
        out_shape=jax.ShapeDtypeStruct(parts[0].shape, bf16),
        in_specs=[in_vmem] * (3 + len(parts)),
        out_specs=in_vmem,
        compiler_params=pltpu.CompilerParams(vmem_limit_bytes=8 * mib),
        name="finish_rows",
    )(gain, cosine, sine, *parts)


def piece_order(count):
    return [0, 1, *range(3, count, 2), *range(2, count, 2)]


def take_keys(keys, pieces, lat_width):
    rows = keys.shape[0] // len(pieces)
    for n, piece in zip(piece_order(len(pieces)), pieces):
        tiles, rest = load_packed(piece, rows)
        there = slice(n * rows, (n + 1) * rows)
        for j, tile in enumerate(tiles):
            keys[there, j * 128 : (j + 1) * 128] = tile
        keys[there, lat_width:] = rest


def merge(layout, which, mine, query_ref, slot_ref, top_ref, sum_ref, mix_ref, keys):
    scale, cap_slots, steps, half_rows = layout
    lat_width = mix_ref.shape[0] * mix_ref.shape[2]
    row = lax.broadcasted_iota(jnp.int32, (mine.stop - mine.start, 1), 0)
    row_slot = (row // steps) % cap_slots
    query = query_ref[mine, :]
    score = lax.dot_general(
        query, keys[...], (((1,), (1,)), ((), ())), preferred_element_type=f32
    )
    count = slot_ref.shape[1]
    part = half_rows
    slots = jnp.concatenate(
        [slot_ref[:, n + which * part : n + (which + 1) * part] for n in range(0, count, 2 * part)],
        axis=1,
    )
    score = jnp.where(slots == row_slot + 1, score * scale, masked_score)
    top_held = top_ref[mine, :1]
    top = jnp.maximum(top_held, jnp.max(score, axis=1, keepdims=True))
    held = jnp.exp(top_held - top)
    weight = jnp.exp(score - top)
    total = sum_ref[mine, :1] * held + jnp.sum(weight, axis=1, keepdims=True)
    mix = jnp.dot(weight.astype(bf16), keys[:, :lat_width], preferred_element_type=f32)
    mix_held = jnp.concatenate([mix_ref[n, mine, :] for n in range(mix_ref.shape[0])], axis=1)
    return top, total, mix_held * held + mix


def absorb_kernel(layout, which, query_ref, slot_ref, top_ref, sum_ref, mix_ref, *refs):
    pieces, (new_top, new_sum, new_mix, keys) = refs[:-4], refs[-4:]
    take_keys(keys, pieces, mix_ref.shape[0] * mix_ref.shape[2])
    rows, lanes = top_ref.shape
    step = rows // 2
    for first in range(0, rows, step):
        mine = slice(first, first + step)
        top, total, mix = merge(
            layout, which, mine, query_ref, slot_ref, top_ref, sum_ref, mix_ref, keys
        )
        new_top[mine, :] = jnp.broadcast_to(top, (step, lanes))
        new_sum[mine, :] = jnp.broadcast_to(total, (step, lanes))
        for n, part in enumerate(lane_tiles(mix.shape[1])):
            new_mix[n, mine, :] = mix[:, part]


def absorb(layout, which, query, row_slot, top, total, mix, pieces):
    return pl.pallas_call(
        functools.partial(absorb_kernel, layout, which),
        out_shape=[jax.ShapeDtypeStruct(x.shape, f32) for x in (top, total, mix)],
        in_specs=[in_vmem] * (5 + len(pieces)),
        out_specs=[in_vmem] * 3,
        scratch_shapes=[pltpu.VMEM((row_slot.shape[1] // 2, query.shape[1]), bf16)],
        compiler_params=pltpu.CompilerParams(vmem_limit_bytes=10 * mib),
        cost_estimate=pl.CostEstimate(flops=2 * 10**9, bytes_accessed=10**6, transcendentals=0),
        name="absorb",
    )(query, row_slot, top, total, mix, *pieces)


def attend_kernel(
    layout, which, first_head, heads, query_ref, slot_ref, top_ref, sum_ref, mix_ref, live_ref,
    value_ref, *refs
):
    pieces, out_ref, keys = refs[:-2], refs[-2], refs[-1]
    per_head = layout[1] * layout[2]
    take_keys(keys, pieces, mix_ref.shape[0] * mix_ref.shape[2])
    mine = slice(first_head * per_head, (first_head + heads) * per_head)
    _, total, mix = merge(
        layout, which, mine, query_ref, slot_ref, top_ref, sum_ref, mix_ref, keys
    )
    latent = (mix / total).astype(bf16)
    live = live_ref[:, :1]
    width = value_ref.shape[2]
    for h in range(heads):
        mixed = latent[h * per_head : (h + 1) * per_head, :]
        value = jnp.dot(mixed, value_ref[first_head + h], preferred_element_type=f32) * live
        out_ref[:, h * width : (h + 1) * width] = value.astype(bf16)


def attend(layout, which, query, row_slot, top, total, mix, live, value, pieces, first_head, heads):
    return pl.pallas_call(
        functools.partial(attend_kernel, layout, which, first_head, heads),
        out_shape=jax.ShapeDtypeStruct((live.shape[0], heads * value.shape[2]), bf16),
        in_specs=[in_vmem] * (7 + len(pieces)),
        out_specs=in_vmem,
        scratch_shapes=[pltpu.VMEM((row_slot.shape[1] // 2, query.shape[1]), bf16)],
        compiler_params=pltpu.CompilerParams(vmem_limit_bytes=10 * mib),
        name="attend",
    )(query, row_slot, top, total, mix, live, value, *pieces)


def output_kernel(dev_count, side_count, start, last, *refs):
    my_dev, my_side = lax.axis_index("dev"), lax.axis_index("side")
    head_refs = refs[:dev_count]
    weight_ref = refs[dev_count]
    earlier_ref = refs[dev_count + 1] if start else None
    out_refs = refs[dev_count + 1 + (start > 0) : -1]
    held = refs[-1]
    rows, depth = head_refs[0].shape
    per_side = dev_count // side_count
    for j in range(dev_count):
        group = my_dev ^ j
        place = (lax.div(group, per_side) ^ my_side) * per_side + lax.rem(group, per_side)
        held[pl.ds(pl.multiple_of(place * rows, 16), rows), :] = head_refs[j][...]
    columns = weight_ref.shape[1]
    tile = 256 if columns % 256 == 0 else columns
    side_rows = rows * per_side
    for n in range(columns // tile):
        here = slice(n * tile, (n + 1) * tile)
        product = jnp.dot(
            held[...], weight_ref[start : start + depth, here],
            preferred_element_type=f32,
        )
        if start:
            product = product + earlier_ref[:, here]
        if not last:
            out_refs[0][:, here] = product
        else:
            for k in range(side_count):
                out_refs[k][:, here] = product[k * side_rows : (k + 1) * side_rows, :].astype(
                    out_refs[k].dtype
                )


def output_product(head_pieces, weight, side_count, earlier, start, last):
    dev_count = len(head_pieces)
    rows, depth = head_pieces[0].shape
    columns = weight.shape[1]
    side_rows = rows * dev_count // side_count
    if not last:
        shapes = [((rows * dev_count, columns), f32)]
    else:
        shapes = [((side_rows, columns), f32 if k == 0 else bf16) for k in range(side_count)]
    earlier = [] if earlier is None else [earlier]
    return pl.pallas_call(
        functools.partial(output_kernel, dev_count, side_count, start, last),
        out_shape=[jax.ShapeDtypeStruct(*shape) for shape in shapes],
        in_specs=[in_vmem] * (dev_count + 1 + len(earlier)),
        out_specs=[in_vmem] * len(shapes),
        scratch_shapes=[pltpu.VMEM((dev_count * rows, depth), bf16)],
        compiler_params=pltpu.CompilerParams(vmem_limit_bytes=10 * mib),
        name="output_product",
    )(*head_pieces, weight, *earlier)


def on_device(
    prompts,
    latent_weight,
    latent_gain,
    row_request,
    context_len,
    request_slot,
    latent_cache,
    new_latent,
    queries,
    key_absorb,
    value_absorb,
    out_weight,
):
    dev_count = lax.axis_size("dev")
    side_count = lax.axis_size("side")
    tok_rows, model_width = prompts.shape
    shard_rows, kv_width = latent_weight.shape
    lat_width = latent_gain.shape[0]
    nope_width = value_absorb.shape[2]
    rope_width = kv_width - lat_width
    cap_slots, ctx_len, _ = latent_cache.shape
    step_count = new_latent.shape[1]
    bucket_rows = 2 * tok_rows // dev_count
    group_rows = dev_count * bucket_rows
    slab = model_width // dev_count

    x_pieces = list(split_columns(prompts, dev_count))
    packs = shard_rows % 32 == 0
    x_pieces[0], own_weight = lax.optimization_barrier((x_pieces[0], latent_weight))
    weights = [pack_weight(own_weight) if packs else own_weight] + [None] * (side_count - 1)
    for k in range(2, side_count, 2):
        weights[k] = swap(weights[0], "side", k)
    for k in sorted(range(1, dev_count), reverse=True):
        x_pieces[k] = swap(x_pieces[k], "dev", k)

    score_scale = queries.shape[-1] ** (-0.5)
    half = rope_width // 2
    inverse = 1.0 / 10000.0 ** (jnp.arange(half, dtype=f32) * (2.0 / rope_width))
    lengths, x_pieces[0] = lax.optimization_barrier((context_len, x_pieces[0]))
    (
        query_full, top_held, sum_held, mix_held, live, target, cosine, sine, row_slot,
        value_here, out_here,
    ) = prepare(
        score_scale, dev_count, side_count, bucket_rows, lengths, request_slot,
        row_request.reshape(-1, 128), inverse.reshape(1, -1), queries, key_absorb,
        jnp.swapaxes(latent_cache, 1, 2), new_latent, value_absorb, out_weight,
    )

    weights[0::2], top_held = lax.optimization_barrier((weights[0::2], top_held))
    for k in range(0, side_count, 2):
        weights[k + 1] = swap(weights[k], "side", 1)
    if not packs:
        my_side = lax.axis_index("side")
        held = jnp.zeros((side_count, shard_rows, kv_width), bf16)
        for k in range(side_count):
            held = lax.dynamic_update_slice(held, weights[k][None], (my_side ^ k, 0, 0))
        weights = [held.reshape(slab, kv_width)]

    routed = project(stack_rows(x_pieces), weights, target, kv_width, dev_count)
    layout = (score_scale, cap_slots, step_count, group_rows // 2)
    state = top_held, sum_held, mix_held
    for which in range(2):
        half = list(routed[which * dev_count : (which + 1) * dev_count])
        for k in sorted(range(1, dev_count), reverse=True):
            half[k] = swap(half[k], "dev", k)
        latent_rows = finish(half[:1] + half[:0:-1], latent_gain.reshape(1, -1), cosine, sine, which)
        pieces = [
            swap(latent_rows, "side", k) if k else latent_rows for k in piece_order(side_count)
        ]
        if which == 0:
            state = absorb(layout, which, query_full, row_slot, *state, pieces)
    product, first_head, head_count = None, 0, value_absorb.shape[0]
    for part_heads in (head_count * 3 // 4, head_count // 4):
        head_out = attend(
            layout, 1, query_full, row_slot, *state, live, value_here, pieces, first_head,
            part_heads,
        )
        heads = [head_out] + [None] * (dev_count - 1)
        for k in sorted(range(1, dev_count), reverse=True):
            heads[k] = swap(head_out, "dev", k)
        start, first_head = first_head * nope_width, first_head + part_heads
        products = output_product(
            heads, out_here, side_count, product, start, first_head == head_count
        )
        product = products[0]
    result = products[0]
    for k in sorted(range(1, side_count), reverse=True):
        result = result + swap(products[k], "side", k).astype(f32)
    return result.astype(bf16)


def solution(mesh):
    placed = (
        P(("rep", "dev", "side"), None),
        P(("dev", "side"), None),
        P(),
        P("rep"),
        P("rep"),
        P("rep"),
        P(("rep", "dev"), None, None),
        P(("rep", "dev"), None, None),
        P(("rep", "dev"), None, "side", None),
        P("side", None, None),
        P("side", None, None),
        P("side", "dev"),
    )
    return jax.shard_map(
        on_device, mesh=mesh, in_specs=placed, out_specs=P(("rep", "side"), "dev"), check_vma=False
    )
```

```python
import functools

import jax
import jax.numpy as jnp
from jax import lax
from jax.experimental import pallas as pl
from jax.experimental.pallas import tpu as pltpu
from jax.sharding import PartitionSpec as P

masked_score = -1e30
bf16, f32 = jnp.bfloat16, jnp.float32
in_vmem = pl.BlockSpec(memory_space=pltpu.VMEM)
in_smem = pl.BlockSpec(memory_space=pltpu.SMEM)
in_hbm = pl.BlockSpec(memory_space=pltpu.HBM)
mib = 1024 * 1024
prepare_mib = 16


def swap(value, axis, step):
    count = lax.axis_size(axis)
    return lax.ppermute(value, axis, [(i, i ^ step) for i in range(count)])


def pick(pieces, index):
    out = pieces[0]
    for k in range(1, len(pieces)):
        out = jnp.where(index == k, pieces[k], out)
    return out


def lane_tiles(width):
    return [slice(n, min(n + 128, width)) for n in range(0, width, 128)]


def packed_rows(rows, width):
    return rows * (width // 128) + rows // 2


def pack(value):
    rows, width = value.shape
    full = width // 128
    rest = value[:, full * 128 :]
    parts = [value[:, n * 128 : (n + 1) * 128] for n in range(full)]
    return parts + [jnp.concatenate([rest[: rows // 2], rest[rows // 2 :]], axis=1)]


def store_packed(ref, value):
    first = 0
    for part in pack(value):
        ref[first : first + part.shape[0], :] = part.astype(ref.dtype)
        first += part.shape[0]


def load_packed(ref, rows):
    full = ref.shape[0] // rows
    tiles = [ref[n * rows : (n + 1) * rows, :] for n in range(full)]
    rest = ref[full * rows :, :]
    return tiles, jnp.concatenate([rest[:, :64], rest[:, 64:]], axis=0)


def pack_kernel(value_ref, out_ref):
    store_packed(out_ref, value_ref[...])


def pack_weight(weight):
    rows, width = weight.shape
    return pl.pallas_call(
        pack_kernel,
        out_shape=jax.ShapeDtypeStruct((packed_rows(rows, width), 128), weight.dtype),
        in_specs=[in_vmem],
        out_specs=in_vmem,
        compiler_params=pltpu.CompilerParams(vmem_limit_bytes=8 * mib),
        cost_estimate=pl.CostEstimate(flops=10**10, bytes_accessed=10**6, transcendentals=0),
        name="pack_weight",
    )(weight)


def split_kernel(slab, prompts_ref, *refs):
    my_dev = lax.axis_index("dev")
    out_refs, sems = refs[:-1], refs[-1]
    copies = []
    for k in range(len(out_refs))[::-1]:
        first = pl.multiple_of((my_dev ^ k) * slab, 128)
        copies.append(
            pltpu.make_async_copy(prompts_ref.at[:, pl.ds(first, slab)], out_refs[k], sems.at[k])
        )
    for copy in copies:
        copy.start()
    for copy in copies:
        copy.wait()


def split_columns(prompts, count):
    rows, width = prompts.shape
    slab = width // count
    if slab % 128:
        columns = [prompts[:, k * slab : (k + 1) * slab] for k in range(count)]
        my_dev = lax.axis_index("dev")
        return [pick(columns, my_dev ^ k) for k in range(count)]
    return pl.pallas_call(
        functools.partial(split_kernel, slab),
        out_shape=[jax.ShapeDtypeStruct((rows, slab), prompts.dtype)] * count,
        in_specs=[in_hbm],
        out_specs=[in_vmem] * count,
        scratch_shapes=[pltpu.SemaphoreType.DMA((count,))],
        compiler_params=pltpu.CompilerParams(vmem_limit_bytes=8 * mib),
        cost_estimate=pl.CostEstimate(
            flops=10**10, bytes_accessed=4 * 10**7, transcendentals=0
        ),
        name="split_columns",
    )(pltpu.with_memory_space_constraint(prompts, pltpu.HBM))


def fill_tables(
    dev_count, side_count, bucket, cap_slots, length_ref, slot_ref, request_ref, inverse_ref,
    target_ref, cos_ref, sin_ref, spot_ref, to_ref, place_ref, local_ref, position_ref,
):
    my_dev, my_side = lax.axis_index("dev"), lax.axis_index("side")
    requests = request_ref[...]
    lane_rows, lanes = requests.shape
    tok_rows = bucket * dev_count // 2
    per_row = lanes // tok_rows
    half_bucket = bucket // 2
    half_rows = dev_count * half_bucket
    group_rows = 2 * half_rows
    before = lax.broadcasted_iota(jnp.int32, (lanes, lanes), 0)
    after = lax.broadcasted_iota(jnp.int32, (lanes, lanes), 1)
    below = jnp.where(before < after, 1.0, 0.0)
    near = jnp.where((before < after) & (before // tok_rows == after // tok_rows), 1.0, 0.0)
    scan = jnp.concatenate([below, jnp.ones_like(below)], axis=1).astype(bf16)
    lower = lax.broadcasted_iota(jnp.int32, (lane_rows, lane_rows), 0)
    upper = lax.broadcasted_iota(jnp.int32, (lane_rows, lane_rows), 1)
    rows_before = jnp.where(upper < lower, 1.0, 0.0)
    position = jnp.zeros(requests.shape, f32)
    slot = jnp.zeros(requests.shape, jnp.int32)
    for q in range(slot_ref.shape[0]):
        hit = requests == q
        ranks = jnp.dot(
            jnp.where(hit, 1.0, 0.0).astype(bf16), scan, preferred_element_type=f32
        )
        earlier = jnp.dot(rows_before, ranks[:, lanes:], preferred_element_type=f32)
        start = length_ref[q].astype(f32)
        position = jnp.where(hit, ranks[:, :lanes] + earlier + start, position)
        slot = jnp.where(hit, slot_ref[q], slot)
    group = lax.div(slot, cap_slots)
    rank = jnp.zeros(requests.shape, f32)
    for g in range(dev_count):
        hit = group == g
        ranks = jnp.dot(
            jnp.where(hit, 1.0, 0.0).astype(bf16), near.astype(bf16), preferred_element_type=f32
        )
        rank = jnp.where(hit, ranks, rank)
    block = lax.broadcasted_iota(jnp.int32, requests.shape, 0) * per_row + lax.div(
        lax.broadcasted_iota(jnp.int32, requests.shape, 1), tok_rows
    )
    rank = rank.astype(jnp.int32)
    which = lax.div(rank, half_bucket)
    place = lax.div(block, side_count) * half_bucket + lax.rem(rank, half_bucket)
    to_ref[...] = (which * dev_count + (group ^ my_dev)) * half_rows + place
    place = which * half_rows + place
    place_ref[...] = jnp.where(group == my_dev, place, -1)
    local_ref[...] = (slot - my_dev * cap_slots + 1).astype(f32)
    position_ref[...] = position
    lane_block = lax.div(lax.broadcasted_iota(jnp.int32, (1, lanes), 1), tok_rows)
    ids = lax.broadcasted_iota(jnp.int32, (group_rows, 1), 0)

    def find(dev, side):
        held = dev * side_count + side
        return pl.ds(lax.div(held, per_row), 1), lane_block == lax.rem(held, per_row)

    targets = []
    for k in range(dev_count):
        held = (my_dev ^ k) * side_count + my_side
        row = jnp.broadcast_to(to_ref[pl.ds(lax.div(held, per_row), 1), :], (8, lanes))
        start = lax.rem(lanes - tok_rows * lax.rem(held, per_row), lanes)
        targets.append(pltpu.roll(row, start, 1)[:1, :tok_rows])
    for k in range(0, dev_count, per_row):
        target_ref[:, k * tok_rows : k * tok_rows + lanes] = jnp.concatenate(
            targets[k : k + per_row], axis=1
        )
    found = jnp.zeros((group_rows, lanes), f32)
    for d in range(dev_count):
        row, inside = find(d, my_side)
        found = jnp.where((place_ref[row, :] == ids) & inside, position_ref[row, :], found)
    angles = jnp.sum(found, axis=1, keepdims=True) * inverse_ref[...]
    cos_ref[...] = jnp.cos(angles)
    sin_ref[...] = jnp.sin(angles)
    for k in range(side_count):
        total = jnp.zeros((8, group_rows), f32)
        for d in range(dev_count):
            row, inside = find(d, my_side ^ k)
            chosen = jnp.where((place_ref[row, :] == ids) & inside, 1.0, 0.0).astype(bf16)
            values = jnp.broadcast_to(local_ref[row, :], (8, lanes)).astype(bf16)
            total = total + lax.dot_general(
                values, chosen, (((1,), (1,)), ((), ())), preferred_element_type=f32
            )
        spot_ref[:, k * group_rows : (k + 1) * group_rows] = total[:1].astype(jnp.int32)


def prepare_kernel(
    scale, steps, layout, inverse_ref, length_hbm, slot_hbm, request_hbm, query_hbm, absorb_hbm,
    cache_hbm, fresh_hbm, value_hbm, out_hbm, full_ref, top_ref, sum_ref, mix_ref, live_ref, target_ref,
    cos_ref, sin_ref, spot_ref, value_ref, out_ref, length_ref, slot_ref, request_ref, query_ref,
    absorb_ref, cache_ref, fresh_ref, plain, full, to_ref, place_ref, local_ref, position_ref, sems,
):
    pairs = [
        (length_hbm, length_ref), (slot_hbm, slot_ref), (request_hbm, request_ref),
        (query_hbm, query_ref), (absorb_hbm, absorb_ref), (cache_hbm, cache_ref),
        (fresh_hbm, fresh_ref), (value_hbm, value_ref),
    ]
    parts = sems.shape[0] - len(pairs)
    rows = out_hbm.shape[0] // parts
    for n in range(parts):
        part = pl.ds(n * rows, rows)
        pairs.append((out_hbm.at[part], out_ref.at[part]))
    copies = [pltpu.make_async_copy(*pair, sems.at[n]) for n, pair in enumerate(pairs)]
    for copy in copies:
        copy.start()
    for copy in copies[:3]:
        copy.wait()
    slots, _, context = cache_ref.shape
    heads, nope, lat_width = absorb_ref.shape
    per_head = slots * steps
    fill_tables(
        *layout, slots, length_ref, slot_ref, request_ref, inverse_ref, target_ref, cos_ref,
        sin_ref, spot_ref, to_ref, place_ref, local_ref, position_ref,
    )
    first_slot = lax.axis_index("dev") * slots
    lengths = []
    for s in range(slots):
        length = jnp.int32(0)
        for q in range(slot_ref.shape[0]):
            length = jnp.where(slot_ref[q] == first_slot + s, length_ref[q], length)
        lengths.append(length)
    slot_of = lax.div(lax.broadcasted_iota(jnp.int32, live_ref.shape, 0), steps)
    live = jnp.zeros(live_ref.shape, f32)
    for s in range(slots):
        live = jnp.where((slot_of == s) & (lengths[s] > 0), 1.0, live)
    live_ref[...] = live
    copies[3].wait()
    copies[4].wait()
    for n, here in enumerate(lane_tiles(query_ref.shape[1])):
        plain[n, :, : here.stop - here.start] = query_ref[:, here].astype(f32)
    wide = lane_tiles(full_ref.shape[1])
    for h in range(heads):
        there = pl.ds(h, per_head, stride=heads)
        query = plain[0, there, :].astype(bf16)
        latent = jnp.dot(query, absorb_ref[h], preferred_element_type=f32).astype(bf16).astype(f32)
        here = slice(h * per_head, (h + 1) * per_head)
        for n, lanes in enumerate(lane_tiles(lat_width)):
            full[n, here, :] = latent[:, lanes]
        full[len(wide) - 1, here, :] = plain[1, there, :]
    for n, lanes in enumerate(wide):
        full_ref[:, lanes] = full[n, :, : lanes.stop - lanes.start].astype(bf16)
    key = lax.broadcasted_iota(jnp.int32, (1, context), 1)
    copies[5].wait()
    copies[6].wait()
    late = lax.broadcasted_iota(jnp.int32, (steps * heads, steps), 1)
    late = late > lax.div(lax.broadcasted_iota(jnp.int32, (steps * heads, steps), 0), heads)
    for s in range(slots):
        theres = [pl.ds(s * steps + t, heads, stride=per_head) for t in range(steps)]
        query = jnp.concatenate(
            [
                jnp.concatenate([full[n, there, :] for there in theres], axis=0)[
                    :, : lanes.stop - lanes.start
                ].astype(bf16)
                for n, lanes in enumerate(wide)
            ],
            axis=1,
        )
        rows = cache_ref[s]
        score = jnp.dot(query, rows, preferred_element_type=f32)
        score = jnp.where(key < lengths[s], score * scale, masked_score)
        fresh = fresh_ref[s]
        new = lax.dot_general(
            query, fresh, (((1,), (1,)), ((), ())), preferred_element_type=f32
        )
        new = jnp.where(late, masked_score, new * scale)
        top = jnp.maximum(
            jnp.max(score, axis=1, keepdims=True), jnp.max(new, axis=1, keepdims=True)
        )
        weight = jnp.exp(score - top)
        new = jnp.exp(new - top)
        total = jnp.sum(weight, axis=1, keepdims=True) + jnp.sum(new, axis=1, keepdims=True)
        mix = lax.dot_general(
            weight.astype(bf16), rows[:lat_width, :], (((1,), (1,)), ((), ())),
            preferred_element_type=f32,
        )
        for u in range(steps):
            mix = mix + new[:, u : u + 1].astype(bf16).astype(f32) * fresh[
                u : u + 1, :lat_width
            ].astype(f32)
        lanes = top_ref.shape[1]
        for t in range(steps):
            there = theres[t]
            here = slice(t * heads, (t + 1) * heads)
            top_ref[there, :] = jnp.broadcast_to(top[here], (heads, lanes))
            sum_ref[there, :] = jnp.broadcast_to(total[here], (heads, lanes))
            for n, part in enumerate(lane_tiles(lat_width)):
                mix_ref[n, there, :] = mix[here, part]
    for copy in copies[7:]:
        copy.wait()


def prepare(
    scale, dev_count, side_count, bucket, lengths, request_slot, requests, inverse, queries,
    absorb, cache, fresh, value, out_weight,
):
    slots, steps, heads, width = queries.shape
    kv_width = cache.shape[1]
    lat_width = absorb.shape[2]
    rows = slots * steps * heads
    group_rows = dev_count * bucket
    parts = 8
    lanes = requests.shape[1]
    half = inverse.shape[1]
    shapes = [
        ((rows, kv_width), bf16), ((rows, 128), f32), ((rows, 128), f32),
        ((lat_width // 128, rows, 128), f32), ((slots * steps, 128), f32),
        ((1, group_rows // 2 * dev_count), jnp.int32), ((group_rows, half), f32), ((group_rows, half), f32),
        ((1, side_count * group_rows), jnp.int32), (value.shape, bf16), (out_weight.shape, bf16),
    ]
    return pl.pallas_call(
        functools.partial(prepare_kernel, scale, steps, (dev_count, side_count, bucket)),
        out_shape=[jax.ShapeDtypeStruct(*shape) for shape in shapes],
        in_specs=[in_vmem] + [in_hbm] * 9,
        out_specs=[in_vmem] * len(shapes),
        scratch_shapes=[
            pltpu.SMEM(lengths.shape, lengths.dtype),
            pltpu.SMEM(request_slot.shape, request_slot.dtype),
            pltpu.VMEM(requests.shape, requests.dtype),
            pltpu.VMEM((rows, width), queries.dtype),
            pltpu.VMEM(absorb.shape, absorb.dtype),
            pltpu.VMEM(cache.shape, cache.dtype),
            pltpu.VMEM(fresh.shape, fresh.dtype),
            pltpu.VMEM((len(lane_tiles(width)), rows, 128), f32),
            pltpu.VMEM((len(lane_tiles(kv_width)), rows, 128), f32),
            pltpu.VMEM(requests.shape, jnp.int32),
            pltpu.VMEM(requests.shape, jnp.int32),
            pltpu.VMEM(requests.shape, f32),
            pltpu.VMEM(requests.shape, f32),
            pltpu.SemaphoreType.DMA((parts + 8,)),
        ],
        compiler_params=pltpu.CompilerParams(vmem_limit_bytes=prepare_mib * mib),
        cost_estimate=pl.CostEstimate(
            flops=4 * 10**10, bytes_accessed=28 * 10**6, transcendentals=10**5
        ),
        name="prepare",
    )(inverse, lengths, request_slot, requests, queries.reshape(rows, width), absorb, cache, fresh,
      value, out_weight)


def stack_kernel(*refs):
    out_ref = refs[-1]
    rows = refs[0].shape[0]
    for n, ref in enumerate(refs[:-1]):
        k = (len(refs) - 1 - n) % (len(refs) - 1)
        out_ref[k * rows : (k + 1) * rows, :] = ref[...]


def stack_rows(pieces):
    rows, width = pieces[0].shape
    return pl.pallas_call(
        stack_kernel,
        out_shape=jax.ShapeDtypeStruct((len(pieces) * rows, width), bf16),
        in_specs=[in_vmem] * len(pieces),
        out_specs=in_vmem,
        compiler_params=pltpu.CompilerParams(vmem_limit_bytes=8 * mib),
        cost_estimate=pl.CostEstimate(flops=2 * 10**10, bytes_accessed=10**6, transcendentals=0),
        name="stack_rows",
    )(pieces[0], *pieces[:0:-1])


def project_kernel(dev_count, side_count, target_ref, x_ref, *refs):
    my_side = lax.axis_index("side")
    weight_refs = refs[:side_count]
    out_refs = refs[side_count:-2]
    slab_weight, rows = refs[-2:]
    tok_rows = x_ref.shape[0] // dev_count
    full = slab_weight.shape[1] // 128
    if side_count > 1:
        shard = slab_weight.shape[0] // side_count
        for k in range(side_count):
            first = pl.multiple_of((my_side ^ k) * shard, 16)
            tiles, rest = load_packed(weight_refs[k], shard)
            for n, tile in enumerate(tiles):
                slab_weight[pl.ds(first, shard), n * 128 : (n + 1) * 128] = tile
            slab_weight[pl.ds(first, shard), full * 128 :] = rest
    slab = slab_weight[...] if side_count > 1 else weight_refs[0][...]
    raw = jnp.dot(x_ref[...], slab, preferred_element_type=f32).astype(bf16)
    rows[...] = raw
    target = target_ref[...]
    half_rows = tok_rows
    step = min(4, 2 * dev_count)
    for j in range(0, 2 * dev_count, step):
        ids = lax.broadcasted_iota(jnp.int32, (step * half_rows, target.shape[1]), 0)
        route = jnp.where(ids + j * half_rows == target, 1.0, 0.0).astype(bf16)
        placed = jnp.dot(route, rows[...], preferred_element_type=f32)
        for n in range(step):
            store_packed(out_refs[j + n], placed[n * half_rows : (n + 1) * half_rows])


def project(x_rows, weights, target, width, dev_count):
    tok_rows, slab = x_rows.shape[0] // dev_count, x_rows.shape[1]
    return pl.pallas_call(
        functools.partial(project_kernel, dev_count, len(weights)),
        out_shape=[
            jax.ShapeDtypeStruct(
                (packed_rows(tok_rows, width), 128), f32 if j % dev_count == 0 else bf16
            )
            for j in range(2 * dev_count)
        ],
        in_specs=[in_vmem] * (2 + len(weights)),
        out_specs=[in_vmem] * (2 * dev_count),
        scratch_shapes=[
            pltpu.VMEM((slab, width), bf16),
            pltpu.VMEM((target.shape[1], width), bf16),
        ],
        compiler_params=pltpu.CompilerParams(vmem_limit_bytes=20 * mib),
        name="project",
    )(target, x_rows, *weights)


def finish_kernel(which, gain_ref, cos_ref, sin_ref, *refs):
    parts, out_ref = refs[:-1], refs[-1]
    rows, half = cos_ref.shape[0] // 2, cos_ref.shape[1]
    mine = slice(which * rows, (which + 1) * rows)
    total = parts[0][...].astype(f32)
    for part in parts[1:]:
        total = total + part[...].astype(f32)
    tiles, rest = load_packed(total, rows)
    latent = jnp.concatenate(tiles, axis=1)
    spread = jnp.mean(latent * latent, axis=1, keepdims=True)
    latent = latent * lax.rsqrt(spread + 1e-06) * gain_ref[...]
    first, second = rest[:, :half], rest[:, half:]
    cosine, sine = cos_ref[mine, :], sin_ref[mine, :]
    store_packed(
        out_ref,
        jnp.concatenate(
            [latent, first * cosine - second * sine, second * cosine + first * sine], axis=1
        ),
    )


def finish(parts, gain, cosine, sine, which):
    return pl.pallas_call(
        functools.partial(finish_kernel, which),
        out_shape=jax.ShapeDtypeStruct(parts[0].shape, bf16),
        in_specs=[in_vmem] * (3 + len(parts)),
        out_specs=in_vmem,
        compiler_params=pltpu.CompilerParams(vmem_limit_bytes=8 * mib),
        name="finish_rows",
    )(gain, cosine, sine, *parts)


def piece_order(count):
    return [0, 1, *range(3, count, 2), *range(2, count, 2)]


def take_keys(keys, pieces, lat_width):
    rows = keys.shape[0] // len(pieces)
    for n, piece in zip(piece_order(len(pieces)), pieces):
        tiles, rest = load_packed(piece, rows)
        there = slice(n * rows, (n + 1) * rows)
        for j, tile in enumerate(tiles):
            keys[there, j * 128 : (j + 1) * 128] = tile
        keys[there, lat_width:] = rest


def merge(layout, which, mine, query_ref, slot_ref, top_ref, sum_ref, mix_ref, keys):
    scale, cap_slots, steps, half_rows = layout
    lat_width = mix_ref.shape[0] * mix_ref.shape[2]
    row = lax.broadcasted_iota(jnp.int32, (mine.stop - mine.start, 1), 0)
    row_slot = (row // steps) % cap_slots
    query = query_ref[mine, :]
    score = lax.dot_general(
        query, keys[...], (((1,), (1,)), ((), ())), preferred_element_type=f32
    )
    count = slot_ref.shape[1]
    part = half_rows
    slots = jnp.concatenate(
        [slot_ref[:, n + which * part : n + (which + 1) * part] for n in range(0, count, 2 * part)],
        axis=1,
    )
    score = jnp.where(slots == row_slot + 1, score * scale, masked_score)
    top_held = top_ref[mine, :1]
    top = jnp.maximum(top_held, jnp.max(score, axis=1, keepdims=True))
    held = jnp.exp(top_held - top)
    weight = jnp.exp(score - top)
    total = sum_ref[mine, :1] * held + jnp.sum(weight, axis=1, keepdims=True)
    mix = jnp.dot(weight.astype(bf16), keys[:, :lat_width], preferred_element_type=f32)
    mix_held = jnp.concatenate([mix_ref[n, mine, :] for n in range(mix_ref.shape[0])], axis=1)
    return top, total, mix_held * held + mix


def absorb_kernel(layout, which, query_ref, slot_ref, top_ref, sum_ref, mix_ref, *refs):
    pieces, (new_top, new_sum, new_mix, keys) = refs[:-4], refs[-4:]
    take_keys(keys, pieces, mix_ref.shape[0] * mix_ref.shape[2])
    rows, lanes = top_ref.shape
    step = rows // 2
    for first in range(0, rows, step):
        mine = slice(first, first + step)
        top, total, mix = merge(
            layout, which, mine, query_ref, slot_ref, top_ref, sum_ref, mix_ref, keys
        )
        new_top[mine, :] = jnp.broadcast_to(top, (step, lanes))
        new_sum[mine, :] = jnp.broadcast_to(total, (step, lanes))
        for n, part in enumerate(lane_tiles(mix.shape[1])):
            new_mix[n, mine, :] = mix[:, part]


def absorb(layout, which, query, row_slot, top, total, mix, pieces):
    return pl.pallas_call(
        functools.partial(absorb_kernel, layout, which),
        out_shape=[jax.ShapeDtypeStruct(x.shape, f32) for x in (top, total, mix)],
        in_specs=[in_vmem] * (5 + len(pieces)),
        out_specs=[in_vmem] * 3,
        scratch_shapes=[pltpu.VMEM((row_slot.shape[1] // 2, query.shape[1]), bf16)],
        compiler_params=pltpu.CompilerParams(vmem_limit_bytes=10 * mib),
        cost_estimate=pl.CostEstimate(flops=2 * 10**9, bytes_accessed=10**6, transcendentals=0),
        name="absorb",
    )(query, row_slot, top, total, mix, *pieces)


def attend_kernel(
    layout, which, first_head, heads, query_ref, slot_ref, top_ref, sum_ref, mix_ref, live_ref,
    value_ref, *refs
):
    pieces, out_ref, keys = refs[:-2], refs[-2], refs[-1]
    per_head = layout[1] * layout[2]
    take_keys(keys, pieces, mix_ref.shape[0] * mix_ref.shape[2])
    mine = slice(first_head * per_head, (first_head + heads) * per_head)
    _, total, mix = merge(
        layout, which, mine, query_ref, slot_ref, top_ref, sum_ref, mix_ref, keys
    )
    latent = (mix / total).astype(bf16)
    live = live_ref[:, :1]
    width = value_ref.shape[2]
    for h in range(heads):
        mixed = latent[h * per_head : (h + 1) * per_head, :]
        value = jnp.dot(mixed, value_ref[first_head + h], preferred_element_type=f32) * live
        out_ref[:, h * width : (h + 1) * width] = value.astype(bf16)


def attend(layout, which, query, row_slot, top, total, mix, live, value, pieces, first_head, heads):
    return pl.pallas_call(
        functools.partial(attend_kernel, layout, which, first_head, heads),
        out_shape=jax.ShapeDtypeStruct((live.shape[0], heads * value.shape[2]), bf16),
        in_specs=[in_vmem] * (7 + len(pieces)),
        out_specs=in_vmem,
        scratch_shapes=[pltpu.VMEM((row_slot.shape[1] // 2, query.shape[1]), bf16)],
        compiler_params=pltpu.CompilerParams(vmem_limit_bytes=10 * mib),
        name="attend",
    )(query, row_slot, top, total, mix, live, value, *pieces)


def output_kernel(dev_count, side_count, start, last, *refs):
    my_dev, my_side = lax.axis_index("dev"), lax.axis_index("side")
    head_refs = refs[:dev_count]
    weight_ref = refs[dev_count]
    earlier_ref = refs[dev_count + 1] if start else None
    out_refs = refs[dev_count + 1 + (start > 0) : -1]
    held = refs[-1]
    rows, depth = head_refs[0].shape
    per_side = dev_count // side_count
    for j in range(dev_count):
        group = my_dev ^ j
        place = (lax.div(group, per_side) ^ my_side) * per_side + lax.rem(group, per_side)
        held[pl.ds(pl.multiple_of(place * rows, 16), rows), :] = head_refs[j][...]
    columns = weight_ref.shape[1]
    tile = 256 if columns % 256 == 0 else columns
    side_rows = rows * per_side
    for n in range(columns // tile):
        here = slice(n * tile, (n + 1) * tile)
        product = jnp.dot(
            held[...], weight_ref[start : start + depth, here],
            preferred_element_type=f32,
        )
        if start:
            product = product + earlier_ref[:, here]
        if not last:
            out_refs[0][:, here] = product
        else:
            for k in range(side_count):
                out_refs[k][:, here] = product[k * side_rows : (k + 1) * side_rows, :].astype(
                    out_refs[k].dtype
                )


def output_product(head_pieces, weight, side_count, earlier, start, last):
    dev_count = len(head_pieces)
    rows, depth = head_pieces[0].shape
    columns = weight.shape[1]
    side_rows = rows * dev_count // side_count
    if not last:
        shapes = [((rows * dev_count, columns), f32)]
    else:
        shapes = [((side_rows, columns), f32 if k == 0 else bf16) for k in range(side_count)]
    earlier = [] if earlier is None else [earlier]
    return pl.pallas_call(
        functools.partial(output_kernel, dev_count, side_count, start, last),
        out_shape=[jax.ShapeDtypeStruct(*shape) for shape in shapes],
        in_specs=[in_vmem] * (dev_count + 1 + len(earlier)),
        out_specs=[in_vmem] * len(shapes),
        scratch_shapes=[pltpu.VMEM((dev_count * rows, depth), bf16)],
        compiler_params=pltpu.CompilerParams(vmem_limit_bytes=10 * mib),
        name="output_product",
    )(*head_pieces, weight, *earlier)


def on_device(
    prompts,
    latent_weight,
    latent_gain,
    row_request,
    context_len,
    request_slot,
    latent_cache,
    new_latent,
    queries,
    key_absorb,
    value_absorb,
    out_weight,
):
    dev_count = lax.axis_size("dev")
    side_count = lax.axis_size("side")
    tok_rows, model_width = prompts.shape
    shard_rows, kv_width = latent_weight.shape
    lat_width = latent_gain.shape[0]
    nope_width = value_absorb.shape[2]
    rope_width = kv_width - lat_width
    cap_slots, ctx_len, _ = latent_cache.shape
    step_count = new_latent.shape[1]
    bucket_rows = 2 * tok_rows // dev_count
    group_rows = dev_count * bucket_rows
    slab = model_width // dev_count

    x_pieces = list(split_columns(prompts, dev_count))
    packs = shard_rows % 32 == 0
    x_pieces[0], own_weight = lax.optimization_barrier((x_pieces[0], latent_weight))
    weights = [pack_weight(own_weight) if packs else own_weight] + [None] * (side_count - 1)
    for k in range(2, side_count, 2):
        weights[k] = swap(weights[0], "side", k)
    for k in sorted(range(1, dev_count), reverse=True):
        x_pieces[k] = swap(x_pieces[k], "dev", k)

    score_scale = queries.shape[-1] ** (-0.5)
    half = rope_width // 2
    inverse = 1.0 / 10000.0 ** (jnp.arange(half, dtype=f32) * (2.0 / rope_width))
    lengths, x_pieces[0] = lax.optimization_barrier((context_len, x_pieces[0]))
    (
        query_full, top_held, sum_held, mix_held, live, target, cosine, sine, row_slot,
        value_here, out_here,
    ) = prepare(
        score_scale, dev_count, side_count, bucket_rows, lengths, request_slot,
        row_request.reshape(-1, 128), inverse.reshape(1, -1), queries, key_absorb,
        jnp.swapaxes(latent_cache, 1, 2), new_latent, value_absorb, out_weight,
    )

    weights[0::2], top_held = lax.optimization_barrier((weights[0::2], top_held))
    for k in range(0, side_count, 2):
        weights[k + 1] = swap(weights[k], "side", 1)
    if not packs:
        my_side = lax.axis_index("side")
        held = jnp.zeros((side_count, shard_rows, kv_width), bf16)
        for k in range(side_count):
            held = lax.dynamic_update_slice(held, weights[k][None], (my_side ^ k, 0, 0))
        weights = [held.reshape(slab, kv_width)]

    routed = project(stack_rows(x_pieces), weights, target, kv_width, dev_count)
    layout = (score_scale, cap_slots, step_count, group_rows // 2)
    state = top_held, sum_held, mix_held
    for which in range(2):
        half = list(routed[which * dev_count : (which + 1) * dev_count])
        for k in sorted(range(1, dev_count), reverse=True):
            half[k] = swap(half[k], "dev", k)
        latent_rows = finish(half[:1] + half[:0:-1], latent_gain.reshape(1, -1), cosine, sine, which)
        pieces = [
            swap(latent_rows, "side", k) if k else latent_rows for k in piece_order(side_count)
        ]
        if which == 0:
            state = absorb(layout, which, query_full, row_slot, *state, pieces)
    product, first_head, head_count = None, 0, value_absorb.shape[0]
    for part_heads in (head_count * 9 // 16, head_count * 7 // 16):
        head_out = attend(
            layout, 1, query_full, row_slot, *state, live, value_here, pieces, first_head,
            part_heads,
        )
        heads = [head_out] + [None] * (dev_count - 1)
        for k in sorted(range(1, dev_count), reverse=True):
            if k == 1 or k % 2 == 0:
                heads[k] = swap(head_out, "dev", k)
        for k in range(3, dev_count, 2):
            heads[k] = swap(heads[k - 1], "dev", 1)
        start, first_head = first_head * nope_width, first_head + part_heads
        products = output_product(
            heads, out_here, side_count, product, start, first_head == head_count
        )
        product = products[0]
    result = products[0]
    for k in sorted(range(1, side_count), reverse=True):
        result = result + swap(products[k], "side", k).astype(f32)
    return result.astype(bf16)


def solution(mesh):
    placed = (
        P(("rep", "dev", "side"), None),
        P(("dev", "side"), None),
        P(),
        P("rep"),
        P("rep"),
        P("rep"),
        P(("rep", "dev"), None, None),
        P(("rep", "dev"), None, None),
        P(("rep", "dev"), None, "side", None),
        P("side", None, None),
        P("side", None, None),
        P("side", "dev"),
    )
    return jax.shard_map(
        on_device, mesh=mesh, in_specs=placed, out_specs=P(("rep", "side"), "dev"), check_vma=False
    )
```

```python
import functools

import jax
import jax.numpy as jnp
from jax import lax
from jax.experimental import pallas as pl
from jax.experimental.pallas import tpu as pltpu
from jax.sharding import PartitionSpec as P

masked_score = -1e30
bf16, f32 = jnp.bfloat16, jnp.float32
in_vmem = pl.BlockSpec(memory_space=pltpu.VMEM)
in_smem = pl.BlockSpec(memory_space=pltpu.SMEM)
in_hbm = pl.BlockSpec(memory_space=pltpu.HBM)
mib = 1024 * 1024
prepare_mib = 16


def swap(value, axis, step):
    count = lax.axis_size(axis)
    return lax.ppermute(value, axis, [(i, i ^ step) for i in range(count)])


def pick(pieces, index):
    out = pieces[0]
    for k in range(1, len(pieces)):
        out = jnp.where(index == k, pieces[k], out)
    return out


def lane_tiles(width):
    return [slice(n, min(n + 128, width)) for n in range(0, width, 128)]


def packed_rows(rows, width):
    return rows * (width // 128) + rows // 2


def pack(value):
    rows, width = value.shape
    full = width // 128
    rest = value[:, full * 128 :]
    parts = [value[:, n * 128 : (n + 1) * 128] for n in range(full)]
    return parts + [jnp.concatenate([rest[: rows // 2], rest[rows // 2 :]], axis=1)]


def store_packed(ref, value):
    first = 0
    for part in pack(value):
        ref[first : first + part.shape[0], :] = part.astype(ref.dtype)
        first += part.shape[0]


def load_packed(ref, rows):
    full = ref.shape[0] // rows
    tiles = [ref[n * rows : (n + 1) * rows, :] for n in range(full)]
    rest = ref[full * rows :, :]
    return tiles, jnp.concatenate([rest[:, :64], rest[:, 64:]], axis=0)


def pack_kernel(value_ref, out_ref):
    store_packed(out_ref, value_ref[...])


def pack_weight(weight):
    rows, width = weight.shape
    return pl.pallas_call(
        pack_kernel,
        out_shape=jax.ShapeDtypeStruct((packed_rows(rows, width), 128), weight.dtype),
        in_specs=[in_vmem],
        out_specs=in_vmem,
        compiler_params=pltpu.CompilerParams(vmem_limit_bytes=8 * mib),
        cost_estimate=pl.CostEstimate(flops=10**10, bytes_accessed=10**6, transcendentals=0),
        name="pack_weight",
    )(weight)


def split_kernel(slab, prompts_ref, *refs):
    my_dev = lax.axis_index("dev")
    out_refs, sems = refs[:-1], refs[-1]
    copies = []
    for k in range(len(out_refs))[::-1]:
        first = pl.multiple_of((my_dev ^ k) * slab, 128)
        copies.append(
            pltpu.make_async_copy(prompts_ref.at[:, pl.ds(first, slab)], out_refs[k], sems.at[k])
        )
    for copy in copies:
        copy.start()
    for copy in copies:
        copy.wait()


def split_columns(prompts, count):
    rows, width = prompts.shape
    slab = width // count
    if slab % 128:
        columns = [prompts[:, k * slab : (k + 1) * slab] for k in range(count)]
        my_dev = lax.axis_index("dev")
        return [pick(columns, my_dev ^ k) for k in range(count)]
    return pl.pallas_call(
        functools.partial(split_kernel, slab),
        out_shape=[jax.ShapeDtypeStruct((rows, slab), prompts.dtype)] * count,
        in_specs=[in_hbm],
        out_specs=[in_vmem] * count,
        scratch_shapes=[pltpu.SemaphoreType.DMA((count,))],
        compiler_params=pltpu.CompilerParams(vmem_limit_bytes=8 * mib),
        cost_estimate=pl.CostEstimate(
            flops=10**10, bytes_accessed=4 * 10**7, transcendentals=0
        ),
        name="split_columns",
    )(pltpu.with_memory_space_constraint(prompts, pltpu.HBM))


def fill_tables(
    dev_count, side_count, bucket, cap_slots, length_ref, slot_ref, request_ref, inverse_ref,
    target_ref, cos_ref, sin_ref, spot_ref, to_ref, place_ref, local_ref, position_ref,
):
    my_dev, my_side = lax.axis_index("dev"), lax.axis_index("side")
    requests = request_ref[...]
    lane_rows, lanes = requests.shape
    tok_rows = bucket * dev_count // 2
    per_row = lanes // tok_rows
    half_bucket = bucket // 2
    half_rows = dev_count * half_bucket
    group_rows = 2 * half_rows
    before = lax.broadcasted_iota(jnp.int32, (lanes, lanes), 0)
    after = lax.broadcasted_iota(jnp.int32, (lanes, lanes), 1)
    below = jnp.where(before < after, 1.0, 0.0)
    near = jnp.where((before < after) & (before // tok_rows == after // tok_rows), 1.0, 0.0)
    scan = jnp.concatenate([below, jnp.ones_like(below)], axis=1).astype(bf16)
    lower = lax.broadcasted_iota(jnp.int32, (lane_rows, lane_rows), 0)
    upper = lax.broadcasted_iota(jnp.int32, (lane_rows, lane_rows), 1)
    rows_before = jnp.where(upper < lower, 1.0, 0.0)
    position = jnp.zeros(requests.shape, f32)
    slot = jnp.zeros(requests.shape, jnp.int32)
    for q in range(slot_ref.shape[0]):
        hit = requests == q
        ranks = jnp.dot(
            jnp.where(hit, 1.0, 0.0).astype(bf16), scan, preferred_element_type=f32
        )
        earlier = jnp.dot(rows_before, ranks[:, lanes:], preferred_element_type=f32)
        start = length_ref[q].astype(f32)
        position = jnp.where(hit, ranks[:, :lanes] + earlier + start, position)
        slot = jnp.where(hit, slot_ref[q], slot)
    group = lax.div(slot, cap_slots)
    rank = jnp.zeros(requests.shape, f32)
    for g in range(dev_count):
        hit = group == g
        ranks = jnp.dot(
            jnp.where(hit, 1.0, 0.0).astype(bf16), near.astype(bf16), preferred_element_type=f32
        )
        rank = jnp.where(hit, ranks, rank)
    block = lax.broadcasted_iota(jnp.int32, requests.shape, 0) * per_row + lax.div(
        lax.broadcasted_iota(jnp.int32, requests.shape, 1), tok_rows
    )
    rank = rank.astype(jnp.int32)
    which = lax.div(rank, half_bucket)
    place = lax.div(block, side_count) * half_bucket + lax.rem(rank, half_bucket)
    to_ref[...] = (which * dev_count + (group ^ my_dev)) * half_rows + place
    place = which * half_rows + place
    place_ref[...] = jnp.where(group == my_dev, place, -1)
    local_ref[...] = (slot - my_dev * cap_slots + 1).astype(f32)
    position_ref[...] = position
    lane_block = lax.div(lax.broadcasted_iota(jnp.int32, (1, lanes), 1), tok_rows)
    ids = lax.broadcasted_iota(jnp.int32, (group_rows, 1), 0)

    def find(dev, side):
        held = dev * side_count + side
        return pl.ds(lax.div(held, per_row), 1), lane_block == lax.rem(held, per_row)

    targets = []
    for k in range(dev_count):
        held = (my_dev ^ k) * side_count + my_side
        row = jnp.broadcast_to(to_ref[pl.ds(lax.div(held, per_row), 1), :], (8, lanes))
        start = lax.rem(lanes - tok_rows * lax.rem(held, per_row), lanes)
        targets.append(pltpu.roll(row, start, 1)[:1, :tok_rows])
    for k in range(0, dev_count, per_row):
        target_ref[:, k * tok_rows : k * tok_rows + lanes] = jnp.concatenate(
            targets[k : k + per_row], axis=1
        )
    found = jnp.zeros((group_rows, lanes), f32)
    for d in range(dev_count):
        row, inside = find(d, my_side)
        found = jnp.where((place_ref[row, :] == ids) & inside, position_ref[row, :], found)
    angles = jnp.sum(found, axis=1, keepdims=True) * inverse_ref[...]
    cos_ref[...] = jnp.cos(angles)
    sin_ref[...] = jnp.sin(angles)
    for k in range(side_count):
        total = jnp.zeros((8, group_rows), f32)
        for d in range(dev_count):
            row, inside = find(d, my_side ^ k)
            chosen = jnp.where((place_ref[row, :] == ids) & inside, 1.0, 0.0).astype(bf16)
            values = jnp.broadcast_to(local_ref[row, :], (8, lanes)).astype(bf16)
            total = total + lax.dot_general(
                values, chosen, (((1,), (1,)), ((), ())), preferred_element_type=f32
            )
        spot_ref[:, k * group_rows : (k + 1) * group_rows] = total[:1].astype(jnp.int32)


def prepare_kernel(
    scale, steps, layout, inverse_ref, length_hbm, slot_hbm, request_hbm, query_hbm, absorb_hbm,
    cache_hbm, fresh_hbm, value_hbm, out_hbm, full_ref, top_ref, sum_ref, mix_ref, live_ref, target_ref,
    cos_ref, sin_ref, spot_ref, value_ref, out_ref, length_ref, slot_ref, request_ref, query_ref,
    absorb_ref, cache_ref, fresh_ref, plain, full, to_ref, place_ref, local_ref, position_ref, sems,
):
    pairs = [
        (length_hbm, length_ref), (slot_hbm, slot_ref), (request_hbm, request_ref),
        (query_hbm, query_ref), (absorb_hbm, absorb_ref), (cache_hbm, cache_ref),
        (fresh_hbm, fresh_ref), (value_hbm, value_ref),
    ]
    parts = sems.shape[0] - len(pairs)
    rows = out_hbm.shape[0] // parts
    for n in range(parts):
        part = pl.ds(n * rows, rows)
        pairs.append((out_hbm.at[part], out_ref.at[part]))
    copies = [pltpu.make_async_copy(*pair, sems.at[n]) for n, pair in enumerate(pairs)]
    for copy in copies:
        copy.start()
    for copy in copies[:3]:
        copy.wait()
    slots, _, context = cache_ref.shape
    heads, nope, lat_width = absorb_ref.shape
    per_head = slots * steps
    fill_tables(
        *layout, slots, length_ref, slot_ref, request_ref, inverse_ref, target_ref, cos_ref,
        sin_ref, spot_ref, to_ref, place_ref, local_ref, position_ref,
    )
    first_slot = lax.axis_index("dev") * slots
    lengths = []
    for s in range(slots):
        length = jnp.int32(0)
        for q in range(slot_ref.shape[0]):
            length = jnp.where(slot_ref[q] == first_slot + s, length_ref[q], length)
        lengths.append(length)
    slot_of = lax.div(lax.broadcasted_iota(jnp.int32, live_ref.shape, 0), steps)
    live = jnp.zeros(live_ref.shape, f32)
    for s in range(slots):
        live = jnp.where((slot_of == s) & (lengths[s] > 0), 1.0, live)
    live_ref[...] = live
    copies[3].wait()
    copies[4].wait()
    for n, here in enumerate(lane_tiles(query_ref.shape[1])):
        plain[n, :, : here.stop - here.start] = query_ref[:, here].astype(f32)
    wide = lane_tiles(full_ref.shape[1])
    for h in range(heads):
        there = pl.ds(h, per_head, stride=heads)
        query = plain[0, there, :].astype(bf16)
        latent = jnp.dot(query, absorb_ref[h], preferred_element_type=f32).astype(bf16).astype(f32)
        here = slice(h * per_head, (h + 1) * per_head)
        for n, lanes in enumerate(lane_tiles(lat_width)):
            full[n, here, :] = latent[:, lanes]
        full[len(wide) - 1, here, :] = plain[1, there, :]
    for n, lanes in enumerate(wide):
        full_ref[:, lanes] = full[n, :, : lanes.stop - lanes.start].astype(bf16)
    key = lax.broadcasted_iota(jnp.int32, (1, context), 1)
    copies[5].wait()
    copies[6].wait()
    late = lax.broadcasted_iota(jnp.int32, (steps * heads, steps), 1)
    late = late > lax.div(lax.broadcasted_iota(jnp.int32, (steps * heads, steps), 0), heads)
    for s in range(slots):
        theres = [pl.ds(s * steps + t, heads, stride=per_head) for t in range(steps)]
        query = jnp.concatenate(
            [
                jnp.concatenate([full[n, there, :] for there in theres], axis=0)[
                    :, : lanes.stop - lanes.start
                ].astype(bf16)
                for n, lanes in enumerate(wide)
            ],
            axis=1,
        )
        rows = cache_ref[s]
        score = jnp.dot(query, rows, preferred_element_type=f32)
        score = jnp.where(key < lengths[s], score * scale, masked_score)
        fresh = fresh_ref[s]
        new = lax.dot_general(
            query, fresh, (((1,), (1,)), ((), ())), preferred_element_type=f32
        )
        new = jnp.where(late, masked_score, new * scale)
        top = jnp.maximum(
            jnp.max(score, axis=1, keepdims=True), jnp.max(new, axis=1, keepdims=True)
        )
        weight = jnp.exp(score - top)
        new = jnp.exp(new - top)
        total = jnp.sum(weight, axis=1, keepdims=True) + jnp.sum(new, axis=1, keepdims=True)
        mix = lax.dot_general(
            weight.astype(bf16), rows[:lat_width, :], (((1,), (1,)), ((), ())),
            preferred_element_type=f32,
        )
        for u in range(steps):
            mix = mix + new[:, u : u + 1].astype(bf16).astype(f32) * fresh[
                u : u + 1, :lat_width
            ].astype(f32)
        lanes = top_ref.shape[1]
        for t in range(steps):
            there = theres[t]
            here = slice(t * heads, (t + 1) * heads)
            top_ref[there, :] = jnp.broadcast_to(top[here], (heads, lanes))
            sum_ref[there, :] = jnp.broadcast_to(total[here], (heads, lanes))
            for n, part in enumerate(lane_tiles(lat_width)):
                mix_ref[n, there, :] = mix[here, part]
    for copy in copies[7:]:
        copy.wait()


def prepare(
    scale, dev_count, side_count, bucket, lengths, request_slot, requests, inverse, queries,
    absorb, cache, fresh, value, out_weight,
):
    slots, steps, heads, width = queries.shape
    kv_width = cache.shape[1]
    lat_width = absorb.shape[2]
    rows = slots * steps * heads
    group_rows = dev_count * bucket
    parts = 8
    lanes = requests.shape[1]
    half = inverse.shape[1]
    shapes = [
        ((rows, kv_width), bf16), ((rows, 128), f32), ((rows, 128), f32),
        ((lat_width // 128, rows, 128), f32), ((slots * steps, 128), f32),
        ((1, group_rows // 2 * dev_count), jnp.int32), ((group_rows, half), f32), ((group_rows, half), f32),
        ((1, side_count * group_rows), jnp.int32), (value.shape, bf16), (out_weight.shape, bf16),
    ]
    return pl.pallas_call(
        functools.partial(prepare_kernel, scale, steps, (dev_count, side_count, bucket)),
        out_shape=[jax.ShapeDtypeStruct(*shape) for shape in shapes],
        in_specs=[in_vmem] + [in_hbm] * 9,
        out_specs=[in_vmem] * len(shapes),
        scratch_shapes=[
            pltpu.SMEM(lengths.shape, lengths.dtype),
            pltpu.SMEM(request_slot.shape, request_slot.dtype),
            pltpu.VMEM(requests.shape, requests.dtype),
            pltpu.VMEM((rows, width), queries.dtype),
            pltpu.VMEM(absorb.shape, absorb.dtype),
            pltpu.VMEM(cache.shape, cache.dtype),
            pltpu.VMEM(fresh.shape, fresh.dtype),
            pltpu.VMEM((len(lane_tiles(width)), rows, 128), f32),
            pltpu.VMEM((len(lane_tiles(kv_width)), rows, 128), f32),
            pltpu.VMEM(requests.shape, jnp.int32),
            pltpu.VMEM(requests.shape, jnp.int32),
            pltpu.VMEM(requests.shape, f32),
            pltpu.VMEM(requests.shape, f32),
            pltpu.SemaphoreType.DMA((parts + 8,)),
        ],
        compiler_params=pltpu.CompilerParams(vmem_limit_bytes=prepare_mib * mib),
        cost_estimate=pl.CostEstimate(
            flops=4 * 10**10, bytes_accessed=28 * 10**6, transcendentals=10**5
        ),
        name="prepare",
    )(inverse, lengths, request_slot, requests, queries.reshape(rows, width), absorb, cache, fresh,
      value, out_weight)


def stack_kernel(*refs):
    out_ref = refs[-1]
    rows = refs[0].shape[0]
    for n, ref in enumerate(refs[:-1]):
        k = (len(refs) - 1 - n) % (len(refs) - 1)
        out_ref[k * rows : (k + 1) * rows, :] = ref[...]


def stack_rows(pieces):
    rows, width = pieces[0].shape
    return pl.pallas_call(
        stack_kernel,
        out_shape=jax.ShapeDtypeStruct((len(pieces) * rows, width), bf16),
        in_specs=[in_vmem] * len(pieces),
        out_specs=in_vmem,
        compiler_params=pltpu.CompilerParams(vmem_limit_bytes=8 * mib),
        cost_estimate=pl.CostEstimate(flops=2 * 10**10, bytes_accessed=10**6, transcendentals=0),
        name="stack_rows",
    )(pieces[0], *pieces[:0:-1])


def project_kernel(dev_count, side_count, target_ref, x_ref, *refs):
    my_side = lax.axis_index("side")
    weight_refs = refs[:side_count]
    out_refs, slab_weight = refs[side_count:-1], refs[-1]
    tok_rows = x_ref.shape[0] // dev_count
    full = slab_weight.shape[1] // 128
    if side_count > 1:
        shard = slab_weight.shape[0] // side_count
        for k in range(side_count):
            first = pl.multiple_of((my_side ^ k) * shard, 16)
            tiles, rest = load_packed(weight_refs[k], shard)
            for n, tile in enumerate(tiles):
                slab_weight[pl.ds(first, shard), n * 128 : (n + 1) * 128] = tile
            slab_weight[pl.ds(first, shard), full * 128 :] = rest
    slab = slab_weight[...] if side_count > 1 else weight_refs[0][...]
    raw = jnp.dot(x_ref[...], slab, preferred_element_type=f32).astype(bf16)
    target = target_ref[...]
    half_rows = tok_rows
    step = min(4, 2 * dev_count)
    for j in range(0, 2 * dev_count, step):
        ids = lax.broadcasted_iota(jnp.int32, (step * half_rows, target.shape[1]), 0)
        route = jnp.where(ids + j * half_rows == target, 1.0, 0.0).astype(bf16)
        placed = jnp.dot(route, raw, preferred_element_type=f32)
        for n in range(step):
            store_packed(out_refs[j + n], placed[n * half_rows : (n + 1) * half_rows])


def project(x_rows, weights, target, width, dev_count):
    tok_rows, slab = x_rows.shape[0] // dev_count, x_rows.shape[1]
    return pl.pallas_call(
        functools.partial(project_kernel, dev_count, len(weights)),
        out_shape=[
            jax.ShapeDtypeStruct(
                (packed_rows(tok_rows, width), 128), f32 if j % dev_count == 0 else bf16
            )
            for j in range(2 * dev_count)
        ],
        in_specs=[in_vmem] * (2 + len(weights)),
        out_specs=[in_vmem] * (2 * dev_count),
        scratch_shapes=[
            pltpu.VMEM((slab, width), bf16),
        ],
        compiler_params=pltpu.CompilerParams(vmem_limit_bytes=20 * mib),
        name="project",
    )(target, x_rows, *weights)


def finish_kernel(which, gain_ref, cos_ref, sin_ref, *refs):
    parts, out_ref = refs[:-1], refs[-1]
    rows, half = cos_ref.shape[0] // 2, cos_ref.shape[1]
    mine = slice(which * rows, (which + 1) * rows)
    total = parts[0][...].astype(f32)
    for part in parts[1:]:
        total = total + part[...].astype(f32)
    tiles, rest = load_packed(total, rows)
    latent = jnp.concatenate(tiles, axis=1)
    spread = jnp.mean(latent * latent, axis=1, keepdims=True)
    latent = latent * lax.rsqrt(spread + 1e-06) * gain_ref[...]
    first, second = rest[:, :half], rest[:, half:]
    cosine, sine = cos_ref[mine, :], sin_ref[mine, :]
    store_packed(
        out_ref,
        jnp.concatenate(
            [latent, first * cosine - second * sine, second * cosine + first * sine], axis=1
        ),
    )


def finish(parts, gain, cosine, sine, which):
    return pl.pallas_call(
        functools.partial(finish_kernel, which),
        out_shape=jax.ShapeDtypeStruct(parts[0].shape, bf16),
        in_specs=[in_vmem] * (3 + len(parts)),
        out_specs=in_vmem,
        compiler_params=pltpu.CompilerParams(vmem_limit_bytes=8 * mib),
        name="finish_rows",
    )(gain, cosine, sine, *parts)


def piece_order(count):
    return [0, 1, *range(3, count, 2), *range(2, count, 2)]


def take_keys(keys, pieces, lat_width):
    rows = keys.shape[0] // len(pieces)
    for n, piece in zip(piece_order(len(pieces)), pieces):
        tiles, rest = load_packed(piece, rows)
        there = slice(n * rows, (n + 1) * rows)
        for j, tile in enumerate(tiles):
            keys[there, j * 128 : (j + 1) * 128] = tile
        keys[there, lat_width:] = rest


def merge(layout, which, mine, query_ref, slot_ref, top_ref, sum_ref, mix_ref, keys):
    scale, cap_slots, steps, half_rows = layout
    lat_width = mix_ref.shape[0] * mix_ref.shape[2]
    row = lax.broadcasted_iota(jnp.int32, (mine.stop - mine.start, 1), 0)
    row_slot = (row // steps) % cap_slots
    query = query_ref[mine, :]
    score = lax.dot_general(
        query, keys[...], (((1,), (1,)), ((), ())), preferred_element_type=f32
    )
    count = slot_ref.shape[1]
    part = half_rows
    slots = jnp.concatenate(
        [slot_ref[:, n + which * part : n + (which + 1) * part] for n in range(0, count, 2 * part)],
        axis=1,
    )
    score = jnp.where(slots == row_slot + 1, score * scale, masked_score)
    top_held = top_ref[mine, :1]
    top = jnp.maximum(top_held, jnp.max(score, axis=1, keepdims=True))
    held = jnp.exp(top_held - top)
    weight = jnp.exp(score - top)
    total = sum_ref[mine, :1] * held + jnp.sum(weight, axis=1, keepdims=True)
    mix = jnp.dot(weight.astype(bf16), keys[:, :lat_width], preferred_element_type=f32)
    mix_held = jnp.concatenate([mix_ref[n, mine, :] for n in range(mix_ref.shape[0])], axis=1)
    return top, total, mix_held * held + mix


def absorb_kernel(layout, which, query_ref, slot_ref, top_ref, sum_ref, mix_ref, *refs):
    pieces, (new_top, new_sum, new_mix, keys) = refs[:-4], refs[-4:]
    take_keys(keys, pieces, mix_ref.shape[0] * mix_ref.shape[2])
    rows, lanes = top_ref.shape
    step = rows // 2
    for first in range(0, rows, step):
        mine = slice(first, first + step)
        top, total, mix = merge(
            layout, which, mine, query_ref, slot_ref, top_ref, sum_ref, mix_ref, keys
        )
        new_top[mine, :] = jnp.broadcast_to(top, (step, lanes))
        new_sum[mine, :] = jnp.broadcast_to(total, (step, lanes))
        for n, part in enumerate(lane_tiles(mix.shape[1])):
            new_mix[n, mine, :] = mix[:, part]


def absorb(layout, which, query, row_slot, top, total, mix, pieces):
    return pl.pallas_call(
        functools.partial(absorb_kernel, layout, which),
        out_shape=[jax.ShapeDtypeStruct(x.shape, f32) for x in (top, total, mix)],
        in_specs=[in_vmem] * (5 + len(pieces)),
        out_specs=[in_vmem] * 3,
        scratch_shapes=[pltpu.VMEM((row_slot.shape[1] // 2, query.shape[1]), bf16)],
        compiler_params=pltpu.CompilerParams(vmem_limit_bytes=10 * mib),
        cost_estimate=pl.CostEstimate(flops=2 * 10**9, bytes_accessed=10**6, transcendentals=0),
        name="absorb",
    )(query, row_slot, top, total, mix, *pieces)


def attend_kernel(
    layout, which, first_head, heads, query_ref, slot_ref, top_ref, sum_ref, mix_ref, live_ref,
    value_ref, *refs
):
    pieces, out_ref, keys = refs[:-2], refs[-2], refs[-1]
    per_head = layout[1] * layout[2]
    take_keys(keys, pieces, mix_ref.shape[0] * mix_ref.shape[2])
    mine = slice(first_head * per_head, (first_head + heads) * per_head)
    _, total, mix = merge(
        layout, which, mine, query_ref, slot_ref, top_ref, sum_ref, mix_ref, keys
    )
    latent = (mix / total).astype(bf16)
    live = live_ref[:, :1]
    width = value_ref.shape[2]
    for h in range(heads):
        mixed = latent[h * per_head : (h + 1) * per_head, :]
        value = jnp.dot(mixed, value_ref[first_head + h], preferred_element_type=f32) * live
        out_ref[:, h * width : (h + 1) * width] = value.astype(bf16)


def attend(layout, which, query, row_slot, top, total, mix, live, value, pieces, first_head, heads):
    return pl.pallas_call(
        functools.partial(attend_kernel, layout, which, first_head, heads),
        out_shape=jax.ShapeDtypeStruct((live.shape[0], heads * value.shape[2]), bf16),
        in_specs=[in_vmem] * (7 + len(pieces)),
        out_specs=in_vmem,
        scratch_shapes=[pltpu.VMEM((row_slot.shape[1] // 2, query.shape[1]), bf16)],
        compiler_params=pltpu.CompilerParams(vmem_limit_bytes=10 * mib),
        name="attend",
    )(query, row_slot, top, total, mix, live, value, *pieces)


def output_kernel(dev_count, side_count, start, last, *refs):
    my_dev, my_side = lax.axis_index("dev"), lax.axis_index("side")
    head_refs = refs[:dev_count]
    weight_ref = refs[dev_count]
    earlier_ref = refs[dev_count + 1] if start else None
    out_refs = refs[dev_count + 1 + (start > 0) : -1]
    held = refs[-1]
    rows, depth = head_refs[0].shape
    per_side = dev_count // side_count
    for j in range(dev_count):
        group = my_dev ^ j
        place = (lax.div(group, per_side) ^ my_side) * per_side + lax.rem(group, per_side)
        held[pl.ds(pl.multiple_of(place * rows, 16), rows), :] = head_refs[j][...]
    columns = weight_ref.shape[1]
    tile = 256 if columns % 256 == 0 else columns
    side_rows = rows * per_side
    for n in range(columns // tile):
        here = slice(n * tile, (n + 1) * tile)
        product = jnp.dot(
            held[...], weight_ref[start : start + depth, here],
            preferred_element_type=f32,
        )
        if start:
            product = product + earlier_ref[:, here]
        if not last:
            out_refs[0][:, here] = product
        else:
            for k in range(side_count):
                out_refs[k][:, here] = product[k * side_rows : (k + 1) * side_rows, :].astype(
                    out_refs[k].dtype
                )


def output_product(head_pieces, weight, side_count, earlier, start, last):
    dev_count = len(head_pieces)
    rows, depth = head_pieces[0].shape
    columns = weight.shape[1]
    side_rows = rows * dev_count // side_count
    if not last:
        shapes = [((rows * dev_count, columns), f32)]
    else:
        shapes = [((side_rows, columns), f32 if k == 0 else bf16) for k in range(side_count)]
    earlier = [] if earlier is None else [earlier]
    return pl.pallas_call(
        functools.partial(output_kernel, dev_count, side_count, start, last),
        out_shape=[jax.ShapeDtypeStruct(*shape) for shape in shapes],
        in_specs=[in_vmem] * (dev_count + 1 + len(earlier)),
        out_specs=[in_vmem] * len(shapes),
        scratch_shapes=[pltpu.VMEM((dev_count * rows, depth), bf16)],
        compiler_params=pltpu.CompilerParams(vmem_limit_bytes=10 * mib),
        name="output_product",
    )(*head_pieces, weight, *earlier)


def on_device(
    prompts,
    latent_weight,
    latent_gain,
    row_request,
    context_len,
    request_slot,
    latent_cache,
    new_latent,
    queries,
    key_absorb,
    value_absorb,
    out_weight,
):
    dev_count = lax.axis_size("dev")
    side_count = lax.axis_size("side")
    tok_rows, model_width = prompts.shape
    shard_rows, kv_width = latent_weight.shape
    lat_width = latent_gain.shape[0]
    nope_width = value_absorb.shape[2]
    rope_width = kv_width - lat_width
    cap_slots, ctx_len, _ = latent_cache.shape
    step_count = new_latent.shape[1]
    bucket_rows = 2 * tok_rows // dev_count
    group_rows = dev_count * bucket_rows
    slab = model_width // dev_count

    x_pieces = list(split_columns(prompts, dev_count))
    packs = shard_rows % 32 == 0
    x_pieces[0], own_weight = lax.optimization_barrier((x_pieces[0], latent_weight))
    weights = [pack_weight(own_weight) if packs else own_weight] + [None] * (side_count - 1)
    for k in range(2, side_count, 2):
        weights[k] = swap(weights[0], "side", k)
    for k in sorted(range(1, dev_count), reverse=True):
        x_pieces[k] = swap(x_pieces[k], "dev", k)

    score_scale = queries.shape[-1] ** (-0.5)
    half = rope_width // 2
    inverse = 1.0 / 10000.0 ** (jnp.arange(half, dtype=f32) * (2.0 / rope_width))
    lengths, x_pieces[0] = lax.optimization_barrier((context_len, x_pieces[0]))
    (
        query_full, top_held, sum_held, mix_held, live, target, cosine, sine, row_slot,
        value_here, out_here,
    ) = prepare(
        score_scale, dev_count, side_count, bucket_rows, lengths, request_slot,
        row_request.reshape(-1, 128), inverse.reshape(1, -1), queries, key_absorb,
        jnp.swapaxes(latent_cache, 1, 2), new_latent, value_absorb, out_weight,
    )

    weights[0::2], top_held = lax.optimization_barrier((weights[0::2], top_held))
    for k in range(0, side_count, 2):
        weights[k + 1] = swap(weights[k], "side", 1)
    if not packs:
        my_side = lax.axis_index("side")
        held = jnp.zeros((side_count, shard_rows, kv_width), bf16)
        for k in range(side_count):
            held = lax.dynamic_update_slice(held, weights[k][None], (my_side ^ k, 0, 0))
        weights = [held.reshape(slab, kv_width)]

    routed = project(stack_rows(x_pieces), weights, target, kv_width, dev_count)
    layout = (score_scale, cap_slots, step_count, group_rows // 2)
    state = top_held, sum_held, mix_held
    for which in range(2):
        half = list(routed[which * dev_count : (which + 1) * dev_count])
        for k in sorted(range(1, dev_count), reverse=True):
            half[k] = swap(half[k], "dev", k)
        latent_rows = finish(half[:1] + half[:0:-1], latent_gain.reshape(1, -1), cosine, sine, which)
        pieces = [
            swap(latent_rows, "side", k) if k else latent_rows for k in piece_order(side_count)
        ]
        if which == 0:
            state = absorb(layout, which, query_full, row_slot, *state, pieces)
    product, first_head, head_count = None, 0, value_absorb.shape[0]
    for part_heads in (head_count * 9 // 16, head_count * 7 // 16):
        head_out = attend(
            layout, 1, query_full, row_slot, *state, live, value_here, pieces, first_head,
            part_heads,
        )
        heads = [head_out] + [None] * (dev_count - 1)
        for k in sorted(range(1, dev_count), reverse=True):
            if k == 1 or k % 2 == 0:
                heads[k] = swap(head_out, "dev", k)
        for k in range(3, dev_count, 2):
            heads[k] = swap(heads[k - 1], "dev", 1)
        start, first_head = first_head * nope_width, first_head + part_heads
        products = output_product(
            heads, out_here, side_count, product, start, first_head == head_count
        )
        product = products[0]
    result = products[0]
    for k in piece_order(side_count)[:0:-1]:
        result = result + swap(products[k], "side", k).astype(f32)
    return result.astype(bf16)


def solution(mesh):
    placed = (
        P(("rep", "dev", "side"), None),
        P(("dev", "side"), None),
        P(),
        P("rep"),
        P("rep"),
        P("rep"),
        P(("rep", "dev"), None, None),
        P(("rep", "dev"), None, None),
        P(("rep", "dev"), None, "side", None),
        P("side", None, None),
        P("side", None, None),
        P("side", "dev"),
    )
    return jax.shard_map(
        on_device, mesh=mesh, in_specs=placed, out_specs=P(("rep", "side"), "dev"), check_vma=False
    )
```

```python
import functools

import jax
import jax.numpy as jnp
from jax import lax
from jax.experimental import pallas as pl
from jax.experimental.pallas import tpu as pltpu
from jax.sharding import PartitionSpec as P

masked_score = -1e30
bf16, f32 = jnp.bfloat16, jnp.float32
in_vmem = pl.BlockSpec(memory_space=pltpu.VMEM)
in_smem = pl.BlockSpec(memory_space=pltpu.SMEM)
in_hbm = pl.BlockSpec(memory_space=pltpu.HBM)
mib = 1024 * 1024
prepare_mib = 16


def swap(value, axis, step):
    count = lax.axis_size(axis)
    return lax.ppermute(value, axis, [(i, i ^ step) for i in range(count)])


def pick(pieces, index):
    out = pieces[0]
    for k in range(1, len(pieces)):
        out = jnp.where(index == k, pieces[k], out)
    return out


def lane_tiles(width):
    return [slice(n, min(n + 128, width)) for n in range(0, width, 128)]


def packed_rows(rows, width):
    return rows * (width // 128) + rows // 2


def pack(value):
    rows, width = value.shape
    full = width // 128
    rest = value[:, full * 128 :]
    parts = [value[:, n * 128 : (n + 1) * 128] for n in range(full)]
    return parts + [jnp.concatenate([rest[: rows // 2], rest[rows // 2 :]], axis=1)]


def store_packed(ref, value):
    first = 0
    for part in pack(value):
        ref[first : first + part.shape[0], :] = part.astype(ref.dtype)
        first += part.shape[0]


def load_packed(ref, rows):
    full = ref.shape[0] // rows
    tiles = [ref[n * rows : (n + 1) * rows, :] for n in range(full)]
    rest = ref[full * rows :, :]
    return tiles, jnp.concatenate([rest[:, :64], rest[:, 64:]], axis=0)


def pack_kernel(value_ref, out_ref):
    store_packed(out_ref, value_ref[...])


def pack_weight(weight):
    rows, width = weight.shape
    return pl.pallas_call(
        pack_kernel,
        out_shape=jax.ShapeDtypeStruct((packed_rows(rows, width), 128), weight.dtype),
        in_specs=[in_vmem],
        out_specs=in_vmem,
        compiler_params=pltpu.CompilerParams(vmem_limit_bytes=8 * mib),
        cost_estimate=pl.CostEstimate(flops=10**10, bytes_accessed=10**6, transcendentals=0),
        name="pack_weight",
    )(weight)


def split_kernel(slab, prompts_ref, *refs):
    my_dev = lax.axis_index("dev")
    out_refs, sems = refs[:-1], refs[-1]
    copies = []
    for k in range(len(out_refs))[::-1]:
        first = pl.multiple_of((my_dev ^ k) * slab, 128)
        copies.append(
            pltpu.make_async_copy(prompts_ref.at[:, pl.ds(first, slab)], out_refs[k], sems.at[k])
        )
    for copy in copies:
        copy.start()
    for copy in copies:
        copy.wait()


def split_columns(prompts, count):
    rows, width = prompts.shape
    slab = width // count
    if slab % 128:
        columns = [prompts[:, k * slab : (k + 1) * slab] for k in range(count)]
        my_dev = lax.axis_index("dev")
        return [pick(columns, my_dev ^ k) for k in range(count)]
    return pl.pallas_call(
        functools.partial(split_kernel, slab),
        out_shape=[jax.ShapeDtypeStruct((rows, slab), prompts.dtype)] * count,
        in_specs=[in_hbm],
        out_specs=[in_vmem] * count,
        scratch_shapes=[pltpu.SemaphoreType.DMA((count,))],
        compiler_params=pltpu.CompilerParams(vmem_limit_bytes=8 * mib),
        cost_estimate=pl.CostEstimate(
            flops=10**10, bytes_accessed=4 * 10**7, transcendentals=0
        ),
        name="split_columns",
    )(pltpu.with_memory_space_constraint(prompts, pltpu.HBM))


def fill_tables(
    dev_count, side_count, bucket, cap_slots, length_ref, slot_ref, request_ref, inverse_ref,
    target_ref, cos_ref, sin_ref, spot_ref, to_ref, place_ref, local_ref, position_ref,
):
    my_dev, my_side = lax.axis_index("dev"), lax.axis_index("side")
    requests = request_ref[...]
    lane_rows, lanes = requests.shape
    tok_rows = bucket * dev_count // 2
    per_row = lanes // tok_rows
    half_bucket = bucket // 2
    half_rows = dev_count * half_bucket
    group_rows = 2 * half_rows
    before = lax.broadcasted_iota(jnp.int32, (lanes, lanes), 0)
    after = lax.broadcasted_iota(jnp.int32, (lanes, lanes), 1)
    below = jnp.where(before < after, 1.0, 0.0)
    near = jnp.where((before < after) & (before // tok_rows == after // tok_rows), 1.0, 0.0)
    scan = jnp.concatenate([below, jnp.ones_like(below)], axis=1).astype(bf16)
    lower = lax.broadcasted_iota(jnp.int32, (lane_rows, lane_rows), 0)
    upper = lax.broadcasted_iota(jnp.int32, (lane_rows, lane_rows), 1)
    rows_before = jnp.where(upper < lower, 1.0, 0.0)
    position = jnp.zeros(requests.shape, f32)
    slot = jnp.zeros(requests.shape, jnp.int32)
    for q in range(slot_ref.shape[0]):
        hit = requests == q
        ranks = jnp.dot(
            jnp.where(hit, 1.0, 0.0).astype(bf16), scan, preferred_element_type=f32
        )
        earlier = jnp.dot(rows_before, ranks[:, lanes:], preferred_element_type=f32)
        start = length_ref[q].astype(f32)
        position = jnp.where(hit, ranks[:, :lanes] + earlier + start, position)
        slot = jnp.where(hit, slot_ref[q], slot)
    group = lax.div(slot, cap_slots)
    rank = jnp.zeros(requests.shape, f32)
    for g in range(dev_count):
        hit = group == g
        ranks = jnp.dot(
            jnp.where(hit, 1.0, 0.0).astype(bf16), near.astype(bf16), preferred_element_type=f32
        )
        rank = jnp.where(hit, ranks, rank)
    block = lax.broadcasted_iota(jnp.int32, requests.shape, 0) * per_row + lax.div(
        lax.broadcasted_iota(jnp.int32, requests.shape, 1), tok_rows
    )
    rank = rank.astype(jnp.int32)
    which = lax.div(rank, half_bucket)
    place = lax.div(block, side_count) * half_bucket + lax.rem(rank, half_bucket)
    to_ref[...] = (which * dev_count + (group ^ my_dev)) * half_rows + place
    place = which * half_rows + place
    place_ref[...] = jnp.where(group == my_dev, place, -1)
    local_ref[...] = (slot - my_dev * cap_slots + 1).astype(f32)
    position_ref[...] = position
    lane_block = lax.div(lax.broadcasted_iota(jnp.int32, (1, lanes), 1), tok_rows)
    ids = lax.broadcasted_iota(jnp.int32, (group_rows, 1), 0)

    def find(dev, side):
        held = dev * side_count + side
        return pl.ds(lax.div(held, per_row), 1), lane_block == lax.rem(held, per_row)

    targets = []
    for k in range(dev_count):
        held = (my_dev ^ k) * side_count + my_side
        row = jnp.broadcast_to(to_ref[pl.ds(lax.div(held, per_row), 1), :], (8, lanes))
        start = lax.rem(lanes - tok_rows * lax.rem(held, per_row), lanes)
        targets.append(pltpu.roll(row, start, 1)[:1, :tok_rows])
    for k in range(0, dev_count, per_row):
        target_ref[:, k * tok_rows : k * tok_rows + lanes] = jnp.concatenate(
            targets[k : k + per_row], axis=1
        )
    found = jnp.zeros((group_rows, lanes), f32)
    for d in range(dev_count):
        row, inside = find(d, my_side)
        found = jnp.where((place_ref[row, :] == ids) & inside, position_ref[row, :], found)
    angles = jnp.sum(found, axis=1, keepdims=True) * inverse_ref[...]
    cos_ref[...] = jnp.cos(angles)
    sin_ref[...] = jnp.sin(angles)
    for k in range(side_count):
        total = jnp.zeros((8, group_rows), f32)
        for d in range(dev_count):
            row, inside = find(d, my_side ^ k)
            chosen = jnp.where((place_ref[row, :] == ids) & inside, 1.0, 0.0).astype(bf16)
            values = jnp.broadcast_to(local_ref[row, :], (8, lanes)).astype(bf16)
            total = total + lax.dot_general(
                values, chosen, (((1,), (1,)), ((), ())), preferred_element_type=f32
            )
        spot_ref[:, k * group_rows : (k + 1) * group_rows] = total[:1].astype(jnp.int32)


def prepare_kernel(
    scale, steps, layout, inverse_ref, length_hbm, slot_hbm, request_hbm, query_hbm, absorb_hbm,
    cache_hbm, fresh_hbm, value_hbm, out_hbm, full_ref, top_ref, sum_ref, mix_ref, live_ref, target_ref,
    cos_ref, sin_ref, spot_ref, value_ref, out_ref, length_ref, slot_ref, request_ref, query_ref,
    absorb_ref, cache_ref, fresh_ref, plain, full, to_ref, place_ref, local_ref, position_ref, sems,
):
    pairs = [
        (length_hbm, length_ref), (slot_hbm, slot_ref), (request_hbm, request_ref),
        (query_hbm, query_ref), (absorb_hbm, absorb_ref), (cache_hbm, cache_ref),
        (fresh_hbm, fresh_ref), (value_hbm, value_ref),
    ]
    parts = sems.shape[0] - len(pairs)
    rows = out_hbm.shape[0] // parts
    for n in range(parts):
        part = pl.ds(n * rows, rows)
        pairs.append((out_hbm.at[part], out_ref.at[part]))
    copies = [pltpu.make_async_copy(*pair, sems.at[n]) for n, pair in enumerate(pairs)]
    for copy in copies:
        copy.start()
    for copy in copies[:3]:
        copy.wait()
    slots, _, context = cache_ref.shape
    heads, nope, lat_width = absorb_ref.shape
    per_head = slots * steps
    fill_tables(
        *layout, slots, length_ref, slot_ref, request_ref, inverse_ref, target_ref, cos_ref,
        sin_ref, spot_ref, to_ref, place_ref, local_ref, position_ref,
    )
    first_slot = lax.axis_index("dev") * slots
    lengths = []
    for s in range(slots):
        length = jnp.int32(0)
        for q in range(slot_ref.shape[0]):
            length = jnp.where(slot_ref[q] == first_slot + s, length_ref[q], length)
        lengths.append(length)
    slot_of = lax.div(lax.broadcasted_iota(jnp.int32, live_ref.shape, 0), steps)
    live = jnp.zeros(live_ref.shape, f32)
    for s in range(slots):
        live = jnp.where((slot_of == s) & (lengths[s] > 0), 1.0, live)
    live_ref[...] = live
    copies[3].wait()
    copies[4].wait()
    for n, here in enumerate(lane_tiles(query_ref.shape[1])):
        plain[n, :, : here.stop - here.start] = query_ref[:, here].astype(f32)
    wide = lane_tiles(full_ref.shape[1])
    for h in range(heads):
        there = pl.ds(h, per_head, stride=heads)
        query = plain[0, there, :].astype(bf16)
        latent = jnp.dot(query, absorb_ref[h], preferred_element_type=f32).astype(bf16).astype(f32)
        here = slice(h * per_head, (h + 1) * per_head)
        for n, lanes in enumerate(lane_tiles(lat_width)):
            full[n, here, :] = latent[:, lanes]
        full[len(wide) - 1, here, :] = plain[1, there, :]
    for n, lanes in enumerate(wide):
        full_ref[:, lanes] = full[n, :, : lanes.stop - lanes.start].astype(bf16)
    key = lax.broadcasted_iota(jnp.int32, (1, context), 1)
    copies[5].wait()
    copies[6].wait()
    late = lax.broadcasted_iota(jnp.int32, (steps * heads, steps), 1)
    late = late > lax.div(lax.broadcasted_iota(jnp.int32, (steps * heads, steps), 0), heads)
    for s in range(slots):
        theres = [pl.ds(s * steps + t, heads, stride=per_head) for t in range(steps)]
        query = jnp.concatenate(
            [
                jnp.concatenate([full[n, there, :] for there in theres], axis=0)[
                    :, : lanes.stop - lanes.start
                ].astype(bf16)
                for n, lanes in enumerate(wide)
            ],
            axis=1,
        )
        rows = cache_ref[s]
        score = jnp.dot(query, rows, preferred_element_type=f32)
        score = jnp.where(key < lengths[s], score * scale, masked_score)
        fresh = fresh_ref[s]
        new = lax.dot_general(
            query, fresh, (((1,), (1,)), ((), ())), preferred_element_type=f32
        )
        new = jnp.where(late, masked_score, new * scale)
        top = jnp.maximum(
            jnp.max(score, axis=1, keepdims=True), jnp.max(new, axis=1, keepdims=True)
        )
        weight = jnp.exp(score - top)
        new = jnp.exp(new - top)
        total = jnp.sum(weight, axis=1, keepdims=True) + jnp.sum(new, axis=1, keepdims=True)
        mix = lax.dot_general(
            weight.astype(bf16), rows[:lat_width, :], (((1,), (1,)), ((), ())),
            preferred_element_type=f32,
        )
        for u in range(steps):
            mix = mix + new[:, u : u + 1].astype(bf16).astype(f32) * fresh[
                u : u + 1, :lat_width
            ].astype(f32)
        lanes = top_ref.shape[1]
        for t in range(steps):
            there = theres[t]
            here = slice(t * heads, (t + 1) * heads)
            top_ref[there, :] = jnp.broadcast_to(top[here], (heads, lanes))
            sum_ref[there, :] = jnp.broadcast_to(total[here], (heads, lanes))
            for n, part in enumerate(lane_tiles(lat_width)):
                mix_ref[n, there, :] = mix[here, part]
    for copy in copies[7:]:
        copy.wait()


def prepare(
    scale, dev_count, side_count, bucket, lengths, request_slot, requests, inverse, queries,
    absorb, cache, fresh, value, out_weight,
):
    slots, steps, heads, width = queries.shape
    kv_width = cache.shape[1]
    lat_width = absorb.shape[2]
    rows = slots * steps * heads
    group_rows = dev_count * bucket
    parts = 8
    lanes = requests.shape[1]
    half = inverse.shape[1]
    shapes = [
        ((rows, kv_width), bf16), ((rows, 128), f32), ((rows, 128), f32),
        ((lat_width // 128, rows, 128), f32), ((slots * steps, 128), f32),
        ((1, group_rows // 2 * dev_count), jnp.int32), ((group_rows, half), f32), ((group_rows, half), f32),
        ((1, side_count * group_rows), jnp.int32), (value.shape, bf16), (out_weight.shape, bf16),
    ]
    return pl.pallas_call(
        functools.partial(prepare_kernel, scale, steps, (dev_count, side_count, bucket)),
        out_shape=[jax.ShapeDtypeStruct(*shape) for shape in shapes],
        in_specs=[in_vmem] + [in_hbm] * 9,
        out_specs=[in_vmem] * len(shapes),
        scratch_shapes=[
            pltpu.SMEM(lengths.shape, lengths.dtype),
            pltpu.SMEM(request_slot.shape, request_slot.dtype),
            pltpu.VMEM(requests.shape, requests.dtype),
            pltpu.VMEM((rows, width), queries.dtype),
            pltpu.VMEM(absorb.shape, absorb.dtype),
            pltpu.VMEM(cache.shape, cache.dtype),
            pltpu.VMEM(fresh.shape, fresh.dtype),
            pltpu.VMEM((len(lane_tiles(width)), rows, 128), f32),
            pltpu.VMEM((len(lane_tiles(kv_width)), rows, 128), f32),
            pltpu.VMEM(requests.shape, jnp.int32),
            pltpu.VMEM(requests.shape, jnp.int32),
            pltpu.VMEM(requests.shape, f32),
            pltpu.VMEM(requests.shape, f32),
            pltpu.SemaphoreType.DMA((parts + 8,)),
        ],
        compiler_params=pltpu.CompilerParams(vmem_limit_bytes=prepare_mib * mib),
        cost_estimate=pl.CostEstimate(
            flops=4 * 10**10, bytes_accessed=28 * 10**6, transcendentals=10**5
        ),
        name="prepare",
    )(inverse, lengths, request_slot, requests, queries.reshape(rows, width), absorb, cache, fresh,
      value, out_weight)


def stack_kernel(*refs):
    out_ref = refs[-1]
    rows = refs[0].shape[0]
    for n, ref in enumerate(refs[:-1]):
        k = (len(refs) - 1 - n) % (len(refs) - 1)
        out_ref[k * rows : (k + 1) * rows, :] = ref[...]


def stack_rows(pieces):
    rows, width = pieces[0].shape
    return pl.pallas_call(
        stack_kernel,
        out_shape=jax.ShapeDtypeStruct((len(pieces) * rows, width), bf16),
        in_specs=[in_vmem] * len(pieces),
        out_specs=in_vmem,
        compiler_params=pltpu.CompilerParams(vmem_limit_bytes=8 * mib),
        cost_estimate=pl.CostEstimate(flops=2 * 10**10, bytes_accessed=10**6, transcendentals=0),
        name="stack_rows",
    )(pieces[0], *pieces[:0:-1])


def project_kernel(dev_count, side_count, target_ref, x_ref, *refs):
    my_side = lax.axis_index("side")
    weight_refs = refs[:side_count]
    out_refs = refs[side_count:-2]
    slab_weight, rows = refs[-2:]
    tok_rows = x_ref.shape[0] // dev_count
    full = slab_weight.shape[1] // 128
    if side_count > 1:
        shard = slab_weight.shape[0] // side_count
        for k in range(side_count):
            first = pl.multiple_of((my_side ^ k) * shard, 16)
            tiles, rest = load_packed(weight_refs[k], shard)
            for n, tile in enumerate(tiles):
                slab_weight[pl.ds(first, shard), n * 128 : (n + 1) * 128] = tile
            slab_weight[pl.ds(first, shard), full * 128 :] = rest
    slab = slab_weight[...] if side_count > 1 else weight_refs[0][...]
    raw = jnp.dot(x_ref[...], slab, preferred_element_type=f32).astype(bf16)
    rows[...] = raw
    target = target_ref[...]
    half_rows = tok_rows
    step = min(4, 2 * dev_count)
    for j in range(0, 2 * dev_count, step):
        ids = lax.broadcasted_iota(jnp.int32, (step * half_rows, target.shape[1]), 0)
        route = jnp.where(ids + j * half_rows == target, 1.0, 0.0).astype(bf16)
        placed = jnp.dot(route, rows[...], preferred_element_type=f32)
        for n in range(step):
            store_packed(out_refs[j + n], placed[n * half_rows : (n + 1) * half_rows])


def project(x_rows, weights, target, width, dev_count):
    tok_rows, slab = x_rows.shape[0] // dev_count, x_rows.shape[1]
    return pl.pallas_call(
        functools.partial(project_kernel, dev_count, len(weights)),
        out_shape=[
            jax.ShapeDtypeStruct(
                (packed_rows(tok_rows, width), 128), f32 if j % dev_count == 0 else bf16
            )
            for j in range(2 * dev_count)
        ],
        in_specs=[in_vmem] * (2 + len(weights)),
        out_specs=[in_vmem] * (2 * dev_count),
        scratch_shapes=[
            pltpu.VMEM((slab, width), bf16),
            pltpu.VMEM((target.shape[1], width), bf16),
        ],
        compiler_params=pltpu.CompilerParams(vmem_limit_bytes=20 * mib),
        name="project",
    )(target, x_rows, *weights)


def finish_kernel(which, gain_ref, cos_ref, sin_ref, *refs):
    parts, out_ref = refs[:-1], refs[-1]
    rows, half = cos_ref.shape[0] // 2, cos_ref.shape[1]
    mine = slice(which * rows, (which + 1) * rows)
    total = parts[0][...].astype(f32)
    for part in parts[1:]:
        total = total + part[...].astype(f32)
    tiles, rest = load_packed(total, rows)
    latent = jnp.concatenate(tiles, axis=1)
    spread = jnp.mean(latent * latent, axis=1, keepdims=True)
    latent = latent * lax.rsqrt(spread + 1e-06) * gain_ref[...]
    first, second = rest[:, :half], rest[:, half:]
    cosine, sine = cos_ref[mine, :], sin_ref[mine, :]
    store_packed(
        out_ref,
        jnp.concatenate(
            [latent, first * cosine - second * sine, second * cosine + first * sine], axis=1
        ),
    )


def finish(parts, gain, cosine, sine, which):
    return pl.pallas_call(
        functools.partial(finish_kernel, which),
        out_shape=jax.ShapeDtypeStruct(parts[0].shape, bf16),
        in_specs=[in_vmem] * (3 + len(parts)),
        out_specs=in_vmem,
        compiler_params=pltpu.CompilerParams(vmem_limit_bytes=8 * mib),
        name="finish_rows",
    )(gain, cosine, sine, *parts)


def piece_order(count):
    return [0, 1, *range(3, count, 2), *range(2, count, 2)]


def take_keys(keys, pieces, lat_width):
    rows = keys.shape[0] // len(pieces)
    for n, piece in zip(piece_order(len(pieces)), pieces):
        tiles, rest = load_packed(piece, rows)
        there = slice(n * rows, (n + 1) * rows)
        for j, tile in enumerate(tiles):
            keys[there, j * 128 : (j + 1) * 128] = tile
        keys[there, lat_width:] = rest


def merge(layout, which, mine, query_ref, slot_ref, top_ref, sum_ref, mix_ref, keys):
    scale, cap_slots, steps, half_rows = layout
    lat_width = mix_ref.shape[0] * mix_ref.shape[2]
    row = lax.broadcasted_iota(jnp.int32, (mine.stop - mine.start, 1), 0)
    row_slot = (row // steps) % cap_slots
    query = query_ref[mine, :]
    score = lax.dot_general(
        query, keys[...], (((1,), (1,)), ((), ())), preferred_element_type=f32
    )
    count = slot_ref.shape[1]
    part = half_rows
    slots = jnp.concatenate(
        [slot_ref[:, n + which * part : n + (which + 1) * part] for n in range(0, count, 2 * part)],
        axis=1,
    )
    score = jnp.where(slots == row_slot + 1, score * scale, masked_score)
    top_held = top_ref[mine, :1]
    top = jnp.maximum(top_held, jnp.max(score, axis=1, keepdims=True))
    held = jnp.exp(top_held - top)
    weight = jnp.exp(score - top)
    total = sum_ref[mine, :1] * held + jnp.sum(weight, axis=1, keepdims=True)
    mix = jnp.dot(weight.astype(bf16), keys[:, :lat_width], preferred_element_type=f32)
    mix_held = jnp.concatenate([mix_ref[n, mine, :] for n in range(mix_ref.shape[0])], axis=1)
    return top, total, mix_held * held + mix


def absorb_kernel(layout, which, query_ref, slot_ref, top_ref, sum_ref, mix_ref, *refs):
    pieces, (new_top, new_sum, new_mix, keys) = refs[:-4], refs[-4:]
    take_keys(keys, pieces, mix_ref.shape[0] * mix_ref.shape[2])
    rows, lanes = top_ref.shape
    step = rows // 2
    for first in range(0, rows, step):
        mine = slice(first, first + step)
        top, total, mix = merge(
            layout, which, mine, query_ref, slot_ref, top_ref, sum_ref, mix_ref, keys
        )
        new_top[mine, :] = jnp.broadcast_to(top, (step, lanes))
        new_sum[mine, :] = jnp.broadcast_to(total, (step, lanes))
        for n, part in enumerate(lane_tiles(mix.shape[1])):
            new_mix[n, mine, :] = mix[:, part]


def absorb(layout, which, query, row_slot, top, total, mix, pieces):
    return pl.pallas_call(
        functools.partial(absorb_kernel, layout, which),
        out_shape=[jax.ShapeDtypeStruct(x.shape, f32) for x in (top, total, mix)],
        in_specs=[in_vmem] * (5 + len(pieces)),
        out_specs=[in_vmem] * 3,
        scratch_shapes=[pltpu.VMEM((row_slot.shape[1] // 2, query.shape[1]), bf16)],
        compiler_params=pltpu.CompilerParams(vmem_limit_bytes=10 * mib),
        cost_estimate=pl.CostEstimate(flops=2 * 10**9, bytes_accessed=10**6, transcendentals=0),
        name="absorb",
    )(query, row_slot, top, total, mix, *pieces)


def attend_kernel(
    layout, which, first_head, heads, query_ref, slot_ref, top_ref, sum_ref, mix_ref, live_ref,
    value_ref, *refs
):
    pieces, out_ref, keys = refs[:-2], refs[-2], refs[-1]
    per_head = layout[1] * layout[2]
    take_keys(keys, pieces, mix_ref.shape[0] * mix_ref.shape[2])
    mine = slice(first_head * per_head, (first_head + heads) * per_head)
    _, total, mix = merge(
        layout, which, mine, query_ref, slot_ref, top_ref, sum_ref, mix_ref, keys
    )
    latent = (mix / total).astype(bf16)
    live = live_ref[:, :1]
    width = value_ref.shape[2]
    for h in range(heads):
        mixed = latent[h * per_head : (h + 1) * per_head, :]
        value = jnp.dot(mixed, value_ref[first_head + h], preferred_element_type=f32) * live
        out_ref[:, h * width : (h + 1) * width] = value.astype(bf16)


def attend(layout, which, query, row_slot, top, total, mix, live, value, pieces, first_head, heads):
    return pl.pallas_call(
        functools.partial(attend_kernel, layout, which, first_head, heads),
        out_shape=jax.ShapeDtypeStruct((live.shape[0], heads * value.shape[2]), bf16),
        in_specs=[in_vmem] * (7 + len(pieces)),
        out_specs=in_vmem,
        scratch_shapes=[pltpu.VMEM((row_slot.shape[1] // 2, query.shape[1]), bf16)],
        compiler_params=pltpu.CompilerParams(vmem_limit_bytes=10 * mib),
        name="attend",
    )(query, row_slot, top, total, mix, live, value, *pieces)


def output_kernel(dev_count, side_count, start, last, *refs):
    my_dev, my_side = lax.axis_index("dev"), lax.axis_index("side")
    head_refs = refs[:dev_count]
    weight_ref = refs[dev_count]
    earlier_ref = refs[dev_count + 1] if start else None
    out_refs = refs[dev_count + 1 + (start > 0) : -1]
    held = refs[-1]
    rows, depth = head_refs[0].shape
    per_side = dev_count // side_count
    for j in range(dev_count):
        group = my_dev ^ j
        place = (lax.div(group, per_side) ^ my_side) * per_side + lax.rem(group, per_side)
        held[pl.ds(pl.multiple_of(place * rows, 16), rows), :] = head_refs[j][...]
    columns = weight_ref.shape[1]
    tile = 256 if columns % 256 == 0 else columns
    side_rows = rows * per_side
    for n in range(columns // tile):
        here = slice(n * tile, (n + 1) * tile)
        product = jnp.dot(
            held[...], weight_ref[start : start + depth, here],
            preferred_element_type=f32,
        )
        if start:
            product = product + earlier_ref[:, here]
        if not last:
            out_refs[0][:, here] = product
        else:
            for k in range(side_count):
                out_refs[k][:, here] = product[k * side_rows : (k + 1) * side_rows, :].astype(
                    out_refs[k].dtype
                )


def output_product(head_pieces, weight, side_count, earlier, start, last):
    dev_count = len(head_pieces)
    rows, depth = head_pieces[0].shape
    columns = weight.shape[1]
    side_rows = rows * dev_count // side_count
    if not last:
        shapes = [((rows * dev_count, columns), f32)]
    else:
        shapes = [((side_rows, columns), f32 if k == 0 else bf16) for k in range(side_count)]
    earlier = [] if earlier is None else [earlier]
    return pl.pallas_call(
        functools.partial(output_kernel, dev_count, side_count, start, last),
        out_shape=[jax.ShapeDtypeStruct(*shape) for shape in shapes],
        in_specs=[in_vmem] * (dev_count + 1 + len(earlier)),
        out_specs=[in_vmem] * len(shapes),
        scratch_shapes=[pltpu.VMEM((dev_count * rows, depth), bf16)],
        compiler_params=pltpu.CompilerParams(vmem_limit_bytes=10 * mib),
        name="output_product",
    )(*head_pieces, weight, *earlier)


def on_device(
    prompts,
    latent_weight,
    latent_gain,
    row_request,
    context_len,
    request_slot,
    latent_cache,
    new_latent,
    queries,
    key_absorb,
    value_absorb,
    out_weight,
):
    dev_count = lax.axis_size("dev")
    side_count = lax.axis_size("side")
    tok_rows, model_width = prompts.shape
    shard_rows, kv_width = latent_weight.shape
    lat_width = latent_gain.shape[0]
    nope_width = value_absorb.shape[2]
    rope_width = kv_width - lat_width
    cap_slots, ctx_len, _ = latent_cache.shape
    step_count = new_latent.shape[1]
    bucket_rows = 2 * tok_rows // dev_count
    group_rows = dev_count * bucket_rows
    slab = model_width // dev_count

    x_pieces = list(split_columns(prompts, dev_count))
    packs = shard_rows % 32 == 0
    x_pieces[0], own_weight = lax.optimization_barrier((x_pieces[0], latent_weight))
    weights = [pack_weight(own_weight) if packs else own_weight] + [None] * (side_count - 1)
    for k in range(2, side_count, 2):
        weights[k] = swap(weights[0], "side", k)
    for k in sorted(range(1, dev_count), reverse=True):
        x_pieces[k] = swap(x_pieces[k], "dev", k)

    score_scale = queries.shape[-1] ** (-0.5)
    half = rope_width // 2
    inverse = 1.0 / 10000.0 ** (jnp.arange(half, dtype=f32) * (2.0 / rope_width))
    lengths, x_pieces[0] = lax.optimization_barrier((context_len, x_pieces[0]))
    (
        query_full, top_held, sum_held, mix_held, live, target, cosine, sine, row_slot,
        value_here, out_here,
    ) = prepare(
        score_scale, dev_count, side_count, bucket_rows, lengths, request_slot,
        row_request.reshape(-1, 128), inverse.reshape(1, -1), queries, key_absorb,
        jnp.swapaxes(latent_cache, 1, 2), new_latent, value_absorb, out_weight,
    )

    weights[0::2], top_held = lax.optimization_barrier((weights[0::2], top_held))
    for k in range(0, side_count, 2):
        weights[k + 1] = swap(weights[k], "side", 1)
    if not packs:
        my_side = lax.axis_index("side")
        held = jnp.zeros((side_count, shard_rows, kv_width), bf16)
        for k in range(side_count):
            held = lax.dynamic_update_slice(held, weights[k][None], (my_side ^ k, 0, 0))
        weights = [held.reshape(slab, kv_width)]

    routed = project(stack_rows(x_pieces), weights, target, kv_width, dev_count)
    layout = (score_scale, cap_slots, step_count, group_rows // 2)
    state = top_held, sum_held, mix_held
    for which in range(2):
        half = list(routed[which * dev_count : (which + 1) * dev_count])
        for k in sorted(range(1, dev_count), reverse=True):
            half[k] = swap(half[k], "dev", k)
        latent_rows = finish(half[:1] + half[:0:-1], latent_gain.reshape(1, -1), cosine, sine, which)
        pieces = [
            swap(latent_rows, "side", k) if k else latent_rows for k in piece_order(side_count)
        ]
        if which == 0:
            state = absorb(layout, which, query_full, row_slot, *state, pieces)
    product, first_head, head_count = None, 0, value_absorb.shape[0]
    for part_heads in (head_count // 2, head_count // 2):
        head_out = attend(
            layout, 1, query_full, row_slot, *state, live, value_here, pieces, first_head,
            part_heads,
        )
        heads = [head_out] + [None] * (dev_count - 1)
        for k in sorted(range(1, dev_count), reverse=True):
            if k == 1 or k % 2 == 0:
                heads[k] = swap(head_out, "dev", k)
        for k in range(3, dev_count, 2):
            heads[k] = swap(heads[k - 1], "dev", 1)
        start, first_head = first_head * nope_width, first_head + part_heads
        products = output_product(
            heads, out_here, side_count, product, start, first_head == head_count
        )
        product = products[0]
    result = products[0]
    for k in sorted(range(1, side_count), reverse=True):
        result = result + swap(products[k], "side", k).astype(f32)
    return result.astype(bf16)


def solution(mesh):
    placed = (
        P(("rep", "dev", "side"), None),
        P(("dev", "side"), None),
        P(),
        P("rep"),
        P("rep"),
        P("rep"),
        P(("rep", "dev"), None, None),
        P(("rep", "dev"), None, None),
        P(("rep", "dev"), None, "side", None),
        P("side", None, None),
        P("side", None, None),
        P("side", "dev"),
    )
    return jax.shard_map(
        on_device, mesh=mesh, in_specs=placed, out_specs=P(("rep", "side"), "dev"), check_vma=False
    )
```

```python
import functools

import jax
import jax.numpy as jnp
from jax import lax
from jax.experimental import pallas as pl
from jax.experimental.pallas import tpu as pltpu
from jax.sharding import PartitionSpec as P

masked_score = -1e30
bf16, f32 = jnp.bfloat16, jnp.float32
in_vmem = pl.BlockSpec(memory_space=pltpu.VMEM)
in_smem = pl.BlockSpec(memory_space=pltpu.SMEM)
in_hbm = pl.BlockSpec(memory_space=pltpu.HBM)
mib = 1024 * 1024
prepare_mib = 16


def swap(value, axis, step):
    count = lax.axis_size(axis)
    return lax.ppermute(value, axis, [(i, i ^ step) for i in range(count)])


def pick(pieces, index):
    out = pieces[0]
    for k in range(1, len(pieces)):
        out = jnp.where(index == k, pieces[k], out)
    return out


def lane_tiles(width):
    return [slice(n, min(n + 128, width)) for n in range(0, width, 128)]


def packed_rows(rows, width):
    return rows * (width // 128) + rows // 2


def pack(value):
    rows, width = value.shape
    full = width // 128
    rest = value[:, full * 128 :]
    parts = [value[:, n * 128 : (n + 1) * 128] for n in range(full)]
    return parts + [jnp.concatenate([rest[: rows // 2], rest[rows // 2 :]], axis=1)]


def store_packed(ref, value):
    first = 0
    for part in pack(value):
        ref[first : first + part.shape[0], :] = part.astype(ref.dtype)
        first += part.shape[0]


def load_packed(ref, rows):
    full = ref.shape[0] // rows
    tiles = [ref[n * rows : (n + 1) * rows, :] for n in range(full)]
    rest = ref[full * rows :, :]
    return tiles, jnp.concatenate([rest[:, :64], rest[:, 64:]], axis=0)


def pack_kernel(value_ref, out_ref):
    store_packed(out_ref, value_ref[...])


def pack_weight(weight):
    rows, width = weight.shape
    return pl.pallas_call(
        pack_kernel,
        out_shape=jax.ShapeDtypeStruct((packed_rows(rows, width), 128), weight.dtype),
        in_specs=[in_vmem],
        out_specs=in_vmem,
        compiler_params=pltpu.CompilerParams(vmem_limit_bytes=8 * mib),
        cost_estimate=pl.CostEstimate(flops=10**10, bytes_accessed=10**6, transcendentals=0),
        name="pack_weight",
    )(weight)


def split_kernel(slab, prompts_ref, *refs):
    my_dev = lax.axis_index("dev")
    out_refs, sems = refs[:-1], refs[-1]
    copies = []
    for k in range(len(out_refs))[::-1]:
        first = pl.multiple_of((my_dev ^ k) * slab, 128)
        copies.append(
            pltpu.make_async_copy(prompts_ref.at[:, pl.ds(first, slab)], out_refs[k], sems.at[k])
        )
    for copy in copies:
        copy.start()
    for copy in copies:
        copy.wait()


def split_columns(prompts, count):
    rows, width = prompts.shape
    slab = width // count
    if slab % 128:
        columns = [prompts[:, k * slab : (k + 1) * slab] for k in range(count)]
        my_dev = lax.axis_index("dev")
        return [pick(columns, my_dev ^ k) for k in range(count)]
    return pl.pallas_call(
        functools.partial(split_kernel, slab),
        out_shape=[jax.ShapeDtypeStruct((rows, slab), prompts.dtype)] * count,
        in_specs=[in_hbm],
        out_specs=[in_vmem] * count,
        scratch_shapes=[pltpu.SemaphoreType.DMA((count,))],
        compiler_params=pltpu.CompilerParams(vmem_limit_bytes=8 * mib),
        cost_estimate=pl.CostEstimate(
            flops=10**10, bytes_accessed=4 * 10**7, transcendentals=0
        ),
        name="split_columns",
    )(pltpu.with_memory_space_constraint(prompts, pltpu.HBM))


def fill_tables(
    dev_count, side_count, bucket, cap_slots, length_ref, slot_ref, request_ref, inverse_ref,
    target_ref, cos_ref, sin_ref, spot_ref, to_ref, place_ref, local_ref, position_ref,
):
    my_dev, my_side = lax.axis_index("dev"), lax.axis_index("side")
    requests = request_ref[...]
    lane_rows, lanes = requests.shape
    tok_rows = bucket * dev_count // 2
    per_row = lanes // tok_rows
    half_bucket = bucket // 2
    half_rows = dev_count * half_bucket
    group_rows = 2 * half_rows
    before = lax.broadcasted_iota(jnp.int32, (lanes, lanes), 0)
    after = lax.broadcasted_iota(jnp.int32, (lanes, lanes), 1)
    below = jnp.where(before < after, 1.0, 0.0)
    near = jnp.where((before < after) & (before // tok_rows == after // tok_rows), 1.0, 0.0)
    scan = jnp.concatenate([below, jnp.ones_like(below)], axis=1).astype(bf16)
    lower = lax.broadcasted_iota(jnp.int32, (lane_rows, lane_rows), 0)
    upper = lax.broadcasted_iota(jnp.int32, (lane_rows, lane_rows), 1)
    rows_before = jnp.where(upper < lower, 1.0, 0.0)
    position = jnp.zeros(requests.shape, f32)
    slot = jnp.zeros(requests.shape, jnp.int32)
    for q in range(slot_ref.shape[0]):
        hit = requests == q
        ranks = jnp.dot(
            jnp.where(hit, 1.0, 0.0).astype(bf16), scan, preferred_element_type=f32
        )
        earlier = jnp.dot(rows_before, ranks[:, lanes:], preferred_element_type=f32)
        start = length_ref[q].astype(f32)
        position = jnp.where(hit, ranks[:, :lanes] + earlier + start, position)
        slot = jnp.where(hit, slot_ref[q], slot)
    group = lax.div(slot, cap_slots)
    rank = jnp.zeros(requests.shape, f32)
    for g in range(dev_count):
        hit = group == g
        ranks = jnp.dot(
            jnp.where(hit, 1.0, 0.0).astype(bf16), near.astype(bf16), preferred_element_type=f32
        )
        rank = jnp.where(hit, ranks, rank)
    block = lax.broadcasted_iota(jnp.int32, requests.shape, 0) * per_row + lax.div(
        lax.broadcasted_iota(jnp.int32, requests.shape, 1), tok_rows
    )
    rank = rank.astype(jnp.int32)
    which = lax.div(rank, half_bucket)
    place = lax.div(block, side_count) * half_bucket + lax.rem(rank, half_bucket)
    to_ref[...] = (which * dev_count + (group ^ my_dev)) * half_rows + place
    place = which * half_rows + place
    place_ref[...] = jnp.where(group == my_dev, place, -1)
    local_ref[...] = (slot - my_dev * cap_slots + 1).astype(f32)
    position_ref[...] = position
    lane_block = lax.div(lax.broadcasted_iota(jnp.int32, (1, lanes), 1), tok_rows)
    ids = lax.broadcasted_iota(jnp.int32, (group_rows, 1), 0)

    def find(dev, side):
        held = dev * side_count + side
        return pl.ds(lax.div(held, per_row), 1), lane_block == lax.rem(held, per_row)

    targets = []
    for k in range(dev_count):
        held = (my_dev ^ k) * side_count + my_side
        row = jnp.broadcast_to(to_ref[pl.ds(lax.div(held, per_row), 1), :], (8, lanes))
        start = lax.rem(lanes - tok_rows * lax.rem(held, per_row), lanes)
        targets.append(pltpu.roll(row, start, 1)[:1, :tok_rows])
    for k in range(0, dev_count, per_row):
        target_ref[:, k * tok_rows : k * tok_rows + lanes] = jnp.concatenate(
            targets[k : k + per_row], axis=1
        )
    found = jnp.zeros((group_rows, lanes), f32)
    for d in range(dev_count):
        row, inside = find(d, my_side)
        found = jnp.where((place_ref[row, :] == ids) & inside, position_ref[row, :], found)
    angles = jnp.sum(found, axis=1, keepdims=True) * inverse_ref[...]
    cos_ref[...] = jnp.cos(angles)
    sin_ref[...] = jnp.sin(angles)
    for k in range(side_count):
        total = jnp.zeros((8, group_rows), f32)
        for d in range(dev_count):
            row, inside = find(d, my_side ^ k)
            chosen = jnp.where((place_ref[row, :] == ids) & inside, 1.0, 0.0).astype(bf16)
            values = jnp.broadcast_to(local_ref[row, :], (8, lanes)).astype(bf16)
            total = total + lax.dot_general(
                values, chosen, (((1,), (1,)), ((), ())), preferred_element_type=f32
            )
        spot_ref[:, k * group_rows : (k + 1) * group_rows] = total[:1].astype(jnp.int32)


def prepare_kernel(
    scale, steps, layout, inverse_ref, length_hbm, slot_hbm, request_hbm, query_hbm, absorb_hbm,
    cache_hbm, fresh_hbm, value_hbm, out_hbm, full_ref, top_ref, sum_ref, mix_ref, live_ref, target_ref,
    cos_ref, sin_ref, spot_ref, value_ref, out_ref, length_ref, slot_ref, request_ref, query_ref,
    absorb_ref, cache_ref, fresh_ref, plain, full, to_ref, place_ref, local_ref, position_ref, sems,
):
    pairs = [
        (length_hbm, length_ref), (slot_hbm, slot_ref), (request_hbm, request_ref),
        (query_hbm, query_ref), (absorb_hbm, absorb_ref), (cache_hbm, cache_ref),
        (fresh_hbm, fresh_ref), (value_hbm, value_ref),
    ]
    parts = sems.shape[0] - len(pairs)
    rows = out_hbm.shape[0] // parts
    for n in range(parts):
        part = pl.ds(n * rows, rows)
        pairs.append((out_hbm.at[part], out_ref.at[part]))
    copies = [pltpu.make_async_copy(*pair, sems.at[n]) for n, pair in enumerate(pairs)]
    for copy in copies:
        copy.start()
    for copy in copies[:3]:
        copy.wait()
    slots, _, context = cache_ref.shape
    heads, nope, lat_width = absorb_ref.shape
    per_head = slots * steps
    fill_tables(
        *layout, slots, length_ref, slot_ref, request_ref, inverse_ref, target_ref, cos_ref,
        sin_ref, spot_ref, to_ref, place_ref, local_ref, position_ref,
    )
    first_slot = lax.axis_index("dev") * slots
    lengths = []
    for s in range(slots):
        length = jnp.int32(0)
        for q in range(slot_ref.shape[0]):
            length = jnp.where(slot_ref[q] == first_slot + s, length_ref[q], length)
        lengths.append(length)
    slot_of = lax.div(lax.broadcasted_iota(jnp.int32, live_ref.shape, 0), steps)
    live = jnp.zeros(live_ref.shape, f32)
    for s in range(slots):
        live = jnp.where((slot_of == s) & (lengths[s] > 0), 1.0, live)
    live_ref[...] = live
    copies[3].wait()
    copies[4].wait()
    for n, here in enumerate(lane_tiles(query_ref.shape[1])):
        plain[n, :, : here.stop - here.start] = query_ref[:, here].astype(f32)
    wide = lane_tiles(full_ref.shape[1])
    for h in range(heads):
        there = pl.ds(h, per_head, stride=heads)
        query = plain[0, there, :].astype(bf16)
        latent = jnp.dot(query, absorb_ref[h], preferred_element_type=f32).astype(bf16).astype(f32)
        here = slice(h * per_head, (h + 1) * per_head)
        for n, lanes in enumerate(lane_tiles(lat_width)):
            full[n, here, :] = latent[:, lanes]
        full[len(wide) - 1, here, :] = plain[1, there, :]
    for n, lanes in enumerate(wide):
        full_ref[:, lanes] = full[n, :, : lanes.stop - lanes.start].astype(bf16)
    key = lax.broadcasted_iota(jnp.int32, (1, context), 1)
    copies[5].wait()
    copies[6].wait()
    late = lax.broadcasted_iota(jnp.int32, (steps * heads, steps), 1)
    late = late > lax.div(lax.broadcasted_iota(jnp.int32, (steps * heads, steps), 0), heads)
    for s in range(slots):
        theres = [pl.ds(s * steps + t, heads, stride=per_head) for t in range(steps)]
        query = jnp.concatenate(
            [
                jnp.concatenate([full[n, there, :] for there in theres], axis=0)[
                    :, : lanes.stop - lanes.start
                ].astype(bf16)
                for n, lanes in enumerate(wide)
            ],
            axis=1,
        )
        rows = cache_ref[s]
        score = jnp.dot(query, rows, preferred_element_type=f32)
        score = jnp.where(key < lengths[s], score * scale, masked_score)
        fresh = fresh_ref[s]
        new = lax.dot_general(
            query, fresh, (((1,), (1,)), ((), ())), preferred_element_type=f32
        )
        new = jnp.where(late, masked_score, new * scale)
        top = jnp.maximum(
            jnp.max(score, axis=1, keepdims=True), jnp.max(new, axis=1, keepdims=True)
        )
        weight = jnp.exp(score - top)
        new = jnp.exp(new - top)
        total = jnp.sum(weight, axis=1, keepdims=True) + jnp.sum(new, axis=1, keepdims=True)
        mix = lax.dot_general(
            weight.astype(bf16), rows[:lat_width, :], (((1,), (1,)), ((), ())),
            preferred_element_type=f32,
        )
        for u in range(steps):
            mix = mix + new[:, u : u + 1].astype(bf16).astype(f32) * fresh[
                u : u + 1, :lat_width
            ].astype(f32)
        lanes = top_ref.shape[1]
        for t in range(steps):
            there = theres[t]
            here = slice(t * heads, (t + 1) * heads)
            top_ref[there, :] = jnp.broadcast_to(top[here], (heads, lanes))
            sum_ref[there, :] = jnp.broadcast_to(total[here], (heads, lanes))
            for n, part in enumerate(lane_tiles(lat_width)):
                mix_ref[n, there, :] = mix[here, part]
    for copy in copies[7:]:
        copy.wait()


def prepare(
    scale, dev_count, side_count, bucket, lengths, request_slot, requests, inverse, queries,
    absorb, cache, fresh, value, out_weight,
):
    slots, steps, heads, width = queries.shape
    kv_width = cache.shape[1]
    lat_width = absorb.shape[2]
    rows = slots * steps * heads
    group_rows = dev_count * bucket
    parts = 8
    lanes = requests.shape[1]
    half = inverse.shape[1]
    shapes = [
        ((rows, kv_width), bf16), ((rows, 128), f32), ((rows, 128), f32),
        ((lat_width // 128, rows, 128), f32), ((slots * steps, 128), f32),
        ((1, group_rows // 2 * dev_count), jnp.int32), ((group_rows, half), f32), ((group_rows, half), f32),
        ((1, side_count * group_rows), jnp.int32), (value.shape, bf16), (out_weight.shape, bf16),
    ]
    return pl.pallas_call(
        functools.partial(prepare_kernel, scale, steps, (dev_count, side_count, bucket)),
        out_shape=[jax.ShapeDtypeStruct(*shape) for shape in shapes],
        in_specs=[in_vmem] + [in_hbm] * 9,
        out_specs=[in_vmem] * len(shapes),
        scratch_shapes=[
            pltpu.SMEM(lengths.shape, lengths.dtype),
            pltpu.SMEM(request_slot.shape, request_slot.dtype),
            pltpu.VMEM(requests.shape, requests.dtype),
            pltpu.VMEM((rows, width), queries.dtype),
            pltpu.VMEM(absorb.shape, absorb.dtype),
            pltpu.VMEM(cache.shape, cache.dtype),
            pltpu.VMEM(fresh.shape, fresh.dtype),
            pltpu.VMEM((len(lane_tiles(width)), rows, 128), f32),
            pltpu.VMEM((len(lane_tiles(kv_width)), rows, 128), f32),
            pltpu.VMEM(requests.shape, jnp.int32),
            pltpu.VMEM(requests.shape, jnp.int32),
            pltpu.VMEM(requests.shape, f32),
            pltpu.VMEM(requests.shape, f32),
            pltpu.SemaphoreType.DMA((parts + 8,)),
        ],
        compiler_params=pltpu.CompilerParams(vmem_limit_bytes=prepare_mib * mib),
        cost_estimate=pl.CostEstimate(
            flops=4 * 10**10, bytes_accessed=28 * 10**6, transcendentals=10**5
        ),
        name="prepare",
    )(inverse, lengths, request_slot, requests, queries.reshape(rows, width), absorb, cache, fresh,
      value, out_weight)


def hop_order(count):
    return [0, *range(2, count, 2), *range(3, count, 2), 1]


def stack_kernel(*refs):
    out_ref = refs[-1]
    rows = refs[0].shape[0]
    for k, ref in zip(hop_order(len(refs) - 1), refs[:-1]):
        out_ref[k * rows : (k + 1) * rows, :] = ref[...]


def stack_rows(pieces):
    rows, width = pieces[0].shape
    return pl.pallas_call(
        stack_kernel,
        out_shape=jax.ShapeDtypeStruct((len(pieces) * rows, width), bf16),
        in_specs=[in_vmem] * len(pieces),
        out_specs=in_vmem,
        compiler_params=pltpu.CompilerParams(vmem_limit_bytes=8 * mib),
        cost_estimate=pl.CostEstimate(flops=2 * 10**10, bytes_accessed=10**6, transcendentals=0),
        name="stack_rows",
    )(*[pieces[k] for k in hop_order(len(pieces))])


def project_kernel(dev_count, side_count, target_ref, x_ref, *refs):
    my_side = lax.axis_index("side")
    weight_refs = refs[:side_count]
    out_refs = refs[side_count:-2]
    slab_weight, rows = refs[-2:]
    tok_rows = x_ref.shape[0] // dev_count
    full = slab_weight.shape[1] // 128
    if side_count > 1:
        shard = slab_weight.shape[0] // side_count
        for k in range(side_count):
            first = pl.multiple_of((my_side ^ k) * shard, 16)
            tiles, rest = load_packed(weight_refs[k], shard)
            for n, tile in enumerate(tiles):
                slab_weight[pl.ds(first, shard), n * 128 : (n + 1) * 128] = tile
            slab_weight[pl.ds(first, shard), full * 128 :] = rest
    slab = slab_weight[...] if side_count > 1 else weight_refs[0][...]
    raw = jnp.dot(x_ref[...], slab, preferred_element_type=f32).astype(bf16)
    rows[...] = raw
    target = target_ref[...]
    half_rows = tok_rows
    step = min(4, 2 * dev_count)
    for j in range(0, 2 * dev_count, step):
        ids = lax.broadcasted_iota(jnp.int32, (step * half_rows, target.shape[1]), 0)
        route = jnp.where(ids + j * half_rows == target, 1.0, 0.0).astype(bf16)
        placed = jnp.dot(route, rows[...], preferred_element_type=f32)
        for n in range(step):
            store_packed(out_refs[j + n], placed[n * half_rows : (n + 1) * half_rows])


def project(x_rows, weights, target, width, dev_count):
    tok_rows, slab = x_rows.shape[0] // dev_count, x_rows.shape[1]
    return pl.pallas_call(
        functools.partial(project_kernel, dev_count, len(weights)),
        out_shape=[
            jax.ShapeDtypeStruct(
                (packed_rows(tok_rows, width), 128), f32 if j % dev_count == 0 else bf16
            )
            for j in range(2 * dev_count)
        ],
        in_specs=[in_vmem] * (2 + len(weights)),
        out_specs=[in_vmem] * (2 * dev_count),
        scratch_shapes=[
            pltpu.VMEM((slab, width), bf16),
            pltpu.VMEM((target.shape[1], width), bf16),
        ],
        compiler_params=pltpu.CompilerParams(vmem_limit_bytes=20 * mib),
        name="project",
    )(target, x_rows, *weights)


def finish_kernel(which, gain_ref, cos_ref, sin_ref, *refs):
    parts, out_ref = refs[:-1], refs[-1]
    rows, half = cos_ref.shape[0] // 2, cos_ref.shape[1]
    mine = slice(which * rows, (which + 1) * rows)
    total = parts[0][...].astype(f32)
    for part in parts[1:]:
        total = total + part[...].astype(f32)
    tiles, rest = load_packed(total, rows)
    latent = jnp.concatenate(tiles, axis=1)
    spread = jnp.mean(latent * latent, axis=1, keepdims=True)
    latent = latent * lax.rsqrt(spread + 1e-06) * gain_ref[...]
    first, second = rest[:, :half], rest[:, half:]
    cosine, sine = cos_ref[mine, :], sin_ref[mine, :]
    store_packed(
        out_ref,
        jnp.concatenate(
            [latent, first * cosine - second * sine, second * cosine + first * sine], axis=1
        ),
    )


def finish(parts, gain, cosine, sine, which):
    return pl.pallas_call(
        functools.partial(finish_kernel, which),
        out_shape=jax.ShapeDtypeStruct(parts[0].shape, bf16),
        in_specs=[in_vmem] * (3 + len(parts)),
        out_specs=in_vmem,
        compiler_params=pltpu.CompilerParams(vmem_limit_bytes=8 * mib),
        name="finish_rows",
    )(gain, cosine, sine, *parts)


def piece_order(count):
    return [0, 1, *range(3, count, 2), *range(2, count, 2)]


def take_keys(keys, pieces, lat_width):
    rows = keys.shape[0] // len(pieces)
    for n, piece in zip(piece_order(len(pieces)), pieces):
        tiles, rest = load_packed(piece, rows)
        there = slice(n * rows, (n + 1) * rows)
        for j, tile in enumerate(tiles):
            keys[there, j * 128 : (j + 1) * 128] = tile
        keys[there, lat_width:] = rest


def merge(layout, which, mine, query_ref, slot_ref, top_ref, sum_ref, mix_ref, keys):
    scale, cap_slots, steps, half_rows = layout
    lat_width = mix_ref.shape[0] * mix_ref.shape[2]
    row = lax.broadcasted_iota(jnp.int32, (mine.stop - mine.start, 1), 0)
    row_slot = (row // steps) % cap_slots
    query = query_ref[mine, :]
    score = lax.dot_general(
        query, keys[...], (((1,), (1,)), ((), ())), preferred_element_type=f32
    )
    count = slot_ref.shape[1]
    part = half_rows
    slots = jnp.concatenate(
        [slot_ref[:, n + which * part : n + (which + 1) * part] for n in range(0, count, 2 * part)],
        axis=1,
    )
    score = jnp.where(slots == row_slot + 1, score * scale, masked_score)
    top_held = top_ref[mine, :1]
    top = jnp.maximum(top_held, jnp.max(score, axis=1, keepdims=True))
    held = jnp.exp(top_held - top)
    weight = jnp.exp(score - top)
    total = sum_ref[mine, :1] * held + jnp.sum(weight, axis=1, keepdims=True)
    mix = jnp.dot(weight.astype(bf16), keys[:, :lat_width], preferred_element_type=f32)
    mix_held = jnp.concatenate([mix_ref[n, mine, :] for n in range(mix_ref.shape[0])], axis=1)
    return top, total, mix_held * held + mix


def absorb_kernel(layout, which, query_ref, slot_ref, top_ref, sum_ref, mix_ref, *refs):
    pieces, (new_top, new_sum, new_mix, keys) = refs[:-4], refs[-4:]
    take_keys(keys, pieces, mix_ref.shape[0] * mix_ref.shape[2])
    rows, lanes = top_ref.shape
    step = rows // 2
    for first in range(0, rows, step):
        mine = slice(first, first + step)
        top, total, mix = merge(
            layout, which, mine, query_ref, slot_ref, top_ref, sum_ref, mix_ref, keys
        )
        new_top[mine, :] = jnp.broadcast_to(top, (step, lanes))
        new_sum[mine, :] = jnp.broadcast_to(total, (step, lanes))
        for n, part in enumerate(lane_tiles(mix.shape[1])):
            new_mix[n, mine, :] = mix[:, part]


def absorb(layout, which, query, row_slot, top, total, mix, pieces):
    return pl.pallas_call(
        functools.partial(absorb_kernel, layout, which),
        out_shape=[jax.ShapeDtypeStruct(x.shape, f32) for x in (top, total, mix)],
        in_specs=[in_vmem] * (5 + len(pieces)),
        out_specs=[in_vmem] * 3,
        scratch_shapes=[pltpu.VMEM((row_slot.shape[1] // 2, query.shape[1]), bf16)],
        compiler_params=pltpu.CompilerParams(vmem_limit_bytes=10 * mib),
        cost_estimate=pl.CostEstimate(flops=2 * 10**9, bytes_accessed=10**6, transcendentals=0),
        name="absorb",
    )(query, row_slot, top, total, mix, *pieces)


def attend_kernel(
    layout, which, first_head, heads, query_ref, slot_ref, top_ref, sum_ref, mix_ref, live_ref,
    value_ref, *refs
):
    pieces, out_ref, keys = refs[:-2], refs[-2], refs[-1]
    per_head = layout[1] * layout[2]
    take_keys(keys, pieces, mix_ref.shape[0] * mix_ref.shape[2])
    mine = slice(first_head * per_head, (first_head + heads) * per_head)
    _, total, mix = merge(
        layout, which, mine, query_ref, slot_ref, top_ref, sum_ref, mix_ref, keys
    )
    latent = (mix / total).astype(bf16)
    live = live_ref[:, :1]
    width = value_ref.shape[2]
    for h in range(heads):
        mixed = latent[h * per_head : (h + 1) * per_head, :]
        value = jnp.dot(mixed, value_ref[first_head + h], preferred_element_type=f32) * live
        out_ref[:, h * width : (h + 1) * width] = value.astype(bf16)


def attend(layout, which, query, row_slot, top, total, mix, live, value, pieces, first_head, heads):
    return pl.pallas_call(
        functools.partial(attend_kernel, layout, which, first_head, heads),
        out_shape=jax.ShapeDtypeStruct((live.shape[0], heads * value.shape[2]), bf16),
        in_specs=[in_vmem] * (7 + len(pieces)),
        out_specs=in_vmem,
        scratch_shapes=[pltpu.VMEM((row_slot.shape[1] // 2, query.shape[1]), bf16)],
        compiler_params=pltpu.CompilerParams(vmem_limit_bytes=10 * mib),
        name="attend",
    )(query, row_slot, top, total, mix, live, value, *pieces)


def output_kernel(dev_count, side_count, start, last, *refs):
    my_dev, my_side = lax.axis_index("dev"), lax.axis_index("side")
    head_refs = refs[:dev_count]
    weight_ref = refs[dev_count]
    earlier_ref = refs[dev_count + 1] if start else None
    out_refs = refs[dev_count + 1 + (start > 0) : -1]
    held = refs[-1]
    rows, depth = head_refs[0].shape
    per_side = dev_count // side_count
    for j in range(dev_count):
        group = my_dev ^ j
        place = (lax.div(group, per_side) ^ my_side) * per_side + lax.rem(group, per_side)
        held[pl.ds(pl.multiple_of(place * rows, 16), rows), :] = head_refs[j][...]
    columns = weight_ref.shape[1]
    tile = 256 if columns % 256 == 0 else columns
    side_rows = rows * per_side
    for n in range(columns // tile):
        here = slice(n * tile, (n + 1) * tile)
        product = jnp.dot(
            held[...], weight_ref[start : start + depth, here],
            preferred_element_type=f32,
        )
        if start:
            product = product + earlier_ref[:, here]
        if not last:
            out_refs[0][:, here] = product
        else:
            for k in range(side_count):
                out_refs[k][:, here] = product[k * side_rows : (k + 1) * side_rows, :].astype(
                    out_refs[k].dtype
                )


def output_product(head_pieces, weight, side_count, earlier, start, last):
    dev_count = len(head_pieces)
    rows, depth = head_pieces[0].shape
    columns = weight.shape[1]
    side_rows = rows * dev_count // side_count
    if not last:
        shapes = [((rows * dev_count, columns), f32)]
    else:
        shapes = [((side_rows, columns), f32 if k == 0 else bf16) for k in range(side_count)]
    earlier = [] if earlier is None else [earlier]
    return pl.pallas_call(
        functools.partial(output_kernel, dev_count, side_count, start, last),
        out_shape=[jax.ShapeDtypeStruct(*shape) for shape in shapes],
        in_specs=[in_vmem] * (dev_count + 1 + len(earlier)),
        out_specs=[in_vmem] * len(shapes),
        scratch_shapes=[pltpu.VMEM((dev_count * rows, depth), bf16)],
        compiler_params=pltpu.CompilerParams(vmem_limit_bytes=10 * mib),
        name="output_product",
    )(*head_pieces, weight, *earlier)


def on_device(
    prompts,
    latent_weight,
    latent_gain,
    row_request,
    context_len,
    request_slot,
    latent_cache,
    new_latent,
    queries,
    key_absorb,
    value_absorb,
    out_weight,
):
    dev_count = lax.axis_size("dev")
    side_count = lax.axis_size("side")
    tok_rows, model_width = prompts.shape
    shard_rows, kv_width = latent_weight.shape
    lat_width = latent_gain.shape[0]
    nope_width = value_absorb.shape[2]
    rope_width = kv_width - lat_width
    cap_slots, ctx_len, _ = latent_cache.shape
    step_count = new_latent.shape[1]
    bucket_rows = 2 * tok_rows // dev_count
    group_rows = dev_count * bucket_rows
    slab = model_width // dev_count

    x_pieces = list(split_columns(prompts, dev_count))
    packs = shard_rows % 32 == 0
    x_pieces[0], own_weight = lax.optimization_barrier((x_pieces[0], latent_weight))
    weights = [pack_weight(own_weight) if packs else own_weight] + [None] * (side_count - 1)
    for k in range(2, side_count, 2):
        weights[k] = swap(weights[0], "side", k)
    for k in sorted(range(1, dev_count), reverse=True):
        x_pieces[k] = swap(x_pieces[k], "dev", k)

    score_scale = queries.shape[-1] ** (-0.5)
    half = rope_width // 2
    inverse = 1.0 / 10000.0 ** (jnp.arange(half, dtype=f32) * (2.0 / rope_width))
    lengths, x_pieces[0] = lax.optimization_barrier((context_len, x_pieces[0]))
    (
        query_full, top_held, sum_held, mix_held, live, target, cosine, sine, row_slot,
        value_here, out_here,
    ) = prepare(
        score_scale, dev_count, side_count, bucket_rows, lengths, request_slot,
        row_request.reshape(-1, 128), inverse.reshape(1, -1), queries, key_absorb,
        jnp.swapaxes(latent_cache, 1, 2), new_latent, value_absorb, out_weight,
    )

    weights[0::2], top_held = lax.optimization_barrier((weights[0::2], top_held))
    for k in range(0, side_count, 2):
        weights[k + 1] = swap(weights[k], "side", 1)
    if not packs:
        my_side = lax.axis_index("side")
        held = jnp.zeros((side_count, shard_rows, kv_width), bf16)
        for k in range(side_count):
            held = lax.dynamic_update_slice(held, weights[k][None], (my_side ^ k, 0, 0))
        weights = [held.reshape(slab, kv_width)]

    routed = project(stack_rows(x_pieces), weights, target, kv_width, dev_count)
    layout = (score_scale, cap_slots, step_count, group_rows // 2)
    state = top_held, sum_held, mix_held
    for which in range(2):
        half = list(routed[which * dev_count : (which + 1) * dev_count])
        for k in sorted(range(1, dev_count), reverse=True):
            half[k] = swap(half[k], "dev", k)
        latent_rows = finish(
            [half[k] for k in hop_order(dev_count)], latent_gain.reshape(1, -1), cosine, sine, which
        )
        pieces = [
            swap(latent_rows, "side", k) if k else latent_rows for k in piece_order(side_count)
        ]
        if which == 0:
            state = absorb(layout, which, query_full, row_slot, *state, pieces)
    product, first_head, head_count = None, 0, value_absorb.shape[0]
    for part_heads in (head_count // 2, head_count // 2):
        head_out = attend(
            layout, 1, query_full, row_slot, *state, live, value_here, pieces, first_head,
            part_heads,
        )
        heads = [head_out] + [None] * (dev_count - 1)
        for k in sorted(range(1, dev_count), reverse=True):
            if k == 1 or k % 2 == 0:
                heads[k] = swap(head_out, "dev", k)
        for k in range(3, dev_count, 2):
            heads[k] = swap(heads[k - 1], "dev", 1)
        start, first_head = first_head * nope_width, first_head + part_heads
        products = output_product(
            heads, out_here, side_count, product, start, first_head == head_count
        )
        product = products[0]
    result = products[0]
    for k in sorted(range(1, side_count), reverse=True):
        result = result + swap(products[k], "side", k).astype(f32)
    return result.astype(bf16)


def solution(mesh):
    placed = (
        P(("rep", "dev", "side"), None),
        P(("dev", "side"), None),
        P(),
        P("rep"),
        P("rep"),
        P("rep"),
        P(("rep", "dev"), None, None),
        P(("rep", "dev"), None, None),
        P(("rep", "dev"), None, "side", None),
        P("side", None, None),
        P("side", None, None),
        P("side", "dev"),
    )
    return jax.shard_map(
        on_device, mesh=mesh, in_specs=placed, out_specs=P(("rep", "side"), "dev"), check_vma=False
    )
```

```python
import functools

import jax
import jax.numpy as jnp
from jax import lax
from jax.experimental import pallas as pl
from jax.experimental.pallas import tpu as pltpu
from jax.sharding import PartitionSpec as P

masked_score = -1e30
bf16, f32 = jnp.bfloat16, jnp.float32
in_vmem = pl.BlockSpec(memory_space=pltpu.VMEM)
in_smem = pl.BlockSpec(memory_space=pltpu.SMEM)
in_hbm = pl.BlockSpec(memory_space=pltpu.HBM)
mib = 1024 * 1024
prepare_mib = 16


def swap(value, axis, step):
    count = lax.axis_size(axis)
    return lax.ppermute(value, axis, [(i, i ^ step) for i in range(count)])


def pick(pieces, index):
    out = pieces[0]
    for k in range(1, len(pieces)):
        out = jnp.where(index == k, pieces[k], out)
    return out


def lane_tiles(width):
    return [slice(n, min(n + 128, width)) for n in range(0, width, 128)]


def packed_rows(rows, width):
    return rows * (width // 128) + rows // 2


def pack(value):
    rows, width = value.shape
    full = width // 128
    rest = value[:, full * 128 :]
    parts = [value[:, n * 128 : (n + 1) * 128] for n in range(full)]
    return parts + [jnp.concatenate([rest[: rows // 2], rest[rows // 2 :]], axis=1)]


def store_packed(ref, value):
    first = 0
    for part in pack(value):
        ref[first : first + part.shape[0], :] = part.astype(ref.dtype)
        first += part.shape[0]


def load_packed(ref, rows):
    full = ref.shape[0] // rows
    tiles = [ref[n * rows : (n + 1) * rows, :] for n in range(full)]
    rest = ref[full * rows :, :]
    return tiles, jnp.concatenate([rest[:, :64], rest[:, 64:]], axis=0)


def pack_kernel(value_ref, out_ref):
    store_packed(out_ref, value_ref[...])


def pack_weight(weight):
    rows, width = weight.shape
    return pl.pallas_call(
        pack_kernel,
        out_shape=jax.ShapeDtypeStruct((packed_rows(rows, width), 128), weight.dtype),
        in_specs=[in_vmem],
        out_specs=in_vmem,
        compiler_params=pltpu.CompilerParams(vmem_limit_bytes=8 * mib),
        cost_estimate=pl.CostEstimate(flops=10**10, bytes_accessed=10**6, transcendentals=0),
        name="pack_weight",
    )(weight)


def split_kernel(slab, prompts_ref, *refs):
    my_dev = lax.axis_index("dev")
    out_refs, sems = refs[:-1], refs[-1]
    copies = []
    for k in range(len(out_refs))[::-1]:
        first = pl.multiple_of((my_dev ^ k) * slab, 128)
        copies.append(
            pltpu.make_async_copy(prompts_ref.at[:, pl.ds(first, slab)], out_refs[k], sems.at[k])
        )
    for copy in copies:
        copy.start()
    for copy in copies:
        copy.wait()


def split_columns(prompts, count):
    rows, width = prompts.shape
    slab = width // count
    if slab % 128:
        columns = [prompts[:, k * slab : (k + 1) * slab] for k in range(count)]
        my_dev = lax.axis_index("dev")
        return [pick(columns, my_dev ^ k) for k in range(count)]
    return pl.pallas_call(
        functools.partial(split_kernel, slab),
        out_shape=[jax.ShapeDtypeStruct((rows, slab), prompts.dtype)] * count,
        in_specs=[in_hbm],
        out_specs=[in_vmem] * count,
        scratch_shapes=[pltpu.SemaphoreType.DMA((count,))],
        compiler_params=pltpu.CompilerParams(vmem_limit_bytes=8 * mib),
        cost_estimate=pl.CostEstimate(
            flops=10**10, bytes_accessed=4 * 10**7, transcendentals=0
        ),
        name="split_columns",
    )(pltpu.with_memory_space_constraint(prompts, pltpu.HBM))


def fill_tables(
    dev_count, side_count, bucket, cap_slots, length_ref, slot_ref, request_ref, inverse_ref,
    target_ref, cos_ref, sin_ref, spot_ref, to_ref, place_ref, local_ref, position_ref,
):
    my_dev, my_side = lax.axis_index("dev"), lax.axis_index("side")
    requests = request_ref[...]
    lane_rows, lanes = requests.shape
    tok_rows = bucket * dev_count // 2
    per_row = lanes // tok_rows
    half_bucket = bucket // 2
    half_rows = dev_count * half_bucket
    group_rows = 2 * half_rows
    before = lax.broadcasted_iota(jnp.int32, (lanes, lanes), 0)
    after = lax.broadcasted_iota(jnp.int32, (lanes, lanes), 1)
    below = jnp.where(before < after, 1.0, 0.0)
    near = jnp.where((before < after) & (before // tok_rows == after // tok_rows), 1.0, 0.0)
    scan = jnp.concatenate([below, jnp.ones_like(below)], axis=1).astype(bf16)
    lower = lax.broadcasted_iota(jnp.int32, (lane_rows, lane_rows), 0)
    upper = lax.broadcasted_iota(jnp.int32, (lane_rows, lane_rows), 1)
    rows_before = jnp.where(upper < lower, 1.0, 0.0)
    position = jnp.zeros(requests.shape, f32)
    slot = jnp.zeros(requests.shape, jnp.int32)
    for q in range(slot_ref.shape[0]):
        hit = requests == q
        ranks = jnp.dot(
            jnp.where(hit, 1.0, 0.0).astype(bf16), scan, preferred_element_type=f32
        )
        earlier = jnp.dot(rows_before, ranks[:, lanes:], preferred_element_type=f32)
        start = length_ref[q].astype(f32)
        position = jnp.where(hit, ranks[:, :lanes] + earlier + start, position)
        slot = jnp.where(hit, slot_ref[q], slot)
    group = lax.div(slot, cap_slots)
    rank = jnp.zeros(requests.shape, f32)
    for g in range(dev_count):
        hit = group == g
        ranks = jnp.dot(
            jnp.where(hit, 1.0, 0.0).astype(bf16), near.astype(bf16), preferred_element_type=f32
        )
        rank = jnp.where(hit, ranks, rank)
    block = lax.broadcasted_iota(jnp.int32, requests.shape, 0) * per_row + lax.div(
        lax.broadcasted_iota(jnp.int32, requests.shape, 1), tok_rows
    )
    rank = rank.astype(jnp.int32)
    which = lax.div(rank, half_bucket)
    place = lax.div(block, side_count) * half_bucket + lax.rem(rank, half_bucket)
    to_ref[...] = (which * dev_count + (group ^ my_dev)) * half_rows + place
    place = which * half_rows + place
    place_ref[...] = jnp.where(group == my_dev, place, -1)
    local_ref[...] = (slot - my_dev * cap_slots + 1).astype(f32)
    position_ref[...] = position
    lane_block = lax.div(lax.broadcasted_iota(jnp.int32, (1, lanes), 1), tok_rows)
    ids = lax.broadcasted_iota(jnp.int32, (group_rows, 1), 0)

    def find(dev, side):
        held = dev * side_count + side
        return pl.ds(lax.div(held, per_row), 1), lane_block == lax.rem(held, per_row)

    targets = []
    for k in range(dev_count):
        held = (my_dev ^ k) * side_count + my_side
        row = jnp.broadcast_to(to_ref[pl.ds(lax.div(held, per_row), 1), :], (8, lanes))
        start = lax.rem(lanes - tok_rows * lax.rem(held, per_row), lanes)
        targets.append(pltpu.roll(row, start, 1)[:1, :tok_rows])
    for k in range(0, dev_count, per_row):
        target_ref[:, k * tok_rows : k * tok_rows + lanes] = jnp.concatenate(
            targets[k : k + per_row], axis=1
        )
    found = jnp.zeros((group_rows, lanes), f32)
    for d in range(dev_count):
        row, inside = find(d, my_side)
        found = jnp.where((place_ref[row, :] == ids) & inside, position_ref[row, :], found)
    angles = jnp.sum(found, axis=1, keepdims=True) * inverse_ref[...]
    cos_ref[...] = jnp.cos(angles)
    sin_ref[...] = jnp.sin(angles)
    for k in range(side_count):
        total = jnp.zeros((8, group_rows), f32)
        for d in range(dev_count):
            row, inside = find(d, my_side ^ k)
            chosen = jnp.where((place_ref[row, :] == ids) & inside, 1.0, 0.0).astype(bf16)
            values = jnp.broadcast_to(local_ref[row, :], (8, lanes)).astype(bf16)
            total = total + lax.dot_general(
                values, chosen, (((1,), (1,)), ((), ())), preferred_element_type=f32
            )
        spot_ref[:, k * group_rows : (k + 1) * group_rows] = total[:1].astype(jnp.int32)


def prepare_kernel(
    scale, steps, layout, inverse_ref, length_hbm, slot_hbm, request_hbm, query_hbm, absorb_hbm,
    cache_hbm, fresh_hbm, value_hbm, out_hbm, full_ref, top_ref, sum_ref, mix_ref, live_ref, target_ref,
    cos_ref, sin_ref, spot_ref, value_ref, out_ref, length_ref, slot_ref, request_ref, query_ref,
    absorb_ref, cache_ref, fresh_ref, plain, full, to_ref, place_ref, local_ref, position_ref, sems,
):
    pairs = [
        (length_hbm, length_ref), (slot_hbm, slot_ref), (request_hbm, request_ref),
        (query_hbm, query_ref), (absorb_hbm, absorb_ref), (cache_hbm, cache_ref),
        (fresh_hbm, fresh_ref), (value_hbm, value_ref),
    ]
    parts = sems.shape[0] - len(pairs)
    rows = out_hbm.shape[0] // parts
    for n in range(parts):
        part = pl.ds(n * rows, rows)
        pairs.append((out_hbm.at[part], out_ref.at[part]))
    copies = [pltpu.make_async_copy(*pair, sems.at[n]) for n, pair in enumerate(pairs)]
    for copy in copies:
        copy.start()
    for copy in copies[:3]:
        copy.wait()
    slots, _, context = cache_ref.shape
    heads, nope, lat_width = absorb_ref.shape
    per_head = slots * steps
    fill_tables(
        *layout, slots, length_ref, slot_ref, request_ref, inverse_ref, target_ref, cos_ref,
        sin_ref, spot_ref, to_ref, place_ref, local_ref, position_ref,
    )
    first_slot = lax.axis_index("dev") * slots
    lengths = []
    for s in range(slots):
        length = jnp.int32(0)
        for q in range(slot_ref.shape[0]):
            length = jnp.where(slot_ref[q] == first_slot + s, length_ref[q], length)
        lengths.append(length)
    slot_of = lax.div(lax.broadcasted_iota(jnp.int32, live_ref.shape, 0), steps)
    live = jnp.zeros(live_ref.shape, f32)
    for s in range(slots):
        live = jnp.where((slot_of == s) & (lengths[s] > 0), 1.0, live)
    live_ref[...] = live
    copies[3].wait()
    copies[4].wait()
    for n, here in enumerate(lane_tiles(query_ref.shape[1])):
        plain[n, :, : here.stop - here.start] = query_ref[:, here].astype(f32)
    wide = lane_tiles(full_ref.shape[1])
    for h in range(heads):
        there = pl.ds(h, per_head, stride=heads)
        query = plain[0, there, :].astype(bf16)
        latent = jnp.dot(query, absorb_ref[h], preferred_element_type=f32).astype(bf16).astype(f32)
        here = slice(h * per_head, (h + 1) * per_head)
        for n, lanes in enumerate(lane_tiles(lat_width)):
            full[n, here, :] = latent[:, lanes]
        full[len(wide) - 1, here, :] = plain[1, there, :]
    for n, lanes in enumerate(wide):
        full_ref[:, lanes] = full[n, :, : lanes.stop - lanes.start].astype(bf16)
    key = lax.broadcasted_iota(jnp.int32, (1, context), 1)
    copies[5].wait()
    copies[6].wait()
    late = lax.broadcasted_iota(jnp.int32, (steps * heads, steps), 1)
    late = late > lax.div(lax.broadcasted_iota(jnp.int32, (steps * heads, steps), 0), heads)
    for s in range(slots):
        theres = [pl.ds(s * steps + t, heads, stride=per_head) for t in range(steps)]
        query = jnp.concatenate(
            [
                jnp.concatenate([full[n, there, :] for there in theres], axis=0)[
                    :, : lanes.stop - lanes.start
                ].astype(bf16)
                for n, lanes in enumerate(wide)
            ],
            axis=1,
        )
        rows = cache_ref[s]
        score = jnp.dot(query, rows, preferred_element_type=f32)
        score = jnp.where(key < lengths[s], score * scale, masked_score)
        fresh = fresh_ref[s]
        new = lax.dot_general(
            query, fresh, (((1,), (1,)), ((), ())), preferred_element_type=f32
        )
        new = jnp.where(late, masked_score, new * scale)
        top = jnp.maximum(
            jnp.max(score, axis=1, keepdims=True), jnp.max(new, axis=1, keepdims=True)
        )
        weight = jnp.exp(score - top)
        new = jnp.exp(new - top)
        total = jnp.sum(weight, axis=1, keepdims=True) + jnp.sum(new, axis=1, keepdims=True)
        mix = lax.dot_general(
            weight.astype(bf16), rows[:lat_width, :], (((1,), (1,)), ((), ())),
            preferred_element_type=f32,
        )
        for u in range(steps):
            mix = mix + new[:, u : u + 1].astype(bf16).astype(f32) * fresh[
                u : u + 1, :lat_width
            ].astype(f32)
        lanes = top_ref.shape[1]
        for t in range(steps):
            there = theres[t]
            here = slice(t * heads, (t + 1) * heads)
            top_ref[there, :] = jnp.broadcast_to(top[here], (heads, lanes))
            sum_ref[there, :] = jnp.broadcast_to(total[here], (heads, lanes))
            for n, part in enumerate(lane_tiles(lat_width)):
                mix_ref[n, there, :] = mix[here, part]
    for copy in copies[7:]:
        copy.wait()


def prepare(
    scale, dev_count, side_count, bucket, lengths, request_slot, requests, inverse, queries,
    absorb, cache, fresh, value, out_weight,
):
    slots, steps, heads, width = queries.shape
    kv_width = cache.shape[1]
    lat_width = absorb.shape[2]
    rows = slots * steps * heads
    group_rows = dev_count * bucket
    parts = 8
    lanes = requests.shape[1]
    half = inverse.shape[1]
    shapes = [
        ((rows, kv_width), bf16), ((rows, 128), f32), ((rows, 128), f32),
        ((lat_width // 128, rows, 128), f32), ((slots * steps, 128), f32),
        ((1, group_rows // 2 * dev_count), jnp.int32), ((group_rows, half), f32), ((group_rows, half), f32),
        ((1, side_count * group_rows), jnp.int32), (value.shape, bf16), (out_weight.shape, bf16),
    ]
    return pl.pallas_call(
        functools.partial(prepare_kernel, scale, steps, (dev_count, side_count, bucket)),
        out_shape=[jax.ShapeDtypeStruct(*shape) for shape in shapes],
        in_specs=[in_vmem] + [in_hbm] * 9,
        out_specs=[in_vmem] * len(shapes),
        scratch_shapes=[
            pltpu.SMEM(lengths.shape, lengths.dtype),
            pltpu.SMEM(request_slot.shape, request_slot.dtype),
            pltpu.VMEM(requests.shape, requests.dtype),
            pltpu.VMEM((rows, width), queries.dtype),
            pltpu.VMEM(absorb.shape, absorb.dtype),
            pltpu.VMEM(cache.shape, cache.dtype),
            pltpu.VMEM(fresh.shape, fresh.dtype),
            pltpu.VMEM((len(lane_tiles(width)), rows, 128), f32),
            pltpu.VMEM((len(lane_tiles(kv_width)), rows, 128), f32),
            pltpu.VMEM(requests.shape, jnp.int32),
            pltpu.VMEM(requests.shape, jnp.int32),
            pltpu.VMEM(requests.shape, f32),
            pltpu.VMEM(requests.shape, f32),
            pltpu.SemaphoreType.DMA((parts + 8,)),
        ],
        compiler_params=pltpu.CompilerParams(vmem_limit_bytes=prepare_mib * mib),
        cost_estimate=pl.CostEstimate(
            flops=4 * 10**10, bytes_accessed=28 * 10**6, transcendentals=10**5
        ),
        name="prepare",
    )(inverse, lengths, request_slot, requests, queries.reshape(rows, width), absorb, cache, fresh,
      value, out_weight)


def stack_kernel(*refs):
    out_ref = refs[-1]
    rows = refs[0].shape[0]
    for n, ref in enumerate(refs[:-1]):
        k = (len(refs) - 1 - n) % (len(refs) - 1)
        out_ref[k * rows : (k + 1) * rows, :] = ref[...]


def stack_rows(pieces):
    rows, width = pieces[0].shape
    return pl.pallas_call(
        stack_kernel,
        out_shape=jax.ShapeDtypeStruct((len(pieces) * rows, width), bf16),
        in_specs=[in_vmem] * len(pieces),
        out_specs=in_vmem,
        compiler_params=pltpu.CompilerParams(vmem_limit_bytes=8 * mib),
        cost_estimate=pl.CostEstimate(flops=2 * 10**10, bytes_accessed=10**6, transcendentals=0),
        name="stack_rows",
    )(pieces[0], *pieces[:0:-1])


def project_kernel(dev_count, side_count, target_ref, x_ref, *refs):
    my_side = lax.axis_index("side")
    weight_refs = refs[:side_count]
    out_refs = refs[side_count:-2]
    slab_weight, rows = refs[-2:]
    tok_rows = x_ref.shape[0] // dev_count
    full = slab_weight.shape[1] // 128
    if side_count > 1:
        shard = slab_weight.shape[0] // side_count
        for k in range(side_count):
            first = pl.multiple_of((my_side ^ k) * shard, 16)
            tiles, rest = load_packed(weight_refs[k], shard)
            for n, tile in enumerate(tiles):
                slab_weight[pl.ds(first, shard), n * 128 : (n + 1) * 128] = tile
            slab_weight[pl.ds(first, shard), full * 128 :] = rest
    slab = slab_weight[...] if side_count > 1 else weight_refs[0][...]
    raw = jnp.dot(x_ref[...], slab, preferred_element_type=f32).astype(bf16)
    rows[...] = raw
    target = target_ref[...]
    half_rows = tok_rows
    step = min(4, 2 * dev_count)
    for j in range(0, 2 * dev_count, step):
        ids = lax.broadcasted_iota(jnp.int32, (step * half_rows, target.shape[1]), 0)
        route = jnp.where(ids + j * half_rows == target, 1.0, 0.0).astype(bf16)
        placed = jnp.dot(route, rows[...], preferred_element_type=f32)
        for n in range(step):
            store_packed(out_refs[j + n], placed[n * half_rows : (n + 1) * half_rows])


def project(x_rows, weights, target, width, dev_count):
    tok_rows, slab = x_rows.shape[0] // dev_count, x_rows.shape[1]
    return pl.pallas_call(
        functools.partial(project_kernel, dev_count, len(weights)),
        out_shape=[
            jax.ShapeDtypeStruct(
                (packed_rows(tok_rows, width), 128), f32 if j % dev_count == 0 else bf16
            )
            for j in range(2 * dev_count)
        ],
        in_specs=[in_vmem] * (2 + len(weights)),
        out_specs=[in_vmem] * (2 * dev_count),
        scratch_shapes=[
            pltpu.VMEM((slab, width), bf16),
            pltpu.VMEM((target.shape[1], width), bf16),
        ],
        compiler_params=pltpu.CompilerParams(vmem_limit_bytes=20 * mib),
        name="project",
    )(target, x_rows, *weights)


def finish_kernel(which, gain_ref, cos_ref, sin_ref, *refs):
    parts, out_ref = refs[:-1], refs[-1]
    rows, half = cos_ref.shape[0] // 2, cos_ref.shape[1]
    mine = slice(which * rows, (which + 1) * rows)
    total = parts[0][...].astype(f32)
    for part in parts[1:]:
        total = total + part[...].astype(f32)
    tiles, rest = load_packed(total, rows)
    latent = jnp.concatenate(tiles, axis=1)
    spread = jnp.mean(latent * latent, axis=1, keepdims=True)
    latent = latent * lax.rsqrt(spread + 1e-06) * gain_ref[...]
    first, second = rest[:, :half], rest[:, half:]
    cosine, sine = cos_ref[mine, :], sin_ref[mine, :]
    store_packed(
        out_ref,
        jnp.concatenate(
            [latent, first * cosine - second * sine, second * cosine + first * sine], axis=1
        ),
    )


def finish(parts, gain, cosine, sine, which):
    return pl.pallas_call(
        functools.partial(finish_kernel, which),
        out_shape=jax.ShapeDtypeStruct(parts[0].shape, bf16),
        in_specs=[in_vmem] * (3 + len(parts)),
        out_specs=in_vmem,
        compiler_params=pltpu.CompilerParams(vmem_limit_bytes=8 * mib),
        name="finish_rows",
    )(gain, cosine, sine, *parts)


def piece_order(count):
    return [0, 1, *range(3, count, 2), *range(2, count, 2)]


def take_keys(keys, pieces, lat_width):
    rows = keys.shape[0] // len(pieces)
    for n, piece in zip(piece_order(len(pieces)), pieces):
        tiles, rest = load_packed(piece, rows)
        there = slice(n * rows, (n + 1) * rows)
        for j, tile in enumerate(tiles):
            keys[there, j * 128 : (j + 1) * 128] = tile
        keys[there, lat_width:] = rest


def merge(layout, which, mine, query_ref, slot_ref, top_ref, sum_ref, mix_ref, keys):
    scale, cap_slots, steps, half_rows = layout
    lat_width = mix_ref.shape[0] * mix_ref.shape[2]
    row = lax.broadcasted_iota(jnp.int32, (mine.stop - mine.start, 1), 0)
    row_slot = (row // steps) % cap_slots
    query = query_ref[mine, :]
    score = lax.dot_general(
        query, keys[...], (((1,), (1,)), ((), ())), preferred_element_type=f32
    )
    count = slot_ref.shape[1]
    part = half_rows
    slots = jnp.concatenate(
        [slot_ref[:, n + which * part : n + (which + 1) * part] for n in range(0, count, 2 * part)],
        axis=1,
    )
    score = jnp.where(slots == row_slot + 1, score * scale, masked_score)
    top_held = top_ref[mine, :1]
    top = jnp.maximum(top_held, jnp.max(score, axis=1, keepdims=True))
    held = jnp.exp(top_held - top)
    weight = jnp.exp(score - top)
    total = sum_ref[mine, :1] * held + jnp.sum(weight, axis=1, keepdims=True)
    mix = jnp.dot(weight.astype(bf16), keys[:, :lat_width], preferred_element_type=f32)
    mix_held = jnp.concatenate([mix_ref[n, mine, :] for n in range(mix_ref.shape[0])], axis=1)
    return top, total, mix_held * held + mix


def absorb_kernel(layout, which, query_ref, slot_ref, top_ref, sum_ref, mix_ref, *refs):
    pieces, (new_top, new_sum, new_mix, keys) = refs[:-4], refs[-4:]
    take_keys(keys, pieces, mix_ref.shape[0] * mix_ref.shape[2])
    rows, lanes = top_ref.shape
    step = rows // 2
    for first in range(0, rows, step):
        mine = slice(first, first + step)
        top, total, mix = merge(
            layout, which, mine, query_ref, slot_ref, top_ref, sum_ref, mix_ref, keys
        )
        new_top[mine, :] = jnp.broadcast_to(top, (step, lanes))
        new_sum[mine, :] = jnp.broadcast_to(total, (step, lanes))
        for n, part in enumerate(lane_tiles(mix.shape[1])):
            new_mix[n, mine, :] = mix[:, part]


def absorb(layout, which, query, row_slot, top, total, mix, pieces):
    return pl.pallas_call(
        functools.partial(absorb_kernel, layout, which),
        out_shape=[jax.ShapeDtypeStruct(x.shape, f32) for x in (top, total, mix)],
        in_specs=[in_vmem] * (5 + len(pieces)),
        out_specs=[in_vmem] * 3,
        scratch_shapes=[pltpu.VMEM((row_slot.shape[1] // 2, query.shape[1]), bf16)],
        compiler_params=pltpu.CompilerParams(vmem_limit_bytes=10 * mib),
        cost_estimate=pl.CostEstimate(flops=2 * 10**9, bytes_accessed=10**6, transcendentals=0),
        name="absorb",
    )(query, row_slot, top, total, mix, *pieces)


def attend_kernel(
    layout, which, first_head, heads, query_ref, slot_ref, top_ref, sum_ref, mix_ref, live_ref,
    value_ref, *refs
):
    pieces, out_ref, keys = refs[:-2], refs[-2], refs[-1]
    per_head = layout[1] * layout[2]
    take_keys(keys, pieces, mix_ref.shape[0] * mix_ref.shape[2])
    mine = slice(first_head * per_head, (first_head + heads) * per_head)
    _, total, mix = merge(
        layout, which, mine, query_ref, slot_ref, top_ref, sum_ref, mix_ref, keys
    )
    latent = (mix / total).astype(bf16)
    live = live_ref[:, :1]
    width = value_ref.shape[2]
    for h in range(heads):
        mixed = latent[h * per_head : (h + 1) * per_head, :]
        value = jnp.dot(mixed, value_ref[first_head + h], preferred_element_type=f32) * live
        out_ref[:, h * width : (h + 1) * width] = value.astype(bf16)


def attend(layout, which, query, row_slot, top, total, mix, live, value, pieces, first_head, heads):
    return pl.pallas_call(
        functools.partial(attend_kernel, layout, which, first_head, heads),
        out_shape=jax.ShapeDtypeStruct((live.shape[0], heads * value.shape[2]), bf16),
        in_specs=[in_vmem] * (7 + len(pieces)),
        out_specs=in_vmem,
        scratch_shapes=[pltpu.VMEM((row_slot.shape[1] // 2, query.shape[1]), bf16)],
        compiler_params=pltpu.CompilerParams(vmem_limit_bytes=10 * mib),
        name="attend",
    )(query, row_slot, top, total, mix, live, value, *pieces)


def output_kernel(dev_count, side_count, start, last, *refs):
    my_dev, my_side = lax.axis_index("dev"), lax.axis_index("side")
    head_refs = refs[:dev_count]
    weight_ref = refs[dev_count]
    earlier_ref = refs[dev_count + 1] if start else None
    out_refs = refs[dev_count + 1 + (start > 0) : -1]
    held = refs[-1]
    rows, depth = head_refs[0].shape
    per_side = dev_count // side_count
    for j in range(dev_count):
        group = my_dev ^ j
        place = (lax.div(group, per_side) ^ my_side) * per_side + lax.rem(group, per_side)
        held[pl.ds(pl.multiple_of(place * rows, 16), rows), :] = head_refs[j][...]
    columns = weight_ref.shape[1]
    tile = 256 if columns % 256 == 0 else columns
    side_rows = rows * per_side
    for n in range(columns // tile):
        here = slice(n * tile, (n + 1) * tile)
        product = jnp.dot(
            held[...], weight_ref[start : start + depth, here],
            preferred_element_type=f32,
        )
        if start:
            product = product + earlier_ref[:, here]
        if not last:
            out_refs[0][:, here] = product
        else:
            for k in range(side_count):
                out_refs[k][:, here] = product[k * side_rows : (k + 1) * side_rows, :].astype(
                    out_refs[k].dtype
                )


def output_product(head_pieces, weight, side_count, earlier, start, last):
    dev_count = len(head_pieces)
    rows, depth = head_pieces[0].shape
    columns = weight.shape[1]
    side_rows = rows * dev_count // side_count
    if not last:
        shapes = [((rows * dev_count, columns), f32)]
    else:
        shapes = [((side_rows, columns), f32 if k == 0 else bf16) for k in range(side_count)]
    earlier = [] if earlier is None else [earlier]
    return pl.pallas_call(
        functools.partial(output_kernel, dev_count, side_count, start, last),
        out_shape=[jax.ShapeDtypeStruct(*shape) for shape in shapes],
        in_specs=[in_vmem] * (dev_count + 1 + len(earlier)),
        out_specs=[in_vmem] * len(shapes),
        scratch_shapes=[pltpu.VMEM((dev_count * rows, depth), bf16)],
        compiler_params=pltpu.CompilerParams(vmem_limit_bytes=10 * mib),
        name="output_product",
    )(*head_pieces, weight, *earlier)


def on_device(
    prompts,
    latent_weight,
    latent_gain,
    row_request,
    context_len,
    request_slot,
    latent_cache,
    new_latent,
    queries,
    key_absorb,
    value_absorb,
    out_weight,
):
    dev_count = lax.axis_size("dev")
    side_count = lax.axis_size("side")
    tok_rows, model_width = prompts.shape
    shard_rows, kv_width = latent_weight.shape
    lat_width = latent_gain.shape[0]
    nope_width = value_absorb.shape[2]
    rope_width = kv_width - lat_width
    cap_slots, ctx_len, _ = latent_cache.shape
    step_count = new_latent.shape[1]
    bucket_rows = 2 * tok_rows // dev_count
    group_rows = dev_count * bucket_rows
    slab = model_width // dev_count

    x_pieces = list(split_columns(prompts, dev_count))
    packs = shard_rows % 32 == 0
    x_pieces[0], own_weight = lax.optimization_barrier((x_pieces[0], latent_weight))
    weights = [pack_weight(own_weight) if packs else own_weight] + [None] * (side_count - 1)
    for k in range(2, side_count, 2):
        weights[k] = swap(weights[0], "side", k)
    for k in sorted(range(1, dev_count), reverse=True):
        x_pieces[k] = swap(x_pieces[k], "dev", k)

    score_scale = queries.shape[-1] ** (-0.5)
    half = rope_width // 2
    inverse = 1.0 / 10000.0 ** (jnp.arange(half, dtype=f32) * (2.0 / rope_width))
    lengths, x_pieces[0] = lax.optimization_barrier((context_len, x_pieces[0]))
    (
        query_full, top_held, sum_held, mix_held, live, target, cosine, sine, row_slot,
        value_here, out_here,
    ) = prepare(
        score_scale, dev_count, side_count, bucket_rows, lengths, request_slot,
        row_request.reshape(-1, 128), inverse.reshape(1, -1), queries, key_absorb,
        jnp.swapaxes(latent_cache, 1, 2), new_latent, value_absorb, out_weight,
    )

    weights[0::2], top_held = lax.optimization_barrier((weights[0::2], top_held))
    for k in range(0, side_count, 2):
        weights[k + 1] = swap(weights[k], "side", 1)
    if not packs:
        my_side = lax.axis_index("side")
        held = jnp.zeros((side_count, shard_rows, kv_width), bf16)
        for k in range(side_count):
            held = lax.dynamic_update_slice(held, weights[k][None], (my_side ^ k, 0, 0))
        weights = [held.reshape(slab, kv_width)]

    routed = project(stack_rows(x_pieces), weights, target, kv_width, dev_count)
    layout = (score_scale, cap_slots, step_count, group_rows // 2)
    state = top_held, sum_held, mix_held
    for which in range(2):
        half = list(routed[which * dev_count : (which + 1) * dev_count])
        for k in sorted(range(1, dev_count), reverse=True):
            half[k] = swap(half[k], "dev", k)
        latent_rows = finish(half[:1] + half[:0:-1], latent_gain.reshape(1, -1), cosine, sine, which)
        pieces = [
            swap(latent_rows, "side", k) if k else latent_rows for k in piece_order(side_count)
        ]
        if which == 0:
            state = absorb(layout, which, query_full, row_slot, *state, pieces)
    product, first_head, head_count = None, 0, value_absorb.shape[0]
    for part_heads in (head_count // 2, head_count // 2):
        head_out = attend(
            layout, 1, query_full, row_slot, *state, live, value_here, pieces, first_head,
            part_heads,
        )
        heads = [head_out] + [None] * (dev_count - 1)
        for k in sorted(range(1, dev_count), reverse=True):
            if k == 1 or k % 2 == 0:
                heads[k] = swap(head_out, "dev", k)
        for k in range(3, dev_count, 2):
            heads[k] = swap(heads[k - 1], "dev", 1)
        start, first_head = first_head * nope_width, first_head + part_heads
        products = output_product(
            heads, out_here, side_count, product, start, first_head == head_count
        )
        product = products[0]
    result = products[0]
    for k in piece_order(side_count)[:0:-1]:
        result = result + swap(products[k], "side", k).astype(f32)
    return result.astype(bf16)


def solution(mesh):
    placed = (
        P(("rep", "dev", "side"), None),
        P(("dev", "side"), None),
        P(),
        P("rep"),
        P("rep"),
        P("rep"),
        P(("rep", "dev"), None, None),
        P(("rep", "dev"), None, None),
        P(("rep", "dev"), None, "side", None),
        P("side", None, None),
        P("side", None, None),
        P("side", "dev"),
    )
    return jax.shard_map(
        on_device, mesh=mesh, in_specs=placed, out_specs=P(("rep", "side"), "dev"), check_vma=False
    )
```
